32 devices in a mesh: groups: 2 (over y), streams: 4 (over z), heads: 2 (over x), sub: 2 (over core).
Axes of the slice: x: 2, y: 2, z: 4, core: 2. Of those that a mesh axis runs over, the one named last changes fastest.
Arguments:
- inputs: bfloat16 [4, 1024, 3584], P(None, ('groups', 'streams', 'sub')), parts along dimension 1, may hold values from -6 to 6
- input_norm_gain: float32 [3584], replicated, may hold values from 0.1 to 1.9
- projection_weight: bfloat16 [3584, 4608], P(None, 'heads'), may hold values from -0.09375 to 0.09375
- projection_bias: float32 [4608], P('heads'), may hold values from -3 to 3
- speaker: int32 [1024, 1], P(('groups', 'streams', 'sub')), parts along dimension 0, may hold values from 0 to 31; in each aligned block of 64 rows (0 to 63, 64 to 127, ...) at most 2 rows name the same one
- speaker_adapter_slot: int32 [64], P('groups'), parts along dimension 0, may hold values from 0 to 31, each once
- cache_fill_length: int32 [1024], P(('groups', 'streams', 'sub')), parts along dimension 0, may hold values from 1 to 32, as said below
- rotated_key_cache: bfloat16 [1024, 32, 512], P(('groups', 'streams', 'sub'), None, 'heads'), parts along dimension 0
- value_cache_rows: bfloat16 [1024, 32, 512], P(('groups', 'streams', 'sub'), None, 'heads'), parts along dimension 0, may hold values from -6 to 6
- adapter_down_maps: bfloat16 [64, 3584, 128], P(('groups', 'streams', 'sub'), 'heads'), parts along dimension 0, may hold values from -0.09375 to 0.09375
- adapter_query_up: bfloat16 [64, 64, 3584], P(('groups', 'streams', 'sub'), None, 'heads'), parts along dimension 0, may hold values from -0.75 to 0.75
- adapter_value_up: bfloat16 [64, 64, 512], P(('groups', 'streams', 'sub'), None, 'heads'), parts along dimension 0, may hold values from -0.75 to 0.75
- flow_decoder_owner: int32 [1024, 1], P(('groups', 'streams', 'sub')), parts along dimension 0, may hold values from 0 to 7; in each aligned block of 64 rows (0 to 63, 64 to 127, ...) at most 16 rows name the same one
Outputs:
- flow_input: bfloat16 [16, 128, 4, 3584], P(('groups', 'streams', 'sub'), None, None, 'heads'), parts along dimension 0
The draws below stay inside these ranges and needn't reach their ends.
There are 2 independent parts, one for each index of `groups`. The reference program is written for one: setup_inputs(seed, part) draws one part's arguments, and reference() takes and returns one part's arrays. A program takes and returns all parts, laid end to end along the dimension named above; an argument that names none is the same for every part. Nothing has to cross between parts.
Inputs may be any that keep to these rules, and one draw needn't show every extreme that they name: In the streams of one device no speaker appears more than 2 times. `speaker_adapter_slot`: each speaker has its own slot; slot j is held by device j // 4 of the stream axes. `cache_fill_length`: the first stream of every device has a full cache. `flow_decoder_owner`: no owner gets more than 16 streams from one device.
All inputs are finite; a program needn't handle non-finite values.
Results may differ from the reference program's by a relative error of at most 0.0055.
The reference program's roundings to bfloat16 on the way count: a program that leaves them out, or rounds other values in their place, can miss the bound.
Values may be sent and summed in bfloat16 or wider, within the bound.
No kernel may reach another device: no remote copies, remote signals or barrier semaphores. Data moves between devices by JAX's collectives and lax.ppermute only.
A program may use at most 128 MiB of HBM per device.

```python
import math
import jax
import jax.numpy as jnp
import numpy as np
from jax import lax

MODEL_WIDTH = 3584
QUERY_HEADS = 28
KEY_VALUE_HEADS = 4
HEAD_WIDTH = 128
ADAPTER_RANK = 64
STEPS = 4
MOST = 2
ROWS = 64
CACHE = 32
LANES = 8
STREAMS = 512
SPEAKER_SLOTS = 32
FMOST = 16


def draw_cache_fill_length(key, part):
    key = jax.random.fold_in(key, 1)
    lengths = jax.random.randint(key, (STREAMS,), 1, CACHE + 1, dtype=jnp.int32)
    position = jnp.arange(STREAMS, dtype=jnp.int32)
    return jnp.where(position % ROWS == 0, CACHE, lengths).astype(jnp.int32)


def draw_rotated_key_cache(key, part):
    key = jax.random.fold_in(key, 2)
    array_extent = (STREAMS, CACHE, KEY_VALUE_HEADS * HEAD_WIDTH)
    values = jax.random.normal(key, array_extent, jnp.float32)
    return values.astype(jnp.bfloat16)


def level_of(rng, shape, split, smallest, high):
    def one(dim, parts):
        steps = jax.random.uniform(jax.random.fold_in(jax.random.fold_in(rng, 6), dim), (parts,), jnp.float32, smallest / len(split), high / len(split))
        return jnp.repeat(jnp.exp(steps), shape[dim] // parts).reshape((-1,) + (1,) * (len(shape) - dim - 1))

    loudness = one(*split[0])
    for cut in split[1:]:
        loudness = loudness * one(*cut)
    return loudness


def routed_block(own_key, own, number, rows, count, top, most, slope):
    ranking = jax.random.permutation(own_key, count)
    crowded, ordinary = portions_of(count, rows * top, most, slope, True), portions_of(count, rows * top, most, slope, False)
    places = jnp.arange(count)

    def named(sizes, turn):
        used = int((sizes > 0).sum())
        fixed = max(1, used // 4)
        shifted = fixed + (places - fixed + turn * (used - fixed)) % max(1, count - fixed)
        return jnp.zeros((count,), jnp.int32).at[ranking[jnp.where(places < fixed, places, shifted)]].set(jnp.asarray(sizes, jnp.int32))

    sizes = jnp.where(number % 4 == 0, named(crowded, number // 4), named(ordinary, number - number // 4 - 1))
    mixed = jax.random.permutation(jax.random.fold_in(own, 3), count)
    source_of, sink = mixed[0:count // 2 * 2:2], mixed[1:count // 2 * 2:2]
    margin = jnp.minimum(sizes[source_of] - 1, most - sizes[sink]) // 2
    margin = jnp.where((source_of == ranking[0]) | (sink == ranking[0]) | (sizes[sink] == 0), 0, jnp.maximum(margin, 0))
    shifted = jax.random.randint(jax.random.fold_in(own, 4), (count // 2,), 0, 1 << 20) % (margin + 1)
    sizes = sizes.at[source_of].add(-shifted).at[sink].add(shifted)
    members = jnp.searchsorted(jnp.cumsum(sizes), jnp.arange(rows * top), side="right").astype(jnp.int32)
    listing = members.reshape(top, rows).T
    listing = listing[jax.random.permutation(jax.random.fold_in(own, 1), rows)]
    turn = jax.random.randint(jax.random.fold_in(own, 2), (rows, 1), 0, top)
    return jnp.take_along_axis(listing, (jnp.arange(top)[None, :] + turn) % top, axis=1)


def portions_of(amount, total, most, skew, full):
    portions = [(1 << 20) // math.isqrt(grade ** skew) + 1 for grade in range(1, amount + 1)]
    largest = most if full else min(most, max(-(-total // amount), total * portions[0] // sum(portions)))
    least = 1 if total - largest >= amount - 1 else 0
    counts, rest = [largest] + [least] * (amount - 1), total - largest - least * (amount - 1)
    while rest > 0:
        movable = [i for i in range(1, amount) if counts[i] < largest] or [i for i in range(1, amount) if counts[i] < most]
        pool, remaining = sum([portions[i] for i in movable]), rest
        for i in movable:
            extra = min(most - counts[i], max(1, remaining * portions[i] // pool), rest)
            counts[i] = counts[i] + extra
            rest = rest - extra
    return np.array(counts)


def normal_values(key, dims, scale, most, split=(), kind=jnp.bfloat16):
    result = jax.random.normal(key, dims, jnp.float32) * scale
    if len(split) > 0:
        result = level_of(key, dims, split, -0.22, 0.18) * result
    return jnp.clip(result, min=-most, max=most).astype(kind)


def setup_inputs(seed: int = 0, part: int = 0) -> dict:
    arg_keys = jax.random.split(jax.random.key(seed), 14)
    part_splits = jax.random.split(jax.random.fold_in(arg_keys[13], part), 14)
    inputs = normal_values(part_splits[0], (STEPS, STREAMS, MODEL_WIDTH), 1.0, 6.0, ((1, 8),))
    input_norm_gain = jnp.clip(1.0 + 0.18 * jax.random.normal(arg_keys[1], (MODEL_WIDTH,), jnp.float32), 0.1, 1.9)
    projection_weight = normal_values(arg_keys[2], (MODEL_WIDTH, (QUERY_HEADS + 2 * KEY_VALUE_HEADS) * HEAD_WIDTH), MODEL_WIDTH ** -0.5, 0.09375, ((1, 2),))
    projection_bias = normal_values(arg_keys[3], ((QUERY_HEADS + 2 * KEY_VALUE_HEADS) * HEAD_WIDTH,), 0.5, 3.0, ((0, 2),), jnp.float32)
    speaker_keys = jax.random.split(jax.random.fold_in(part_splits[4], 1), STREAMS // ROWS)
    speaker_turns = jax.random.permutation(jax.random.fold_in(part_splits[4], 3), STREAMS // ROWS)
    speaker = jax.vmap(lambda own, number: routed_block(jax.random.fold_in(part_splits[4], 2), own, number, ROWS, SPEAKER_SLOTS, 1, MOST, 2))(speaker_keys, speaker_turns).reshape((STREAMS, 1))
    speaker_adapter_slot = jax.random.permutation(part_splits[5], SPEAKER_SLOTS).astype(jnp.int32)
    cache_fill_length = draw_cache_fill_length(jax.random.fold_in(jax.random.fold_in(arg_keys[13], part), 71), part)
    rotated_key_cache = draw_rotated_key_cache(jax.random.fold_in(jax.random.fold_in(arg_keys[13], part), 71), part)
    value_cache_rows = normal_values(part_splits[8], (STREAMS, CACHE, KEY_VALUE_HEADS * HEAD_WIDTH), 1.0, 6.0, ((0, 8), (2, 2)))
    adapter_down_maps = normal_values(part_splits[9], (SPEAKER_SLOTS, MODEL_WIDTH, 2 * ADAPTER_RANK), MODEL_WIDTH ** -0.5, 0.09375, ((0, 8), (1, 2)))
    adapter_query_up = normal_values(part_splits[10], (SPEAKER_SLOTS, ADAPTER_RANK, QUERY_HEADS * HEAD_WIDTH), ADAPTER_RANK ** -0.5, 0.75, ((0, 8), (2, 2)))
    adapter_value_up = normal_values(part_splits[11], (SPEAKER_SLOTS, ADAPTER_RANK, KEY_VALUE_HEADS * HEAD_WIDTH), ADAPTER_RANK ** -0.5, 0.75, ((0, 8), (2, 2)))
    flow_decoder_owner_keys = jax.random.split(jax.random.fold_in(part_splits[12], 1), STREAMS // ROWS)
    flow_decoder_owner_turns = jax.random.permutation(jax.random.fold_in(part_splits[12], 3), STREAMS // ROWS)
    flow_decoder_owner = jax.vmap(lambda own, number: routed_block(jax.random.fold_in(part_splits[12], 2), own, number, ROWS, LANES, 1, FMOST, 1))(flow_decoder_owner_keys, flow_decoder_owner_turns).reshape((STREAMS, 1))
    return dict(inputs=inputs, input_norm_gain=input_norm_gain, projection_weight=projection_weight, projection_bias=projection_bias, speaker=speaker, speaker_adapter_slot=speaker_adapter_slot, cache_fill_length=cache_fill_length, rotated_key_cache=rotated_key_cache, value_cache_rows=value_cache_rows, adapter_down_maps=adapter_down_maps, adapter_query_up=adapter_query_up, adapter_value_up=adapter_value_up, flow_decoder_owner=flow_decoder_owner)


def rms_normed(inputs, gain):
    values = inputs.astype(jnp.float32)
    mean_sq = lax.optimization_barrier(jnp.mean(values * values, axis=-1, keepdims=True))
    return (values * lax.rsqrt(mean_sq + 1e-06) * gain.astype(jnp.float32)).astype(jnp.bfloat16)

def rotate(vectors, cosine, sine_part):
    half = vectors.shape[-1] // 2
    first = vectors[..., :half]
    second = vectors[..., half:]
    return jnp.concatenate([first * cosine - second * sine_part, second * cosine + first * sine_part], axis=-1)

def angles(lengths, steps_count, half):
    position = (lengths[None, :] + jnp.arange(steps_count, dtype=jnp.int32)[:, None]).astype(jnp.float32)
    freq = jnp.exp(jnp.arange(half, dtype=jnp.float32) * (-math.log(1000000.0) / half))
    return position[..., None] * freq

def attend(queries, new_keys, new_values, rotated_key_cache, value_cache_rows, lengths):
    steps_count, rows, groups, per_group, head_dim = queries.shape
    cache_count = rotated_key_cache.shape[1]
    keys_all = jnp.concatenate([rotated_key_cache.reshape(rows, cache_count, groups, head_dim), jnp.transpose(new_keys, (1, 0, 2, 3))], axis=1)
    values_all = jnp.concatenate([value_cache_rows.reshape(rows, cache_count, groups, head_dim), jnp.transpose(new_values, (1, 0, 2, 3))], axis=1)
    scores = jnp.einsum('trgqd,rcgd->rgtqc', queries.astype(jnp.float32), keys_all.astype(jnp.float32)) * head_dim ** (-0.5)
    column = jnp.arange(cache_count + steps_count, dtype=jnp.int32)
    step_index = jnp.arange(steps_count, dtype=jnp.int32)
    in_cache = column[None, None, :] < lengths[:, None, None]
    fresh = (column[None, :] - cache_count <= step_index[:, None]) & (column[None, :] >= cache_count)
    allowed = jnp.where(column[None, None, :] < cache_count, in_cache, fresh[None, :, :])
    scores = jnp.where(allowed[:, None, :, None, :], scores, -1e+30)
    peak = lax.optimization_barrier(jnp.max(scores, axis=-1, keepdims=True))
    expo = jnp.exp(scores - peak)
    weights = (expo / lax.optimization_barrier(jnp.sum(expo, axis=-1, keepdims=True))).astype(jnp.bfloat16)
    context = jnp.einsum('rgtqc,rcgd->trgqd', weights.astype(jnp.float32), values_all.astype(jnp.float32))
    return context.astype(jnp.bfloat16).reshape(steps_count, rows, groups * per_group * head_dim)

def reference(inputs, input_norm_gain, projection_weight, projection_bias, speaker, speaker_adapter_slot, cache_fill_length, rotated_key_cache, value_cache_rows, adapter_down_maps, adapter_query_up, adapter_value_up, flow_decoder_owner):
    groups = KEY_VALUE_HEADS
    per_group = QUERY_HEADS // KEY_VALUE_HEADS
    query_columns = QUERY_HEADS * HEAD_WIDTH
    value_columns = KEY_VALUE_HEADS * HEAD_WIDTH
    normed = rms_normed(inputs, input_norm_gain)
    qkv = jnp.dot(normed.reshape(STEPS * STREAMS, MODEL_WIDTH), projection_weight, preferred_element_type=jnp.float32) + projection_bias.astype(jnp.float32)
    qkv = qkv.reshape(STEPS, STREAMS, groups, per_group + 2, HEAD_WIDTH)
    slots = speaker_adapter_slot[speaker[:, 0]].astype(jnp.int32)
    blocks_in = jnp.transpose(normed.reshape(STEPS, LANES, ROWS, MODEL_WIDTH), (1, 0, 2, 3))

    def adapt(pair):
        block_rows, block_slot_list = pair
        down_projected = adapter_down_maps[block_slot_list].astype(jnp.float32)
        adapter_latent = jnp.einsum('trd,rde->tre', block_rows.astype(jnp.float32), down_projected).astype(jnp.bfloat16)
        adapter_latent = lax.optimization_barrier(adapter_latent).astype(jnp.float32)
        query_up_weight = adapter_query_up[block_slot_list].astype(jnp.float32)
        value_up_weight = adapter_value_up[block_slot_list].astype(jnp.float32)
        query_adapter_delta = jnp.einsum('azi,zib->azb', adapter_latent[..., :ADAPTER_RANK], query_up_weight).astype(jnp.bfloat16)
        value_adapter_delta = jnp.einsum('azi,zib->azb', adapter_latent[..., ADAPTER_RANK:], value_up_weight).astype(jnp.bfloat16)
        return (query_adapter_delta, value_adapter_delta)
    query_adapter_delta, value_adapter_delta = lax.map(adapt, (blocks_in, slots.reshape(LANES, ROWS)))
    query_adapter_delta = jnp.transpose(query_adapter_delta, (1, 0, 2, 3)).reshape(STEPS, STREAMS, query_columns).astype(jnp.float32)
    value_adapter_delta = jnp.transpose(value_adapter_delta, (1, 0, 2, 3)).reshape(STEPS, STREAMS, value_columns).astype(jnp.float32)
    angle = angles(cache_fill_length, STEPS, HEAD_WIDTH // 2)
    cosine = jnp.cos(angle)
    sine_part = jnp.sin(angle)
    queries = qkv[..., :per_group, :] + query_adapter_delta.reshape(STEPS, STREAMS, groups, per_group, HEAD_WIDTH)
    queries = rotate(queries, cosine[:, :, None, None, :], sine_part[:, :, None, None, :]).astype(jnp.bfloat16)
    new_keys = rotate(qkv[..., per_group, :], cosine[:, :, None, :], sine_part[:, :, None, :]).astype(jnp.bfloat16)
    new_values = (qkv[..., per_group + 1, :] + value_adapter_delta.reshape(STEPS, STREAMS, groups, HEAD_WIDTH)).astype(jnp.bfloat16)
    context = attend(queries, new_keys, new_values, rotated_key_cache, value_cache_rows, cache_fill_length)
    owner = flow_decoder_owner[:, 0]
    blocked = owner.reshape(LANES, ROWS)
    order = jnp.arange(ROWS, dtype=jnp.int32)
    earlier = (blocked[:, :, None] == blocked[:, None, :]) & (order[None, None, :] < order[None, :, None])
    rank = lax.optimization_barrier(jnp.sum(earlier.astype(jnp.int32), axis=2)).reshape(STREAMS)
    source = jnp.arange(STREAMS, dtype=jnp.int32) // ROWS
    place = (source * FMOST + rank).astype(jnp.int32)
    flow = jnp.zeros((LANES, LANES * FMOST, STEPS, QUERY_HEADS * HEAD_WIDTH), jnp.bfloat16)
    return flow.at[owner, place].set(jnp.transpose(context, (1, 0, 2)))
```

```python
import math

import jax
import jax.numpy as jnp
from jax import lax
from jax.sharding import PartitionSpec as P

QUERY_HEADS = 28
KEY_VALUE_HEADS = 4
HEAD_WIDTH = 128
ADAPTER_RANK = 64
MOST = 2


def rms_normed(inputs, gain):
    values = inputs.astype(jnp.float32)
    mean_sq = jnp.mean(values * values, axis=-1, keepdims=True)
    return (values * lax.rsqrt(mean_sq + 1e-06) * gain).astype(jnp.bfloat16)


def rotate(vectors, cosine, sine_part):
    half = vectors.shape[-1] // 2
    first = vectors[..., :half]
    second = vectors[..., half:]
    return jnp.concatenate(
        [first * cosine - second * sine_part, second * cosine + first * sine_part], axis=-1
    )


def angles(lengths, steps_count, half):
    position = (lengths[None, :] + jnp.arange(steps_count, dtype=jnp.int32)[:, None]).astype(
        jnp.float32
    )
    freq = jnp.exp(jnp.arange(half, dtype=jnp.float32) * (-math.log(1000000.0) / half))
    return position[..., None] * freq


def attend(queries, new_keys, new_values, rotated_key_cache, value_cache_rows, lengths):
    steps_count, rows, groups, per_group, head_dim = queries.shape
    cache_count = rotated_key_cache.shape[1]
    keys_all = jnp.concatenate(
        [
            rotated_key_cache.reshape(rows, cache_count, groups, head_dim),
            jnp.transpose(new_keys, (1, 0, 2, 3)),
        ],
        axis=1,
    )
    values_all = jnp.concatenate(
        [
            value_cache_rows.reshape(rows, cache_count, groups, head_dim),
            jnp.transpose(new_values, (1, 0, 2, 3)),
        ],
        axis=1,
    )
    scores = jnp.einsum(
        "trgqd,rcgd->rgtqc", queries, keys_all, preferred_element_type=jnp.float32
    ) * head_dim ** (-0.5)
    column = jnp.arange(cache_count + steps_count, dtype=jnp.int32)
    step_index = jnp.arange(steps_count, dtype=jnp.int32)
    in_cache = column[None, None, :] < lengths[:, None, None]
    fresh = (column[None, :] - cache_count <= step_index[:, None]) & (
        column[None, :] >= cache_count
    )
    allowed = jnp.where(column[None, None, :] < cache_count, in_cache, fresh[None, :, :])
    scores = jnp.where(allowed[:, None, :, None, :], scores, -1e30)
    peak = jnp.max(scores, axis=-1, keepdims=True)
    expo = jnp.exp(scores - peak)
    weights = (expo / jnp.sum(expo, axis=-1, keepdims=True)).astype(jnp.bfloat16)
    context = jnp.einsum(
        "rgtqc,rcgd->trgqd", weights, values_all, preferred_element_type=jnp.float32
    )
    return context.astype(jnp.bfloat16).reshape(steps_count, rows, groups * per_group * head_dim)


def ranks_within(labels):
    count = labels.shape[0]
    order = jnp.arange(count, dtype=jnp.int32)
    earlier = (labels[:, None] == labels[None, :]) & (order[None, :] < order[:, None])
    return jnp.sum(earlier.astype(jnp.int32), axis=1)


LANE_AXES = ("streams", "sub")


def exchange(blocks):
    count = len(blocks)
    landed = [blocks[0]]
    for shift in range(1, count):
        pairs = [(lane, lane ^ shift) for lane in range(count)]
        landed.append(lax.ppermute(blocks[shift], LANE_AXES, pairs))
    return landed


def summed_over_heads(partial):
    count = lax.axis_size("heads")
    total = partial
    for shift in range(1, count):
        pairs = [(place, (place + shift) % count) for place in range(count)]
        total = total + lax.ppermute(partial, "heads", pairs)
    return total


def selector(places, total):
    return (jnp.arange(total, dtype=jnp.int32)[:, None] == places[None, :]).astype(jnp.bfloat16)


def on_device(
    inputs,
    input_norm_gain,
    projection_weight,
    projection_bias,
    speaker,
    speaker_adapter_slot,
    cache_fill_length,
    rotated_key_cache,
    value_cache_rows,
    adapter_down_maps,
    adapter_query_up,
    adapter_value_up,
    flow_decoder_owner,
):
    steps_count, rows, width = inputs.shape
    lanes = lax.axis_size(("streams", "sub"))
    sliced_rows = adapter_down_maps.shape[1]
    query_columns = adapter_query_up.shape[2]
    value_columns = adapter_value_up.shape[2]
    delta_cols = query_columns + value_columns
    groups = value_columns // HEAD_WIDTH
    per_group = QUERY_HEADS // KEY_VALUE_HEADS
    replica_local_slots = adapter_down_maps.shape[0]
    speakers_all = speaker_adapter_slot.shape[0]
    send_slots = speakers_all * MOST
    normed = rms_normed(inputs, input_norm_gain)
    qkv = (
        jnp.dot(
            normed.reshape(steps_count * rows, width),
            projection_weight,
            preferred_element_type=jnp.float32,
        )
        + projection_bias
    )
    qkv = qkv.reshape(steps_count, rows, groups, per_group + 2, HEAD_WIDTH)
    match = speaker[:, 0][:, None] == jnp.arange(speakers_all, dtype=jnp.int32)[None, :]
    slots = jnp.sum(jnp.where(match, speaker_adapter_slot[None, :], 0), axis=1)
    lane = lax.axis_index(LANE_AXES)
    slots = slots ^ (lane * replica_local_slots)
    places = slots * MOST + ranks_within(slots)
    pick = selector(places, send_slots)
    own_cols = lax.dynamic_slice_in_dim(
        normed, lax.axis_index("heads") * sliced_rows, sliced_rows, 2
    )
    outgoing = jnp.einsum("jr,trd->jtd", pick, own_cols, preferred_element_type=jnp.float32).astype(
        jnp.bfloat16
    )
    outgoing = outgoing.reshape(lanes, replica_local_slots * MOST, steps_count, sliced_rows)
    arrived = jnp.stack(exchange([outgoing[shift] for shift in range(lanes)]))
    items = arrived.shape[2]
    regrouped_rows = arrived.reshape(lanes, replica_local_slots, MOST, items, sliced_rows)
    partial_latent = jnp.einsum(
        "zqyhc,qcx->zqyhx", regrouped_rows, adapter_down_maps, preferred_element_type=jnp.float32
    )
    adapter_latent = summed_over_heads(partial_latent).astype(jnp.bfloat16)
    query_adapter_delta = jnp.einsum(
        "xrpzq,rqw->xrpzw",
        adapter_latent[..., :ADAPTER_RANK],
        adapter_query_up,
        preferred_element_type=jnp.float32,
    )
    value_adapter_delta = jnp.einsum(
        "xrpzq,rqw->xrpzw",
        adapter_latent[..., ADAPTER_RANK:],
        adapter_value_up,
        preferred_element_type=jnp.float32,
    )
    joined = jnp.concatenate([query_adapter_delta, value_adapter_delta], axis=-1).astype(
        jnp.bfloat16
    )
    joined = joined.reshape(lanes, replica_local_slots * MOST, items, delta_cols)
    returned = jnp.stack(exchange([joined[shift] for shift in range(lanes)]))
    returned = returned.reshape(send_slots, steps_count, delta_cols)
    gathered = jnp.einsum("jr,jtc->trc", pick, returned, preferred_element_type=jnp.float32)
    angle = angles(cache_fill_length, steps_count, HEAD_WIDTH // 2)
    cosine = jnp.cos(angle)
    sine_part = jnp.sin(angle)
    queries = qkv[..., :per_group, :] + gathered[..., :query_columns].reshape(
        steps_count, rows, groups, per_group, HEAD_WIDTH
    )
    queries = rotate(queries, cosine[:, :, None, None, :], sine_part[:, :, None, None, :]).astype(
        jnp.bfloat16
    )
    new_keys = rotate(
        qkv[..., per_group, :], cosine[:, :, None, :], sine_part[:, :, None, :]
    ).astype(jnp.bfloat16)
    new_values = (
        qkv[..., per_group + 1, :]
        + gathered[..., query_columns:].reshape(steps_count, rows, groups, HEAD_WIDTH)
    ).astype(jnp.bfloat16)
    context = attend(
        queries, new_keys, new_values, rotated_key_cache, value_cache_rows, cache_fill_length
    )
    fmost = max(2, (2 * rows + lanes - 1) // lanes)
    owner = flow_decoder_owner[:, 0] ^ lane
    flow_places = owner * fmost + ranks_within(owner)
    flow_pick = selector(flow_places, lanes * fmost)
    packed = jnp.einsum(
        "jr,trc->jtc", flow_pick, context, preferred_element_type=jnp.float32
    ).astype(jnp.bfloat16)
    packed = packed.reshape(lanes, fmost, steps_count, query_columns)
    landed = exchange([packed[shift] for shift in range(lanes)])
    flow = jnp.zeros((lanes * fmost, steps_count, query_columns), jnp.bfloat16)
    for shift in range(lanes):
        flow = lax.dynamic_update_slice_in_dim(flow, landed[shift], (lane ^ shift) * fmost, 0)
    return flow[None]


def solution(mesh):
    placed = (
        P(None, ("groups", "streams", "sub"), None),
        P(),
        P(None, "heads"),
        P("heads"),
        P(("groups", "streams", "sub"), None),
        P("groups"),
        P(("groups", "streams", "sub")),
        P(("groups", "streams", "sub"), None, "heads"),
        P(("groups", "streams", "sub"), None, "heads"),
        P(("groups", "streams", "sub"), "heads", None),
        P(("groups", "streams", "sub"), None, "heads"),
        P(("groups", "streams", "sub"), None, "heads"),
        P(("groups", "streams", "sub"), None),
    )
    return jax.shard_map(
        on_device,
        mesh=mesh,
        in_specs=placed,
        out_specs=P(("groups", "streams", "sub"), None, None, "heads"),
        check_vma=False,
    )
```

```python
import functools
import math

import jax
import jax.numpy as jnp
from jax import lax
from jax.experimental import pallas as pl
from jax.experimental.pallas import tpu as pltpu
from jax.sharding import PartitionSpec as P

QUERY_HEADS = 28
KEY_VALUE_HEADS = 4
HEAD_WIDTH = 128
ADAPTER_RANK = 64
MOST = 2
PER_GROUP = QUERY_HEADS // KEY_VALUE_HEADS
LANE_AXES = ("streams", "sub")
BATCH = 8
VMEM = pl.BlockSpec(memory_space=pltpu.VMEM)
MIB = 1 << 20


def iota(shape, dim):
    return lax.broadcasted_iota(jnp.int32, shape, dim)


def as_column(row):
    count = row.shape[1]
    square = (count, count)
    same = iota(square, 0) == iota(square, 1)
    return jnp.sum(jnp.where(same, jnp.broadcast_to(row, square), 0), axis=1, keepdims=True)


def ranked(labels, most):
    count = labels.shape[1]
    square = (count, count)
    earlier = (as_column(labels) == labels) & (iota(square, 0) < iota(square, 1))
    return labels * most + jnp.sum(earlier.astype(jnp.int32), axis=0, keepdims=True)


def slot_places(speaker, table, lane_base):
    speakers_all = table.shape[1]
    rows = speaker.shape[1]
    match = iota((speakers_all, rows), 0) == speaker
    slots = jnp.sum(jnp.where(match, as_column(table), 0), axis=0, keepdims=True)
    return ranked(slots ^ lane_base, MOST)


def lane_index():
    return lax.axis_index("streams") * lax.axis_size("sub") + lax.axis_index("sub")


def pack_kernel(steps, rows, local_slots, aliased, *refs):
    speaker_ref, table_ref, gain_ref, x_ref = refs[:4]
    normed_ref = refs[4 + aliased]
    message_refs = refs[5 + aliased :]
    width = x_ref.shape[1]
    sliced = message_refs[0].shape[1]
    per_message = message_refs[0].shape[0]
    spots = per_message // steps

    def one(index, carry):
        span = pl.ds(pl.multiple_of(index * 16, 16), 16)
        values = x_ref[span, :].astype(jnp.float32)
        mean_sq = jnp.sum(values * values, axis=1, keepdims=True) * (1.0 / width)
        normed = values * lax.rsqrt(mean_sq + 1e-06) * gain_ref[...]
        normed_ref[span, :] = normed.astype(jnp.bfloat16)
        return carry

    lax.fori_loop(0, steps * rows // 16, one, 0)
    places = slot_places(speaker_ref[...], table_ref[...], lane_index() * local_slots)
    total = len(message_refs) * per_message
    shape = (total, steps * rows)
    out_row = iota(shape, 0)
    wanted = out_row // per_message * spots + out_row % spots
    out_step = out_row % per_message // spots
    places = jnp.concatenate([places] * steps, axis=1)
    pick = (wanted == places) & (out_step == iota(shape, 1) // rows)
    pick = pick.astype(jnp.float32).astype(jnp.bfloat16)
    begin = pl.multiple_of(lax.axis_index("heads") * sliced, 128)
    own = normed_ref[:, pl.ds(begin, sliced)]
    packed = jnp.dot(pick, own, preferred_element_type=jnp.float32).astype(jnp.bfloat16)
    for number, message_ref in enumerate(message_refs):
        message_ref[...] = packed[number * per_message : (number + 1) * per_message]


def row_slots(shape, spots):
    return iota(shape, 0) % spots // MOST


def down_kernel(lanes, spots, *refs):
    message_refs, map_refs, partial_ref = refs[:lanes], refs[lanes:-1], refs[-1]
    rows = jnp.concatenate([ref[...] for ref in message_refs], axis=0)
    local_slots = map_refs[0].shape[0]
    own_slot = row_slots(partial_ref.shape, spots)
    total = jnp.zeros(partial_ref.shape, jnp.float32)
    for number, map_ref in enumerate(map_refs):
        for slot in range(local_slots):
            part = jnp.dot(rows, map_ref[slot], preferred_element_type=jnp.float32)
            total = jnp.where(own_slot == number * local_slots + slot, part, total)
    partial_ref[...] = total


def up_kernel(heads, subs, spots, groups, split, *refs):
    partial_refs = refs[:heads]
    query_refs = refs[heads : heads + subs]
    value_refs = refs[heads + subs : heads + 2 * subs]
    message_refs = refs[heads + 2 * subs :]
    total = partial_refs[0][...]
    for ref in partial_refs[1:]:
        total = total + ref[...]
    latent = total.astype(jnp.bfloat16).astype(jnp.float32)
    own_slot = row_slots(latent.shape, spots)
    column = iota(latent.shape, 1) // ADAPTER_RANK
    local = query_refs[0].shape[0]
    turned = pltpu.roll(latent, ADAPTER_RANK, 1)
    low = iota(latent.shape, 1) < ADAPTER_RANK
    query_pair = jnp.where(low, latent, turned)
    value_pair = jnp.where(low, turned, latent)

    def expanded(pair, number):
        pieces = []
        for block in range(local // latent.shape[1]):
            slot = number * (local // ADAPTER_RANK) + block * 2
            kept = jnp.where(own_slot == slot + column, pair, 0.0)
            pieces.append(kept.astype(jnp.bfloat16))
        return jnp.concatenate(pieces, axis=1)

    def product(pair, map_refs):
        result = None
        for number, ref in enumerate(map_refs):
            part = jnp.dot(
                expanded(pair, number), ref[...], preferred_element_type=jnp.float32
            )
            result = part if result is None else result + part
        return result.astype(jnp.bfloat16)

    queries = product(query_pair, query_refs)
    values = product(value_pair, value_refs)
    query_width = queries.shape[1] // groups
    value_width = values.shape[1] // groups
    block_width = query_width + value_width
    per_message = message_refs[0].shape[0]
    lanes = latent.shape[0] // per_message
    for lane in range(lanes):
        span = slice(lane * per_message, (lane + 1) * per_message)
        for group in range(groups):
            ref = message_refs[group * lanes + lane] if split else message_refs[lane]
            begin = 0 if split else group * block_width
            ref[:, begin : begin + query_width] = queries[
                span, group * query_width : (group + 1) * query_width
            ]
            ref[:, begin + query_width : begin + block_width] = values[
                span, group * value_width : (group + 1) * value_width
            ]


def attend_kernel(steps, rows, cache, lanes, flow_lanes, chunks, local_slots, *refs):
    speaker_ref, table_ref, owner_ref, length_ref = refs[:4]
    cos_ref, sin_ref, qkv_ref, key_ref, value_ref = refs[4:9]
    delta_refs = refs[9 : 9 + chunks * lanes]
    message_refs = refs[9 + chunks * lanes : 9 + chunks * lanes + flow_lanes]
    delta_ref, context_ref, bias_ref = refs[9 + chunks * lanes + flow_lanes :]
    chunk_steps = steps // chunks
    per_message = delta_refs[0].shape[0]
    spots = per_message // chunk_steps
    query_width = PER_GROUP * HEAD_WIDTH
    lane = lane_index()

    places = slot_places(speaker_ref[...], table_ref[...], lane * local_slots)
    column = as_column(places)
    column = jnp.concatenate([column] * chunk_steps, axis=0)
    shape = (chunk_steps * rows, lanes * per_message)
    out_row = iota(shape, 1)
    wanted = out_row // per_message * spots + out_row % spots
    pick = (wanted == column) & (out_row % per_message // spots == iota(shape, 0) // rows)
    pick = pick.astype(jnp.float32).astype(jnp.bfloat16)
    for chunk in range(chunks):
        block = [ref[...] for ref in delta_refs[chunk * lanes : (chunk + 1) * lanes]]
        begin = chunk * chunk_steps * rows
        delta_ref[begin : begin + chunk_steps * rows, :] = jnp.dot(
            pick, jnp.concatenate(block, axis=0), preferred_element_type=jnp.float32
        )

    wide = (rows, BATCH * cache)
    lengths = as_column(length_ref[...])
    slot_column = iota(wide, 1)
    allowed = (slot_column // cache == iota(wide, 0) % BATCH) & (slot_column % cache < lengths)
    bias_ref[...] = jnp.where(allowed, 0.0, -1e30)
    fresh = (steps, BATCH, steps * BATCH)
    fresh_column = iota(fresh, 2)
    fresh_allowed = (fresh_column % BATCH == iota(fresh, 1)) & (
        fresh_column // BATCH <= iota(fresh, 0)
    )
    fresh_bias = jnp.where(fresh_allowed, 0.0, -1e30)
    scale = HEAD_WIDTH ** (-0.5)
    transposed = (((1,), (1,)), ((), ()))

    def batch(index, carry):
        first = pl.multiple_of(index * BATCH, BATCH)
        query_tiles, key_tiles, value_tiles = [], [], []
        for step in range(steps):
            span = pl.ds(pl.multiple_of(step * rows + first, BATCH), BATCH)
            cosine, sine_part = cos_ref[span, :], sin_ref[span, :]

            def rotated(values):
                return values * cosine + pltpu.roll(values, HEAD_WIDTH // 2, 1) * sine_part

            for head in range(PER_GROUP):
                place = slice(head * HEAD_WIDTH, (head + 1) * HEAD_WIDTH)
                query_tiles.append(rotated(qkv_ref[span, place] + delta_ref[span, place]))
            key_place = slice(query_width, query_width + HEAD_WIDTH)
            value_place = slice(query_width + HEAD_WIDTH, query_width + 2 * HEAD_WIDTH)
            key_tiles.append(rotated(qkv_ref[span, key_place]))
            value_tiles.append(qkv_ref[span, value_place] + delta_ref[span, key_place])
        queries = jnp.concatenate(query_tiles, axis=0).astype(jnp.bfloat16)
        new_keys = jnp.concatenate(key_tiles, axis=0).astype(jnp.bfloat16)
        new_values = jnp.concatenate(value_tiles, axis=0).astype(jnp.bfloat16)
        old_keys = key_ref[pl.ds(first, BATCH)].reshape(BATCH * cache, HEAD_WIDTH)
        old_values = value_ref[pl.ds(first, BATCH)].reshape(BATCH * cache, HEAD_WIDTH)
        old_scores = lax.dot_general(
            queries, old_keys, transposed, preferred_element_type=jnp.float32
        )
        new_scores = lax.dot_general(
            queries, new_keys, transposed, preferred_element_type=jnp.float32
        )
        heads = steps * PER_GROUP
        old_scores = (old_scores * scale).reshape(heads, BATCH, BATCH * cache) + bias_ref[
            pl.ds(first, BATCH), :
        ][None]
        new_scores = (new_scores * scale).reshape(
            steps, PER_GROUP, BATCH, steps * BATCH
        ) + fresh_bias[:, None]
        new_scores = new_scores.reshape(heads, BATCH, steps * BATCH)
        peak = jnp.maximum(
            jnp.max(old_scores, axis=-1, keepdims=True), jnp.max(new_scores, axis=-1, keepdims=True)
        )
        old_scores = jnp.exp(old_scores - peak)
        new_scores = jnp.exp(new_scores - peak)
        share = 1.0 / (
            jnp.sum(old_scores, axis=-1, keepdims=True)
            + jnp.sum(new_scores, axis=-1, keepdims=True)
        )
        old_weights = (old_scores * share).reshape(heads * BATCH, BATCH * cache)
        new_weights = (new_scores * share).reshape(heads * BATCH, steps * BATCH)
        context = jnp.dot(
            old_weights.astype(jnp.bfloat16), old_values, preferred_element_type=jnp.float32
        ) + jnp.dot(
            new_weights.astype(jnp.bfloat16), new_values, preferred_element_type=jnp.float32
        )
        for step in range(steps):
            span = pl.ds(pl.multiple_of(step * rows + first, BATCH), BATCH)
            for head in range(PER_GROUP):
                begin = (step * PER_GROUP + head) * BATCH
                context_ref[span, head * HEAD_WIDTH : (head + 1) * HEAD_WIDTH] = context[
                    begin : begin + BATCH
                ]
        return carry

    lax.fori_loop(0, rows // BATCH, batch, 0)

    most = message_refs[0].shape[0]
    flow_places = ranked(owner_ref[...] ^ lane, most)
    flow_places = jnp.concatenate([flow_places] * steps, axis=1)
    context = context_ref[...].astype(jnp.bfloat16)
    shape = (most * steps, steps * rows)
    out_row = iota(shape, 0)
    same_step = out_row % steps == iota(shape, 1) // rows
    for number, message_ref in enumerate(message_refs):
        pick = (flow_places == number * most + out_row // steps) & same_step
        packed = jnp.dot(
            pick.astype(jnp.float32).astype(jnp.bfloat16),
            context,
            preferred_element_type=jnp.float32,
        )
        message_ref[...] = packed.reshape(most, steps, query_width).astype(jnp.bfloat16)


def place_kernel(flow_lanes, groups, *refs):
    block_refs, out_ref, semaphore = refs[:-2], refs[-2], refs[-1]
    lane = lane_index()
    most, _, width = block_refs[0].shape
    copies = []
    for group in range(groups):
        for number in range(flow_lanes):
            copy = pltpu.make_async_copy(
                block_refs[group * flow_lanes + number],
                out_ref.at[
                    pl.ds((lane ^ number) * most, most), :, pl.ds(group * width, width)
                ],
                semaphore.at[group * flow_lanes + number],
            )
            copy.start()
            copies.append(copy)
    for copy in copies:
        copy.wait()


def traded(blocks, axes):
    landed = list(blocks)
    count = len(blocks)
    order = sorted(range(1, count), key=lambda shift: -(shift ^ (shift >> 1)))
    for shift in order:
        pairs = [(place, place ^ shift) for place in range(count)]
        landed[shift] = lax.ppermute(blocks[shift], axes, pairs)
    return landed


def from_others(block, axis):
    count = lax.axis_size(axis)
    landed = [block]
    for shift in range(1, count):
        pairs = [(place, place ^ shift) for place in range(count)]
        landed.append(lax.ppermute(block, axis, pairs))
    return landed


def cost(flops, size):
    return pl.CostEstimate(flops=int(flops), bytes_accessed=int(size), transcendentals=0)


def on_device(
    inputs,
    input_norm_gain,
    projection_weight,
    projection_bias,
    speaker,
    speaker_adapter_slot,
    cache_fill_length,
    rotated_key_cache,
    value_cache_rows,
    adapter_down_maps,
    adapter_query_up,
    adapter_value_up,
    flow_decoder_owner,
):
    steps, rows, width = inputs.shape
    lanes = lax.axis_size("streams")
    subs = lax.axis_size("sub")
    heads = lax.axis_size("heads")
    flow_lanes = lanes * subs
    local_slots, sliced, _ = adapter_down_maps.shape
    query_columns = adapter_query_up.shape[2]
    value_columns = adapter_value_up.shape[2]
    groups = value_columns // HEAD_WIDTH
    cache = rotated_key_cache.shape[1]
    spots = subs * local_slots * MOST
    chunks = 2
    chunk_steps = steps // chunks
    chunk_rows = chunk_steps * rows
    per_message = chunk_steps * spots
    bf16, f32 = jnp.bfloat16, jnp.float32

    down_maps = from_others(adapter_down_maps, "sub")
    query_maps = from_others(
        adapter_query_up.reshape(local_slots * ADAPTER_RANK, query_columns), "sub"
    )
    value_maps = from_others(
        adapter_value_up.reshape(local_slots * ADAPTER_RANK, value_columns), "sub"
    )

    speaker_row = speaker.reshape(1, rows)
    table_row = speaker_adapter_slot.reshape(1, -1)
    owner_row = flow_decoder_owner.reshape(1, rows)
    length_row = cache_fill_length.reshape(1, rows)
    flat = inputs.reshape(steps * rows, width)
    gain = input_norm_gain.reshape(1, width)

    normed = None
    arrived = []
    for chunk in range(chunks):
        aliased = int(chunk > 0)
        operands = [speaker_row, table_row, gain, flat] + ([normed] if aliased else [])
        whole = lambda shape: pl.BlockSpec(shape, lambda i: (0,) * len(shape))
        half = pl.BlockSpec((chunk_rows, width), lambda i, chunk=chunk: (chunk, 0))
        message = jax.ShapeDtypeStruct((per_message, sliced), bf16)
        normed, *messages = pl.pallas_call(
            functools.partial(pack_kernel, chunk_steps, rows, local_slots, aliased),
            grid=(1,),
            in_specs=[whole(speaker_row.shape), whole(table_row.shape), whole(gain.shape), half]
            + [pl.BlockSpec(memory_space=pl.ANY)] * aliased,
            out_specs=[half] + [whole(message.shape)] * lanes,
            out_shape=[jax.ShapeDtypeStruct((steps * rows, width), bf16)] + [message] * lanes,
            input_output_aliases={4: 0} if aliased else {},
            compiler_params=pltpu.CompilerParams(vmem_limit_bytes=16 * MIB),
            cost_estimate=cost(2 * lanes * per_message * chunk_rows * sliced, 3 * MIB),
            name="norm_and_pack",
        )(*operands)
        arrived.append(traded(messages, "streams"))

    qkv = jnp.dot(normed, projection_weight, preferred_element_type=f32) + projection_bias

    half_width = HEAD_WIDTH // 2
    position = (
        cache_fill_length[None, :] + jnp.arange(steps, dtype=jnp.int32)[:, None]
    ).astype(f32)
    freq = jnp.exp(jnp.arange(half_width, dtype=f32) * (-math.log(1000000.0) / half_width))
    freq = jnp.concatenate([freq, freq])
    angle = position.reshape(steps * rows, 1) * freq
    sign = jnp.where(jnp.arange(HEAD_WIDTH) < half_width, -1.0, 1.0).astype(f32)
    cosine = jnp.cos(angle)
    sine_part = jnp.sin(angle) * sign

    block_width = (PER_GROUP + 1) * HEAD_WIDTH
    returned = []
    for chunk in range(chunks):
        latent = jax.ShapeDtypeStruct((lanes * per_message, 2 * ADAPTER_RANK), f32)
        partial_latent = pl.pallas_call(
            functools.partial(down_kernel, lanes, spots),
            in_specs=[VMEM] * (lanes + subs),
            out_specs=VMEM,
            out_shape=latent,
            compiler_params=pltpu.CompilerParams(vmem_limit_bytes=16 * MIB),
            cost_estimate=cost(
                2 * lanes * per_message * sliced * 128 * subs * local_slots, 4 * MIB
            ),
            name="down",
        )(*arrived[chunk], *down_maps)
        partials = from_others(partial_latent, "heads")
        split = chunk == chunks - 1
        shape = (per_message, block_width if split else groups * block_width)
        message = jax.ShapeDtypeStruct(shape, bf16)
        count = lanes * groups if split else lanes
        messages = pl.pallas_call(
            functools.partial(up_kernel, heads, subs, spots, groups, split),
            in_specs=[VMEM] * (heads + 2 * subs),
            out_specs=[VMEM] * count,
            out_shape=[message] * count,
            compiler_params=pltpu.CompilerParams(vmem_limit_bytes=24 * MIB),
            cost_estimate=cost(
                2 * lanes * per_message * subs * local_slots * 64 * groups * block_width, 3 * MIB
            ),
            name="up",
        )(*partials, *query_maps, *value_maps)
        if split:
            returned.append(
                [
                    traded(messages[group * lanes : (group + 1) * lanes], "streams")
                    for group in range(groups)
                ]
            )
        else:
            returned.append(traded(messages, "streams"))

    flow_most = max(2, (2 * rows + flow_lanes - 1) // flow_lanes)
    query_width = PER_GROUP * HEAD_WIDTH
    landed = []
    for group in range(groups):
        whole = lambda shape: pl.BlockSpec(shape, lambda i: (0,) * len(shape))
        message = jax.ShapeDtypeStruct((flow_most, steps, query_width), bf16)
        column = lambda shape: pl.BlockSpec(shape, lambda i, group=group: (0, group))
        layer = pl.BlockSpec((rows, cache, HEAD_WIDTH), lambda i, group=group: (0, 0, group))
        messages = pl.pallas_call(
            functools.partial(
                attend_kernel, steps, rows, cache, lanes, flow_lanes, chunks, local_slots
            ),
            grid=(1,),
            in_specs=[whole((1, rows)), whole(table_row.shape), whole((1, rows)), whole((1, rows))]
            + [whole(cosine.shape)] * 2
            + [column((steps * rows, (PER_GROUP + 2) * HEAD_WIDTH)), layer, layer]
            + [column((per_message, block_width))] * (lanes * (chunks - 1))
            + [whole((per_message, block_width))] * lanes,
            out_specs=[whole(message.shape)] * flow_lanes,
            out_shape=[message] * flow_lanes,
            scratch_shapes=[
                pltpu.VMEM((steps * rows, block_width), f32),
                pltpu.VMEM((steps * rows, query_width), f32),
                pltpu.VMEM((rows, BATCH * cache), f32),
            ],
            compiler_params=pltpu.CompilerParams(vmem_limit_bytes=24 * MIB),
            cost_estimate=cost(2e9, 4 * MIB),
            name="attend",
        )(
            speaker_row,
            table_row,
            owner_row,
            length_row,
            cosine,
            sine_part,
            qkv,
            rotated_key_cache,
            value_cache_rows,
            *[block for chunk in returned[:-1] for block in chunk],
            *returned[-1][group],
        )
        landed += traded(messages, LANE_AXES)

    flow = pl.pallas_call(
        functools.partial(place_kernel, flow_lanes, groups),
        in_specs=[pl.BlockSpec(memory_space=pl.ANY)] * len(landed),
        out_specs=pl.BlockSpec(memory_space=pl.ANY),
        out_shape=jax.ShapeDtypeStruct((flow_lanes * flow_most, steps, query_columns), bf16),
        scratch_shapes=[pltpu.SemaphoreType.DMA((len(landed),))],
        cost_estimate=cost(0, 4 * MIB),
        name="place",
    )(*landed)
    return flow[None]


def solution(mesh):
    placed = (
        P(None, ("groups", "streams", "sub"), None),
        P(),
        P(None, "heads"),
        P("heads"),
        P(("groups", "streams", "sub"), None),
        P("groups"),
        P(("groups", "streams", "sub")),
        P(("groups", "streams", "sub"), None, "heads"),
        P(("groups", "streams", "sub"), None, "heads"),
        P(("groups", "streams", "sub"), "heads", None),
        P(("groups", "streams", "sub"), None, "heads"),
        P(("groups", "streams", "sub"), None, "heads"),
        P(("groups", "streams", "sub"), None),
    )
    return jax.shard_map(
        on_device,
        mesh=mesh,
        in_specs=placed,
        out_specs=P(("groups", "streams", "sub"), None, None, "heads"),
        check_vma=False,
    )
```

```python
import functools
import math

import jax
import jax.numpy as jnp
from jax import lax
from jax.experimental import pallas as pl
from jax.experimental.pallas import tpu as pltpu
from jax.sharding import PartitionSpec as P

QUERY_HEADS = 28
KEY_VALUE_HEADS = 4
HEAD_WIDTH = 128
ADAPTER_RANK = 64
MOST = 2
PER_GROUP = QUERY_HEADS // KEY_VALUE_HEADS
LANE_AXES = ("streams", "sub")
BATCH = 8
VMEM = pl.BlockSpec(memory_space=pltpu.VMEM)
MIB = 1 << 20


def iota(shape, dim):
    return lax.broadcasted_iota(jnp.int32, shape, dim)


def as_column(row):
    count = row.shape[1]
    square = (count, count)
    same = iota(square, 0) == iota(square, 1)
    return jnp.sum(jnp.where(same, jnp.broadcast_to(row, square), 0), axis=1, keepdims=True)


def ranked(labels, most):
    count = labels.shape[1]
    square = (count, count)
    earlier = (as_column(labels) == labels) & (iota(square, 0) < iota(square, 1))
    return labels * most + jnp.sum(earlier.astype(jnp.int32), axis=0, keepdims=True)


def slot_places(speaker, table, lane_base):
    speakers_all = table.shape[1]
    rows = speaker.shape[1]
    match = iota((speakers_all, rows), 0) == speaker
    slots = jnp.sum(jnp.where(match, as_column(table), 0), axis=0, keepdims=True)
    return ranked(slots ^ lane_base, MOST)


def pack_kernel(steps, rows, flow_most, first, *refs):
    if first:
        speaker_ref, table_ref, owner_ref, gain_ref, x_ref = refs[:5]
        normed_ref, places_ref, message_refs = refs[5], refs[6], refs[7:]
    else:
        places_ref, gain_ref, x_ref, _, normed_ref = refs[:5]
        message_refs = refs[5:]
    width = x_ref.shape[1]
    per_message, sliced = message_refs[0].shape
    spots = per_message // steps
    gain = jnp.concatenate([gain_ref[i : i + 1, :] for i in range(gain_ref.shape[0])], axis=1)

    def one(index, carry):
        span = pl.ds(pl.multiple_of(index * 16, 16), 16)
        values = x_ref[span, :].astype(jnp.float32)
        mean_sq = jnp.sum(values * values, axis=1, keepdims=True) * (1.0 / width)
        normed = values * lax.rsqrt(mean_sq + 1e-06) * gain
        normed_ref[span, :] = normed.astype(jnp.bfloat16)
        return carry

    lax.fori_loop(0, steps * rows // 16, one, 0)
    if first:
        base = lax.axis_index("streams") * (spots // MOST)
        places = slot_places(speaker_ref[...], table_ref[...], base)
        lane = lax.axis_index("streams") * lax.axis_size("sub") + lax.axis_index("sub")
        places_ref[0:1, :] = places
        places_ref[1:2, :] = ranked(owner_ref[...] ^ lane, flow_most)
    else:
        places = places_ref[0:1, :]
    total = len(message_refs) * per_message
    shape = (total, steps * rows)
    out_row = iota(shape, 0)
    wanted = out_row // per_message * spots + out_row % spots
    out_step = out_row % per_message // spots
    places = jnp.concatenate([places] * steps, axis=1)
    pick = (wanted == places) & (out_step == iota(shape, 1) // rows)
    pick = pick.astype(jnp.float32).astype(jnp.bfloat16)
    begin = pl.multiple_of(lax.axis_index("heads") * sliced, 128)
    own = normed_ref[:, pl.ds(begin, sliced)]
    packed = jnp.dot(pick, own, preferred_element_type=jnp.float32).astype(jnp.bfloat16)
    for number, message_ref in enumerate(message_refs):
        message_ref[...] = packed[number * per_message : (number + 1) * per_message]


def row_slots(shape, spots):
    return iota(shape, 0) % spots // MOST


def down_kernel(lanes, spots, *refs):
    message_refs, map_ref, partial_ref = refs[:lanes], refs[-2], refs[-1]
    rows = jnp.concatenate([ref[...] for ref in message_refs], axis=0)
    own_slot = row_slots(partial_ref.shape, spots)
    total = jnp.zeros(partial_ref.shape, jnp.float32)
    for slot in range(map_ref.shape[0]):
        part = jnp.dot(rows, map_ref[slot], preferred_element_type=jnp.float32)
        total = jnp.where(own_slot == slot, part, total)
    partial_ref[...] = total


def up_kernel(heads, spots, *refs):
    partial_refs, query_ref, value_ref = refs[:heads], refs[heads], refs[heads + 1]
    message_refs = refs[heads + 2 :]
    total = partial_refs[0][...]
    for ref in partial_refs[1:]:
        total = total + ref[...]
    latent = total.astype(jnp.bfloat16).astype(jnp.float32)
    own_slot = row_slots(latent.shape, spots)
    column = iota(latent.shape, 1) // ADAPTER_RANK
    turned = pltpu.roll(latent, ADAPTER_RANK, 1)
    low = iota(latent.shape, 1) < ADAPTER_RANK
    query_pair = jnp.where(low, latent, turned)
    value_pair = jnp.where(low, turned, latent)

    def product(pair, map_ref):
        pieces = []
        for slot in range(0, map_ref.shape[0] // ADAPTER_RANK, 2):
            kept = jnp.where(own_slot == slot + column, pair, 0.0)
            pieces.append(kept.astype(jnp.bfloat16))
        wide = jnp.concatenate(pieces, axis=1)
        return jnp.dot(wide, map_ref[...], preferred_element_type=jnp.float32).astype(jnp.bfloat16)

    queries = product(query_pair, query_ref)
    values = product(value_pair, value_ref)
    query_width = queries.shape[1]
    per_message = message_refs[0].shape[0]
    for number, ref in enumerate(message_refs):
        span = slice(number * per_message, (number + 1) * per_message)
        ref[:, :query_width] = queries[span]
        ref[:, query_width:] = values[span]


def attend_kernel(before, steps, rows, cache, groups, lanes, subs, last, *refs):
    places_ref, length_ref, cos_ref, sin_ref, qkv_ref, key_ref, value_ref = refs[:7]
    delta_refs, refs = refs[7 : 7 + lanes], refs[7 + lanes :]
    if before:
        earlier_ref, refs = refs[0], refs[1:]
    if not last:
        fresh_ref, refs = refs[0], refs[1:]
    message_refs = refs[:subs]
    delta_ref, context_ref, bias_ref = refs[subs:]
    per_message = delta_refs[0].shape[0]
    spots = per_message // steps
    query_width = PER_GROUP * HEAD_WIDTH
    block_width = query_width + 2 * HEAD_WIDTH
    known = before + steps
    wide = groups * HEAD_WIDTH

    column = as_column(places_ref[0:1, :])
    column = jnp.concatenate([column] * steps, axis=0)
    shape = (steps * rows, lanes * per_message)
    out_row = iota(shape, 1)
    wanted = out_row // per_message * spots + out_row % spots
    pick = (wanted == column) & (out_row % per_message // spots == iota(shape, 0) // rows)
    pick = pick.astype(jnp.float32).astype(jnp.bfloat16)
    delta_ref[...] = jnp.dot(
        pick,
        jnp.concatenate([ref[...] for ref in delta_refs], axis=0),
        preferred_element_type=jnp.float32,
    )

    shape = (rows, BATCH * cache)
    lengths = as_column(length_ref[...])
    slot_column = iota(shape, 1)
    allowed = (slot_column // cache == iota(shape, 0) % BATCH) & (slot_column % cache < lengths)
    bias_ref[...] = jnp.where(allowed, 0.0, -1e30)
    shape = (steps, BATCH, known * BATCH)
    fresh_column = iota(shape, 2)
    allowed = (fresh_column % BATCH == iota(shape, 1)) & (
        fresh_column // BATCH <= iota(shape, 0) + before
    )
    fresh_bias = jnp.where(allowed, 0.0, -1e30)
    scale = HEAD_WIDTH ** (-0.5)
    transposed = (((1,), (1,)), ((), ()))

    def batch(index, carry):
        first = pl.multiple_of(index * BATCH, BATCH)
        spans = [pl.ds(pl.multiple_of(step * rows + first, BATCH), BATCH) for step in range(steps)]
        past = [pl.ds(pl.multiple_of(step * rows + first, BATCH), BATCH) for step in range(before)]
        for group in range(groups):
            query_tiles, key_tiles, value_tiles = [], [], []
            base = group * block_width
            lane_span = slice(group * HEAD_WIDTH, (group + 1) * HEAD_WIDTH)
            value_span = slice(wide + group * HEAD_WIDTH, wide + (group + 1) * HEAD_WIDTH)
            for span in past:
                key_tiles.append(earlier_ref[span, lane_span])
                value_tiles.append(earlier_ref[span, value_span])
            for span in spans:
                cosine, sine_part = cos_ref[span, :], sin_ref[span, :]

                def rotated(values):
                    return values * cosine + pltpu.roll(values, HEAD_WIDTH // 2, 1) * sine_part

                for head in range(PER_GROUP):
                    begin = head * HEAD_WIDTH
                    from_qkv = slice(base + begin, base + begin + HEAD_WIDTH)
                    begin += group * query_width
                    from_delta = slice(begin, begin + HEAD_WIDTH)
                    query_tiles.append(
                        rotated(qkv_ref[span, from_qkv] + delta_ref[span, from_delta])
                    )
                begin = base + query_width
                key = rotated(qkv_ref[span, begin : begin + HEAD_WIDTH])
                begin += HEAD_WIDTH
                from_delta = groups * query_width + group * HEAD_WIDTH
                value = (
                    qkv_ref[span, begin : begin + HEAD_WIDTH]
                    + delta_ref[span, from_delta : from_delta + HEAD_WIDTH]
                )
                if not last:
                    fresh_ref[span, lane_span] = key
                    fresh_ref[span, value_span] = value
                key_tiles.append(key)
                value_tiles.append(value)
            queries = jnp.concatenate(query_tiles, axis=0).astype(jnp.bfloat16)
            new_keys = jnp.concatenate(key_tiles, axis=0).astype(jnp.bfloat16)
            new_values = jnp.concatenate(value_tiles, axis=0).astype(jnp.bfloat16)
            old_keys = key_ref[pl.ds(first, BATCH), :, lane_span]
            old_keys = old_keys.reshape(BATCH * cache, HEAD_WIDTH)
            old_values = value_ref[pl.ds(first, BATCH), :, lane_span]
            old_values = old_values.reshape(BATCH * cache, HEAD_WIDTH)
            old_scores = lax.dot_general(
                queries, old_keys, transposed, preferred_element_type=jnp.float32
            )
            new_scores = lax.dot_general(
                queries, new_keys, transposed, preferred_element_type=jnp.float32
            )
            heads = steps * PER_GROUP
            old_scores = (old_scores * scale).reshape(heads, BATCH, BATCH * cache) + bias_ref[
                pl.ds(first, BATCH), :
            ][None]
            new_scores = (new_scores * scale).reshape(
                steps, PER_GROUP, BATCH, known * BATCH
            ) + fresh_bias[:, None]
            new_scores = new_scores.reshape(heads, BATCH, known * BATCH)
            peak = jnp.maximum(
                jnp.max(old_scores, axis=-1, keepdims=True),
                jnp.max(new_scores, axis=-1, keepdims=True),
            )
            old_scores = jnp.exp(old_scores - peak)
            new_scores = jnp.exp(new_scores - peak)
            share = 1.0 / (
                jnp.sum(old_scores, axis=-1, keepdims=True)
                + jnp.sum(new_scores, axis=-1, keepdims=True)
            )
            old_weights = (old_scores * share).reshape(heads * BATCH, BATCH * cache)
            new_weights = (new_scores * share).reshape(heads * BATCH, known * BATCH)
            context = jnp.dot(
                old_weights.astype(jnp.bfloat16), old_values, preferred_element_type=jnp.float32
            ) + jnp.dot(
                new_weights.astype(jnp.bfloat16), new_values, preferred_element_type=jnp.float32
            )
            for step, span in enumerate(spans):
                for head in range(PER_GROUP):
                    row = (step * PER_GROUP + head) * BATCH
                    begin = group * query_width + head * HEAD_WIDTH
                    context_ref[span, begin : begin + HEAD_WIDTH] = context[row : row + BATCH]
        return carry

    lax.fori_loop(0, rows // BATCH, batch, 0)

    flow_places = jnp.concatenate([places_ref[1:2, :]] * steps, axis=1)
    context = context_ref[...].astype(jnp.bfloat16)
    count = message_refs[0].shape[0]
    most = count // (lanes * steps)
    shape = (count, steps * rows)
    out_row = iota(shape, 0)
    spot = out_row // steps
    same_step = out_row % steps == iota(shape, 1) // rows
    for number, message_ref in enumerate(message_refs):
        wanted = (spot // most * subs + number) * most + spot % most
        pick = ((flow_places == wanted) & same_step).astype(jnp.float32).astype(jnp.bfloat16)
        message_ref[...] = jnp.dot(
            pick, context, preferred_element_type=jnp.float32
        ).astype(jnp.bfloat16)


def place_kernel(chunks, lanes, subs, most, *refs):
    out_ref = refs[-1]
    steps = out_ref.shape[1]
    chunk_steps = steps // chunks
    block = most * chunk_steps
    per_chunk = subs + lanes - 1
    here = lax.axis_index("streams")
    core = lax.axis_index("sub")
    shape = (chunks * block, chunks * block)
    out_row, in_row = iota(shape, 0), iota(shape, 1)
    step = out_row % steps
    wanted = step // chunk_steps * block + out_row // steps * chunk_steps + step % chunk_steps
    pick = (wanted == in_row).astype(jnp.float32).astype(jnp.bfloat16)
    for number in range(lanes):
        for other in range(subs):
            pieces = []
            for chunk in range(chunks):
                mine = refs[chunk * per_chunk : (chunk + 1) * per_chunk]
                if number == 0:
                    pieces.append(mine[other][...][:block])
                else:
                    landed = mine[subs + number - 1]
                    pieces.append(landed[...][other * block : (other + 1) * block])
            rows = jnp.dot(
                pick, jnp.concatenate(pieces, axis=0), preferred_element_type=jnp.float32
            )
            source = (here ^ number) * subs + (core ^ other)
            out_ref[pl.ds(source * most, most)] = rows.reshape(
                most, steps, rows.shape[1]
            ).astype(jnp.bfloat16)


def traded(blocks, axes):
    landed = list(blocks)
    count = len(blocks)
    order = sorted(range(1, count), key=lambda shift: -(shift ^ (shift >> 1)))
    for shift in order:
        pairs = [(place, place ^ shift) for place in range(count)]
        landed[shift] = lax.ppermute(blocks[shift], axes, pairs)
    return landed


def from_others(block, axis):
    count = lax.axis_size(axis)
    landed = [block]
    for shift in range(1, count):
        pairs = [(place, place ^ shift) for place in range(count)]
        landed.append(lax.ppermute(block, axis, pairs))
    return landed


def cost(flops, size):
    return pl.CostEstimate(flops=int(flops), bytes_accessed=int(size), transcendentals=0)


def on_device(
    inputs,
    input_norm_gain,
    projection_weight,
    projection_bias,
    speaker,
    speaker_adapter_slot,
    cache_fill_length,
    rotated_key_cache,
    value_cache_rows,
    adapter_down_maps,
    adapter_query_up,
    adapter_value_up,
    flow_decoder_owner,
):
    steps, rows, width = inputs.shape
    lanes = lax.axis_size("streams")
    subs = lax.axis_size("sub")
    heads = lax.axis_size("heads")
    flow_lanes = lanes * subs
    local_slots, sliced, _ = adapter_down_maps.shape
    query_columns = adapter_query_up.shape[2]
    value_columns = adapter_value_up.shape[2]
    groups = value_columns // HEAD_WIDTH
    cache = rotated_key_cache.shape[1]
    spots = subs * local_slots * MOST
    chunks = 2
    chunk_steps = steps // chunks
    chunk_rows = chunk_steps * rows
    per_message = chunk_steps * spots
    chip_slots = subs * local_slots
    flow_most = max(2, (2 * rows + flow_lanes - 1) // flow_lanes)
    bf16, f32 = jnp.bfloat16, jnp.float32

    def whole(shape):
        return pl.BlockSpec(shape, lambda i: (0,) * len(shape))

    down_maps = lax.all_gather(adapter_down_maps, "sub", axis=0, tiled=True)
    query_maps = lax.all_gather(
        adapter_query_up.reshape(local_slots * ADAPTER_RANK, query_columns),
        "sub",
        axis=0,
        tiled=True,
    )
    value_maps = lax.all_gather(
        adapter_value_up.reshape(local_slots * ADAPTER_RANK, value_columns),
        "sub",
        axis=0,
        tiled=True,
    )

    flat = inputs.reshape(steps * rows, width)
    gain = input_norm_gain.reshape(width // 128, 128)
    row_block = [
        pl.BlockSpec((chunk_rows, width), lambda i, chunk=chunk: (chunk, 0))
        for chunk in range(chunks)
    ]
    message = jax.ShapeDtypeStruct((per_message, sliced), bf16)
    normed_shape = jax.ShapeDtypeStruct((steps * rows, width), bf16)
    places_shape = jax.ShapeDtypeStruct((8, rows), jnp.int32)
    tables = [
        speaker.reshape(1, rows),
        speaker_adapter_slot.reshape(1, -1),
        flow_decoder_owner.reshape(1, rows),
    ]
    packing = dict(
        grid=(1,),
        compiler_params=pltpu.CompilerParams(vmem_limit_bytes=56 * MIB),
        cost_estimate=cost(2 * lanes * per_message * chunk_rows * sliced, 3 * MIB),
    )
    normed, places, *messages = pl.pallas_call(
        functools.partial(pack_kernel, chunk_steps, rows, flow_most, True),
        in_specs=[whole(table.shape) for table in tables] + [whole(gain.shape), row_block[0]],
        out_specs=[row_block[0], whole(places_shape.shape)] + [whole(message.shape)] * lanes,
        out_shape=[normed_shape, places_shape] + [message] * lanes,
        name="norm_and_pack",
        **packing,
    )(*tables, gain, flat)
    arrived = [traded(messages, "streams")]
    packed = []
    for chunk in range(1, chunks):
        normed, *messages = pl.pallas_call(
            functools.partial(pack_kernel, chunk_steps, rows, flow_most, False),
            in_specs=[whole(places.shape), whole(gain.shape), row_block[chunk]]
            + [pl.BlockSpec(memory_space=pl.ANY)],
            out_specs=[row_block[chunk]] + [whole(message.shape)] * lanes,
            out_shape=[normed_shape] + [message] * lanes,
            input_output_aliases={3: 0},
            name="norm_and_pack_next",
            **packing,
        )(places, gain, flat, normed)
        packed.append(messages)

    qkv = jnp.dot(normed, projection_weight, preferred_element_type=f32) + projection_bias
    qkv, packed = lax.optimization_barrier((qkv, packed))
    arrived += [traded(messages, "streams") for messages in packed]

    half_width = HEAD_WIDTH // 2
    position = jnp.concatenate([cache_fill_length + step for step in range(steps)]).astype(f32)
    freq = jnp.exp(jnp.arange(half_width, dtype=f32) * (-math.log(1000000.0) / half_width))
    freq = jnp.concatenate([freq, freq])
    angle = position[:, None] * freq
    sign = jnp.where(jnp.arange(HEAD_WIDTH) < half_width, -1.0, 1.0).astype(f32)
    cosine = jnp.cos(angle)
    sine_part = jnp.sin(angle) * sign

    returned = []
    for chunk in range(chunks):
        partial_latent = pl.pallas_call(
            functools.partial(down_kernel, lanes, spots),
            in_specs=[VMEM] * (lanes + 1),
            out_specs=VMEM,
            out_shape=jax.ShapeDtypeStruct((lanes * per_message, 2 * ADAPTER_RANK), f32),
            compiler_params=pltpu.CompilerParams(vmem_limit_bytes=16 * MIB),
            cost_estimate=cost(2 * lanes * per_message * sliced * 128 * chip_slots, 4 * MIB),
            name="down",
        )(*arrived[chunk], down_maps)
        partials = from_others(partial_latent, "heads")
        message = jax.ShapeDtypeStruct((per_message, query_columns + value_columns), bf16)
        messages = pl.pallas_call(
            functools.partial(up_kernel, heads, spots),
            in_specs=[VMEM] * (heads + 2),
            out_specs=[VMEM] * lanes,
            out_shape=[message] * lanes,
            compiler_params=pltpu.CompilerParams(vmem_limit_bytes=24 * MIB),
            cost_estimate=cost(
                2 * lanes * per_message * chip_slots * 64 * message.shape[1], 3 * MIB
            ),
            name="up",
        )(*partials, query_maps, value_maps)
        returned.append(traded(messages, "streams"))

    length_row = cache_fill_length.reshape(1, rows)
    block = flow_most * chunk_steps
    earlier = []
    landed = []
    for chunk in range(chunks):
        last = chunk == chunks - 1
        message = jax.ShapeDtypeStruct((lanes * block, query_columns), bf16)
        fresh = jax.ShapeDtypeStruct((chunk_rows, 2 * value_columns), f32)
        rows_of = lambda shape: pl.BlockSpec(shape, lambda i, chunk=chunk: (chunk, 0))
        results = pl.pallas_call(
            functools.partial(
                attend_kernel,
                chunk * chunk_steps,
                chunk_steps,
                rows,
                cache,
                groups,
                lanes,
                subs,
                last,
            ),
            grid=(1,),
            in_specs=[whole(places.shape), whole(length_row.shape)]
            + [rows_of((chunk_rows, HEAD_WIDTH))] * 2
            + [rows_of((chunk_rows, qkv.shape[1]))]
            + [whole(rotated_key_cache.shape)] * 2
            + [whole((per_message, query_columns + value_columns))] * lanes
            + [whole(block_rows.shape) for block_rows in earlier],
            out_specs=[whole(fresh.shape)] * (not last) + [whole(message.shape)] * subs,
            out_shape=[fresh] * (not last) + [message] * subs,
            scratch_shapes=[
                pltpu.VMEM((chunk_rows, query_columns + value_columns), f32),
                pltpu.VMEM((chunk_rows, query_columns), f32),
                pltpu.VMEM((rows, BATCH * cache), f32),
            ],
            compiler_params=pltpu.CompilerParams(vmem_limit_bytes=32 * MIB),
            cost_estimate=cost(2e9, 6 * MIB),
            name="attend",
        )(
            places,
            length_row,
            cosine,
            sine_part,
            qkv,
            rotated_key_cache,
            value_cache_rows,
            *returned[chunk],
            *earlier,
        )
        if not last:
            earlier, results = [results[0]], results[1:]
        parts = [results[0]]
        for shift in range(1, subs):
            pairs = [(core, core ^ shift) for core in range(subs)]
            parts.append(lax.ppermute(results[shift], "sub", pairs))
        joined = [
            jnp.concatenate([part[lane * block : (lane + 1) * block] for part in parts])
            for lane in range(1, lanes)
        ]
        landed += parts + traded([None] + joined, "streams")[1:]

    flow = pl.pallas_call(
        functools.partial(place_kernel, chunks, lanes, subs, flow_most),
        in_specs=[VMEM] * len(landed),
        out_specs=VMEM,
        out_shape=jax.ShapeDtypeStruct((flow_lanes * flow_most, steps, query_columns), bf16),
        compiler_params=pltpu.CompilerParams(vmem_limit_bytes=24 * MIB),
        cost_estimate=cost(0, 4 * MIB),
        name="place",
    )(*landed)
    return flow[None]


def solution(mesh):
    placed = (
        P(None, ("groups", "streams", "sub"), None),
        P(),
        P(None, "heads"),
        P("heads"),
        P(("groups", "streams", "sub"), None),
        P("groups"),
        P(("groups", "streams", "sub")),
        P(("groups", "streams", "sub"), None, "heads"),
        P(("groups", "streams", "sub"), None, "heads"),
        P(("groups", "streams", "sub"), "heads", None),
        P(("groups", "streams", "sub"), None, "heads"),
        P(("groups", "streams", "sub"), None, "heads"),
        P(("groups", "streams", "sub"), None),
    )
    return jax.shard_map(
        on_device,
        mesh=mesh,
        in_specs=placed,
        out_specs=P(("groups", "streams", "sub"), None, None, "heads"),
        check_vma=False,
    )
```

```python
import functools
import math

import jax
import jax.numpy as jnp
from jax import lax
from jax.experimental import pallas as pl
from jax.experimental.pallas import tpu as pltpu
from jax.sharding import PartitionSpec as P

QUERY_HEADS = 28
KEY_VALUE_HEADS = 4
HEAD_WIDTH = 128
ADAPTER_RANK = 64
MOST = 2
PER_GROUP = QUERY_HEADS // KEY_VALUE_HEADS
LANE_AXES = ("streams", "sub")
BATCH = 8
VMEM = pl.BlockSpec(memory_space=pltpu.VMEM)
MIB = 1 << 20


def iota(shape, dim):
    return lax.broadcasted_iota(jnp.int32, shape, dim)


def as_column(row):
    count = row.shape[1]
    square = (count, count)
    same = iota(square, 0) == iota(square, 1)
    return jnp.sum(jnp.where(same, jnp.broadcast_to(row, square), 0), axis=1, keepdims=True)


def ranked(labels, most):
    count = labels.shape[1]
    square = (count, count)
    earlier = (as_column(labels) == labels) & (iota(square, 0) < iota(square, 1))
    return labels * most + jnp.sum(earlier.astype(jnp.int32), axis=0, keepdims=True)


def slot_places(speaker, table, lane_base):
    speakers_all = table.shape[1]
    rows = speaker.shape[1]
    match = iota((speakers_all, rows), 0) == speaker
    slots = jnp.sum(jnp.where(match, as_column(table), 0), axis=0, keepdims=True)
    return ranked(slots ^ lane_base, MOST)


def norm_in_pieces(pieces, begin, x_hbm, gain_hbm, x_buf, gain_buf, semaphores, normed_ref):
    count, width = x_buf.shape
    size = count // pieces
    gain_copy = pltpu.make_async_copy(gain_hbm, gain_buf, semaphores.at[pieces])
    copies = []
    for piece in range(pieces):
        copies.append(
            pltpu.make_async_copy(
                x_hbm.at[pl.ds(begin + piece * size, size)],
                x_buf.at[pl.ds(piece * size, size)],
                semaphores.at[piece],
            )
        )
        copies[-1].start()
        if piece == 0:
            gain_copy.start()
    gain_copy.wait()
    gain = jnp.concatenate([gain_buf[i : i + 1, :] for i in range(gain_buf.shape[0])], axis=1)
    for piece in range(pieces):
        copies[piece].wait()

        def one(index, carry):
            span = pl.ds(pl.multiple_of(piece * size + index * 16, 16), 16)
            values = x_buf[span, :].astype(jnp.float32)
            mean_sq = jnp.sum(values * values, axis=1, keepdims=True) * (1.0 / width)
            normed = values * lax.rsqrt(mean_sq + 1e-06) * gain
            normed_ref[span, :] = normed.astype(jnp.bfloat16)
            return carry

        lax.fori_loop(0, size // 16, one, 0)


def pack_messages(steps, rows, places, normed_ref, message_refs):
    per_message, sliced = message_refs[0].shape
    spots = per_message // steps
    shape = (len(message_refs) * per_message, steps * rows)
    out_row = iota(shape, 0)
    wanted = out_row // per_message * spots + out_row % spots
    out_step = out_row % per_message // spots
    places = jnp.concatenate([places] * steps, axis=1)
    pick = (wanted == places) & (out_step == iota(shape, 1) // rows)
    pick = pick.astype(jnp.float32).astype(jnp.bfloat16)
    begin = pl.multiple_of(lax.axis_index("heads") * sliced, 128)
    own = normed_ref[:, pl.ds(begin, sliced)]
    packed = jnp.dot(pick, own, preferred_element_type=jnp.float32).astype(jnp.bfloat16)
    for number, message_ref in enumerate(message_refs):
        message_ref[...] = packed[number * per_message : (number + 1) * per_message]


def norm_pack_kernel(steps, rows, flow_most, lanes, pieces, *refs):
    table_hbms, gain_hbm, x_hbm = refs[:3], refs[3], refs[4]
    normed_ref, places_ref, message_refs = refs[5], refs[6], refs[7 : 7 + lanes]
    x_buf, gain_buf, *table_bufs, semaphores = refs[7 + lanes :]
    copies = [
        pltpu.make_async_copy(source, target, semaphores.at[pieces + 1 + number])
        for number, (source, target) in enumerate(zip(table_hbms, table_bufs))
    ]
    for copy in copies:
        copy.start()
    norm_in_pieces(pieces, 0, x_hbm, gain_hbm, x_buf, gain_buf, semaphores, normed_ref)
    for copy in copies:
        copy.wait()
    speaker, table, owner = [buffer[...] for buffer in table_bufs]
    core, subs = lax.axis_index("sub"), lax.axis_size("sub")
    spots = message_refs[0].shape[0] // steps
    places = slot_places(speaker, table, lax.axis_index("streams") * (spots // MOST))
    places_ref[0:1, :] = places
    places_ref[1:2, :] = ranked(owner ^ (lax.axis_index("streams") * subs + core), flow_most)
    pack_messages(steps, rows, places, normed_ref, message_refs)


def norm_kernel(begin, pieces, gain_hbm, x_hbm, normed_ref, x_buf, gain_buf, semaphores):
    norm_in_pieces(pieces, begin, x_hbm, gain_hbm, x_buf, gain_buf, semaphores, normed_ref)


def pack_kernel(steps, rows, places_ref, normed_ref, *message_refs):
    pack_messages(steps, rows, places_ref[0:1, :], normed_ref, message_refs)


def project_kernel(chunks, first_row, *refs):
    normed_refs, weight_ref, bias_ref = refs[:chunks], refs[chunks], refs[chunks + 1]
    out_ref, rows_ref = refs[-2:]
    size = normed_refs[0].shape[0]
    step = pl.program_id(0)

    @pl.when(step == 0)
    def _():
        for number, ref in enumerate(normed_refs):
            rows_ref[number * size : (number + 1) * size, :] = ref[...]

    tiles = weight_ref.shape[1] // 128
    bias = [bias_ref[pl.ds(first_row + step * tiles + tile, 1), :] for tile in range(tiles)]
    product = jnp.dot(rows_ref[...], weight_ref[...], preferred_element_type=jnp.float32)
    out_ref[...] = product + jnp.concatenate(bias, axis=1)


def row_slots(shape, spots):
    return iota(shape, 0) % spots // MOST


def down_kernel(lanes, spots, *refs):
    message_refs, map_refs, partial_ref = refs[:lanes], refs[lanes:-1], refs[-1]
    local_slots = map_refs[0].shape[0]
    rows = jnp.concatenate([ref[...] for ref in message_refs], axis=0)
    own_slot = row_slots(partial_ref.shape, spots)
    total = jnp.zeros(partial_ref.shape, jnp.float32)
    for number, map_ref in enumerate(map_refs):
        shift = (lax.axis_index("sub") ^ number) * local_slots
        for slot in range(local_slots):
            part = jnp.dot(rows, map_ref[slot], preferred_element_type=jnp.float32)
            total = jnp.where(own_slot == shift + slot, part, total)
    partial_ref[...] = total


def up_kernel(heads, subs, spots, *refs):
    partial_refs, refs = refs[:heads], refs[heads:]
    query_refs, value_refs, message_refs = refs[:subs], refs[subs : 2 * subs], refs[2 * subs :]
    total = partial_refs[0][...]
    for ref in partial_refs[1:]:
        total = total + ref[...]
    latent = total.astype(jnp.bfloat16).astype(jnp.float32)
    own_slot = row_slots(latent.shape, spots)
    column = iota(latent.shape, 1) // ADAPTER_RANK
    turned = pltpu.roll(latent, ADAPTER_RANK, 1)
    low = iota(latent.shape, 1) < ADAPTER_RANK
    query_pair = jnp.where(low, latent, turned)
    value_pair = jnp.where(low, turned, latent)

    def product(pair, map_refs):
        result = None
        for number, map_ref in enumerate(map_refs):
            local_slots = map_ref.shape[0] // ADAPTER_RANK
            shift = (lax.axis_index("sub") ^ number) * local_slots
            pieces = []
            for slot in range(0, local_slots, 2):
                kept = jnp.where(own_slot == shift + slot + column, pair, 0.0)
                pieces.append(kept.astype(jnp.bfloat16))
            wide = jnp.concatenate(pieces, axis=1)
            part = jnp.dot(wide, map_ref[...], preferred_element_type=jnp.float32)
            result = part if result is None else result + part
        return result.astype(jnp.bfloat16)

    queries = product(query_pair, query_refs)
    values = product(value_pair, value_refs)
    query_width = queries.shape[1]
    per_message = message_refs[0].shape[0]
    for number, ref in enumerate(message_refs):
        span = slice(number * per_message, (number + 1) * per_message)
        ref[:, :query_width] = queries[span]
        ref[:, query_width:] = values[span]


def attend_kernel(before, steps, rows, cache, groups, lanes, subs, last, *refs):
    places_ref, length_ref, cos_ref, sin_ref, key_ref, value_ref = refs[:6]
    qkv_refs, refs = refs[6 : 6 + groups], refs[6 + groups :]
    delta_refs, refs = refs[:lanes], refs[lanes:]
    if before:
        earlier_ref, refs = refs[0], refs[1:]
    if not last:
        fresh_ref, refs = refs[0], refs[1:]
    message_refs = refs[:subs]
    delta_ref, context_ref, bias_ref = refs[subs:]
    per_message = delta_refs[0].shape[0]
    spots = per_message // steps
    query_width = PER_GROUP * HEAD_WIDTH
    known = before + steps
    wide = groups * HEAD_WIDTH

    column = as_column(places_ref[0:1, :])
    column = jnp.concatenate([column] * steps, axis=0)
    shape = (steps * rows, lanes * per_message)
    out_row = iota(shape, 1)
    wanted = out_row // per_message * spots + out_row % spots
    pick = (wanted == column) & (out_row % per_message // spots == iota(shape, 0) // rows)
    pick = pick.astype(jnp.float32).astype(jnp.bfloat16)
    delta_ref[...] = jnp.dot(
        pick,
        jnp.concatenate([ref[...] for ref in delta_refs], axis=0),
        preferred_element_type=jnp.float32,
    )

    shape = (rows, BATCH * cache)
    lengths = as_column(length_ref[...])
    slot_column = iota(shape, 1)
    allowed = (slot_column // cache == iota(shape, 0) % BATCH) & (slot_column % cache < lengths)
    bias_ref[...] = jnp.where(allowed, 0.0, -1e30)
    shape = (steps, BATCH, known * BATCH)
    fresh_column = iota(shape, 2)
    allowed = (fresh_column % BATCH == iota(shape, 1)) & (
        fresh_column // BATCH <= iota(shape, 0) + before
    )
    fresh_bias = jnp.where(allowed, 0.0, -1e30)
    scale = HEAD_WIDTH ** (-0.5)
    transposed = (((1,), (1,)), ((), ()))

    def batch(index, carry):
        first = pl.multiple_of(index * BATCH, BATCH)
        spans = [pl.ds(pl.multiple_of(step * rows + first, BATCH), BATCH) for step in range(steps)]
        past = [pl.ds(pl.multiple_of(step * rows + first, BATCH), BATCH) for step in range(before)]
        for group in range(groups):
            query_tiles, key_tiles, value_tiles = [], [], []
            qkv_ref = qkv_refs[group]
            lane_span = slice(group * HEAD_WIDTH, (group + 1) * HEAD_WIDTH)
            value_span = slice(wide + group * HEAD_WIDTH, wide + (group + 1) * HEAD_WIDTH)
            for span in past:
                key_tiles.append(earlier_ref[span, lane_span])
                value_tiles.append(earlier_ref[span, value_span])
            for span in spans:
                cosine, sine_part = cos_ref[span, :], sin_ref[span, :]

                def rotated(values):
                    return values * cosine + pltpu.roll(values, HEAD_WIDTH // 2, 1) * sine_part

                for head in range(PER_GROUP):
                    begin = head * HEAD_WIDTH
                    from_qkv = slice(begin, begin + HEAD_WIDTH)
                    begin += group * query_width
                    from_delta = slice(begin, begin + HEAD_WIDTH)
                    query_tiles.append(
                        rotated(qkv_ref[span, from_qkv] + delta_ref[span, from_delta])
                    )
                begin = query_width
                key = rotated(qkv_ref[span, begin : begin + HEAD_WIDTH])
                begin += HEAD_WIDTH
                from_delta = groups * query_width + group * HEAD_WIDTH
                value = (
                    qkv_ref[span, begin : begin + HEAD_WIDTH]
                    + delta_ref[span, from_delta : from_delta + HEAD_WIDTH]
                )
                if not last:
                    fresh_ref[span, lane_span] = key
                    fresh_ref[span, value_span] = value
                key_tiles.append(key)
                value_tiles.append(value)
            queries = jnp.concatenate(query_tiles, axis=0).astype(jnp.bfloat16)
            new_keys = jnp.concatenate(key_tiles, axis=0).astype(jnp.bfloat16)
            new_values = jnp.concatenate(value_tiles, axis=0).astype(jnp.bfloat16)
            old_keys = key_ref[pl.ds(first, BATCH), :, lane_span]
            old_keys = old_keys.reshape(BATCH * cache, HEAD_WIDTH)
            old_values = value_ref[pl.ds(first, BATCH), :, lane_span]
            old_values = old_values.reshape(BATCH * cache, HEAD_WIDTH)
            old_scores = lax.dot_general(
                queries, old_keys, transposed, preferred_element_type=jnp.float32
            )
            new_scores = lax.dot_general(
                queries, new_keys, transposed, preferred_element_type=jnp.float32
            )
            heads = steps * PER_GROUP
            old_scores = (old_scores * scale).reshape(heads, BATCH, BATCH * cache) + bias_ref[
                pl.ds(first, BATCH), :
            ][None]
            new_scores = (new_scores * scale).reshape(
                steps, PER_GROUP, BATCH, known * BATCH
            ) + fresh_bias[:, None]
            new_scores = new_scores.reshape(heads, BATCH, known * BATCH)
            peak = jnp.maximum(
                jnp.max(old_scores, axis=-1, keepdims=True),
                jnp.max(new_scores, axis=-1, keepdims=True),
            )
            old_scores = jnp.exp(old_scores - peak)
            new_scores = jnp.exp(new_scores - peak)
            share = 1.0 / (
                jnp.sum(old_scores, axis=-1, keepdims=True)
                + jnp.sum(new_scores, axis=-1, keepdims=True)
            )
            old_weights = (old_scores * share).reshape(heads * BATCH, BATCH * cache)
            new_weights = (new_scores * share).reshape(heads * BATCH, known * BATCH)
            context = jnp.dot(
                old_weights.astype(jnp.bfloat16), old_values, preferred_element_type=jnp.float32
            ) + jnp.dot(
                new_weights.astype(jnp.bfloat16), new_values, preferred_element_type=jnp.float32
            )
            for step, span in enumerate(spans):
                for head in range(PER_GROUP):
                    row = (step * PER_GROUP + head) * BATCH
                    begin = group * query_width + head * HEAD_WIDTH
                    context_ref[span, begin : begin + HEAD_WIDTH] = context[row : row + BATCH]
        return carry

    lax.fori_loop(0, rows // BATCH, batch, 0)

    flow_places = jnp.concatenate([places_ref[1:2, :]] * steps, axis=1)
    context = context_ref[...].astype(jnp.bfloat16)
    count = message_refs[0].shape[0]
    most = count // (lanes * steps)
    shape = (count, steps * rows)
    out_row = iota(shape, 0)
    spot = out_row // steps
    same_step = out_row % steps == iota(shape, 1) // rows
    for number, message_ref in enumerate(message_refs):
        wanted = (spot // most * subs + number) * most + spot % most
        pick = ((flow_places == wanted) & same_step).astype(jnp.float32).astype(jnp.bfloat16)
        message_ref[...] = jnp.dot(
            pick, context, preferred_element_type=jnp.float32
        ).astype(jnp.bfloat16)


def place_kernel(chunks, lanes, subs, most, *refs):
    out_ref = refs[-1]
    steps = out_ref.shape[1]
    chunk_steps = steps // chunks
    block = most * chunk_steps
    per_chunk = subs + lanes - 1
    here = lax.axis_index("streams")
    core = lax.axis_index("sub")
    shape = (chunks * block, chunks * block)
    out_row, in_row = iota(shape, 0), iota(shape, 1)
    step = out_row % steps
    wanted = step // chunk_steps * block + out_row // steps * chunk_steps + step % chunk_steps
    pick = (wanted == in_row).astype(jnp.float32).astype(jnp.bfloat16)
    for number in range(lanes):
        for other in range(subs):
            pieces = []
            for chunk in range(chunks):
                mine = refs[chunk * per_chunk : (chunk + 1) * per_chunk]
                if number == 0:
                    pieces.append(mine[other][...][:block])
                else:
                    landed = mine[subs + lanes - 1 - number]
                    pieces.append(landed[...][other * block : (other + 1) * block])
            rows = jnp.dot(
                pick, jnp.concatenate(pieces, axis=0), preferred_element_type=jnp.float32
            )
            source = (here ^ number) * subs + (core ^ other)
            out_ref[pl.ds(source * most, most)] = rows.reshape(
                most, steps, rows.shape[1]
            ).astype(jnp.bfloat16)


def traded(blocks, axes):
    landed = list(blocks)
    count = len(blocks)
    order = sorted(range(1, count), key=lambda shift: -(shift ^ (shift >> 1)))
    for shift in order:
        pairs = [(place, place ^ shift) for place in range(count)]
        landed[shift] = lax.ppermute(blocks[shift], axes, pairs)
    return landed


def from_others(block, axis):
    count = lax.axis_size(axis)
    landed = [block]
    for shift in range(1, count):
        pairs = [(place, place ^ shift) for place in range(count)]
        landed.append(lax.ppermute(block, axis, pairs))
    return landed


def held(value, others):
    return lax.optimization_barrier((value, others))[0]


SMALL = pl.CostEstimate(flops=1, bytes_accessed=1, transcendentals=0)


def on_device(
    inputs,
    input_norm_gain,
    projection_weight,
    projection_bias,
    speaker,
    speaker_adapter_slot,
    cache_fill_length,
    rotated_key_cache,
    value_cache_rows,
    adapter_down_maps,
    adapter_query_up,
    adapter_value_up,
    flow_decoder_owner,
):
    steps, rows, width = inputs.shape
    lanes = lax.axis_size("streams")
    subs = lax.axis_size("sub")
    heads = lax.axis_size("heads")
    flow_lanes = lanes * subs
    local_slots, sliced, _ = adapter_down_maps.shape
    query_columns = adapter_query_up.shape[2]
    value_columns = adapter_value_up.shape[2]
    groups = value_columns // HEAD_WIDTH
    cache = rotated_key_cache.shape[1]
    spots = subs * local_slots * MOST
    chunks = 2
    chunk_steps = steps // chunks
    chunk_rows = chunk_steps * rows
    per_message = chunk_steps * spots
    chip_slots = subs * local_slots
    flow_most = max(2, (2 * rows + flow_lanes - 1) // flow_lanes)
    bf16, f32 = jnp.bfloat16, jnp.float32

    def whole(shape):
        return pl.BlockSpec(shape, lambda i: (0,) * len(shape))

    in_hbm = pl.BlockSpec(memory_space=pltpu.HBM)

    down_maps = from_others(adapter_down_maps, "sub")
    pieces = 4
    flat = inputs.reshape(steps * rows, width)
    gain = input_norm_gain.reshape(width // 128, 128)
    message = jax.ShapeDtypeStruct((per_message, sliced), bf16)
    normed_shape = jax.ShapeDtypeStruct((chunk_rows, width), bf16)
    places_shape = jax.ShapeDtypeStruct((8, rows), jnp.int32)
    tables = [
        speaker.reshape(1, rows),
        speaker_adapter_slot.reshape(1, -1),
        flow_decoder_owner.reshape(1, rows),
    ]
    buffers = [pltpu.VMEM((chunk_rows, width), bf16), pltpu.VMEM(gain.shape, f32)]
    first_normed, places, *messages = pl.pallas_call(
        functools.partial(norm_pack_kernel, chunk_steps, rows, flow_most, lanes, pieces),
        in_specs=[in_hbm] * 5,
        out_specs=[VMEM] * (2 + lanes),
        out_shape=[normed_shape, places_shape] + [message] * lanes,
        scratch_shapes=buffers
        + [pltpu.VMEM(table.shape, jnp.int32) for table in tables]
        + [pltpu.SemaphoreType.DMA((pieces + 4,))],
        compiler_params=pltpu.CompilerParams(vmem_limit_bytes=56 * MIB),
        cost_estimate=SMALL,
        name="norm_and_pack",
    )(*tables, gain, flat)
    arrived = [traded(messages, "streams")]
    query_map = adapter_query_up.reshape(local_slots * ADAPTER_RANK, query_columns)
    value_map = adapter_value_up.reshape(local_slots * ADAPTER_RANK, value_columns)
    query_map, value_map, places = lax.optimization_barrier((query_map, value_map, places))
    query_maps = from_others(query_map, "sub")
    value_maps = from_others(value_map, "sub")
    normed = [first_normed]
    for chunk in range(1, chunks):
        normed.append(
            pl.pallas_call(
                functools.partial(norm_kernel, chunk * chunk_rows, pieces),
                in_specs=[in_hbm, in_hbm],
                out_specs=VMEM,
                out_shape=normed_shape,
                scratch_shapes=buffers + [pltpu.SemaphoreType.DMA((pieces + 1,))],
                compiler_params=pltpu.CompilerParams(vmem_limit_bytes=56 * MIB),
                cost_estimate=SMALL,
                name="norm",
            )(held(gain, places), flat)
        )

    bias = projection_bias.reshape(-1, 128)
    group_columns = (PER_GROUP + 2) * HEAD_WIDTH
    cut = 3
    block_columns = group_columns // cut
    qkv = []
    waited = down_maps[1:] + query_maps[1:] + value_maps[1:]
    for group in range(groups):
        qkv.append(
            pl.pallas_call(
                functools.partial(
                    project_kernel, chunks, group * group_columns // 128
                ),
                grid=(cut,),
                in_specs=[whole(normed_shape.shape)] * chunks
                + [
                    pl.BlockSpec(
                        (width, block_columns), lambda i, group=group: (0, group * cut + i)
                    ),
                    whole(bias.shape),
                ],
                out_specs=pl.BlockSpec((steps * rows, block_columns), lambda i: (0, i)),
                out_shape=jax.ShapeDtypeStruct((steps * rows, group_columns), f32),
                scratch_shapes=[pltpu.VMEM((steps * rows, width), bf16)],
                compiler_params=pltpu.CompilerParams(vmem_limit_bytes=56 * MIB),
                cost_estimate=SMALL,
                name="project",
            )(*normed, projection_weight, held(bias, waited))
        )
        if group == 0:
            for chunk in range(1, chunks):
                messages = pl.pallas_call(
                    functools.partial(pack_kernel, chunk_steps, rows),
                    in_specs=[VMEM, VMEM],
                    out_specs=[VMEM] * lanes,
                    out_shape=[message] * lanes,
                    compiler_params=pltpu.CompilerParams(vmem_limit_bytes=16 * MIB),
                    cost_estimate=SMALL,
                    name="pack",
                )(held(places, qkv), normed[chunk])
                arrived.append(traded(messages, "streams"))
                waited = messages

    half_width = HEAD_WIDTH // 2
    position = jnp.concatenate([cache_fill_length + step for step in range(steps)]).astype(f32)
    freq = jnp.exp(jnp.arange(half_width, dtype=f32) * (-math.log(1000000.0) / half_width))
    freq = jnp.concatenate([freq, freq])
    angle = position[:, None] * freq
    sign = jnp.where(jnp.arange(HEAD_WIDTH) < half_width, -1.0, 1.0).astype(f32)
    cosine = jnp.cos(angle)
    sine_part = jnp.sin(angle) * sign

    returned = []
    after = qkv
    for chunk in range(chunks):
        partial_latent = pl.pallas_call(
            functools.partial(down_kernel, lanes, spots),
            in_specs=[VMEM] * (lanes + subs),
            out_specs=VMEM,
            out_shape=jax.ShapeDtypeStruct((lanes * per_message, 2 * ADAPTER_RANK), f32),
            compiler_params=pltpu.CompilerParams(vmem_limit_bytes=16 * MIB),
            cost_estimate=SMALL,
            name="down",
        )(held(arrived[chunk][0], after), *arrived[chunk][1:], *down_maps)
        partials = from_others(partial_latent, "heads")
        message = jax.ShapeDtypeStruct((per_message, query_columns + value_columns), bf16)
        messages = pl.pallas_call(
            functools.partial(up_kernel, heads, subs, spots),
            in_specs=[VMEM] * (heads + 2 * subs),
            out_specs=[VMEM] * lanes,
            out_shape=[message] * lanes,
            compiler_params=pltpu.CompilerParams(vmem_limit_bytes=24 * MIB),
            cost_estimate=SMALL,
            name="up",
        )(*partials, *query_maps, *value_maps)
        after = messages
        returned.append(traded(messages, "streams"))

    length_row = cache_fill_length.reshape(1, rows)
    block = flow_most * chunk_steps
    landed = []
    earlier = []
    for chunk in range(chunks):
        last = chunk == chunks - 1
        message = jax.ShapeDtypeStruct((lanes * block, query_columns), bf16)
        fresh = jax.ShapeDtypeStruct((chunk_rows, 2 * value_columns), f32)
        rows_of = lambda shape: pl.BlockSpec(shape, lambda i, chunk=chunk: (chunk, 0))
        results = pl.pallas_call(
            functools.partial(
                attend_kernel,
                chunk * chunk_steps,
                chunk_steps,
                rows,
                cache,
                groups,
                lanes,
                subs,
                last,
            ),
            grid=(1,),
            in_specs=[whole(places.shape), whole(length_row.shape)]
            + [rows_of((chunk_rows, HEAD_WIDTH))] * 2
            + [whole(rotated_key_cache.shape)] * 2
            + [rows_of((chunk_rows, group_columns))] * groups
            + [whole((per_message, query_columns + value_columns))] * lanes
            + [whole(block_rows.shape) for block_rows in earlier],
            out_specs=[whole(fresh.shape)] * (not last) + [whole(message.shape)] * subs,
            out_shape=[fresh] * (not last) + [message] * subs,
            scratch_shapes=[
                pltpu.VMEM((chunk_rows, query_columns + value_columns), f32),
                pltpu.VMEM((chunk_rows, query_columns), f32),
                pltpu.VMEM((rows, BATCH * cache), f32),
            ],
            compiler_params=pltpu.CompilerParams(vmem_limit_bytes=32 * MIB),
            cost_estimate=SMALL,
            name="attend",
        )(
            held(places, landed[-1] if landed else after),
            length_row,
            cosine,
            sine_part,
            rotated_key_cache,
            value_cache_rows,
            *qkv,
            *returned[chunk],
            *earlier,
        )
        if not last:
            earlier, results = [results[0]], results[1:]
        parts = [results[0]]
        for shift in range(1, subs):
            pairs = [(core, core ^ shift) for core in range(subs)]
            parts.append(lax.ppermute(results[shift], "sub", pairs))
        joined = [
            jnp.concatenate([part[lane * block : (lane + 1) * block] for part in parts])
            for lane in range(1, lanes)
        ]
        joined = traded([None] + joined, "streams")[1:]
        landed += parts + joined[::-1]

    flow = pl.pallas_call(
        functools.partial(place_kernel, chunks, lanes, subs, flow_most),
        in_specs=[VMEM] * len(landed),
        out_specs=VMEM,
        out_shape=jax.ShapeDtypeStruct((flow_lanes * flow_most, steps, query_columns), bf16),
        compiler_params=pltpu.CompilerParams(vmem_limit_bytes=24 * MIB),
        cost_estimate=SMALL,
        name="place",
    )(*landed)
    return flow[None]


def solution(mesh):
    placed = (
        P(None, ("groups", "streams", "sub"), None),
        P(),
        P(None, "heads"),
        P("heads"),
        P(("groups", "streams", "sub"), None),
        P("groups"),
        P(("groups", "streams", "sub")),
        P(("groups", "streams", "sub"), None, "heads"),
        P(("groups", "streams", "sub"), None, "heads"),
        P(("groups", "streams", "sub"), "heads", None),
        P(("groups", "streams", "sub"), None, "heads"),
        P(("groups", "streams", "sub"), None, "heads"),
        P(("groups", "streams", "sub"), None),
    )
    return jax.shard_map(
        on_device,
        mesh=mesh,
        in_specs=placed,
        out_specs=P(("groups", "streams", "sub"), None, None, "heads"),
        check_vma=False,
    )
```

```python
import functools
import math

import jax
import jax.numpy as jnp
from jax import lax
from jax.experimental import pallas as pl
from jax.experimental.pallas import tpu as pltpu
from jax.sharding import PartitionSpec as P

QUERY_HEADS = 28
KEY_VALUE_HEADS = 4
HEAD_WIDTH = 128
ADAPTER_RANK = 64
MOST = 2
PER_GROUP = QUERY_HEADS // KEY_VALUE_HEADS
LANE_AXES = ("streams", "sub")
BATCH = 8
VMEM = pl.BlockSpec(memory_space=pltpu.VMEM)
MIB = 1 << 20
PACK_LIMIT = 56
PROJECT_LIMIT = 56


def iota(shape, dim):
    return lax.broadcasted_iota(jnp.int32, shape, dim)


def as_column(row):
    count = row.shape[1]
    square = (count, count)
    same = iota(square, 0) == iota(square, 1)
    return jnp.sum(jnp.where(same, jnp.broadcast_to(row, square), 0), axis=1, keepdims=True)


def ranked(labels, most):
    count = labels.shape[1]
    square = (count, count)
    earlier = (as_column(labels) == labels) & (iota(square, 0) < iota(square, 1))
    return labels * most + jnp.sum(earlier.astype(jnp.int32), axis=0, keepdims=True)


def slot_places(speaker, table, lane_base):
    speakers_all = table.shape[1]
    rows = speaker.shape[1]
    match = iota((speakers_all, rows), 0) == speaker
    slots = jnp.sum(jnp.where(match, as_column(table), 0), axis=0, keepdims=True)
    return ranked(slots ^ lane_base, MOST)


def norm_in_pieces(pieces, begin, x_hbm, gain_hbm, x_buf, gain_buf, semaphores, normed_ref):
    count, width = x_buf.shape
    size = count // pieces
    gain_copy = pltpu.make_async_copy(gain_hbm, gain_buf, semaphores.at[pieces])
    copies = []
    for piece in range(pieces):
        copies.append(
            pltpu.make_async_copy(
                x_hbm.at[pl.ds(begin + piece * size, size)],
                x_buf.at[pl.ds(piece * size, size)],
                semaphores.at[piece],
            )
        )
        copies[-1].start()
        if piece == 0:
            gain_copy.start()
    gain_copy.wait()
    gain = jnp.concatenate([gain_buf[i : i + 1, :] for i in range(gain_buf.shape[0])], axis=1)
    for piece in range(pieces):
        copies[piece].wait()

        def one(index, carry):
            span = pl.ds(pl.multiple_of(piece * size + index * 16, 16), 16)
            values = x_buf[span, :].astype(jnp.float32)
            mean_sq = jnp.sum(values * values, axis=1, keepdims=True) * (1.0 / width)
            normed = values * lax.rsqrt(mean_sq + 1e-06) * gain
            normed_ref[span, :] = normed.astype(jnp.bfloat16)
            return carry

        lax.fori_loop(0, size // 16, one, 0)


def pack_messages(steps, rows, places, normed_ref, message_refs):
    per_message, sliced = message_refs[0].shape
    spots = per_message // steps
    shape = (len(message_refs) * per_message, steps * rows)
    out_row = iota(shape, 0)
    wanted = out_row // per_message * spots + out_row % spots
    out_step = out_row % per_message // spots
    places = jnp.concatenate([places] * steps, axis=1)
    pick = (wanted == places) & (out_step == iota(shape, 1) // rows)
    pick = pick.astype(jnp.float32).astype(jnp.bfloat16)
    begin = pl.multiple_of(lax.axis_index("heads") * sliced, 128)
    own = normed_ref[:, pl.ds(begin, sliced)]
    packed = jnp.dot(pick, own, preferred_element_type=jnp.float32).astype(jnp.bfloat16)
    for number, message_ref in enumerate(message_refs):
        message_ref[...] = packed[number * per_message : (number + 1) * per_message]


def norm_pack_kernel(steps, rows, flow_most, lanes, pieces, chunk, *refs):
    if chunk:
        places_ref, gain_hbm, x_hbm, _, normed_ref = refs[:5]
        message_refs = refs[5 : 5 + lanes]
        x_buf, gain_buf, semaphores = refs[5 + lanes :]
    else:
        table_hbms, gain_hbm, x_hbm = refs[:3], refs[3], refs[4]
        normed_ref, places_ref, message_refs = refs[5], refs[6], refs[7 : 7 + lanes]
        x_buf, gain_buf, *table_bufs, semaphores = refs[7 + lanes :]
        copies = [
            pltpu.make_async_copy(source, target, semaphores.at[pieces + 1 + number])
            for number, (source, target) in enumerate(zip(table_hbms, table_bufs))
        ]
        for copy in copies:
            copy.start()
    begin = chunk * steps * rows
    norm_in_pieces(pieces, begin, x_hbm, gain_hbm, x_buf, gain_buf, semaphores, normed_ref)
    if not chunk:
        for copy in copies:
            copy.wait()
        speaker, table, owner = [buffer[...] for buffer in table_bufs]
        core, subs = lax.axis_index("sub"), lax.axis_size("sub")
        spots = message_refs[0].shape[0] // steps
        places = slot_places(speaker, table, lax.axis_index("streams") * (spots // MOST))
        places_ref[0:1, :] = places
        places_ref[1:2, :] = ranked(owner ^ (lax.axis_index("streams") * subs + core), flow_most)
    pack_messages(steps, rows, places_ref[0:1, :], normed_ref, message_refs)


def project_kernel(first_tile, rows_ref, weight_ref, bias_ref, out_ref):
    tiles = weight_ref.shape[1] // 128
    tile = first_tile + pl.program_id(0) * tiles
    bias = [bias_ref[pl.ds(tile + number, 1), :] for number in range(tiles)]
    product = jnp.dot(rows_ref[...], weight_ref[...], preferred_element_type=jnp.float32)
    out_ref[...] = product + jnp.concatenate(bias, axis=1)


def row_slots(shape, spots):
    return iota(shape, 0) % spots // MOST


def down_kernel(lanes, spots, *refs):
    message_refs, map_refs, partial_ref = refs[:lanes], refs[lanes:-1], refs[-1]
    local_slots = map_refs[0].shape[0]
    rows = jnp.concatenate([ref[...] for ref in message_refs], axis=0)
    own_slot = row_slots(partial_ref.shape, spots)
    total = jnp.zeros(partial_ref.shape, jnp.float32)
    for number, map_ref in enumerate(map_refs):
        shift = (lax.axis_index("sub") ^ number) * local_slots
        for slot in range(local_slots):
            part = jnp.dot(rows, map_ref[slot], preferred_element_type=jnp.float32)
            total = jnp.where(own_slot == shift + slot, part, total)
    partial_ref[...] = total


def up_kernel(heads, subs, spots, *refs):
    partial_refs, refs = refs[:heads], refs[heads:]
    query_refs, value_refs, message_refs = refs[:subs], refs[subs : 2 * subs], refs[2 * subs :]
    total = partial_refs[0][...]
    for ref in partial_refs[1:]:
        total = total + ref[...]
    latent = total.astype(jnp.bfloat16).astype(jnp.float32)
    own_slot = row_slots(latent.shape, spots)
    column = iota(latent.shape, 1) // ADAPTER_RANK
    turned = pltpu.roll(latent, ADAPTER_RANK, 1)
    low = iota(latent.shape, 1) < ADAPTER_RANK
    query_pair = jnp.where(low, latent, turned)
    value_pair = jnp.where(low, turned, latent)

    def product(pair, map_refs):
        result = None
        for number, map_ref in enumerate(map_refs):
            local_slots = map_ref.shape[0] // ADAPTER_RANK
            shift = (lax.axis_index("sub") ^ number) * local_slots
            pieces = []
            for slot in range(0, local_slots, 2):
                kept = jnp.where(own_slot == shift + slot + column, pair, 0.0)
                pieces.append(kept.astype(jnp.bfloat16))
            wide = jnp.concatenate(pieces, axis=1)
            part = jnp.dot(wide, map_ref[...], preferred_element_type=jnp.float32)
            result = part if result is None else result + part
        return result.astype(jnp.bfloat16)

    queries = product(query_pair, query_refs)
    values = product(value_pair, value_refs)
    query_width = queries.shape[1]
    per_message = message_refs[0].shape[0]
    for number, ref in enumerate(message_refs):
        span = slice(number * per_message, (number + 1) * per_message)
        ref[:, :query_width] = queries[span]
        ref[:, query_width:] = values[span]


def attend_kernel(before, steps, rows, cache, groups, lanes, subs, last, *refs):
    places_ref, length_ref, cos_ref, sin_ref, key_ref, value_ref = refs[:6]
    qkv_refs, refs = refs[6:8], refs[8:]
    delta_refs, refs = refs[:lanes], refs[lanes:]
    if before:
        earlier_ref, refs = refs[0], refs[1:]
    if not last:
        fresh_ref, refs = refs[0], refs[1:]
    message_refs = refs[:subs]
    delta_ref, context_ref, bias_ref = refs[subs:]
    per_message = delta_refs[0].shape[0]
    spots = per_message // steps
    query_width = PER_GROUP * HEAD_WIDTH
    known = before + steps

    def qkv_tile(span, group, head):
        begin = (group * (PER_GROUP + 2) + head) * HEAD_WIDTH
        edge = qkv_refs[0].shape[1]
        if begin < edge:
            return qkv_refs[0][span, begin : begin + HEAD_WIDTH]
        return qkv_refs[1][span, begin - edge : begin - edge + HEAD_WIDTH]

    wide = groups * HEAD_WIDTH

    column = as_column(places_ref[0:1, :])
    column = jnp.concatenate([column] * steps, axis=0)
    shape = (steps * rows, lanes * per_message)
    out_row = iota(shape, 1)
    wanted = out_row // per_message * spots + out_row % spots
    pick = (wanted == column) & (out_row % per_message // spots == iota(shape, 0) // rows)
    pick = pick.astype(jnp.float32).astype(jnp.bfloat16)
    delta_ref[...] = jnp.dot(
        pick,
        jnp.concatenate([ref[...] for ref in delta_refs], axis=0),
        preferred_element_type=jnp.float32,
    )

    shape = (rows, BATCH * cache)
    lengths = as_column(length_ref[...])
    slot_column = iota(shape, 1)
    allowed = (slot_column // cache == iota(shape, 0) % BATCH) & (slot_column % cache < lengths)
    bias_ref[...] = jnp.where(allowed, 0.0, -1e30)
    shape = (steps, BATCH, known * BATCH)
    fresh_column = iota(shape, 2)
    allowed = (fresh_column % BATCH == iota(shape, 1)) & (
        fresh_column // BATCH <= iota(shape, 0) + before
    )
    fresh_bias = jnp.where(allowed, 0.0, -1e30)
    scale = HEAD_WIDTH ** (-0.5)
    transposed = (((1,), (1,)), ((), ()))

    def batch(index, carry):
        first = pl.multiple_of(index * BATCH, BATCH)
        spans = [pl.ds(pl.multiple_of(step * rows + first, BATCH), BATCH) for step in range(steps)]
        past = [pl.ds(pl.multiple_of(step * rows + first, BATCH), BATCH) for step in range(before)]
        for group in range(groups):
            query_tiles, key_tiles, value_tiles = [], [], []
            lane_span = slice(group * HEAD_WIDTH, (group + 1) * HEAD_WIDTH)
            value_span = slice(wide + group * HEAD_WIDTH, wide + (group + 1) * HEAD_WIDTH)
            for span in past:
                key_tiles.append(earlier_ref[span, lane_span])
                value_tiles.append(earlier_ref[span, value_span])
            for span in spans:
                cosine, sine_part = cos_ref[span, :], sin_ref[span, :]

                def rotated(values):
                    return values * cosine + pltpu.roll(values, HEAD_WIDTH // 2, 1) * sine_part

                for head in range(PER_GROUP):
                    begin = group * query_width + head * HEAD_WIDTH
                    change = delta_ref[span, begin : begin + HEAD_WIDTH]
                    query_tiles.append(rotated(qkv_tile(span, group, head) + change))
                key = rotated(qkv_tile(span, group, PER_GROUP))
                begin = groups * query_width + group * HEAD_WIDTH
                change = delta_ref[span, begin : begin + HEAD_WIDTH]
                value = qkv_tile(span, group, PER_GROUP + 1) + change
                if not last:
                    fresh_ref[span, lane_span] = key
                    fresh_ref[span, value_span] = value
                key_tiles.append(key)
                value_tiles.append(value)
            queries = jnp.concatenate(query_tiles, axis=0).astype(jnp.bfloat16)
            new_keys = jnp.concatenate(key_tiles, axis=0).astype(jnp.bfloat16)
            new_values = jnp.concatenate(value_tiles, axis=0).astype(jnp.bfloat16)
            old_keys = key_ref[pl.ds(first, BATCH), :, lane_span]
            old_keys = old_keys.reshape(BATCH * cache, HEAD_WIDTH)
            old_values = value_ref[pl.ds(first, BATCH), :, lane_span]
            old_values = old_values.reshape(BATCH * cache, HEAD_WIDTH)
            old_scores = lax.dot_general(
                queries, old_keys, transposed, preferred_element_type=jnp.float32
            )
            new_scores = lax.dot_general(
                queries, new_keys, transposed, preferred_element_type=jnp.float32
            )
            heads = steps * PER_GROUP
            old_scores = (old_scores * scale).reshape(heads, BATCH, BATCH * cache) + bias_ref[
                pl.ds(first, BATCH), :
            ][None]
            new_scores = (new_scores * scale).reshape(
                steps, PER_GROUP, BATCH, known * BATCH
            ) + fresh_bias[:, None]
            new_scores = new_scores.reshape(heads, BATCH, known * BATCH)
            peak = jnp.maximum(
                jnp.max(old_scores, axis=-1, keepdims=True),
                jnp.max(new_scores, axis=-1, keepdims=True),
            )
            old_scores = jnp.exp(old_scores - peak)
            new_scores = jnp.exp(new_scores - peak)
            share = 1.0 / (
                jnp.sum(old_scores, axis=-1, keepdims=True)
                + jnp.sum(new_scores, axis=-1, keepdims=True)
            )
            old_weights = (old_scores * share).reshape(heads * BATCH, BATCH * cache)
            new_weights = (new_scores * share).reshape(heads * BATCH, known * BATCH)
            context = jnp.dot(
                old_weights.astype(jnp.bfloat16), old_values, preferred_element_type=jnp.float32
            ) + jnp.dot(
                new_weights.astype(jnp.bfloat16), new_values, preferred_element_type=jnp.float32
            )
            for step, span in enumerate(spans):
                for head in range(PER_GROUP):
                    row = (step * PER_GROUP + head) * BATCH
                    begin = group * query_width + head * HEAD_WIDTH
                    context_ref[span, begin : begin + HEAD_WIDTH] = context[row : row + BATCH]
        return carry

    lax.fori_loop(0, rows // BATCH, batch, 0)

    flow_places = jnp.concatenate([places_ref[1:2, :]] * steps, axis=1)
    context = context_ref[...].astype(jnp.bfloat16)
    count = message_refs[0].shape[0]
    most = count // (lanes * steps)
    shape = (count, steps * rows)
    out_row = iota(shape, 0)
    spot = out_row // steps
    same_step = out_row % steps == iota(shape, 1) // rows
    for number, message_ref in enumerate(message_refs):
        wanted = (spot // most * subs + number) * most + spot % most
        pick = ((flow_places == wanted) & same_step).astype(jnp.float32).astype(jnp.bfloat16)
        message_ref[...] = jnp.dot(
            pick, context, preferred_element_type=jnp.float32
        ).astype(jnp.bfloat16)


def place_kernel(chunks, lanes, subs, most, *refs):
    out_ref = refs[-1]
    steps = out_ref.shape[1]
    chunk_steps = steps // chunks
    block = most * chunk_steps
    per_chunk = subs + lanes - 1
    here = lax.axis_index("streams")
    core = lax.axis_index("sub")
    shape = (chunks * block, chunks * block)
    out_row, in_row = iota(shape, 0), iota(shape, 1)
    step = out_row % steps
    wanted = step // chunk_steps * block + out_row // steps * chunk_steps + step % chunk_steps
    pick = (wanted == in_row).astype(jnp.float32).astype(jnp.bfloat16)
    for number in range(lanes):
        for other in range(subs):
            pieces = []
            for chunk in range(chunks):
                mine = refs[chunk * per_chunk : (chunk + 1) * per_chunk]
                if number == 0:
                    pieces.append(mine[other][...][:block])
                else:
                    landed = mine[subs + lanes - 1 - number]
                    pieces.append(landed[...][other * block : (other + 1) * block])
            rows = jnp.dot(
                pick, jnp.concatenate(pieces, axis=0), preferred_element_type=jnp.float32
            )
            source = (here ^ number) * subs + (core ^ other)
            out_ref[pl.ds(source * most, most)] = rows.reshape(
                most, steps, rows.shape[1]
            ).astype(jnp.bfloat16)


def traded(blocks, axes):
    landed = list(blocks)
    count = len(blocks)
    order = sorted(range(1, count), key=lambda shift: -(shift ^ (shift >> 1)))
    for shift in order:
        pairs = [(place, place ^ shift) for place in range(count)]
        landed[shift] = lax.ppermute(blocks[shift], axes, pairs)
    return landed


def from_others(block, axis):
    count = lax.axis_size(axis)
    landed = [block]
    for shift in range(1, count):
        pairs = [(place, place ^ shift) for place in range(count)]
        landed.append(lax.ppermute(block, axis, pairs))
    return landed


def held(value, others):
    return lax.optimization_barrier((value, others))[0]


SMALL = pl.CostEstimate(flops=1, bytes_accessed=1, transcendentals=0)


def on_device(
    inputs,
    input_norm_gain,
    projection_weight,
    projection_bias,
    speaker,
    speaker_adapter_slot,
    cache_fill_length,
    rotated_key_cache,
    value_cache_rows,
    adapter_down_maps,
    adapter_query_up,
    adapter_value_up,
    flow_decoder_owner,
):
    steps, rows, width = inputs.shape
    lanes = lax.axis_size("streams")
    subs = lax.axis_size("sub")
    heads = lax.axis_size("heads")
    flow_lanes = lanes * subs
    local_slots, sliced, _ = adapter_down_maps.shape
    query_columns = adapter_query_up.shape[2]
    value_columns = adapter_value_up.shape[2]
    groups = value_columns // HEAD_WIDTH
    cache = rotated_key_cache.shape[1]
    spots = subs * local_slots * MOST
    chunks = 2
    chunk_steps = steps // chunks
    chunk_rows = chunk_steps * rows
    per_message = chunk_steps * spots
    chip_slots = subs * local_slots
    flow_most = max(2, (2 * rows + flow_lanes - 1) // flow_lanes)
    bf16, f32 = jnp.bfloat16, jnp.float32

    def whole(shape):
        return pl.BlockSpec(shape, lambda i: (0,) * len(shape))

    in_hbm = pl.BlockSpec(memory_space=pltpu.HBM)

    down_maps = from_others(adapter_down_maps, "sub")
    query_maps = from_others(
        adapter_query_up.reshape(local_slots * ADAPTER_RANK, query_columns), "sub"
    )
    value_maps = from_others(
        adapter_value_up.reshape(local_slots * ADAPTER_RANK, value_columns), "sub"
    )

    pieces = 4
    flat = inputs.reshape(steps * rows, width)
    gain = input_norm_gain.reshape(width // 128, 128)
    message = jax.ShapeDtypeStruct((per_message, sliced), bf16)
    normed_shape = jax.ShapeDtypeStruct((steps * rows, width), bf16)
    places_shape = jax.ShapeDtypeStruct((8, rows), jnp.int32)
    tables = [
        speaker.reshape(1, rows),
        speaker_adapter_slot.reshape(1, -1),
        flow_decoder_owner.reshape(1, rows),
    ]
    buffers = [pltpu.VMEM((chunk_rows, width), bf16), pltpu.VMEM(gain.shape, f32)]
    table_buffers = [pltpu.VMEM(table.shape, jnp.int32) for table in tables]
    arrived = []
    for chunk in range(chunks):
        rows_block = pl.BlockSpec((chunk_rows, width), lambda i, chunk=chunk: (chunk, 0))
        first = chunk == 0
        operands = [gain, flat]
        if first:
            operands = tables + operands
        else:
            adapters = down_maps[1:], query_maps[1:], value_maps[1:]
            operands = [held(places, adapters)] + operands + [normed]
        normed, *messages = pl.pallas_call(
            functools.partial(
                norm_pack_kernel, chunk_steps, rows, flow_most, lanes, pieces, chunk
            ),
            grid=(1,),
            in_specs=[in_hbm] * 5 if first else [whole(places_shape.shape)] + [in_hbm] * 3,
            out_specs=[rows_block]
            + [whole(places_shape.shape)] * first
            + [whole(message.shape)] * lanes,
            out_shape=[normed_shape] + [places_shape] * first + [message] * lanes,
            scratch_shapes=buffers
            + table_buffers * first
            + [pltpu.SemaphoreType.DMA((pieces + 4,))],
            input_output_aliases={} if first else {3: 0},
            compiler_params=pltpu.CompilerParams(vmem_limit_bytes=PACK_LIMIT * MIB),
            cost_estimate=SMALL,
            name="norm_and_pack",
        )(*operands)
        if first:
            places, *messages = messages
        arrived.append(traded(messages, "streams"))

    bias = projection_bias.reshape(-1, 128)
    columns = projection_weight.shape[1]
    block_columns = 256 if columns % 256 == 0 else 384
    blocks = columns // block_columns

    def project(begin, end, after):
        return pl.pallas_call(
            functools.partial(project_kernel, begin * block_columns // 128),
            grid=(end - begin,),
            in_specs=[
                whole(normed_shape.shape),
                pl.BlockSpec((width, block_columns), lambda i: (0, begin + i)),
                whole(bias.shape),
            ],
            out_specs=pl.BlockSpec((steps * rows, block_columns), lambda i: (0, i)),
            out_shape=jax.ShapeDtypeStruct((steps * rows, (end - begin) * block_columns), f32),
            compiler_params=pltpu.CompilerParams(vmem_limit_bytes=PROJECT_LIMIT * MIB),
            cost_estimate=SMALL,
            name="project",
        )(normed, projection_weight, held(bias, after))

    def down(chunk, after):
        partial_latent = pl.pallas_call(
            functools.partial(down_kernel, lanes, spots),
            in_specs=[VMEM] * (lanes + subs),
            out_specs=VMEM,
            out_shape=jax.ShapeDtypeStruct((lanes * per_message, 2 * ADAPTER_RANK), f32),
            compiler_params=pltpu.CompilerParams(vmem_limit_bytes=16 * MIB),
            cost_estimate=SMALL,
            name="down",
        )(held(arrived[chunk][0], after), *arrived[chunk][1:], *down_maps)
        return from_others(partial_latent, "heads")

    def up(partials, after):
        message = jax.ShapeDtypeStruct((per_message, query_columns + value_columns), bf16)
        messages = pl.pallas_call(
            functools.partial(up_kernel, heads, subs, spots),
            in_specs=[VMEM] * (heads + 2 * subs),
            out_specs=[VMEM] * lanes,
            out_shape=[message] * lanes,
            compiler_params=pltpu.CompilerParams(vmem_limit_bytes=24 * MIB),
            cost_estimate=SMALL,
            name="up",
        )(held(partials[0], after), *partials[1:], *query_maps, *value_maps)
        return messages, traded(messages, "streams")

    cut = blocks // 2
    qkv = [project(0, cut, messages)]
    partials = down(0, qkv)
    qkv.append(project(cut, blocks, partials[0]))

    half_width = HEAD_WIDTH // 2
    position = jnp.concatenate([cache_fill_length + step for step in range(steps)]).astype(f32)
    freq = jnp.exp(jnp.arange(half_width, dtype=f32) * (-math.log(1000000.0) / half_width))
    freq = jnp.concatenate([freq, freq])
    angle = position[:, None] * freq
    sign = jnp.where(jnp.arange(HEAD_WIDTH) < half_width, -1.0, 1.0).astype(f32)
    cosine = jnp.cos(angle)
    sine_part = jnp.sin(angle) * sign

    returned = []
    after = qkv
    for chunk in range(chunks):
        if chunk:
            partials = down(chunk, after)
        after, arrivals = up(partials, after)
        returned.append(arrivals)

    length_row = cache_fill_length.reshape(1, rows)
    block = flow_most * chunk_steps
    landed = []
    earlier = []
    for chunk in range(chunks):
        last = chunk == chunks - 1
        message = jax.ShapeDtypeStruct((lanes * block, query_columns), bf16)
        fresh = jax.ShapeDtypeStruct((chunk_rows, 2 * value_columns), f32)
        rows_of = lambda shape: pl.BlockSpec(shape, lambda i, chunk=chunk: (chunk, 0))
        results = pl.pallas_call(
            functools.partial(
                attend_kernel,
                chunk * chunk_steps,
                chunk_steps,
                rows,
                cache,
                groups,
                lanes,
                subs,
                last,
            ),
            grid=(1,),
            in_specs=[whole(places.shape), whole(length_row.shape)]
            + [rows_of((chunk_rows, HEAD_WIDTH))] * 2
            + [whole(rotated_key_cache.shape)] * 2
            + [rows_of((chunk_rows, part.shape[1])) for part in qkv]
            + [whole((per_message, query_columns + value_columns))] * lanes
            + [whole(block_rows.shape) for block_rows in earlier],
            out_specs=[whole(fresh.shape)] * (not last) + [whole(message.shape)] * subs,
            out_shape=[fresh] * (not last) + [message] * subs,
            scratch_shapes=[
                pltpu.VMEM((chunk_rows, query_columns + value_columns), f32),
                pltpu.VMEM((chunk_rows, query_columns), f32),
                pltpu.VMEM((rows, BATCH * cache), f32),
            ],
            compiler_params=pltpu.CompilerParams(vmem_limit_bytes=32 * MIB),
            cost_estimate=SMALL,
            name="attend",
        )(
            held(places, landed[-1] if landed else after),
            length_row,
            cosine,
            sine_part,
            rotated_key_cache,
            value_cache_rows,
            *qkv,
            *returned[chunk],
            *earlier,
        )
        if not last:
            earlier, results = [results[0]], results[1:]
        parts = [results[0]]
        for shift in range(1, subs):
            pairs = [(core, core ^ shift) for core in range(subs)]
            parts.append(lax.ppermute(results[shift], "sub", pairs))
        joined = [
            jnp.concatenate([part[lane * block : (lane + 1) * block] for part in parts])
            for lane in range(1, lanes)
        ]
        joined = traded([None] + joined, "streams")[1:]
        landed += parts + joined[::-1]

    flow = pl.pallas_call(
        functools.partial(place_kernel, chunks, lanes, subs, flow_most),
        in_specs=[VMEM] * len(landed),
        out_specs=VMEM,
        out_shape=jax.ShapeDtypeStruct((flow_lanes * flow_most, steps, query_columns), bf16),
        compiler_params=pltpu.CompilerParams(vmem_limit_bytes=24 * MIB),
        cost_estimate=SMALL,
        name="place",
    )(*landed)
    return flow[None]


def solution(mesh):
    placed = (
        P(None, ("groups", "streams", "sub"), None),
        P(),
        P(None, "heads"),
        P("heads"),
        P(("groups", "streams", "sub"), None),
        P("groups"),
        P(("groups", "streams", "sub")),
        P(("groups", "streams", "sub"), None, "heads"),
        P(("groups", "streams", "sub"), None, "heads"),
        P(("groups", "streams", "sub"), "heads", None),
        P(("groups", "streams", "sub"), None, "heads"),
        P(("groups", "streams", "sub"), None, "heads"),
        P(("groups", "streams", "sub"), None),
    )
    return jax.shard_map(
        on_device,
        mesh=mesh,
        in_specs=placed,
        out_specs=P(("groups", "streams", "sub"), None, None, "heads"),
        check_vma=False,
    )
```

```python
import functools
import math

import jax
import jax.numpy as jnp
from jax import lax
from jax.experimental import pallas as pl
from jax.experimental.pallas import tpu as pltpu
from jax.sharding import PartitionSpec as P

QUERY_HEADS = 28
KEY_VALUE_HEADS = 4
HEAD_WIDTH = 128
ADAPTER_RANK = 64
MOST = 2
PER_GROUP = QUERY_HEADS // KEY_VALUE_HEADS
LANE_AXES = ("streams", "sub")
BATCH = 8
TOGETHER = 2
VMEM = pl.BlockSpec(memory_space=pltpu.VMEM)
MIB = 1 << 20
PACK_LIMIT = 56
PROJECT_LIMIT = 56
DEPTH_CUTS = 4


def iota(shape, dim):
    return lax.broadcasted_iota(jnp.int32, shape, dim)


def as_column(row):
    count = row.shape[1]
    square = (count, count)
    same = iota(square, 0) == iota(square, 1)
    return jnp.sum(jnp.where(same, jnp.broadcast_to(row, square), 0), axis=1, keepdims=True)


def ranked(labels, most):
    count = labels.shape[1]
    square = (count, count)
    earlier = (as_column(labels) == labels) & (iota(square, 0) < iota(square, 1))
    return labels * most + jnp.sum(earlier.astype(jnp.int32), axis=0, keepdims=True)


def slot_places(speaker, table, lane_base):
    speakers_all = table.shape[1]
    rows = speaker.shape[1]
    match = iota((speakers_all, rows), 0) == speaker
    slots = jnp.sum(jnp.where(match, as_column(table), 0), axis=0, keepdims=True)
    return ranked(slots ^ lane_base, MOST)


def norm_in_pieces(pieces, begin, x_hbm, gain_hbm, x_buf, gain_buf, semaphores, normed_ref):
    count, width = x_buf.shape
    size = count // pieces
    gain_copy = pltpu.make_async_copy(gain_hbm, gain_buf, semaphores.at[pieces])
    copies = []
    for piece in range(pieces):
        copies.append(
            pltpu.make_async_copy(
                x_hbm.at[pl.ds(begin + piece * size, size)],
                x_buf.at[pl.ds(piece * size, size)],
                semaphores.at[piece],
            )
        )
        copies[-1].start()
        if piece == 0:
            gain_copy.start()
    gain_copy.wait()
    gain = jnp.concatenate([gain_buf[i : i + 1, :] for i in range(gain_buf.shape[0])], axis=1)
    for piece in range(pieces):
        copies[piece].wait()

        def one(index, carry):
            span = pl.ds(pl.multiple_of(piece * size + index * 16, 16), 16)
            values = x_buf[span, :].astype(jnp.float32)
            mean_sq = jnp.sum(values * values, axis=1, keepdims=True) * (1.0 / width)
            normed = values * lax.rsqrt(mean_sq + 1e-06) * gain
            normed_ref[span, :] = normed.astype(jnp.bfloat16)
            return carry

        lax.fori_loop(0, size // 16, one, 0)


def pack_messages(steps, rows, places, normed_ref, message_refs):
    per_message, sliced = message_refs[0].shape
    spots = per_message // steps
    shape = (len(message_refs) * per_message, steps * rows)
    out_row = iota(shape, 0)
    wanted = out_row // per_message * spots + out_row % spots
    out_step = out_row % per_message // spots
    places = jnp.concatenate([places] * steps, axis=1)
    pick = (wanted == places) & (out_step == iota(shape, 1) // rows)
    pick = pick.astype(jnp.float32).astype(jnp.bfloat16)
    begin = pl.multiple_of(lax.axis_index("heads") * sliced, 128)
    own = normed_ref[:, pl.ds(begin, sliced)]
    packed = jnp.dot(pick, own, preferred_element_type=jnp.float32).astype(jnp.bfloat16)
    for number, message_ref in enumerate(message_refs):
        message_ref[...] = packed[number * per_message : (number + 1) * per_message]


def norm_pack_kernel(steps, rows, flow_most, lanes, pieces, chunk, *refs):
    if chunk:
        places_ref, gain_hbm, x_hbm, _, normed_ref = refs[:5]
        message_refs = refs[5 : 5 + lanes]
        x_buf, gain_buf, semaphores = refs[5 + lanes :]
    else:
        table_hbms, gain_hbm, x_hbm = refs[:3], refs[3], refs[4]
        normed_ref, places_ref, message_refs = refs[5], refs[6], refs[7 : 7 + lanes]
        x_buf, gain_buf, *table_bufs, semaphores = refs[7 + lanes :]
        copies = [
            pltpu.make_async_copy(source, target, semaphores.at[pieces + 1 + number])
            for number, (source, target) in enumerate(zip(table_hbms, table_bufs))
        ]
        for copy in copies:
            copy.start()
    begin = chunk * steps * rows
    norm_in_pieces(pieces, begin, x_hbm, gain_hbm, x_buf, gain_buf, semaphores, normed_ref)
    if not chunk:
        for copy in copies:
            copy.wait()
        speaker, table, owner = [buffer[...] for buffer in table_bufs]
        core, subs = lax.axis_index("sub"), lax.axis_size("sub")
        spots = message_refs[0].shape[0] // steps
        places = slot_places(speaker, table, lax.axis_index("streams") * (spots // MOST))
        places_ref[0:1, :] = places
        places_ref[1:2, :] = ranked(owner ^ (lax.axis_index("streams") * subs + core), flow_most)
    pack_messages(steps, rows, places_ref[0:1, :], normed_ref, message_refs)


def project_kernel(first_tile, rows_ref, bias_ref, *refs):
    weight_refs, out_ref = refs[:-1], refs[-1]
    depth, columns = weight_refs[0].shape
    tiles = columns // 128
    tile = first_tile + pl.program_id(0) * tiles
    bias = [bias_ref[pl.ds(tile + number, 1), :] for number in range(tiles)]
    total = jnp.concatenate(bias, axis=1)
    for number, ref in enumerate(weight_refs):
        rows = rows_ref[:, number * depth : (number + 1) * depth]
        total = total + jnp.dot(rows, ref[...], preferred_element_type=jnp.float32)
    out_ref[...] = total


def row_slots(shape, spots):
    return iota(shape, 0) % spots // MOST


def down_kernel(lanes, spots, *refs):
    message_refs, map_refs, partial_ref = refs[:lanes], refs[lanes:-1], refs[-1]
    local_slots = map_refs[0].shape[0]
    rows = jnp.concatenate([ref[...] for ref in message_refs], axis=0)
    own_slot = row_slots(partial_ref.shape, spots)
    total = jnp.zeros(partial_ref.shape, jnp.float32)
    for number, map_ref in enumerate(map_refs):
        shift = (lax.axis_index("sub") ^ number) * local_slots
        for slot in range(local_slots):
            part = jnp.dot(rows, map_ref[slot], preferred_element_type=jnp.float32)
            total = jnp.where(own_slot == shift + slot, part, total)
    partial_ref[...] = total


def up_kernel(heads, subs, spots, *refs):
    partial_refs, refs = refs[:heads], refs[heads:]
    query_refs, value_refs, message_refs = refs[:subs], refs[subs : 2 * subs], refs[2 * subs :]
    total = partial_refs[0][...]
    for ref in partial_refs[1:]:
        total = total + ref[...]
    latent = total.astype(jnp.bfloat16).astype(jnp.float32)
    own_slot = row_slots(latent.shape, spots)
    column = iota(latent.shape, 1) // ADAPTER_RANK
    turned = pltpu.roll(latent, ADAPTER_RANK, 1)
    low = iota(latent.shape, 1) < ADAPTER_RANK
    query_pair = jnp.where(low, latent, turned)
    value_pair = jnp.where(low, turned, latent)

    def product(pair, map_refs):
        result = None
        for number, map_ref in enumerate(map_refs):
            local_slots = map_ref.shape[0] // ADAPTER_RANK
            shift = (lax.axis_index("sub") ^ number) * local_slots
            pieces = []
            for slot in range(0, local_slots, 2):
                kept = jnp.where(own_slot == shift + slot + column, pair, 0.0)
                pieces.append(kept.astype(jnp.bfloat16))
            wide = jnp.concatenate(pieces, axis=1)
            part = jnp.dot(wide, map_ref[...], preferred_element_type=jnp.float32)
            result = part if result is None else result + part
        return result.astype(jnp.bfloat16)

    queries = product(query_pair, query_refs)
    values = product(value_pair, value_refs)
    query_width = queries.shape[1]
    per_message = message_refs[0].shape[0]
    for number, ref in enumerate(message_refs):
        span = slice(number * per_message, (number + 1) * per_message)
        ref[:, :query_width] = queries[span]
        ref[:, query_width:] = values[span]


def attend_kernel(before, steps, rows, cache, groups, lanes, subs, last, *refs):
    places_ref, length_ref, cos_ref, sin_ref, key_ref, value_ref = refs[:6]
    qkv_refs, refs = refs[6:8], refs[8:]
    delta_refs, refs = refs[:lanes], refs[lanes:]
    if before:
        earlier_ref, refs = refs[0], refs[1:]
    if not last:
        fresh_ref, refs = refs[0], refs[1:]
    message_refs = refs[:lanes]
    delta_ref, context_ref, bias_ref = refs[lanes:]
    per_message = delta_refs[0].shape[0]
    spots = per_message // steps
    query_width = PER_GROUP * HEAD_WIDTH
    known = before + steps

    def qkv_tile(span, group, head):
        begin = (group * (PER_GROUP + 2) + head) * HEAD_WIDTH
        edge = qkv_refs[0].shape[1]
        if begin < edge:
            return qkv_refs[0][span, begin : begin + HEAD_WIDTH]
        return qkv_refs[1][span, begin - edge : begin - edge + HEAD_WIDTH]

    wide = groups * HEAD_WIDTH

    column = as_column(places_ref[0:1, :])
    column = jnp.concatenate([column] * steps, axis=0)
    shape = (steps * rows, lanes * per_message)
    out_row = iota(shape, 1)
    wanted = out_row // per_message * spots + out_row % spots
    pick = (wanted == column) & (out_row % per_message // spots == iota(shape, 0) // rows)
    pick = pick.astype(jnp.float32).astype(jnp.bfloat16)
    delta_ref[...] = jnp.dot(
        pick,
        jnp.concatenate([ref[...] for ref in delta_refs], axis=0),
        preferred_element_type=jnp.float32,
    )

    shape = (rows, BATCH * cache)
    lengths = as_column(length_ref[...])
    slot_column = iota(shape, 1)
    allowed = (slot_column // cache == iota(shape, 0) % BATCH) & (slot_column % cache < lengths)
    bias_ref[...] = jnp.where(allowed, 0.0, -1e30)
    shape = (steps, BATCH, known * BATCH)
    fresh_column = iota(shape, 2)
    allowed = (fresh_column % BATCH == iota(shape, 1)) & (
        fresh_column // BATCH <= iota(shape, 0) + before
    )
    fresh_bias = jnp.where(allowed, 0.0, -1e30)
    scale = HEAD_WIDTH ** (-0.5)
    transposed = (((1,), (1,)), ((), ()))

    def scored(first, group):
        spans = [pl.ds(pl.multiple_of(step * rows + first, BATCH), BATCH) for step in range(known)]
        query_tiles, key_tiles, value_tiles = [], [], []
        lane_span = slice(group * HEAD_WIDTH, (group + 1) * HEAD_WIDTH)
        value_span = slice(wide + group * HEAD_WIDTH, wide + (group + 1) * HEAD_WIDTH)
        for span in spans[:before]:
            key_tiles.append(earlier_ref[span, lane_span])
            value_tiles.append(earlier_ref[span, value_span])
        for span in spans[:steps]:
            cosine, sine_part = cos_ref[span, :], sin_ref[span, :]

            def rotated(values):
                return values * cosine + pltpu.roll(values, HEAD_WIDTH // 2, 1) * sine_part

            for head in range(PER_GROUP):
                begin = group * query_width + head * HEAD_WIDTH
                change = delta_ref[span, begin : begin + HEAD_WIDTH]
                query_tiles.append(rotated(qkv_tile(span, group, head) + change))
            key = rotated(qkv_tile(span, group, PER_GROUP))
            begin = groups * query_width + group * HEAD_WIDTH
            change = delta_ref[span, begin : begin + HEAD_WIDTH]
            value = qkv_tile(span, group, PER_GROUP + 1) + change
            if not last:
                fresh_ref[span, lane_span] = key
                fresh_ref[span, value_span] = value
            key_tiles.append(key)
            value_tiles.append(value)
        queries = jnp.concatenate(query_tiles, axis=0).astype(jnp.bfloat16)
        new_keys = jnp.concatenate(key_tiles, axis=0).astype(jnp.bfloat16)
        new_values = jnp.concatenate(value_tiles, axis=0).astype(jnp.bfloat16)
        old_keys = key_ref[pl.ds(first, BATCH), :, lane_span].reshape(BATCH * cache, HEAD_WIDTH)
        old_scores = lax.dot_general(
            queries, old_keys, transposed, preferred_element_type=jnp.float32
        )
        new_scores = lax.dot_general(
            queries, new_keys, transposed, preferred_element_type=jnp.float32
        )
        return old_scores, new_scores, new_values

    def weighed(first, old_scores, new_scores):
        heads = steps * PER_GROUP
        old_scores = (old_scores * scale).reshape(heads, BATCH, BATCH * cache)
        old_scores = old_scores + bias_ref[pl.ds(first, BATCH), :][None]
        new_scores = (new_scores * scale).reshape(steps, PER_GROUP, BATCH, known * BATCH)
        new_scores = (new_scores + fresh_bias[:, None]).reshape(heads, BATCH, known * BATCH)
        peak = jnp.maximum(
            jnp.max(old_scores, axis=-1, keepdims=True),
            jnp.max(new_scores, axis=-1, keepdims=True),
        )
        old_scores = jnp.exp(old_scores - peak)
        new_scores = jnp.exp(new_scores - peak)
        share = 1.0 / (
            jnp.sum(old_scores, axis=-1, keepdims=True)
            + jnp.sum(new_scores, axis=-1, keepdims=True)
        )
        old_weights = (old_scores * share).reshape(heads * BATCH, BATCH * cache)
        new_weights = (new_scores * share).reshape(heads * BATCH, known * BATCH)
        return old_weights.astype(jnp.bfloat16), new_weights.astype(jnp.bfloat16)

    def batch(index, carry):
        chains = []
        for number in range(TOGETHER):
            first = pl.multiple_of((index * TOGETHER + number) * BATCH, BATCH)
            chains += [(first, group) for group in range(groups)]
        scores = [scored(*chain) for chain in chains]
        weights = [weighed(chain[0], *score[:2]) for chain, score in zip(chains, scores)]
        for (first, group), (old_weights, new_weights), score in zip(chains, weights, scores):
            lane_span = slice(group * HEAD_WIDTH, (group + 1) * HEAD_WIDTH)
            old_values = value_ref[pl.ds(first, BATCH), :, lane_span]
            old_values = old_values.reshape(BATCH * cache, HEAD_WIDTH)
            context = jnp.dot(
                old_weights, old_values, preferred_element_type=jnp.float32
            ) + jnp.dot(new_weights, score[2], preferred_element_type=jnp.float32)
            for step in range(steps):
                span = pl.ds(pl.multiple_of(step * rows + first, BATCH), BATCH)
                for head in range(PER_GROUP):
                    row = (step * PER_GROUP + head) * BATCH
                    begin = group * query_width + head * HEAD_WIDTH
                    context_ref[span, begin : begin + HEAD_WIDTH] = context[row : row + BATCH]
        return carry

    lax.fori_loop(0, rows // (BATCH * TOGETHER), batch, 0)

    flow_places = jnp.concatenate([places_ref[1:2, :]] * steps, axis=1)
    context = context_ref[...].astype(jnp.bfloat16)
    count = message_refs[0].shape[0]
    shape = (count, steps * rows)
    out_row = iota(shape, 0)
    same_step = out_row % steps == iota(shape, 1) // rows
    for number, message_ref in enumerate(message_refs):
        wanted = number * (count // steps) + out_row // steps
        pick = ((flow_places == wanted) & same_step).astype(jnp.float32).astype(jnp.bfloat16)
        message_ref[...] = jnp.dot(
            pick, context, preferred_element_type=jnp.float32
        ).astype(jnp.bfloat16)


def place_kernel(found, lanes, subs, most, *refs):
    chunks = len(found)
    out_ref = refs[-1]
    steps = out_ref.shape[1]
    chunk_steps = steps // chunks
    block = most * chunk_steps
    here = lax.axis_index("streams")
    core = lax.axis_index("sub")
    shape = (chunks * block, chunks * block)
    out_row, in_row = iota(shape, 0), iota(shape, 1)
    step = out_row % steps
    wanted = step // chunk_steps * block + out_row // steps * chunk_steps + step % chunk_steps
    pick = (wanted == in_row).astype(jnp.float32).astype(jnp.bfloat16)
    for number in range(lanes):
        for other in range(subs):
            pieces = []
            for chunk in range(chunks):
                array, begin = found[chunk][number][other]
                pieces.append(refs[array][...][begin : begin + block])
            rows = jnp.dot(
                pick, jnp.concatenate(pieces, axis=0), preferred_element_type=jnp.float32
            )
            source = (here ^ number) * subs + (core ^ other)
            out_ref[pl.ds(source * most, most)] = rows.reshape(
                most, steps, rows.shape[1]
            ).astype(jnp.bfloat16)


def traded(blocks, axes):
    landed = list(blocks)
    count = len(blocks)
    order = sorted(range(1, count), key=lambda shift: -(shift ^ (shift >> 1)))
    for shift in order:
        pairs = [(place, place ^ shift) for place in range(count)]
        landed[shift] = lax.ppermute(blocks[shift], axes, pairs)
    return landed


def from_others(block, axis):
    count = lax.axis_size(axis)
    landed = [block]
    for shift in range(1, count):
        pairs = [(place, place ^ shift) for place in range(count)]
        landed.append(lax.ppermute(block, axis, pairs))
    return landed


def held(value, others):
    return lax.optimization_barrier((value, others))[0]


SMALL = pl.CostEstimate(flops=1, bytes_accessed=1, transcendentals=0)


def on_device(
    inputs,
    input_norm_gain,
    projection_weight,
    projection_bias,
    speaker,
    speaker_adapter_slot,
    cache_fill_length,
    rotated_key_cache,
    value_cache_rows,
    adapter_down_maps,
    adapter_query_up,
    adapter_value_up,
    flow_decoder_owner,
):
    steps, rows, width = inputs.shape
    lanes = lax.axis_size("streams")
    subs = lax.axis_size("sub")
    heads = lax.axis_size("heads")
    flow_lanes = lanes * subs
    local_slots, sliced, _ = adapter_down_maps.shape
    query_columns = adapter_query_up.shape[2]
    value_columns = adapter_value_up.shape[2]
    groups = value_columns // HEAD_WIDTH
    cache = rotated_key_cache.shape[1]
    spots = subs * local_slots * MOST
    chunks = 2
    chunk_steps = steps // chunks
    chunk_rows = chunk_steps * rows
    per_message = chunk_steps * spots
    chip_slots = subs * local_slots
    flow_most = max(2, (2 * rows + flow_lanes - 1) // flow_lanes)
    bf16, f32 = jnp.bfloat16, jnp.float32

    def whole(shape):
        return pl.BlockSpec(shape, lambda i: (0,) * len(shape))

    in_hbm = pl.BlockSpec(memory_space=pltpu.HBM)

    down_maps = from_others(adapter_down_maps, "sub")
    query_maps = from_others(
        adapter_query_up.reshape(local_slots * ADAPTER_RANK, query_columns), "sub"
    )
    value_maps = from_others(
        adapter_value_up.reshape(local_slots * ADAPTER_RANK, value_columns), "sub"
    )

    pieces = 4
    flat = inputs.reshape(steps * rows, width)
    gain = input_norm_gain.reshape(width // 128, 128)
    message = jax.ShapeDtypeStruct((per_message, sliced), bf16)
    normed_shape = jax.ShapeDtypeStruct((steps * rows, width), bf16)
    places_shape = jax.ShapeDtypeStruct((8, rows), jnp.int32)
    tables = [
        speaker.reshape(1, rows),
        speaker_adapter_slot.reshape(1, -1),
        flow_decoder_owner.reshape(1, rows),
    ]
    buffers = [pltpu.VMEM((chunk_rows, width), bf16), pltpu.VMEM(gain.shape, f32)]
    table_buffers = [pltpu.VMEM(table.shape, jnp.int32) for table in tables]
    arrived = []
    for chunk in range(chunks):
        rows_block = pl.BlockSpec((chunk_rows, width), lambda i, chunk=chunk: (chunk, 0))
        first = chunk == 0
        operands = [gain, flat]
        if first:
            operands = tables + operands
        else:
            adapters = down_maps[1:], query_maps[1:], value_maps[1:]
            operands = [held(places, adapters)] + operands + [normed]
        normed, *messages = pl.pallas_call(
            functools.partial(
                norm_pack_kernel, chunk_steps, rows, flow_most, lanes, pieces, chunk
            ),
            grid=(1,),
            in_specs=[in_hbm] * 5 if first else [whole(places_shape.shape)] + [in_hbm] * 3,
            out_specs=[rows_block]
            + [whole(places_shape.shape)] * first
            + [whole(message.shape)] * lanes,
            out_shape=[normed_shape] + [places_shape] * first + [message] * lanes,
            scratch_shapes=buffers
            + table_buffers * first
            + [pltpu.SemaphoreType.DMA((pieces + 4,))],
            input_output_aliases={} if first else {3: 0},
            compiler_params=pltpu.CompilerParams(vmem_limit_bytes=PACK_LIMIT * MIB),
            cost_estimate=SMALL,
            name="norm_and_pack",
        )(*operands)
        if first:
            places, *messages = messages
        if first:
            arrived.append(traded(messages, "streams"))

    bias = projection_bias.reshape(-1, 128)
    columns = projection_weight.shape[1]
    block_columns = 256 if columns % 256 == 0 else 384
    blocks = columns // block_columns

    def project(begin, end, after):
        return pl.pallas_call(
            functools.partial(project_kernel, begin * block_columns // 128),
            grid=(end - begin,),
            in_specs=[whole(normed_shape.shape), whole(bias.shape)]
            + [
                pl.BlockSpec(
                    (width // DEPTH_CUTS, block_columns),
                    lambda i, number=number: (number, begin + i),
                )
                for number in range(DEPTH_CUTS)
            ],
            out_specs=pl.BlockSpec((steps * rows, block_columns), lambda i: (0, i)),
            out_shape=jax.ShapeDtypeStruct((steps * rows, (end - begin) * block_columns), f32),
            compiler_params=pltpu.CompilerParams(vmem_limit_bytes=PROJECT_LIMIT * MIB),
            cost_estimate=SMALL,
            name="project",
        )(normed, held(bias, after), *[projection_weight] * DEPTH_CUTS)

    def down(chunk, after):
        partial_latent = pl.pallas_call(
            functools.partial(down_kernel, lanes, spots),
            in_specs=[VMEM] * (lanes + subs),
            out_specs=VMEM,
            out_shape=jax.ShapeDtypeStruct((lanes * per_message, 2 * ADAPTER_RANK), f32),
            compiler_params=pltpu.CompilerParams(vmem_limit_bytes=16 * MIB),
            cost_estimate=SMALL,
            name="down",
        )(held(arrived[chunk][0], after), *arrived[chunk][1:], *down_maps)
        return from_others(partial_latent, "heads")

    def up(partials, after):
        message = jax.ShapeDtypeStruct((per_message, query_columns + value_columns), bf16)
        messages = pl.pallas_call(
            functools.partial(up_kernel, heads, subs, spots),
            in_specs=[VMEM] * (heads + 2 * subs),
            out_specs=[VMEM] * lanes,
            out_shape=[message] * lanes,
            compiler_params=pltpu.CompilerParams(vmem_limit_bytes=24 * MIB),
            cost_estimate=SMALL,
            name="up",
        )(held(partials[0], after), *partials[1:], *query_maps, *value_maps)
        return messages

    cut = blocks // 2
    qkv = [project(0, cut, messages)]
    messages = [messages[0]] + [
        held(message, (before, qkv)) for message, before in zip(messages[1:], arrived[0][1:])
    ]
    arrived.append(traded(messages, "streams"))
    partials = down(0, qkv)
    qkv.append(project(cut, blocks, partials[0]))

    half_width = HEAD_WIDTH // 2
    position = jnp.concatenate([cache_fill_length + step for step in range(steps)]).astype(f32)
    freq = jnp.exp(jnp.arange(half_width, dtype=f32) * (-math.log(1000000.0) / half_width))
    freq = jnp.concatenate([freq, freq])
    angle = position[:, None] * freq
    sign = jnp.where(jnp.arange(HEAD_WIDTH) < half_width, -1.0, 1.0).astype(f32)
    cosine = jnp.cos(angle)
    sine_part = jnp.sin(angle) * sign

    returned = []
    after = qkv
    for chunk in range(chunks):
        if chunk:
            partials = down(chunk, after)
        after = up(partials, after)
        messages = list(after)
        if chunk:
            for lane in range(1, lanes):
                messages[lane] = held(messages[lane], returned[-1][lane])
        returned.append(traded(messages, "streams"))

    length_row = cache_fill_length.reshape(1, rows)
    block = flow_most * chunk_steps
    earlier, along, alongs = [], [], []
    for chunk in range(chunks):
        last = chunk == chunks - 1
        message = jax.ShapeDtypeStruct((subs * block, query_columns), bf16)
        fresh = jax.ShapeDtypeStruct((chunk_rows, 2 * value_columns), f32)
        rows_of = lambda shape: pl.BlockSpec(shape, lambda i, chunk=chunk: (chunk, 0))
        results = pl.pallas_call(
            functools.partial(
                attend_kernel,
                chunk * chunk_steps,
                chunk_steps,
                rows,
                cache,
                groups,
                lanes,
                subs,
                last,
            ),
            grid=(1,),
            in_specs=[whole(places.shape), whole(length_row.shape)]
            + [rows_of((chunk_rows, HEAD_WIDTH))] * 2
            + [whole(rotated_key_cache.shape)] * 2
            + [rows_of((chunk_rows, part.shape[1])) for part in qkv]
            + [whole((per_message, query_columns + value_columns))] * lanes
            + [whole(block_rows.shape) for block_rows in earlier],
            out_specs=[whole(fresh.shape)] * (not last) + [whole(message.shape)] * lanes,
            out_shape=[fresh] * (not last) + [message] * lanes,
            scratch_shapes=[
                pltpu.VMEM((chunk_rows, query_columns + value_columns), f32),
                pltpu.VMEM((chunk_rows, query_columns), f32),
                pltpu.VMEM((rows, BATCH * cache), f32),
            ],
            compiler_params=pltpu.CompilerParams(vmem_limit_bytes=32 * MIB),
            cost_estimate=SMALL,
            name="attend",
        )(
            places if chunk else held(places, after),
            length_row,
            cosine,
            sine_part,
            rotated_key_cache,
            value_cache_rows,
            *qkv,
            *returned[chunk],
            *earlier,
        )
        if not last:
            earlier, results = [results[0]], results[1:]
        results = list(results)
        ahead = along or returned[-1]
        for lane in range(1, lanes):
            results[lane] = held(results[lane], ahead[1:])
        along = traded(results, "streams")
        alongs.append(along)

    landed, found = [], []
    for chunk, along in enumerate(alongs):
        base = len(landed)
        landed += along
        where = [[(base + lane, 0)] for lane in range(lanes)]
        for shift in range(1, subs):
            pairs = [(core, core ^ shift) for core in range(subs)]
            span = slice(shift * block, (shift + 1) * block)
            if chunk < chunks - 1:
                joined = jnp.concatenate([block_rows[span] for block_rows in along])
                for lane in range(lanes):
                    where[lane].append((len(landed), lane * block))
                landed.append(lax.ppermute(joined, "sub", pairs))
            else:
                for lane, block_rows in enumerate(along):
                    where[lane].append((len(landed), shift * block))
                    landed.append(lax.ppermute(block_rows, "sub", pairs))
        found.append(where)

    flow = pl.pallas_call(
        functools.partial(place_kernel, found, lanes, subs, flow_most),
        in_specs=[VMEM] * len(landed),
        out_specs=VMEM,
        out_shape=jax.ShapeDtypeStruct((flow_lanes * flow_most, steps, query_columns), bf16),
        compiler_params=pltpu.CompilerParams(vmem_limit_bytes=24 * MIB),
        cost_estimate=SMALL,
        name="place",
    )(*landed)
    return flow[None]


def solution(mesh):
    placed = (
        P(None, ("groups", "streams", "sub"), None),
        P(),
        P(None, "heads"),
        P("heads"),
        P(("groups", "streams", "sub"), None),
        P("groups"),
        P(("groups", "streams", "sub")),
        P(("groups", "streams", "sub"), None, "heads"),
        P(("groups", "streams", "sub"), None, "heads"),
        P(("groups", "streams", "sub"), "heads", None),
        P(("groups", "streams", "sub"), None, "heads"),
        P(("groups", "streams", "sub"), None, "heads"),
        P(("groups", "streams", "sub"), None),
    )
    return jax.shard_map(
        on_device,
        mesh=mesh,
        in_specs=placed,
        out_specs=P(("groups", "streams", "sub"), None, None, "heads"),
        check_vma=False,
    )
```

```python
import functools
import math

import jax
import jax.numpy as jnp
from jax import lax
from jax.experimental import pallas as pl
from jax.experimental.pallas import tpu as pltpu
from jax.sharding import PartitionSpec as P

QUERY_HEADS = 28
KEY_VALUE_HEADS = 4
HEAD_WIDTH = 128
ADAPTER_RANK = 64
MOST = 2
PER_GROUP = QUERY_HEADS // KEY_VALUE_HEADS
LANE_AXES = ("streams", "sub")
BATCH = 8
TOGETHER = 2
VMEM = pl.BlockSpec(memory_space=pltpu.VMEM)
MIB = 1 << 20
PACK_LIMIT = 56
PROJECT_LIMIT = 49


def iota(shape, dim):
    return lax.broadcasted_iota(jnp.int32, shape, dim)


def as_column(row):
    count = row.shape[1]
    square = (count, count)
    same = iota(square, 0) == iota(square, 1)
    return jnp.sum(jnp.where(same, jnp.broadcast_to(row, square), 0), axis=1, keepdims=True)


def ranked(labels, most):
    count = labels.shape[1]
    square = (count, count)
    earlier = (as_column(labels) == labels) & (iota(square, 0) < iota(square, 1))
    return labels * most + jnp.sum(earlier.astype(jnp.int32), axis=0, keepdims=True)


def slot_places(speaker, table, lane_base):
    speakers_all = table.shape[1]
    rows = speaker.shape[1]
    match = iota((speakers_all, rows), 0) == speaker
    slots = jnp.sum(jnp.where(match, as_column(table), 0), axis=0, keepdims=True)
    return ranked(slots ^ lane_base, MOST)


def norm_in_pieces(
    pieces, begin, x_hbm, gain_hbm, x_buf, gain_buf, semaphores, normed_ref, started=None
):
    count, width = x_buf.shape
    size = count // pieces
    gain_copy = pltpu.make_async_copy(gain_hbm, gain_buf, semaphores.at[pieces])
    copies = []
    for piece in range(pieces):
        copies.append(
            pltpu.make_async_copy(
                x_hbm.at[pl.ds(begin + piece * size, size)],
                x_buf.at[pl.ds(piece * size, size)],
                semaphores.at[piece],
            )
        )
        copies[-1].start()
        if piece == 0:
            gain_copy.start()
    if started is not None:
        started()
    gain_copy.wait()
    gain = jnp.concatenate([gain_buf[i : i + 1, :] for i in range(gain_buf.shape[0])], axis=1)
    for piece in range(pieces):
        copies[piece].wait()

        def one(index, carry):
            span = pl.ds(pl.multiple_of(piece * size + index * 16, 16), 16)
            values = x_buf[span, :].astype(jnp.float32)
            mean_sq = jnp.sum(values * values, axis=1, keepdims=True) * (1.0 / width)
            normed = values * lax.rsqrt(mean_sq + 1e-06) * gain
            normed_ref[span, :] = normed.astype(jnp.bfloat16)
            return carry

        lax.fori_loop(0, size // 16, one, 0)


def pack_messages(steps, rows, places, normed_ref, message_refs):
    per_message, sliced = message_refs[0].shape
    spots = per_message // steps
    shape = (len(message_refs) * per_message, steps * rows)
    out_row = iota(shape, 0)
    wanted = out_row // per_message * spots + out_row % spots
    out_step = out_row % per_message // spots
    places = jnp.concatenate([places] * steps, axis=1)
    pick = (wanted == places) & (out_step == iota(shape, 1) // rows)
    pick = pick.astype(jnp.float32).astype(jnp.bfloat16)
    begin = pl.multiple_of(lax.axis_index("heads") * sliced, 128)
    own = normed_ref[:, pl.ds(begin, sliced)]
    packed = jnp.dot(pick, own, preferred_element_type=jnp.float32).astype(jnp.bfloat16)
    for number, message_ref in enumerate(message_refs):
        message_ref[...] = packed[number * per_message : (number + 1) * per_message]


def table_copies(table_hbms, table_bufs, semaphores, first):
    copies = [
        pltpu.make_async_copy(source, target, semaphores.at[first + number])
        for number, (source, target) in enumerate(zip(table_hbms, table_bufs))
    ]
    for copy in copies:
        copy.start()
    return copies


def places_from(table_bufs, spots, flow_most):
    speaker, table, owner = [buffer[...] for buffer in table_bufs]
    here, core, subs = lax.axis_index("streams"), lax.axis_index("sub"), lax.axis_size("sub")
    places = slot_places(speaker, table, here * (spots // MOST))
    return places, ranked(owner ^ (here * subs + core), flow_most)


def norm_pack_kernel(steps, rows, flow_most, lanes, pieces, *refs):
    table_hbms, gain_hbm, x_hbm, message_refs = refs[:3], refs[3], refs[4], refs[5 : 5 + lanes]
    x_buf, gain_buf, *table_bufs, semaphores, normed_ref = refs[5 + lanes :]
    copies = table_copies(table_hbms, table_bufs, semaphores, pieces + 1)
    norm_in_pieces(pieces, 0, x_hbm, gain_hbm, x_buf, gain_buf, semaphores, normed_ref)
    for copy in copies:
        copy.wait()
    spots = message_refs[0].shape[0] // steps
    places, _ = places_from(table_bufs, spots, flow_most)
    pack_messages(steps, rows, places, normed_ref, message_refs)


def weight_copies(begin, weight_hbm, weight_buf, semaphores):
    columns = weight_buf.shape[2]
    return [
        pltpu.make_async_copy(
            weight_hbm.at[:, pl.ds((begin + block) * columns, columns)],
            weight_buf.at[block],
            semaphores.at[block],
        )
        for block in range(weight_buf.shape[0])
    ]


def project_blocks(begin, copies, rows_ref, weight_buf, bias_ref, out_ref):
    columns = weight_buf.shape[2]
    tiles = columns // 128
    for block, copy in enumerate(copies):
        first = (begin + block) * tiles
        bias = [bias_ref[tile : tile + 1, :] for tile in range(first, first + tiles)]
        copy.wait()
        product = jnp.dot(rows_ref[...], weight_buf[block], preferred_element_type=jnp.float32)
        out_ref[:, block * columns : (block + 1) * columns] = product + jnp.concatenate(
            bias, axis=1
        )


def norm_pack_project_kernel(steps, rows, flow_most, lanes, pieces, chunk, *refs):
    table_hbms, bias_ref, gain_hbm, x_hbm, weight_hbm = refs[:3], *refs[3:7]
    normed_ref, out_ref, places_ref, message_refs = *refs[7:10], refs[10 : 10 + lanes]
    x_buf, gain_buf, *table_bufs, semaphores, weight_buf, weight_semaphores = refs[10 + lanes :]
    copies = weight_copies(0, weight_hbm, weight_buf, weight_semaphores)
    tables = table_copies(table_hbms, table_bufs, semaphores, pieces + 1)

    def start_weights():
        for copy in copies:
            copy.start()

    norm_in_pieces(
        pieces, 0, x_hbm, gain_hbm, x_buf, gain_buf, semaphores, normed_ref, start_weights
    )
    for copy in tables:
        copy.wait()
    spots = message_refs[0].shape[0] // steps
    places, flow_places = places_from(table_bufs, spots, flow_most)
    places_ref[0:1, :] = places
    places_ref[1:2, :] = flow_places
    count = steps * rows
    own_ref = normed_ref.at[pl.ds(chunk * count, count)]
    pack_messages(steps, rows, places, own_ref, message_refs)
    project_blocks(0, copies, normed_ref, weight_buf, bias_ref, out_ref)


def project_kernel(begin, rows_ref, bias_ref, weight_hbm, out_ref, weight_buf, semaphores):
    copies = weight_copies(begin, weight_hbm, weight_buf, semaphores)
    for copy in copies:
        copy.start()
    project_blocks(begin, copies, rows_ref, weight_buf, bias_ref, out_ref)


def row_slots(shape, spots):
    return iota(shape, 0) % spots // MOST


def down_kernel(lanes, spots, *refs):
    message_refs, map_refs, partial_ref = refs[:lanes], refs[lanes:-1], refs[-1]
    local_slots = map_refs[0].shape[0]
    rows = jnp.concatenate([ref[...] for ref in message_refs], axis=0)
    own_slot = row_slots(partial_ref.shape, spots)
    total = jnp.zeros(partial_ref.shape, jnp.float32)
    for number, map_ref in enumerate(map_refs):
        shift = (lax.axis_index("sub") ^ number) * local_slots
        for slot in range(local_slots):
            part = jnp.dot(rows, map_ref[slot], preferred_element_type=jnp.float32)
            total = jnp.where(own_slot == shift + slot, part, total)
    partial_ref[...] = total


def up_kernel(heads, subs, spots, *refs):
    partial_refs, refs = refs[:heads], refs[heads:]
    query_refs, value_refs, message_refs = refs[:subs], refs[subs : 2 * subs], refs[2 * subs :]
    total = partial_refs[0][...]
    for ref in partial_refs[1:]:
        total = total + ref[...]
    latent = total.astype(jnp.bfloat16).astype(jnp.float32)
    own_slot = row_slots(latent.shape, spots)
    column = iota(latent.shape, 1) // ADAPTER_RANK
    turned = pltpu.roll(latent, ADAPTER_RANK, 1)
    low = iota(latent.shape, 1) < ADAPTER_RANK
    query_pair = jnp.where(low, latent, turned)
    value_pair = jnp.where(low, turned, latent)

    def product(pair, map_refs):
        result = None
        for number, map_ref in enumerate(map_refs):
            local_slots = map_ref.shape[0] // ADAPTER_RANK
            shift = (lax.axis_index("sub") ^ number) * local_slots
            pieces = []
            for slot in range(0, local_slots, 2):
                kept = jnp.where(own_slot == shift + slot + column, pair, 0.0)
                pieces.append(kept.astype(jnp.bfloat16))
            wide = jnp.concatenate(pieces, axis=1)
            part = jnp.dot(wide, map_ref[...], preferred_element_type=jnp.float32)
            result = part if result is None else result + part
        return result.astype(jnp.bfloat16)

    queries = product(query_pair, query_refs)
    values = product(value_pair, value_refs)
    query_width = queries.shape[1]
    per_message = message_refs[0].shape[0]
    for number, ref in enumerate(message_refs):
        span = slice(number * per_message, (number + 1) * per_message)
        ref[:, :query_width] = queries[span]
        ref[:, query_width:] = values[span]


def attend_kernel(before, steps, rows, cache, groups, lanes, subs, last, *refs):
    places_ref, length_ref, cos_ref, sin_ref, key_ref, value_ref = refs[:6]
    qkv_refs, refs = refs[6:8], refs[8:]
    delta_refs, refs = refs[:lanes], refs[lanes:]
    if before:
        earlier_ref, refs = refs[0], refs[1:]
    if not last:
        fresh_ref, refs = refs[0], refs[1:]
    message_refs = refs[:lanes]
    delta_ref, context_ref, bias_ref = refs[lanes:]
    per_message = delta_refs[0].shape[0]
    spots = per_message // steps
    query_width = PER_GROUP * HEAD_WIDTH
    known = before + steps

    def qkv_tile(span, group, head):
        begin = (group * (PER_GROUP + 2) + head) * HEAD_WIDTH
        edge = qkv_refs[0].shape[1]
        if begin < edge:
            return qkv_refs[0][span, begin : begin + HEAD_WIDTH]
        return qkv_refs[1][span, begin - edge : begin - edge + HEAD_WIDTH]

    wide = groups * HEAD_WIDTH

    column = as_column(places_ref[0:1, :])
    column = jnp.concatenate([column] * steps, axis=0)
    shape = (steps * rows, lanes * per_message)
    out_row = iota(shape, 1)
    wanted = out_row // per_message * spots + out_row % spots
    pick = (wanted == column) & (out_row % per_message // spots == iota(shape, 0) // rows)
    pick = pick.astype(jnp.float32).astype(jnp.bfloat16)
    delta_ref[...] = jnp.dot(
        pick,
        jnp.concatenate([ref[...] for ref in delta_refs], axis=0),
        preferred_element_type=jnp.float32,
    )

    shape = (rows, BATCH * cache)
    lengths = as_column(length_ref[...])
    slot_column = iota(shape, 1)
    allowed = (slot_column // cache == iota(shape, 0) % BATCH) & (slot_column % cache < lengths)
    bias_ref[...] = jnp.where(allowed, 0.0, -1e30)
    shape = (steps, BATCH, known * BATCH)
    fresh_column = iota(shape, 2)
    allowed = (fresh_column % BATCH == iota(shape, 1)) & (
        fresh_column // BATCH <= iota(shape, 0) + before
    )
    fresh_bias = jnp.where(allowed, 0.0, -1e30)
    scale = HEAD_WIDTH ** (-0.5)
    transposed = (((1,), (1,)), ((), ()))

    def scored(first, group):
        spans = [pl.ds(pl.multiple_of(step * rows + first, BATCH), BATCH) for step in range(known)]
        query_tiles, key_tiles, value_tiles = [], [], []
        lane_span = slice(group * HEAD_WIDTH, (group + 1) * HEAD_WIDTH)
        value_span = slice(wide + group * HEAD_WIDTH, wide + (group + 1) * HEAD_WIDTH)
        for span in spans[:before]:
            key_tiles.append(earlier_ref[span, lane_span])
            value_tiles.append(earlier_ref[span, value_span])
        for span in spans[:steps]:
            cosine, sine_part = cos_ref[span, :], sin_ref[span, :]

            def rotated(values):
                return values * cosine + pltpu.roll(values, HEAD_WIDTH // 2, 1) * sine_part

            for head in range(PER_GROUP):
                begin = group * query_width + head * HEAD_WIDTH
                change = delta_ref[span, begin : begin + HEAD_WIDTH]
                query_tiles.append(rotated(qkv_tile(span, group, head) + change))
            key = rotated(qkv_tile(span, group, PER_GROUP))
            begin = groups * query_width + group * HEAD_WIDTH
            change = delta_ref[span, begin : begin + HEAD_WIDTH]
            value = qkv_tile(span, group, PER_GROUP + 1) + change
            if not last:
                fresh_ref[span, lane_span] = key
                fresh_ref[span, value_span] = value
            key_tiles.append(key)
            value_tiles.append(value)
        queries = jnp.concatenate(query_tiles, axis=0).astype(jnp.bfloat16)
        new_keys = jnp.concatenate(key_tiles, axis=0).astype(jnp.bfloat16)
        new_values = jnp.concatenate(value_tiles, axis=0).astype(jnp.bfloat16)
        old_keys = key_ref[pl.ds(first, BATCH), :, lane_span].reshape(BATCH * cache, HEAD_WIDTH)
        old_scores = lax.dot_general(
            queries, old_keys, transposed, preferred_element_type=jnp.float32
        )
        new_scores = lax.dot_general(
            queries, new_keys, transposed, preferred_element_type=jnp.float32
        )
        return old_scores, new_scores, new_values

    def weighed(first, old_scores, new_scores):
        heads = steps * PER_GROUP
        old_scores = (old_scores * scale).reshape(heads, BATCH, BATCH * cache)
        old_scores = old_scores + bias_ref[pl.ds(first, BATCH), :][None]
        new_scores = (new_scores * scale).reshape(steps, PER_GROUP, BATCH, known * BATCH)
        new_scores = (new_scores + fresh_bias[:, None]).reshape(heads, BATCH, known * BATCH)
        peak = jnp.maximum(
            jnp.max(old_scores, axis=-1, keepdims=True),
            jnp.max(new_scores, axis=-1, keepdims=True),
        )
        old_scores = jnp.exp(old_scores - peak)
        new_scores = jnp.exp(new_scores - peak)
        share = 1.0 / (
            jnp.sum(old_scores, axis=-1, keepdims=True)
            + jnp.sum(new_scores, axis=-1, keepdims=True)
        )
        old_weights = (old_scores * share).reshape(heads * BATCH, BATCH * cache)
        new_weights = (new_scores * share).reshape(heads * BATCH, known * BATCH)
        return old_weights.astype(jnp.bfloat16), new_weights.astype(jnp.bfloat16)

    def batch(index, carry):
        chains = []
        for number in range(TOGETHER):
            first = pl.multiple_of((index * TOGETHER + number) * BATCH, BATCH)
            chains += [(first, group) for group in range(groups)]
        scores = [scored(*chain) for chain in chains]
        weights = [weighed(chain[0], *score[:2]) for chain, score in zip(chains, scores)]
        for (first, group), (old_weights, new_weights), score in zip(chains, weights, scores):
            lane_span = slice(group * HEAD_WIDTH, (group + 1) * HEAD_WIDTH)
            old_values = value_ref[pl.ds(first, BATCH), :, lane_span]
            old_values = old_values.reshape(BATCH * cache, HEAD_WIDTH)
            context = jnp.dot(
                old_weights, old_values, preferred_element_type=jnp.float32
            ) + jnp.dot(new_weights, score[2], preferred_element_type=jnp.float32)
            for step in range(steps):
                span = pl.ds(pl.multiple_of(step * rows + first, BATCH), BATCH)
                for head in range(PER_GROUP):
                    row = (step * PER_GROUP + head) * BATCH
                    begin = group * query_width + head * HEAD_WIDTH
                    context_ref[span, begin : begin + HEAD_WIDTH] = context[row : row + BATCH]
        return carry

    lax.fori_loop(0, rows // (BATCH * TOGETHER), batch, 0)

    flow_places = jnp.concatenate([places_ref[1:2, :]] * steps, axis=1)
    context = context_ref[...].astype(jnp.bfloat16)
    count = message_refs[0].shape[0]
    shape = (count, steps * rows)
    out_row = iota(shape, 0)
    same_step = out_row % steps == iota(shape, 1) // rows
    for number, message_ref in enumerate(message_refs):
        wanted = number * (count // steps) + out_row // steps
        pick = ((flow_places == wanted) & same_step).astype(jnp.float32).astype(jnp.bfloat16)
        message_ref[...] = jnp.dot(
            pick, context, preferred_element_type=jnp.float32
        ).astype(jnp.bfloat16)


def place_kernel(found, lanes, subs, most, *refs):
    chunks = len(found)
    out_ref = refs[-1]
    steps = out_ref.shape[1]
    chunk_steps = steps // chunks
    block = most * chunk_steps
    here = lax.axis_index("streams")
    core = lax.axis_index("sub")
    shape = (chunks * block, chunks * block)
    out_row, in_row = iota(shape, 0), iota(shape, 1)
    step = out_row % steps
    wanted = step // chunk_steps * block + out_row // steps * chunk_steps + step % chunk_steps
    pick = (wanted == in_row).astype(jnp.float32).astype(jnp.bfloat16)
    for number in range(lanes):
        for other in range(subs):
            pieces = []
            for chunk in range(chunks):
                array, begin = found[chunk][number][other]
                pieces.append(refs[array][...][begin : begin + block])
            rows = jnp.dot(
                pick, jnp.concatenate(pieces, axis=0), preferred_element_type=jnp.float32
            )
            source = (here ^ number) * subs + (core ^ other)
            out_ref[pl.ds(source * most, most)] = rows.reshape(
                most, steps, rows.shape[1]
            ).astype(jnp.bfloat16)


def traded(blocks, axes):
    landed = list(blocks)
    count = len(blocks)
    order = sorted(range(1, count), key=lambda shift: -(shift ^ (shift >> 1)))
    for shift in order:
        pairs = [(place, place ^ shift) for place in range(count)]
        landed[shift] = lax.ppermute(blocks[shift], axes, pairs)
    return landed


def from_others(block, axis):
    count = lax.axis_size(axis)
    landed = [block]
    for shift in range(1, count):
        pairs = [(place, place ^ shift) for place in range(count)]
        landed.append(lax.ppermute(block, axis, pairs))
    return landed


def held(value, others):
    return lax.optimization_barrier((value, others))[0]


SMALL = pl.CostEstimate(flops=1, bytes_accessed=1, transcendentals=0)


def on_device(
    inputs,
    input_norm_gain,
    projection_weight,
    projection_bias,
    speaker,
    speaker_adapter_slot,
    cache_fill_length,
    rotated_key_cache,
    value_cache_rows,
    adapter_down_maps,
    adapter_query_up,
    adapter_value_up,
    flow_decoder_owner,
):
    steps, rows, width = inputs.shape
    lanes = lax.axis_size("streams")
    subs = lax.axis_size("sub")
    heads = lax.axis_size("heads")
    flow_lanes = lanes * subs
    local_slots, sliced, _ = adapter_down_maps.shape
    query_columns = adapter_query_up.shape[2]
    value_columns = adapter_value_up.shape[2]
    groups = value_columns // HEAD_WIDTH
    cache = rotated_key_cache.shape[1]
    spots = subs * local_slots * MOST
    chunks = 2
    chunk_steps = steps // chunks
    chunk_rows = chunk_steps * rows
    per_message = chunk_steps * spots
    chip_slots = subs * local_slots
    flow_most = max(2, (2 * rows + flow_lanes - 1) // flow_lanes)
    bf16, f32 = jnp.bfloat16, jnp.float32

    def whole(shape):
        return pl.BlockSpec(shape, lambda i: (0,) * len(shape))

    in_hbm = pl.BlockSpec(memory_space=pltpu.HBM)

    down_maps = from_others(adapter_down_maps, "sub")
    query_maps = from_others(
        adapter_query_up.reshape(local_slots * ADAPTER_RANK, query_columns), "sub"
    )
    value_maps = from_others(
        adapter_value_up.reshape(local_slots * ADAPTER_RANK, value_columns), "sub"
    )

    pieces = 4
    flat = inputs.reshape(steps * rows, width)
    gain = input_norm_gain.reshape(width // 128, 128)
    message = jax.ShapeDtypeStruct((per_message, sliced), bf16)
    places_shape = jax.ShapeDtypeStruct((8, rows), jnp.int32)
    tables = [
        speaker.reshape(1, rows),
        speaker_adapter_slot.reshape(1, -1),
        flow_decoder_owner.reshape(1, rows),
    ]

    def row_buffers(count):
        return (
            [pltpu.VMEM((count, width), bf16), pltpu.VMEM(gain.shape, f32)]
            + [pltpu.VMEM(table.shape, jnp.int32) for table in tables]
            + [pltpu.SemaphoreType.DMA((pieces + 4,))]
        )

    messages = pl.pallas_call(
        functools.partial(norm_pack_kernel, chunk_steps, rows, flow_most, lanes, pieces),
        in_specs=[in_hbm] * 5,
        out_specs=[VMEM] * lanes,
        out_shape=[message] * lanes,
        scratch_shapes=row_buffers(chunk_rows) + [pltpu.VMEM((chunk_rows, width), bf16)],
        compiler_params=pltpu.CompilerParams(vmem_limit_bytes=PACK_LIMIT * MIB),
        cost_estimate=SMALL,
        name="norm_and_pack",
    )(*tables, gain, flat)
    arrived = [traded(messages, "streams")]

    bias = projection_bias.reshape(-1, 128)
    columns = projection_weight.shape[1]
    block_columns = 256 if columns % 256 == 0 else 384
    blocks = columns // block_columns
    cut = blocks // 2

    def weight_buffers(count):
        return [
            pltpu.VMEM((count, width, block_columns), bf16),
            pltpu.SemaphoreType.DMA((count,)),
        ]

    def projected(count):
        return jax.ShapeDtypeStruct((steps * rows, count * block_columns), f32)

    adapters = down_maps[1:], query_maps[1:], value_maps[1:]
    weight_buf, weight_semaphores = weight_buffers(cut)
    normed, first_qkv, places, *messages = pl.pallas_call(
        functools.partial(
            norm_pack_project_kernel, chunk_steps, rows, flow_most, lanes, 2 * pieces, 1
        ),
        in_specs=[in_hbm] * 3 + [VMEM] + [in_hbm] * 3,
        out_specs=[VMEM] * (3 + lanes),
        out_shape=[jax.ShapeDtypeStruct((steps * rows, width), bf16), projected(cut)]
        + [places_shape]
        + [message] * lanes,
        scratch_shapes=row_buffers(steps * rows)[:-1]
        + [pltpu.SemaphoreType.DMA((2 * pieces + 4,))]
        + [weight_buf, weight_semaphores],
        compiler_params=pltpu.CompilerParams(vmem_limit_bytes=PROJECT_LIMIT * MIB),
        cost_estimate=SMALL,
        name="norm_pack_project",
    )(*tables, held(bias, (adapters, messages)), gain, flat, projection_weight)
    arrived.append(traded(messages, "streams"))
    qkv = [first_qkv]

    def project(after):
        return pl.pallas_call(
            functools.partial(project_kernel, cut),
            in_specs=[VMEM, VMEM, in_hbm],
            out_specs=VMEM,
            out_shape=projected(blocks - cut),
            scratch_shapes=weight_buffers(blocks - cut),
            compiler_params=pltpu.CompilerParams(vmem_limit_bytes=PROJECT_LIMIT * MIB),
            cost_estimate=SMALL,
            name="project",
        )(normed, held(bias, after), projection_weight)

    def down(chunk, after):
        partial_latent = pl.pallas_call(
            functools.partial(down_kernel, lanes, spots),
            in_specs=[VMEM] * (lanes + subs),
            out_specs=VMEM,
            out_shape=jax.ShapeDtypeStruct((lanes * per_message, 2 * ADAPTER_RANK), f32),
            compiler_params=pltpu.CompilerParams(vmem_limit_bytes=16 * MIB),
            cost_estimate=SMALL,
            name="down",
        )(held(arrived[chunk][0], after), *arrived[chunk][1:], *down_maps)
        return from_others(partial_latent, "heads")

    def up(partials, after):
        message = jax.ShapeDtypeStruct((per_message, query_columns + value_columns), bf16)
        messages = pl.pallas_call(
            functools.partial(up_kernel, heads, subs, spots),
            in_specs=[VMEM] * (heads + 2 * subs),
            out_specs=[VMEM] * lanes,
            out_shape=[message] * lanes,
            compiler_params=pltpu.CompilerParams(vmem_limit_bytes=24 * MIB),
            cost_estimate=SMALL,
            name="up",
        )(held(partials[0], after), *partials[1:], *query_maps, *value_maps)
        return messages

    half_width = HEAD_WIDTH // 2
    position = jnp.concatenate([cache_fill_length + step for step in range(steps)]).astype(f32)
    freq = jnp.exp(jnp.arange(half_width, dtype=f32) * (-math.log(1000000.0) / half_width))
    freq = jnp.concatenate([freq, freq])
    angle = position[:, None] * freq
    sign = jnp.where(jnp.arange(HEAD_WIDTH) < half_width, -1.0, 1.0).astype(f32)
    cosine = jnp.cos(angle)
    sine_part = jnp.sin(angle) * sign

    returned = []
    after = qkv
    for chunk in range(chunks):
        partials = down(chunk, after)
        if chunk:
            qkv.append(project(partials[0]))
        after = up(partials, qkv)
        messages = list(after)
        if chunk:
            for lane in range(1, lanes):
                messages[lane] = held(messages[lane], returned[-1][lane])
        returned.append(traded(messages, "streams"))

    length_row = cache_fill_length.reshape(1, rows)
    block = flow_most * chunk_steps
    earlier, along, alongs = [], [], []
    for chunk in range(chunks):
        last = chunk == chunks - 1
        message = jax.ShapeDtypeStruct((subs * block, query_columns), bf16)
        fresh = jax.ShapeDtypeStruct((chunk_rows, 2 * value_columns), f32)
        rows_of = lambda shape: pl.BlockSpec(shape, lambda i, chunk=chunk: (chunk, 0))
        results = pl.pallas_call(
            functools.partial(
                attend_kernel,
                chunk * chunk_steps,
                chunk_steps,
                rows,
                cache,
                groups,
                lanes,
                subs,
                last,
            ),
            grid=(1,),
            in_specs=[whole(places.shape), whole(length_row.shape)]
            + [rows_of((chunk_rows, HEAD_WIDTH))] * 2
            + [whole(rotated_key_cache.shape)] * 2
            + [rows_of((chunk_rows, part.shape[1])) for part in qkv]
            + [whole((per_message, query_columns + value_columns))] * lanes
            + [whole(block_rows.shape) for block_rows in earlier],
            out_specs=[whole(fresh.shape)] * (not last) + [whole(message.shape)] * lanes,
            out_shape=[fresh] * (not last) + [message] * lanes,
            scratch_shapes=[
                pltpu.VMEM((chunk_rows, query_columns + value_columns), f32),
                pltpu.VMEM((chunk_rows, query_columns), f32),
                pltpu.VMEM((rows, BATCH * cache), f32),
            ],
            compiler_params=pltpu.CompilerParams(vmem_limit_bytes=32 * MIB),
            cost_estimate=SMALL,
            name="attend",
        )(
            places if chunk else held(places, after),
            length_row,
            cosine,
            sine_part,
            rotated_key_cache,
            value_cache_rows,
            *qkv,
            *returned[chunk],
            *earlier,
        )
        if not last:
            earlier, results = [results[0]], results[1:]
        results = list(results)
        ahead = along or returned[-1]
        for lane in range(1, lanes):
            results[lane] = held(results[lane], ahead[1:])
        along = traded(results, "streams")
        alongs.append(along)

    landed, found = [], []
    for chunk, along in enumerate(alongs):
        base = len(landed)
        landed += along
        where = [[(base + lane, 0)] for lane in range(lanes)]
        for shift in range(1, subs):
            pairs = [(core, core ^ shift) for core in range(subs)]
            span = slice(shift * block, (shift + 1) * block)
            if chunk < chunks - 1:
                joined = jnp.concatenate([block_rows[span] for block_rows in along])
                for lane in range(lanes):
                    where[lane].append((len(landed), lane * block))
                landed.append(lax.ppermute(joined, "sub", pairs))
            else:
                for lane, block_rows in enumerate(along):
                    where[lane].append((len(landed), shift * block))
                    landed.append(lax.ppermute(block_rows, "sub", pairs))
        found.append(where)

    flow = pl.pallas_call(
        functools.partial(place_kernel, found, lanes, subs, flow_most),
        in_specs=[VMEM] * len(landed),
        out_specs=VMEM,
        out_shape=jax.ShapeDtypeStruct((flow_lanes * flow_most, steps, query_columns), bf16),
        compiler_params=pltpu.CompilerParams(vmem_limit_bytes=24 * MIB),
        cost_estimate=SMALL,
        name="place",
    )(*landed)
    return flow[None]


def solution(mesh):
    placed = (
        P(None, ("groups", "streams", "sub"), None),
        P(),
        P(None, "heads"),
        P("heads"),
        P(("groups", "streams", "sub"), None),
        P("groups"),
        P(("groups", "streams", "sub")),
        P(("groups", "streams", "sub"), None, "heads"),
        P(("groups", "streams", "sub"), None, "heads"),
        P(("groups", "streams", "sub"), "heads", None),
        P(("groups", "streams", "sub"), None, "heads"),
        P(("groups", "streams", "sub"), None, "heads"),
        P(("groups", "streams", "sub"), None),
    )
    return jax.shard_map(
        on_device,
        mesh=mesh,
        in_specs=placed,
        out_specs=P(("groups", "streams", "sub"), None, None, "heads"),
        check_vma=False,
    )
```

```python
import functools
import math

import jax
import jax.numpy as jnp
from jax import lax
from jax.experimental import pallas as pl
from jax.experimental.pallas import tpu as pltpu
from jax.sharding import PartitionSpec as P

QUERY_HEADS = 28
KEY_VALUE_HEADS = 4
HEAD_WIDTH = 128
ADAPTER_RANK = 64
MOST = 2
PER_GROUP = QUERY_HEADS // KEY_VALUE_HEADS
LANE_AXES = ("streams", "sub")
BATCH = 8
TOGETHER = 2
VMEM = pl.BlockSpec(memory_space=pltpu.VMEM)
MIB = 1 << 20
PACK_LIMIT = 56
PROJECT_LIMIT = 49


def iota(shape, dim):
    return lax.broadcasted_iota(jnp.int32, shape, dim)


def as_column(row):
    count = row.shape[1]
    square = (count, count)
    same = iota(square, 0) == iota(square, 1)
    return jnp.sum(jnp.where(same, jnp.broadcast_to(row, square), 0), axis=1, keepdims=True)


def ranked(labels, most):
    count = labels.shape[1]
    square = (count, count)
    earlier = (as_column(labels) == labels) & (iota(square, 0) < iota(square, 1))
    return labels * most + jnp.sum(earlier.astype(jnp.int32), axis=0, keepdims=True)


def slot_places(speaker, table, lane_base):
    speakers_all = table.shape[1]
    rows = speaker.shape[1]
    match = iota((speakers_all, rows), 0) == speaker
    slots = jnp.sum(jnp.where(match, as_column(table), 0), axis=0, keepdims=True)
    return ranked(slots ^ lane_base, MOST)


def norm_in_pieces(
    pieces, begin, x_hbm, gain_hbm, x_buf, gain_buf, semaphores, normed_ref, started=None
):
    count, width = x_buf.shape
    size = count // pieces
    gain_copy = pltpu.make_async_copy(gain_hbm, gain_buf, semaphores.at[pieces])
    copies = []
    for piece in range(pieces):
        copies.append(
            pltpu.make_async_copy(
                x_hbm.at[pl.ds(begin + piece * size, size)],
                x_buf.at[pl.ds(piece * size, size)],
                semaphores.at[piece],
            )
        )
        copies[-1].start()
        if piece == 0:
            gain_copy.start()
    if started is not None:
        started()
    gain_copy.wait()
    gain = jnp.concatenate([gain_buf[i : i + 1, :] for i in range(gain_buf.shape[0])], axis=1)
    for piece in range(pieces):
        copies[piece].wait()

        def one(index, carry):
            span = pl.ds(pl.multiple_of(piece * size + index * 16, 16), 16)
            values = x_buf[span, :].astype(jnp.float32)
            mean_sq = jnp.sum(values * values, axis=1, keepdims=True) * (1.0 / width)
            normed = values * lax.rsqrt(mean_sq + 1e-06) * gain
            normed_ref[span, :] = normed.astype(jnp.bfloat16)
            return carry

        lax.fori_loop(0, size // 16, one, 0)


def pack_messages(steps, rows, places, normed_ref, message_refs):
    per_message, sliced = message_refs[0].shape
    spots = per_message // steps
    shape = (len(message_refs) * per_message, steps * rows)
    out_row = iota(shape, 0)
    wanted = out_row // per_message * spots + out_row % spots
    out_step = out_row % per_message // spots
    places = jnp.concatenate([places] * steps, axis=1)
    pick = (wanted == places) & (out_step == iota(shape, 1) // rows)
    pick = pick.astype(jnp.float32).astype(jnp.bfloat16)
    begin = pl.multiple_of(lax.axis_index("heads") * sliced, 128)
    own = normed_ref[:, pl.ds(begin, sliced)]
    packed = jnp.dot(pick, own, preferred_element_type=jnp.float32).astype(jnp.bfloat16)
    for number, message_ref in enumerate(message_refs):
        message_ref[...] = packed[number * per_message : (number + 1) * per_message]


def table_copies(table_hbms, table_bufs, semaphores, first):
    copies = [
        pltpu.make_async_copy(source, target, semaphores.at[first + number])
        for number, (source, target) in enumerate(zip(table_hbms, table_bufs))
    ]
    for copy in copies:
        copy.start()
    return copies


def places_from(table_bufs, spots, flow_most):
    speaker, table, owner = [buffer[...] for buffer in table_bufs]
    here, core, subs = lax.axis_index("streams"), lax.axis_index("sub"), lax.axis_size("sub")
    places = slot_places(speaker, table, here * (spots // MOST))
    return places, ranked(owner ^ (here * subs + core), flow_most)


def norm_pack_kernel(steps, rows, flow_most, lanes, pieces, *refs):
    table_hbms, gain_hbm, x_hbm, message_refs = refs[:3], refs[3], refs[4], refs[5 : 5 + lanes]
    x_buf, gain_buf, *table_bufs, semaphores, normed_ref = refs[5 + lanes :]
    copies = table_copies(table_hbms, table_bufs, semaphores, pieces + 1)
    norm_in_pieces(pieces, 0, x_hbm, gain_hbm, x_buf, gain_buf, semaphores, normed_ref)
    for copy in copies:
        copy.wait()
    spots = message_refs[0].shape[0] // steps
    places, _ = places_from(table_bufs, spots, flow_most)
    pack_messages(steps, rows, places, normed_ref, message_refs)


def weight_copies(begin, weight_hbm, weight_buf, semaphores):
    columns = weight_buf.shape[2]
    return [
        pltpu.make_async_copy(
            weight_hbm.at[:, pl.ds((begin + block) * columns, columns)],
            weight_buf.at[block],
            semaphores.at[block],
        )
        for block in range(weight_buf.shape[0])
    ]


def project_blocks(begin, copies, rows_ref, weight_buf, bias_ref, out_ref):
    columns = weight_buf.shape[2]
    tiles = columns // 128
    for block, copy in enumerate(copies):
        first = (begin + block) * tiles
        bias = [bias_ref[tile : tile + 1, :] for tile in range(first, first + tiles)]
        copy.wait()
        product = jnp.dot(rows_ref[...], weight_buf[block], preferred_element_type=jnp.float32)
        out_ref[:, block * columns : (block + 1) * columns] = product + jnp.concatenate(
            bias, axis=1
        )


def norm_pack_project_kernel(steps, rows, flow_most, lanes, pieces, chunk, *refs):
    table_hbms, bias_ref, gain_hbm, x_hbm, weight_hbm = refs[:3], *refs[3:7]
    normed_ref, out_ref, places_ref, message_refs = *refs[7:10], refs[10 : 10 + lanes]
    x_buf, gain_buf, *table_bufs, semaphores, weight_buf, weight_semaphores = refs[10 + lanes :]
    copies = weight_copies(0, weight_hbm, weight_buf, weight_semaphores)
    tables = table_copies(table_hbms, table_bufs, semaphores, pieces + 1)

    def start_weights():
        for copy in copies:
            copy.start()

    norm_in_pieces(
        pieces, 0, x_hbm, gain_hbm, x_buf, gain_buf, semaphores, normed_ref, start_weights
    )
    for copy in tables:
        copy.wait()
    spots = message_refs[0].shape[0] // steps
    places, flow_places = places_from(table_bufs, spots, flow_most)
    places_ref[0:1, :] = places
    places_ref[1:2, :] = flow_places
    count = steps * rows
    own_ref = normed_ref.at[pl.ds(chunk * count, count)]
    pack_messages(steps, rows, places, own_ref, message_refs)
    project_blocks(0, copies, normed_ref, weight_buf, bias_ref, out_ref)


def project_kernel(begin, rows_ref, bias_ref, weight_hbm, out_ref, weight_buf, semaphores):
    copies = weight_copies(begin, weight_hbm, weight_buf, semaphores)
    for copy in copies:
        copy.start()
    project_blocks(begin, copies, rows_ref, weight_buf, bias_ref, out_ref)


def row_slots(shape, spots):
    return iota(shape, 0) % spots // MOST


def down_kernel(lanes, spots, *refs):
    message_refs, map_refs, partial_ref = refs[:lanes], refs[lanes:-1], refs[-1]
    local_slots = map_refs[0].shape[0]
    rows = jnp.concatenate([ref[...] for ref in message_refs], axis=0)
    own_slot = row_slots(partial_ref.shape, spots)
    total = jnp.zeros(partial_ref.shape, jnp.float32)
    for number, map_ref in enumerate(map_refs):
        shift = (lax.axis_index("sub") ^ number) * local_slots
        for slot in range(local_slots):
            part = jnp.dot(rows, map_ref[slot], preferred_element_type=jnp.float32)
            total = jnp.where(own_slot == shift + slot, part, total)
    partial_ref[...] = total


def up_kernel(heads, subs, spots, *refs):
    partial_refs, refs = refs[:heads], refs[heads:]
    query_refs, value_refs, message_refs = refs[:subs], refs[subs : 2 * subs], refs[2 * subs :]
    total = partial_refs[0][...]
    for ref in partial_refs[1:]:
        total = total + ref[...]
    latent = total.astype(jnp.bfloat16).astype(jnp.float32)
    own_slot = row_slots(latent.shape, spots)
    column = iota(latent.shape, 1) // ADAPTER_RANK
    turned = pltpu.roll(latent, ADAPTER_RANK, 1)
    low = iota(latent.shape, 1) < ADAPTER_RANK
    query_pair = jnp.where(low, latent, turned)
    value_pair = jnp.where(low, turned, latent)

    def product(pair, map_refs):
        result = None
        for number, map_ref in enumerate(map_refs):
            local_slots = map_ref.shape[0] // ADAPTER_RANK
            shift = (lax.axis_index("sub") ^ number) * local_slots
            pieces = []
            for slot in range(0, local_slots, 2):
                kept = jnp.where(own_slot == shift + slot + column, pair, 0.0)
                pieces.append(kept.astype(jnp.bfloat16))
            wide = jnp.concatenate(pieces, axis=1)
            part = jnp.dot(wide, map_ref[...], preferred_element_type=jnp.float32)
            result = part if result is None else result + part
        return result.astype(jnp.bfloat16)

    queries = product(query_pair, query_refs)
    values = product(value_pair, value_refs)
    query_width = queries.shape[1]
    per_message = message_refs[0].shape[0]
    for number, ref in enumerate(message_refs):
        span = slice(number * per_message, (number + 1) * per_message)
        ref[:, :query_width] = queries[span]
        ref[:, query_width:] = values[span]


def attend_kernel(before, steps, rows, cache, groups, lanes, subs, last, *refs):
    places_ref, length_ref, cos_ref, sin_ref, key_ref, value_ref = refs[:6]
    qkv_refs, refs = refs[6:8], refs[8:]
    delta_refs, refs = refs[:lanes], refs[lanes:]
    if before:
        earlier_ref, refs = refs[0], refs[1:]
    if not last:
        fresh_ref, refs = refs[0], refs[1:]
    message_refs = refs[:lanes]
    delta_ref, context_ref, bias_ref = refs[lanes:]
    per_message = delta_refs[0].shape[0]
    spots = per_message // steps
    query_width = PER_GROUP * HEAD_WIDTH
    known = before + steps

    def qkv_tile(span, group, head):
        begin = (group * (PER_GROUP + 2) + head) * HEAD_WIDTH
        edge = qkv_refs[0].shape[1]
        if begin < edge:
            return qkv_refs[0][span, begin : begin + HEAD_WIDTH]
        return qkv_refs[1][span, begin - edge : begin - edge + HEAD_WIDTH]

    wide = groups * HEAD_WIDTH

    column = as_column(places_ref[0:1, :])
    column = jnp.concatenate([column] * steps, axis=0)
    shape = (steps * rows, lanes * per_message)
    out_row = iota(shape, 1)
    wanted = out_row // per_message * spots + out_row % spots
    pick = (wanted == column) & (out_row % per_message // spots == iota(shape, 0) // rows)
    pick = pick.astype(jnp.float32).astype(jnp.bfloat16)
    delta_ref[...] = jnp.dot(
        pick,
        jnp.concatenate([ref[...] for ref in delta_refs], axis=0),
        preferred_element_type=jnp.float32,
    )

    shape = (rows, BATCH * cache)
    lengths = as_column(length_ref[...])
    slot_column = iota(shape, 1)
    allowed = (slot_column // cache == iota(shape, 0) % BATCH) & (slot_column % cache < lengths)
    bias_ref[...] = jnp.where(allowed, 0.0, -1e30)
    shape = (steps, BATCH, known * BATCH)
    fresh_column = iota(shape, 2)
    allowed = (fresh_column % BATCH == iota(shape, 1)) & (
        fresh_column // BATCH <= iota(shape, 0) + before
    )
    fresh_bias = jnp.where(allowed, 0.0, -1e30)
    scale = HEAD_WIDTH ** (-0.5)
    transposed = (((1,), (1,)), ((), ()))

    def scored(first, group):
        spans = [pl.ds(pl.multiple_of(step * rows + first, BATCH), BATCH) for step in range(known)]
        query_tiles, key_tiles, value_tiles = [], [], []
        lane_span = slice(group * HEAD_WIDTH, (group + 1) * HEAD_WIDTH)
        value_span = slice(wide + group * HEAD_WIDTH, wide + (group + 1) * HEAD_WIDTH)
        for span in spans[:before]:
            key_tiles.append(earlier_ref[span, lane_span])
            value_tiles.append(earlier_ref[span, value_span])
        for span in spans[:steps]:
            cosine, sine_part = cos_ref[span, :], sin_ref[span, :]

            def rotated(values):
                return values * cosine + pltpu.roll(values, HEAD_WIDTH // 2, 1) * sine_part

            for head in range(PER_GROUP):
                begin = group * query_width + head * HEAD_WIDTH
                change = delta_ref[span, begin : begin + HEAD_WIDTH]
                query_tiles.append(rotated(qkv_tile(span, group, head) + change))
            key = rotated(qkv_tile(span, group, PER_GROUP))
            begin = groups * query_width + group * HEAD_WIDTH
            change = delta_ref[span, begin : begin + HEAD_WIDTH]
            value = qkv_tile(span, group, PER_GROUP + 1) + change
            if not last:
                fresh_ref[span, lane_span] = key
                fresh_ref[span, value_span] = value
            key_tiles.append(key)
            value_tiles.append(value)
        queries = jnp.concatenate(query_tiles, axis=0).astype(jnp.bfloat16)
        new_keys = jnp.concatenate(key_tiles, axis=0).astype(jnp.bfloat16)
        new_values = jnp.concatenate(value_tiles, axis=0).astype(jnp.bfloat16)
        old_keys = key_ref[pl.ds(first, BATCH), :, lane_span].reshape(BATCH * cache, HEAD_WIDTH)
        old_scores = lax.dot_general(
            queries, old_keys, transposed, preferred_element_type=jnp.float32
        )
        new_scores = lax.dot_general(
            queries, new_keys, transposed, preferred_element_type=jnp.float32
        )
        return old_scores, new_scores, new_values

    def weighed(first, old_scores, new_scores):
        heads = steps * PER_GROUP
        old_scores = (old_scores * scale).reshape(heads, BATCH, BATCH * cache)
        old_scores = old_scores + bias_ref[pl.ds(first, BATCH), :][None]
        new_scores = (new_scores * scale).reshape(steps, PER_GROUP, BATCH, known * BATCH)
        new_scores = (new_scores + fresh_bias[:, None]).reshape(heads, BATCH, known * BATCH)
        peak = jnp.maximum(
            jnp.max(old_scores, axis=-1, keepdims=True),
            jnp.max(new_scores, axis=-1, keepdims=True),
        )
        old_scores = jnp.exp(old_scores - peak)
        new_scores = jnp.exp(new_scores - peak)
        share = 1.0 / (
            jnp.sum(old_scores, axis=-1, keepdims=True)
            + jnp.sum(new_scores, axis=-1, keepdims=True)
        )
        old_weights = (old_scores * share).reshape(heads * BATCH, BATCH * cache)
        new_weights = (new_scores * share).reshape(heads * BATCH, known * BATCH)
        return old_weights.astype(jnp.bfloat16), new_weights.astype(jnp.bfloat16)

    def batch(index, carry):
        chains = []
        for number in range(TOGETHER):
            first = pl.multiple_of((index * TOGETHER + number) * BATCH, BATCH)
            chains += [(first, group) for group in range(groups)]
        scores = [scored(*chain) for chain in chains]
        weights = [weighed(chain[0], *score[:2]) for chain, score in zip(chains, scores)]
        for (first, group), (old_weights, new_weights), score in zip(chains, weights, scores):
            lane_span = slice(group * HEAD_WIDTH, (group + 1) * HEAD_WIDTH)
            old_values = value_ref[pl.ds(first, BATCH), :, lane_span]
            old_values = old_values.reshape(BATCH * cache, HEAD_WIDTH)
            context = jnp.dot(
                old_weights, old_values, preferred_element_type=jnp.float32
            ) + jnp.dot(new_weights, score[2], preferred_element_type=jnp.float32)
            for step in range(steps):
                span = pl.ds(pl.multiple_of(step * rows + first, BATCH), BATCH)
                for head in range(PER_GROUP):
                    row = (step * PER_GROUP + head) * BATCH
                    begin = group * query_width + head * HEAD_WIDTH
                    context_ref[span, begin : begin + HEAD_WIDTH] = context[row : row + BATCH]
        return carry

    lax.fori_loop(0, rows // (BATCH * TOGETHER), batch, 0)

    flow_places = jnp.concatenate([places_ref[1:2, :]] * steps, axis=1)
    context = context_ref[...].astype(jnp.bfloat16)
    count = message_refs[0].shape[0]
    shape = (count, steps * rows)
    out_row = iota(shape, 0)
    same_step = out_row % steps == iota(shape, 1) // rows
    for number, message_ref in enumerate(message_refs):
        wanted = number * (count // steps) + out_row // steps
        pick = ((flow_places == wanted) & same_step).astype(jnp.float32).astype(jnp.bfloat16)
        message_ref[...] = jnp.dot(
            pick, context, preferred_element_type=jnp.float32
        ).astype(jnp.bfloat16)


def place_kernel(found, lanes, subs, most, *refs):
    chunks = len(found)
    out_ref = refs[-1]
    steps = out_ref.shape[1]
    chunk_steps = steps // chunks
    block = most * chunk_steps
    here = lax.axis_index("streams")
    core = lax.axis_index("sub")
    shape = (chunks * block, chunks * block)
    out_row, in_row = iota(shape, 0), iota(shape, 1)
    step = out_row % steps
    wanted = step // chunk_steps * block + out_row // steps * chunk_steps + step % chunk_steps
    pick = (wanted == in_row).astype(jnp.float32).astype(jnp.bfloat16)
    for number in range(lanes):
        for other in range(subs):
            pieces = []
            for chunk in range(chunks):
                array, begin = found[chunk][number][other]
                pieces.append(refs[array][...][begin : begin + block])
            rows = jnp.dot(
                pick, jnp.concatenate(pieces, axis=0), preferred_element_type=jnp.float32
            )
            source = (here ^ number) * subs + (core ^ other)
            out_ref[pl.ds(source * most, most)] = rows.reshape(
                most, steps, rows.shape[1]
            ).astype(jnp.bfloat16)


def traded(blocks, axes):
    landed = list(blocks)
    count = len(blocks)
    order = sorted(range(1, count), key=lambda shift: -(shift ^ (shift >> 1)))
    for shift in order:
        pairs = [(place, place ^ shift) for place in range(count)]
        landed[shift] = lax.ppermute(blocks[shift], axes, pairs)
    return landed


def from_others(block, axis):
    count = lax.axis_size(axis)
    landed = [block]
    for shift in range(1, count):
        pairs = [(place, place ^ shift) for place in range(count)]
        landed.append(lax.ppermute(block, axis, pairs))
    return landed


def held(value, others):
    return lax.optimization_barrier((value, others))[0]


SMALL = pl.CostEstimate(flops=1, bytes_accessed=1, transcendentals=0)


def on_device(
    inputs,
    input_norm_gain,
    projection_weight,
    projection_bias,
    speaker,
    speaker_adapter_slot,
    cache_fill_length,
    rotated_key_cache,
    value_cache_rows,
    adapter_down_maps,
    adapter_query_up,
    adapter_value_up,
    flow_decoder_owner,
):
    steps, rows, width = inputs.shape
    lanes = lax.axis_size("streams")
    subs = lax.axis_size("sub")
    heads = lax.axis_size("heads")
    flow_lanes = lanes * subs
    local_slots, sliced, _ = adapter_down_maps.shape
    query_columns = adapter_query_up.shape[2]
    value_columns = adapter_value_up.shape[2]
    groups = value_columns // HEAD_WIDTH
    cache = rotated_key_cache.shape[1]
    spots = subs * local_slots * MOST
    chunks = 2
    chunk_steps = steps // chunks
    chunk_rows = chunk_steps * rows
    per_message = chunk_steps * spots
    chip_slots = subs * local_slots
    flow_most = max(2, (2 * rows + flow_lanes - 1) // flow_lanes)
    bf16, f32 = jnp.bfloat16, jnp.float32

    def whole(shape):
        return pl.BlockSpec(shape, lambda i: (0,) * len(shape))

    in_hbm = pl.BlockSpec(memory_space=pltpu.HBM)

    down_maps = from_others(adapter_down_maps, "sub")
    query_maps = from_others(
        adapter_query_up.reshape(local_slots * ADAPTER_RANK, query_columns), "sub"
    )
    value_maps = from_others(
        adapter_value_up.reshape(local_slots * ADAPTER_RANK, value_columns), "sub"
    )

    pieces = 4
    flat = inputs.reshape(steps * rows, width)
    gain = input_norm_gain.reshape(width // 128, 128)
    message = jax.ShapeDtypeStruct((per_message, sliced), bf16)
    places_shape = jax.ShapeDtypeStruct((8, rows), jnp.int32)
    tables = [
        speaker.reshape(1, rows),
        speaker_adapter_slot.reshape(1, -1),
        flow_decoder_owner.reshape(1, rows),
    ]

    def row_buffers(count):
        return (
            [pltpu.VMEM((count, width), bf16), pltpu.VMEM(gain.shape, f32)]
            + [pltpu.VMEM(table.shape, jnp.int32) for table in tables]
            + [pltpu.SemaphoreType.DMA((pieces + 4,))]
        )

    messages = pl.pallas_call(
        functools.partial(norm_pack_kernel, chunk_steps, rows, flow_most, lanes, pieces),
        in_specs=[in_hbm] * 5,
        out_specs=[VMEM] * lanes,
        out_shape=[message] * lanes,
        scratch_shapes=row_buffers(chunk_rows) + [pltpu.VMEM((chunk_rows, width), bf16)],
        compiler_params=pltpu.CompilerParams(vmem_limit_bytes=PACK_LIMIT * MIB),
        cost_estimate=SMALL,
        name="norm_and_pack",
    )(*tables, gain, flat)
    arrived = [traded(messages, "streams")]

    bias = projection_bias.reshape(-1, 128)
    columns = projection_weight.shape[1]
    block_columns = 256 if columns % 256 == 0 else 384
    blocks = columns // block_columns
    cut = blocks // 2

    def weight_buffers(count):
        return [
            pltpu.VMEM((count, width, block_columns), bf16),
            pltpu.SemaphoreType.DMA((count,)),
        ]

    def projected(count):
        return jax.ShapeDtypeStruct((steps * rows, count * block_columns), f32)

    adapters = down_maps[1:], query_maps[1:], value_maps[1:]
    weight_buf, weight_semaphores = weight_buffers(cut)
    normed, first_qkv, places, *messages = pl.pallas_call(
        functools.partial(
            norm_pack_project_kernel, chunk_steps, rows, flow_most, lanes, 2 * pieces, 1
        ),
        in_specs=[in_hbm] * 3 + [VMEM] + [in_hbm] * 3,
        out_specs=[VMEM] * (3 + lanes),
        out_shape=[jax.ShapeDtypeStruct((steps * rows, width), bf16), projected(cut)]
        + [places_shape]
        + [message] * lanes,
        scratch_shapes=row_buffers(steps * rows)[:-1]
        + [pltpu.SemaphoreType.DMA((2 * pieces + 4,))]
        + [weight_buf, weight_semaphores],
        compiler_params=pltpu.CompilerParams(vmem_limit_bytes=PROJECT_LIMIT * MIB),
        cost_estimate=SMALL,
        name="norm_pack_project",
    )(*tables, held(bias, (adapters, messages)), gain, flat, projection_weight)
    arrived.append(traded(messages, "streams"))
    qkv = [first_qkv]

    def project(after):
        return pl.pallas_call(
            functools.partial(project_kernel, cut),
            in_specs=[VMEM, VMEM, in_hbm],
            out_specs=VMEM,
            out_shape=projected(blocks - cut),
            scratch_shapes=weight_buffers(blocks - cut),
            compiler_params=pltpu.CompilerParams(vmem_limit_bytes=PROJECT_LIMIT * MIB),
            cost_estimate=SMALL,
            name="project",
        )(normed, held(bias, after), projection_weight)

    def down(chunk, after):
        partial_latent = pl.pallas_call(
            functools.partial(down_kernel, lanes, spots),
            in_specs=[VMEM] * (lanes + subs),
            out_specs=VMEM,
            out_shape=jax.ShapeDtypeStruct((lanes * per_message, 2 * ADAPTER_RANK), f32),
            compiler_params=pltpu.CompilerParams(vmem_limit_bytes=16 * MIB),
            cost_estimate=SMALL,
            name="down",
        )(held(arrived[chunk][0], after), *arrived[chunk][1:], *down_maps)
        return from_others(partial_latent, "heads")

    def up(partials, after):
        message = jax.ShapeDtypeStruct((per_message, query_columns + value_columns), bf16)
        messages = pl.pallas_call(
            functools.partial(up_kernel, heads, subs, spots),
            in_specs=[VMEM] * (heads + 2 * subs),
            out_specs=[VMEM] * lanes,
            out_shape=[message] * lanes,
            compiler_params=pltpu.CompilerParams(vmem_limit_bytes=24 * MIB),
            cost_estimate=SMALL,
            name="up",
        )(held(partials[0], after), *partials[1:], *query_maps, *value_maps)
        return messages

    half_width = HEAD_WIDTH // 2
    position = jnp.concatenate([cache_fill_length + step for step in range(steps)]).astype(f32)
    freq = jnp.exp(jnp.arange(half_width, dtype=f32) * (-math.log(1000000.0) / half_width))
    freq = jnp.concatenate([freq, freq])
    angle = position[:, None] * freq
    sign = jnp.where(jnp.arange(HEAD_WIDTH) < half_width, -1.0, 1.0).astype(f32)
    cosine = jnp.cos(angle)
    sine_part = jnp.sin(angle) * sign

    returned = []
    after = qkv
    for chunk in range(chunks):
        if chunk:
            qkv.append(project(after))
        partials = down(chunk, qkv)
        after = up(partials, qkv)
        messages = list(after)
        if chunk:
            for lane in range(1, lanes):
                messages[lane] = held(messages[lane], returned[-1][lane])
        returned.append(traded(messages, "streams"))

    length_row = cache_fill_length.reshape(1, rows)
    block = flow_most * chunk_steps
    earlier, along, alongs = [], [], []
    for chunk in range(chunks):
        last = chunk == chunks - 1
        message = jax.ShapeDtypeStruct((subs * block, query_columns), bf16)
        fresh = jax.ShapeDtypeStruct((chunk_rows, 2 * value_columns), f32)
        rows_of = lambda shape: pl.BlockSpec(shape, lambda i, chunk=chunk: (chunk, 0))
        results = pl.pallas_call(
            functools.partial(
                attend_kernel,
                chunk * chunk_steps,
                chunk_steps,
                rows,
                cache,
                groups,
                lanes,
                subs,
                last,
            ),
            grid=(1,),
            in_specs=[whole(places.shape), whole(length_row.shape)]
            + [rows_of((chunk_rows, HEAD_WIDTH))] * 2
            + [whole(rotated_key_cache.shape)] * 2
            + [rows_of((chunk_rows, part.shape[1])) for part in qkv]
            + [whole((per_message, query_columns + value_columns))] * lanes
            + [whole(block_rows.shape) for block_rows in earlier],
            out_specs=[whole(fresh.shape)] * (not last) + [whole(message.shape)] * lanes,
            out_shape=[fresh] * (not last) + [message] * lanes,
            scratch_shapes=[
                pltpu.VMEM((chunk_rows, query_columns + value_columns), f32),
                pltpu.VMEM((chunk_rows, query_columns), f32),
                pltpu.VMEM((rows, BATCH * cache), f32),
            ],
            compiler_params=pltpu.CompilerParams(vmem_limit_bytes=32 * MIB),
            cost_estimate=SMALL,
            name="attend",
        )(
            places if chunk else held(places, after),
            length_row,
            cosine,
            sine_part,
            rotated_key_cache,
            value_cache_rows,
            *qkv,
            *returned[chunk],
            *earlier,
        )
        if not last:
            earlier, results = [results[0]], results[1:]
        results = list(results)
        ahead = along or returned[-1]
        for lane in range(1, lanes):
            results[lane] = held(results[lane], ahead[1:])
        along = traded(results, "streams")
        alongs.append(along)

    landed, found = [], []
    for chunk, along in enumerate(alongs):
        base = len(landed)
        landed += along
        where = [[(base + lane, 0)] for lane in range(lanes)]
        for shift in range(1, subs):
            pairs = [(core, core ^ shift) for core in range(subs)]
            span = slice(shift * block, (shift + 1) * block)
            if chunk < chunks - 1:
                joined = jnp.concatenate([block_rows[span] for block_rows in along])
                for lane in range(lanes):
                    where[lane].append((len(landed), lane * block))
                landed.append(lax.ppermute(joined, "sub", pairs))
            else:
                for lane, block_rows in enumerate(along):
                    where[lane].append((len(landed), shift * block))
                    landed.append(lax.ppermute(block_rows, "sub", pairs))
        found.append(where)

    flow = pl.pallas_call(
        functools.partial(place_kernel, found, lanes, subs, flow_most),
        in_specs=[VMEM] * len(landed),
        out_specs=VMEM,
        out_shape=jax.ShapeDtypeStruct((flow_lanes * flow_most, steps, query_columns), bf16),
        compiler_params=pltpu.CompilerParams(vmem_limit_bytes=24 * MIB),
        cost_estimate=SMALL,
        name="place",
    )(*landed)
    return flow[None]


def solution(mesh):
    placed = (
        P(None, ("groups", "streams", "sub"), None),
        P(),
        P(None, "heads"),
        P("heads"),
        P(("groups", "streams", "sub"), None),
        P("groups"),
        P(("groups", "streams", "sub")),
        P(("groups", "streams", "sub"), None, "heads"),
        P(("groups", "streams", "sub"), None, "heads"),
        P(("groups", "streams", "sub"), "heads", None),
        P(("groups", "streams", "sub"), None, "heads"),
        P(("groups", "streams", "sub"), None, "heads"),
        P(("groups", "streams", "sub"), None),
    )
    return jax.shard_map(
        on_device,
        mesh=mesh,
        in_specs=placed,
        out_specs=P(("groups", "streams", "sub"), None, None, "heads"),
        check_vma=False,
    )
```

```python
import functools
import math

import jax
import jax.numpy as jnp
from jax import lax
from jax.experimental import pallas as pl
from jax.experimental.pallas import tpu as pltpu
from jax.sharding import PartitionSpec as P

QUERY_HEADS = 28
KEY_VALUE_HEADS = 4
HEAD_WIDTH = 128
ADAPTER_RANK = 64
MOST = 2
PER_GROUP = QUERY_HEADS // KEY_VALUE_HEADS
LANE_AXES = ("streams", "sub")
BATCH = 8
TOGETHER = 2
IN_FLIGHT = 5
VMEM = pl.BlockSpec(memory_space=pltpu.VMEM)
MIB = 1 << 20
PACK_LIMIT = 56
PROJECT_LIMIT = 49


def iota(shape, dim):
    return lax.broadcasted_iota(jnp.int32, shape, dim)


def as_column(row):
    count = row.shape[1]
    square = (count, count)
    same = iota(square, 0) == iota(square, 1)
    return jnp.sum(jnp.where(same, jnp.broadcast_to(row, square), 0), axis=1, keepdims=True)


def ranked(labels, most):
    count = labels.shape[1]
    square = (count, count)
    earlier = (as_column(labels) == labels) & (iota(square, 0) < iota(square, 1))
    return labels * most + jnp.sum(earlier.astype(jnp.int32), axis=0, keepdims=True)


def slot_places(speaker, table, lane_base):
    speakers_all = table.shape[1]
    rows = speaker.shape[1]
    match = iota((speakers_all, rows), 0) == speaker
    slots = jnp.sum(jnp.where(match, as_column(table), 0), axis=0, keepdims=True)
    return ranked(slots ^ lane_base, MOST)


def norm_in_pieces(
    pieces, begin, x_hbm, gain_hbm, x_buf, gain_buf, semaphores, normed_ref, started=None
):
    count, width = x_buf.shape
    size = count // pieces
    gain_copy = pltpu.make_async_copy(gain_hbm, gain_buf, semaphores.at[pieces])
    copies = []
    for piece in range(pieces):
        copies.append(
            pltpu.make_async_copy(
                x_hbm.at[pl.ds(begin + piece * size, size)],
                x_buf.at[pl.ds(piece * size, size)],
                semaphores.at[piece],
            )
        )
        copies[-1].start()
        if piece == 0:
            gain_copy.start()
    if started is not None:
        started()
    gain_copy.wait()
    gain = jnp.concatenate([gain_buf[i : i + 1, :] for i in range(gain_buf.shape[0])], axis=1)
    for piece in range(pieces):
        copies[piece].wait()

        def one(index, carry):
            span = pl.ds(pl.multiple_of(piece * size + index * 16, 16), 16)
            values = x_buf[span, :].astype(jnp.float32)
            mean_sq = jnp.sum(values * values, axis=1, keepdims=True) * (1.0 / width)
            normed = values * lax.rsqrt(mean_sq + 1e-06) * gain
            normed_ref[span, :] = normed.astype(jnp.bfloat16)
            return carry

        lax.fori_loop(0, size // 16, one, 0)


def pack_messages(steps, rows, places, normed_ref, message_refs):
    per_message, sliced = message_refs[0].shape
    spots = per_message // steps
    shape = (len(message_refs) * per_message, steps * rows)
    out_row = iota(shape, 0)
    wanted = out_row // per_message * spots + out_row % spots
    out_step = out_row % per_message // spots
    places = jnp.concatenate([places] * steps, axis=1)
    pick = (wanted == places) & (out_step == iota(shape, 1) // rows)
    pick = pick.astype(jnp.float32).astype(jnp.bfloat16)
    begin = pl.multiple_of(lax.axis_index("heads") * sliced, 128)
    own = normed_ref[:, pl.ds(begin, sliced)]
    packed = jnp.dot(pick, own, preferred_element_type=jnp.float32).astype(jnp.bfloat16)
    for number, message_ref in enumerate(message_refs):
        message_ref[...] = packed[number * per_message : (number + 1) * per_message]


def table_copies(table_hbms, table_bufs, semaphores, first):
    copies = [
        pltpu.make_async_copy(source, target, semaphores.at[first + number])
        for number, (source, target) in enumerate(zip(table_hbms, table_bufs))
    ]
    for copy in copies:
        copy.start()
    return copies


def places_from(table_bufs, spots, flow_most):
    speaker, table, owner = [buffer[...] for buffer in table_bufs]
    here, core, subs = lax.axis_index("streams"), lax.axis_index("sub"), lax.axis_size("sub")
    places = slot_places(speaker, table, here * (spots // MOST))
    return places, ranked(owner ^ (here * subs + core), flow_most)


def norm_pack_kernel(steps, rows, flow_most, lanes, pieces, *refs):
    table_hbms, gain_hbm, x_hbm, message_refs = refs[:3], refs[3], refs[4], refs[5 : 5 + lanes]
    x_buf, gain_buf, *table_bufs, semaphores, normed_ref = refs[5 + lanes :]
    copies = table_copies(table_hbms, table_bufs, semaphores, pieces + 1)
    norm_in_pieces(pieces, 0, x_hbm, gain_hbm, x_buf, gain_buf, semaphores, normed_ref)
    for copy in copies:
        copy.wait()
    spots = message_refs[0].shape[0] // steps
    places, _ = places_from(table_bufs, spots, flow_most)
    pack_messages(steps, rows, places, normed_ref, message_refs)


def weight_copies(begin, weight_hbm, weight_buf, semaphores):
    columns = weight_buf.shape[2]
    return [
        pltpu.make_async_copy(
            weight_hbm.at[:, pl.ds((begin + block) * columns, columns)],
            weight_buf.at[block],
            semaphores.at[block],
        )
        for block in range(weight_buf.shape[0])
    ]


def project_blocks(begin, copies, rows_ref, weight_buf, bias_ref, out_ref):
    columns = weight_buf.shape[2]
    tiles = columns // 128
    for block, copy in enumerate(copies):
        first = (begin + block) * tiles
        bias = [bias_ref[tile : tile + 1, :] for tile in range(first, first + tiles)]
        copy.wait()
        product = jnp.dot(rows_ref[...], weight_buf[block], preferred_element_type=jnp.float32)
        out_ref[:, block * columns : (block + 1) * columns] = product + jnp.concatenate(
            bias, axis=1
        )


def norm_pack_project_kernel(steps, rows, flow_most, lanes, pieces, chunk, *refs):
    table_hbms, bias_ref, gain_hbm, x_hbm, weight_hbm = refs[:3], *refs[3:7]
    normed_ref, out_ref, places_ref, message_refs = *refs[7:10], refs[10 : 10 + lanes]
    x_buf, gain_buf, *table_bufs, semaphores, weight_buf, weight_semaphores = refs[10 + lanes :]
    copies = weight_copies(0, weight_hbm, weight_buf, weight_semaphores)
    tables = table_copies(table_hbms, table_bufs, semaphores, pieces + 1)

    def start_weights():
        for copy in copies:
            copy.start()

    norm_in_pieces(
        pieces, 0, x_hbm, gain_hbm, x_buf, gain_buf, semaphores, normed_ref, start_weights
    )
    for copy in tables:
        copy.wait()
    spots = message_refs[0].shape[0] // steps
    places, flow_places = places_from(table_bufs, spots, flow_most)
    places_ref[0:1, :] = places
    places_ref[1:2, :] = flow_places
    count = steps * rows
    own_ref = normed_ref.at[pl.ds(chunk * count, count)]
    pack_messages(steps, rows, places, own_ref, message_refs)
    project_blocks(0, copies, normed_ref, weight_buf, bias_ref, out_ref)


def project_kernel(begin, rows_ref, bias_ref, weight_hbm, out_ref, weight_buf, semaphores):
    copies = weight_copies(begin, weight_hbm, weight_buf, semaphores)
    for copy in copies:
        copy.start()
    project_blocks(begin, copies, rows_ref, weight_buf, bias_ref, out_ref)


def row_slots(shape, spots):
    return iota(shape, 0) % spots // MOST


def down_kernel(lanes, spots, *refs):
    message_refs, map_refs, partial_ref = refs[:lanes][::-1], refs[lanes:-1], refs[-1]
    local_slots = map_refs[0].shape[0]
    rows = jnp.concatenate([ref[...] for ref in message_refs], axis=0)
    own_slot = row_slots(partial_ref.shape, spots)
    total = jnp.zeros(partial_ref.shape, jnp.float32)
    for number, map_ref in enumerate(map_refs):
        shift = (lax.axis_index("sub") ^ number) * local_slots
        for slot in range(local_slots):
            part = jnp.dot(rows, map_ref[slot], preferred_element_type=jnp.float32)
            total = jnp.where(own_slot == shift + slot, part, total)
    partial_ref[...] = total


def up_kernel(heads, subs, spots, *refs):
    partial_refs, refs = refs[:heads], refs[heads:]
    query_refs, value_refs, message_refs = refs[:subs], refs[subs : 2 * subs], refs[2 * subs :]
    total = partial_refs[0][...]
    for ref in partial_refs[1:]:
        total = total + ref[...]
    latent = total.astype(jnp.bfloat16).astype(jnp.float32)
    own_slot = row_slots(latent.shape, spots)
    column = iota(latent.shape, 1) // ADAPTER_RANK
    turned = pltpu.roll(latent, ADAPTER_RANK, 1)
    low = iota(latent.shape, 1) < ADAPTER_RANK
    query_pair = jnp.where(low, latent, turned)
    value_pair = jnp.where(low, turned, latent)

    def product(pair, map_refs):
        result = None
        for number, map_ref in enumerate(map_refs):
            local_slots = map_ref.shape[0] // ADAPTER_RANK
            shift = (lax.axis_index("sub") ^ number) * local_slots
            pieces = []
            for slot in range(0, local_slots, 2):
                kept = jnp.where(own_slot == shift + slot + column, pair, 0.0)
                pieces.append(kept.astype(jnp.bfloat16))
            wide = jnp.concatenate(pieces, axis=1)
            part = jnp.dot(wide, map_ref[...], preferred_element_type=jnp.float32)
            result = part if result is None else result + part
        return result.astype(jnp.bfloat16)

    queries = product(query_pair, query_refs)
    values = product(value_pair, value_refs)
    query_width = queries.shape[1]
    per_message = message_refs[0].shape[0]
    for number, ref in enumerate(message_refs):
        span = slice(number * per_message, (number + 1) * per_message)
        ref[:, :query_width] = queries[span]
        ref[:, query_width:] = values[span]


def attend_kernel(before, steps, rows, cache, groups, lanes, subs, last, *refs):
    places_ref, length_ref, cos_ref, sin_ref, key_ref, value_ref = refs[:6]
    qkv_refs, refs = refs[6:8], refs[8:]
    delta_refs, refs = refs[:lanes][::-1], refs[lanes:]
    if before:
        earlier_ref, refs = refs[0], refs[1:]
    if not last:
        fresh_ref, refs = refs[0], refs[1:]
    *message_refs, delta_ref, context_ref, bias_ref = refs
    per_message = delta_refs[0].shape[0]
    spots = per_message // steps
    query_width = PER_GROUP * HEAD_WIDTH
    known = before + steps

    def qkv_tile(span, group, head):
        begin = (group * (PER_GROUP + 2) + head) * HEAD_WIDTH
        edge = qkv_refs[0].shape[1]
        if begin < edge:
            return qkv_refs[0][span, begin : begin + HEAD_WIDTH]
        return qkv_refs[1][span, begin - edge : begin - edge + HEAD_WIDTH]

    wide = groups * HEAD_WIDTH

    column = as_column(places_ref[0:1, :])
    column = jnp.concatenate([column] * steps, axis=0)
    shape = (steps * rows, lanes * per_message)
    out_row = iota(shape, 1)
    wanted = out_row // per_message * spots + out_row % spots
    pick = (wanted == column) & (out_row % per_message // spots == iota(shape, 0) // rows)
    pick = pick.astype(jnp.float32).astype(jnp.bfloat16)
    delta_ref[...] = jnp.dot(
        pick,
        jnp.concatenate([ref[...] for ref in delta_refs], axis=0),
        preferred_element_type=jnp.float32,
    )

    shape = (rows, BATCH * cache)
    lengths = as_column(length_ref[...])
    slot_column = iota(shape, 1)
    allowed = (slot_column // cache == iota(shape, 0) % BATCH) & (slot_column % cache < lengths)
    bias_ref[...] = jnp.where(allowed, 0.0, -1e30)
    shape = (steps, BATCH, known * BATCH)
    fresh_column = iota(shape, 2)
    allowed = (fresh_column % BATCH == iota(shape, 1)) & (
        fresh_column // BATCH <= iota(shape, 0) + before
    )
    fresh_bias = jnp.where(allowed, 0.0, -1e30)
    scale = HEAD_WIDTH ** (-0.5)
    transposed = (((1,), (1,)), ((), ()))

    def scored(first, group):
        spans = [pl.ds(pl.multiple_of(step * rows + first, BATCH), BATCH) for step in range(known)]
        query_tiles, key_tiles, value_tiles = [], [], []
        lane_span = slice(group * HEAD_WIDTH, (group + 1) * HEAD_WIDTH)
        value_span = slice(wide + group * HEAD_WIDTH, wide + (group + 1) * HEAD_WIDTH)
        for span in spans[:before]:
            key_tiles.append(earlier_ref[span, lane_span])
            value_tiles.append(earlier_ref[span, value_span])
        for span in spans[:steps]:
            cosine, sine_part = cos_ref[span, :], sin_ref[span, :]

            def rotated(values):
                return values * cosine + pltpu.roll(values, HEAD_WIDTH // 2, 1) * sine_part

            for head in range(PER_GROUP):
                begin = group * query_width + head * HEAD_WIDTH
                change = delta_ref[span, begin : begin + HEAD_WIDTH]
                query_tiles.append(rotated(qkv_tile(span, group, head) + change))
            key = rotated(qkv_tile(span, group, PER_GROUP))
            begin = groups * query_width + group * HEAD_WIDTH
            change = delta_ref[span, begin : begin + HEAD_WIDTH]
            value = qkv_tile(span, group, PER_GROUP + 1) + change
            if not last:
                fresh_ref[span, lane_span] = key
                fresh_ref[span, value_span] = value
            key_tiles.append(key)
            value_tiles.append(value)
        queries = jnp.concatenate(query_tiles, axis=0).astype(jnp.bfloat16)
        new_keys = jnp.concatenate(key_tiles, axis=0).astype(jnp.bfloat16)
        new_values = jnp.concatenate(value_tiles, axis=0).astype(jnp.bfloat16)
        old_keys = key_ref[pl.ds(first, BATCH), :, lane_span].reshape(BATCH * cache, HEAD_WIDTH)
        old_scores = lax.dot_general(
            queries, old_keys, transposed, preferred_element_type=jnp.float32
        )
        new_scores = lax.dot_general(
            queries, new_keys, transposed, preferred_element_type=jnp.float32
        )
        return old_scores, new_scores, new_values

    def weighed(first, old_scores, new_scores):
        heads = steps * PER_GROUP
        old_scores = (old_scores * scale).reshape(heads, BATCH, BATCH * cache)
        old_scores = old_scores + bias_ref[pl.ds(first, BATCH), :][None]
        new_scores = (new_scores * scale).reshape(steps, PER_GROUP, BATCH, known * BATCH)
        new_scores = (new_scores + fresh_bias[:, None]).reshape(heads, BATCH, known * BATCH)
        peak = jnp.maximum(
            jnp.max(old_scores, axis=-1, keepdims=True),
            jnp.max(new_scores, axis=-1, keepdims=True),
        )
        old_scores = jnp.exp(old_scores - peak)
        new_scores = jnp.exp(new_scores - peak)
        share = 1.0 / (
            jnp.sum(old_scores, axis=-1, keepdims=True)
            + jnp.sum(new_scores, axis=-1, keepdims=True)
        )
        old_weights = (old_scores * share).reshape(heads * BATCH, BATCH * cache)
        new_weights = (new_scores * share).reshape(heads * BATCH, known * BATCH)
        return old_weights.astype(jnp.bfloat16), new_weights.astype(jnp.bfloat16)

    def batch(index, carry):
        chains = []
        for number in range(TOGETHER):
            first = pl.multiple_of((index * TOGETHER + number) * BATCH, BATCH)
            chains += [(first, group) for group in range(groups)]
        scores = [scored(*chain) for chain in chains]
        weights = [weighed(chain[0], *score[:2]) for chain, score in zip(chains, scores)]
        for (first, group), (old_weights, new_weights), score in zip(chains, weights, scores):
            lane_span = slice(group * HEAD_WIDTH, (group + 1) * HEAD_WIDTH)
            old_values = value_ref[pl.ds(first, BATCH), :, lane_span]
            old_values = old_values.reshape(BATCH * cache, HEAD_WIDTH)
            context = jnp.dot(
                old_weights, old_values, preferred_element_type=jnp.float32
            ) + jnp.dot(new_weights, score[2], preferred_element_type=jnp.float32)
            for step in range(steps):
                span = pl.ds(pl.multiple_of(step * rows + first, BATCH), BATCH)
                for head in range(PER_GROUP):
                    row = (step * PER_GROUP + head) * BATCH
                    begin = group * query_width + head * HEAD_WIDTH
                    context_ref[span, begin : begin + HEAD_WIDTH] = context[row : row + BATCH]
        return carry

    lax.fori_loop(0, rows // (BATCH * TOGETHER), batch, 0)

    flow_places = jnp.concatenate([places_ref[1:2, :]] * steps, axis=1)
    context = context_ref[...].astype(jnp.bfloat16)
    count = message_refs[0].shape[0]
    shape = (count, steps * rows)
    out_row = iota(shape, 0)
    same_step = out_row % steps == iota(shape, 1) // rows
    for number, message_ref in enumerate(message_refs):
        wanted = number * (count // steps) + out_row // steps
        pick = ((flow_places == wanted) & same_step).astype(jnp.float32).astype(jnp.bfloat16)
        message_ref[...] = jnp.dot(
            pick, context, preferred_element_type=jnp.float32
        ).astype(jnp.bfloat16)


def place_kernel(chunks, lanes, subs, most, *refs):
    *refs, out_ref = refs
    refs = refs[::-1]
    steps = out_ref.shape[1]
    chunk_steps = steps // chunks
    block = most * chunk_steps
    here = lax.axis_index("streams")
    core = lax.axis_index("sub")
    shape = (chunks * block, chunks * block)
    out_row, in_row = iota(shape, 0), iota(shape, 1)
    step = out_row % steps
    wanted = step // chunk_steps * block + out_row // steps * chunk_steps + step % chunk_steps
    pick = (wanted == in_row).astype(jnp.float32).astype(jnp.bfloat16)
    for number in range(lanes):
        for other in range(subs):
            pieces = []
            for chunk in range(chunks):
                pieces.append(refs[(chunk * lanes + number) * subs + other][...])
            rows = jnp.dot(
                pick, jnp.concatenate(pieces, axis=0), preferred_element_type=jnp.float32
            )
            source = (here ^ number) * subs + (core ^ other)
            out_ref[pl.ds(source * most, most)] = rows.reshape(
                most, steps, rows.shape[1]
            ).astype(jnp.bfloat16)


def traded(blocks, axes):
    landed = list(blocks)
    count = len(blocks)
    for shift in range(1, count):
        pairs = [(place, place ^ shift) for place in range(count)]
        landed[shift] = lax.ppermute(blocks[shift], axes, pairs)
    return landed


def from_others(block, axis):
    count = lax.axis_size(axis)
    landed = [block]
    for shift in range(1, count):
        pairs = [(place, place ^ shift) for place in range(count)]
        landed.append(lax.ppermute(block, axis, pairs))
    return landed


def held(value, others):
    return lax.optimization_barrier((value, others))[0]


SMALL = pl.CostEstimate(flops=1, bytes_accessed=1, transcendentals=0)


def on_device(
    inputs,
    input_norm_gain,
    projection_weight,
    projection_bias,
    speaker,
    speaker_adapter_slot,
    cache_fill_length,
    rotated_key_cache,
    value_cache_rows,
    adapter_down_maps,
    adapter_query_up,
    adapter_value_up,
    flow_decoder_owner,
):
    steps, rows, width = inputs.shape
    lanes = lax.axis_size("streams")
    subs = lax.axis_size("sub")
    heads = lax.axis_size("heads")
    flow_lanes = lanes * subs
    local_slots, sliced, _ = adapter_down_maps.shape
    query_columns = adapter_query_up.shape[2]
    value_columns = adapter_value_up.shape[2]
    groups = value_columns // HEAD_WIDTH
    cache = rotated_key_cache.shape[1]
    spots = subs * local_slots * MOST
    chunks = 2
    chunk_steps = steps // chunks
    chunk_rows = chunk_steps * rows
    per_message = chunk_steps * spots
    chip_slots = subs * local_slots
    flow_most = max(2, (2 * rows + flow_lanes - 1) // flow_lanes)
    bf16, f32 = jnp.bfloat16, jnp.float32

    def whole(shape):
        return pl.BlockSpec(shape, lambda i: (0,) * len(shape))

    in_hbm = pl.BlockSpec(memory_space=pltpu.HBM)

    pieces = 4
    flat = inputs.reshape(steps * rows, width)
    gain = input_norm_gain.reshape(width // 128, 128)
    message = jax.ShapeDtypeStruct((per_message, sliced), bf16)
    places_shape = jax.ShapeDtypeStruct((8, rows), jnp.int32)
    tables = [
        speaker.reshape(1, rows),
        speaker_adapter_slot.reshape(1, -1),
        flow_decoder_owner.reshape(1, rows),
    ]

    def row_buffers(count):
        return (
            [pltpu.VMEM((count, width), bf16), pltpu.VMEM(gain.shape, f32)]
            + [pltpu.VMEM(table.shape, jnp.int32) for table in tables]
            + [pltpu.SemaphoreType.DMA((pieces + 4,))]
        )

    messages = pl.pallas_call(
        functools.partial(norm_pack_kernel, chunk_steps, rows, flow_most, lanes, pieces),
        in_specs=[in_hbm] * 5,
        out_specs=[VMEM] * lanes,
        out_shape=[message] * lanes,
        scratch_shapes=row_buffers(chunk_rows) + [pltpu.VMEM((chunk_rows, width), bf16)],
        compiler_params=pltpu.CompilerParams(vmem_limit_bytes=PACK_LIMIT * MIB),
        cost_estimate=SMALL,
        name="norm_and_pack",
    )(*tables, gain, flat)
    arrived = [traded(messages, "streams")]
    maps = [
        adapter_down_maps,
        adapter_query_up.reshape(local_slots * ADAPTER_RANK, query_columns),
        adapter_value_up.reshape(local_slots * ADAPTER_RANK, value_columns),
    ]
    maps = held(maps, messages)
    down_maps, query_maps, value_maps = [from_others(each, "sub") for each in maps]

    bias = projection_bias.reshape(-1, 128)
    columns = projection_weight.shape[1]
    block_columns = 256 if columns % 256 == 0 else 384
    blocks = columns // block_columns
    cut = blocks // 2

    def weight_buffers(count):
        return [
            pltpu.VMEM((count, width, block_columns), bf16),
            pltpu.SemaphoreType.DMA((count,)),
        ]

    def projected(count):
        return jax.ShapeDtypeStruct((steps * rows, count * block_columns), f32)

    adapters = down_maps[1:], query_maps[1:], value_maps[1:]
    weight_buf, weight_semaphores = weight_buffers(cut)
    normed, first_qkv, places, *messages = pl.pallas_call(
        functools.partial(
            norm_pack_project_kernel, chunk_steps, rows, flow_most, lanes, 2 * pieces, 1
        ),
        in_specs=[in_hbm] * 3 + [VMEM] + [in_hbm] * 3,
        out_specs=[VMEM] * (3 + lanes),
        out_shape=[jax.ShapeDtypeStruct((steps * rows, width), bf16), projected(cut)]
        + [places_shape]
        + [message] * lanes,
        scratch_shapes=row_buffers(steps * rows)[:-1]
        + [pltpu.SemaphoreType.DMA((2 * pieces + 4,))]
        + [weight_buf, weight_semaphores],
        compiler_params=pltpu.CompilerParams(vmem_limit_bytes=PROJECT_LIMIT * MIB),
        cost_estimate=SMALL,
        name="norm_pack_project",
    )(*tables, held(bias, (adapters, messages)), gain, flat, projection_weight)
    arrived.append(traded(messages, "streams"))
    qkv = [first_qkv]

    def project(after):
        return pl.pallas_call(
            functools.partial(project_kernel, cut),
            in_specs=[VMEM, VMEM, in_hbm],
            out_specs=VMEM,
            out_shape=projected(blocks - cut),
            scratch_shapes=weight_buffers(blocks - cut),
            compiler_params=pltpu.CompilerParams(vmem_limit_bytes=PROJECT_LIMIT * MIB),
            cost_estimate=SMALL,
            name="project",
        )(normed, held(bias, after), projection_weight)

    def down(chunk, after):
        partial_latent = pl.pallas_call(
            functools.partial(down_kernel, lanes, spots),
            in_specs=[VMEM] * (lanes + subs),
            out_specs=VMEM,
            out_shape=jax.ShapeDtypeStruct((lanes * per_message, 2 * ADAPTER_RANK), f32),
            compiler_params=pltpu.CompilerParams(vmem_limit_bytes=16 * MIB),
            cost_estimate=SMALL,
            name="down",
        )(*arrived[chunk][:0:-1], held(arrived[chunk][0], after), *down_maps)
        return from_others(partial_latent, "heads")

    def up(partials, after):
        message = jax.ShapeDtypeStruct((per_message, query_columns + value_columns), bf16)
        messages = pl.pallas_call(
            functools.partial(up_kernel, heads, subs, spots),
            in_specs=[VMEM] * (heads + 2 * subs),
            out_specs=[VMEM] * lanes,
            out_shape=[message] * lanes,
            compiler_params=pltpu.CompilerParams(vmem_limit_bytes=24 * MIB),
            cost_estimate=SMALL,
            name="up",
        )(held(partials[0], after), *partials[1:], *query_maps, *value_maps)
        return messages

    half_width = HEAD_WIDTH // 2
    position = jnp.concatenate([cache_fill_length + step for step in range(steps)]).astype(f32)
    freq = jnp.exp(jnp.arange(half_width, dtype=f32) * (-math.log(1000000.0) / half_width))
    freq = jnp.concatenate([freq, freq])
    angle = position[:, None] * freq
    sign = jnp.where(jnp.arange(HEAD_WIDTH) < half_width, -1.0, 1.0).astype(f32)
    cosine = jnp.cos(angle)
    sine_part = jnp.sin(angle) * sign

    returned = []
    after = qkv
    for chunk in range(chunks):
        partials = down(chunk, after)
        if chunk:
            qkv.append(project(partials[0]))
        after = up(partials, qkv)
        messages = list(after)
        ahead = returned[-1] if chunk else arrived[-1]
        for lane in range(lanes - 1, 0, -1):
            messages[lane] = held(messages[lane], ahead[lane:])
        returned.append(traded(messages, "streams"))

    length_row = cache_fill_length.reshape(1, rows)
    block = flow_most * chunk_steps
    earlier, blocks_out = [], []
    for chunk in range(chunks):
        last = chunk == chunks - 1
        message = jax.ShapeDtypeStruct((block, query_columns), bf16)
        fresh = jax.ShapeDtypeStruct((chunk_rows, 2 * value_columns), f32)
        rows_of = lambda shape: pl.BlockSpec(shape, lambda i, chunk=chunk: (chunk, 0))
        results = pl.pallas_call(
            functools.partial(
                attend_kernel,
                chunk * chunk_steps,
                chunk_steps,
                rows,
                cache,
                groups,
                lanes,
                subs,
                last,
            ),
            grid=(1,),
            in_specs=[whole(places.shape), whole(length_row.shape)]
            + [rows_of((chunk_rows, HEAD_WIDTH))] * 2
            + [whole(rotated_key_cache.shape)] * 2
            + [rows_of((chunk_rows, part.shape[1])) for part in qkv]
            + [whole((per_message, query_columns + value_columns))] * lanes
            + [whole(block_rows.shape) for block_rows in earlier],
            out_specs=[whole(fresh.shape)] * (not last) + [whole(message.shape)] * flow_lanes,
            out_shape=[fresh] * (not last) + [message] * flow_lanes,
            scratch_shapes=[
                pltpu.VMEM((chunk_rows, query_columns + value_columns), f32),
                pltpu.VMEM((chunk_rows, query_columns), f32),
                pltpu.VMEM((rows, BATCH * cache), f32),
            ],
            compiler_params=pltpu.CompilerParams(vmem_limit_bytes=32 * MIB),
            cost_estimate=SMALL,
            name="attend",
        )(
            places if chunk else held(places, after),
            length_row,
            cosine,
            sine_part,
            rotated_key_cache,
            value_cache_rows,
            *qkv,
            *returned[chunk][::-1],
            *earlier,
        )
        if not last:
            earlier, results = [results[0]], results[1:]
        results = list(results)
        blocks_out.append(results)

    landed = [[results[0]] + [None] * (flow_lanes - 1) for results in blocks_out]
    turns = [(chunk, lane) for chunk in range(chunks) for lane in range(flow_lanes - 1, 0, -1)]
    for number, (chunk, lane) in enumerate(turns):
        if number < IN_FLIGHT:
            before = returned[-1][1:]
        else:
            other, other_lane = turns[number - IN_FLIGHT]
            before = landed[other][other_lane]
        pairs = [(place, place ^ lane) for place in range(flow_lanes)]
        landed[chunk][lane] = lax.ppermute(
            held(blocks_out[chunk][lane], before), LANE_AXES, pairs
        )
    landed = [block_rows for chunk_rows in landed for block_rows in chunk_rows]

    flow = pl.pallas_call(
        functools.partial(place_kernel, chunks, lanes, subs, flow_most),
        in_specs=[VMEM] * len(landed),
        out_specs=VMEM,
        out_shape=jax.ShapeDtypeStruct((flow_lanes * flow_most, steps, query_columns), bf16),
        compiler_params=pltpu.CompilerParams(vmem_limit_bytes=24 * MIB),
        cost_estimate=SMALL,
        name="place",
    )(*landed[::-1])
    return flow[None]


def solution(mesh):
    placed = (
        P(None, ("groups", "streams", "sub"), None),
        P(),
        P(None, "heads"),
        P("heads"),
        P(("groups", "streams", "sub"), None),
        P("groups"),
        P(("groups", "streams", "sub")),
        P(("groups", "streams", "sub"), None, "heads"),
        P(("groups", "streams", "sub"), None, "heads"),
        P(("groups", "streams", "sub"), "heads", None),
        P(("groups", "streams", "sub"), None, "heads"),
        P(("groups", "streams", "sub"), None, "heads"),
        P(("groups", "streams", "sub"), None),
    )
    return jax.shard_map(
        on_device,
        mesh=mesh,
        in_specs=placed,
        out_specs=P(("groups", "streams", "sub"), None, None, "heads"),
        check_vma=False,
    )
```

```python
import functools
import math

import jax
import jax.numpy as jnp
from jax import lax
from jax.experimental import pallas as pl
from jax.experimental.pallas import tpu as pltpu
from jax.sharding import PartitionSpec as P

QUERY_HEADS = 28
KEY_VALUE_HEADS = 4
HEAD_WIDTH = 128
ADAPTER_RANK = 64
MOST = 2
PER_GROUP = QUERY_HEADS // KEY_VALUE_HEADS
LANE_AXES = ("streams", "sub")
BATCH = 8
TOGETHER = 2
VMEM = pl.BlockSpec(memory_space=pltpu.VMEM)
MIB = 1 << 20
PACK_LIMIT = 56
PROJECT_LIMIT = 49


def iota(shape, dim):
    return lax.broadcasted_iota(jnp.int32, shape, dim)


def as_column(row):
    count = row.shape[1]
    square = (count, count)
    same = iota(square, 0) == iota(square, 1)
    return jnp.sum(jnp.where(same, jnp.broadcast_to(row, square), 0), axis=1, keepdims=True)


def ranked(labels, most):
    count = labels.shape[1]
    square = (count, count)
    earlier = (as_column(labels) == labels) & (iota(square, 0) < iota(square, 1))
    return labels * most + jnp.sum(earlier.astype(jnp.int32), axis=0, keepdims=True)


def slot_places(speaker, table, lane_base):
    speakers_all = table.shape[1]
    rows = speaker.shape[1]
    match = iota((speakers_all, rows), 0) == speaker
    slots = jnp.sum(jnp.where(match, as_column(table), 0), axis=0, keepdims=True)
    return ranked(slots ^ lane_base, MOST)


def norm_in_pieces(
    pieces, begin, x_hbm, gain_hbm, x_buf, gain_buf, semaphores, normed_ref
):
    count, width = x_buf.shape
    size = count // pieces
    gain_copy = pltpu.make_async_copy(gain_hbm, gain_buf, semaphores.at[pieces])
    copies = []
    for piece in range(pieces):
        copies.append(
            pltpu.make_async_copy(
                x_hbm.at[pl.ds(begin + piece * size, size)],
                x_buf.at[pl.ds(piece * size, size)],
                semaphores.at[piece],
            )
        )
        copies[-1].start()
        if piece == 0:
            gain_copy.start()
    gain_copy.wait()
    gain = jnp.concatenate([gain_buf[i : i + 1, :] for i in range(gain_buf.shape[0])], axis=1)
    for piece in range(pieces):
        copies[piece].wait()

        def one(index, carry):
            span = pl.ds(pl.multiple_of(piece * size + index * 16, 16), 16)
            values = x_buf[span, :].astype(jnp.float32)
            mean_sq = jnp.sum(values * values, axis=1, keepdims=True) * (1.0 / width)
            normed = values * lax.rsqrt(mean_sq + 1e-06) * gain
            normed_ref[span, :] = normed.astype(jnp.bfloat16)
            return carry

        lax.fori_loop(0, size // 16, one, 0)


def pack_messages(steps, rows, places, normed_ref, message_refs):
    per_message, sliced = message_refs[0].shape
    spots = per_message // steps
    shape = (len(message_refs) * per_message, steps * rows)
    out_row = iota(shape, 0)
    wanted = out_row // per_message * spots + out_row % spots
    out_step = out_row % per_message // spots
    places = jnp.concatenate([places] * steps, axis=1)
    pick = (wanted == places) & (out_step == iota(shape, 1) // rows)
    pick = pick.astype(jnp.float32).astype(jnp.bfloat16)
    begin = pl.multiple_of(lax.axis_index("heads") * sliced, 128)
    own = normed_ref[:, pl.ds(begin, sliced)]
    packed = jnp.dot(pick, own, preferred_element_type=jnp.float32).astype(jnp.bfloat16)
    for number, message_ref in enumerate(message_refs):
        message_ref[...] = packed[number * per_message : (number + 1) * per_message]


def table_copies(table_hbms, table_bufs, semaphores, first):
    copies = [
        pltpu.make_async_copy(source, target, semaphores.at[first + number])
        for number, (source, target) in enumerate(zip(table_hbms, table_bufs))
    ]
    for copy in copies:
        copy.start()
    return copies


def places_from(table_bufs, spots, flow_most):
    speaker, table, owner = [buffer[...] for buffer in table_bufs]
    here, core, subs = lax.axis_index("streams"), lax.axis_index("sub"), lax.axis_size("sub")
    places = slot_places(speaker, table, here * (spots // MOST))
    return places, ranked(owner ^ (here * subs + core), flow_most)


def norm_pack_kernel(steps, rows, flow_most, lanes, pieces, *refs):
    table_hbms, gain_hbm, x_hbm, message_refs = refs[:3], refs[3], refs[4], refs[5 : 5 + lanes]
    x_buf, gain_buf, *table_bufs, semaphores, normed_ref = refs[5 + lanes :]
    copies = table_copies(table_hbms, table_bufs, semaphores, pieces + 1)
    norm_in_pieces(pieces, 0, x_hbm, gain_hbm, x_buf, gain_buf, semaphores, normed_ref)
    for copy in copies:
        copy.wait()
    spots = message_refs[0].shape[0] // steps
    places, _ = places_from(table_bufs, spots, flow_most)
    pack_messages(steps, rows, places, normed_ref, message_refs)


def weight_copies(begin, weight_hbm, weight_buf, semaphores):
    columns = weight_buf.shape[2]
    return [
        pltpu.make_async_copy(
            weight_hbm.at[:, pl.ds((begin + block) * columns, columns)],
            weight_buf.at[block],
            semaphores.at[block],
        )
        for block in range(weight_buf.shape[0])
    ]


def project_blocks(begin, copies, rows_ref, weight_buf, bias_ref, out_ref):
    columns = weight_buf.shape[2]
    tiles = columns // 128
    for block, copy in enumerate(copies):
        first = (begin + block) * tiles
        bias = [bias_ref[tile : tile + 1, :] for tile in range(first, first + tiles)]
        copy.wait()
        product = jnp.dot(rows_ref[...], weight_buf[block], preferred_element_type=jnp.float32)
        out_ref[:, block * columns : (block + 1) * columns] = product + jnp.concatenate(
            bias, axis=1
        )


def norm_all_pack_kernel(steps, rows, flow_most, lanes, pieces, chunk, *refs):
    table_hbms, gain_hbm, x_hbm = refs[:3], refs[3], refs[4]
    normed_ref, places_ref, message_refs = refs[5], refs[6], refs[7 : 7 + lanes]
    x_buf, gain_buf, *table_bufs, semaphores = refs[7 + lanes :]
    copies = table_copies(table_hbms, table_bufs, semaphores, pieces + 1)
    norm_in_pieces(pieces, 0, x_hbm, gain_hbm, x_buf, gain_buf, semaphores, normed_ref)
    for copy in copies:
        copy.wait()
    spots = message_refs[0].shape[0] // steps
    places, flow_places = places_from(table_bufs, spots, flow_most)
    places_ref[0:1, :] = places
    places_ref[1:2, :] = flow_places
    count = steps * rows
    own_ref = normed_ref.at[pl.ds(chunk * count, count)]
    pack_messages(steps, rows, places, own_ref, message_refs)


def project_kernel(begin, rows_ref, bias_ref, weight_hbm, out_ref, weight_buf, semaphores):
    copies = weight_copies(begin, weight_hbm, weight_buf, semaphores)
    for copy in copies:
        copy.start()
    project_blocks(begin, copies, rows_ref, weight_buf, bias_ref, out_ref)


def row_slots(shape, spots):
    return iota(shape, 0) % spots // MOST


def down_kernel(lanes, spots, *refs):
    message_refs, map_refs, partial_ref = refs[:lanes][::-1], refs[lanes:-1], refs[-1]
    local_slots = map_refs[0].shape[0]
    rows = jnp.concatenate([ref[...] for ref in message_refs], axis=0)
    own_slot = row_slots(partial_ref.shape, spots)
    total = jnp.zeros(partial_ref.shape, jnp.float32)
    for number, map_ref in enumerate(map_refs):
        shift = (lax.axis_index("sub") ^ number) * local_slots
        for slot in range(local_slots):
            part = jnp.dot(rows, map_ref[slot], preferred_element_type=jnp.float32)
            total = jnp.where(own_slot == shift + slot, part, total)
    partial_ref[...] = total


def up_kernel(heads, subs, spots, *refs):
    partial_refs, refs = refs[:heads], refs[heads:]
    query_refs, value_refs, message_refs = refs[:subs], refs[subs : 2 * subs], refs[2 * subs :]
    total = partial_refs[0][...]
    for ref in partial_refs[1:]:
        total = total + ref[...]
    latent = total.astype(jnp.bfloat16).astype(jnp.float32)
    own_slot = row_slots(latent.shape, spots)
    column = iota(latent.shape, 1) // ADAPTER_RANK
    turned = pltpu.roll(latent, ADAPTER_RANK, 1)
    low = iota(latent.shape, 1) < ADAPTER_RANK
    query_pair = jnp.where(low, latent, turned)
    value_pair = jnp.where(low, turned, latent)

    def product(pair, map_refs):
        result = None
        for number, map_ref in enumerate(map_refs):
            local_slots = map_ref.shape[0] // ADAPTER_RANK
            shift = (lax.axis_index("sub") ^ number) * local_slots
            pieces = []
            for slot in range(0, local_slots, 2):
                kept = jnp.where(own_slot == shift + slot + column, pair, 0.0)
                pieces.append(kept.astype(jnp.bfloat16))
            wide = jnp.concatenate(pieces, axis=1)
            part = jnp.dot(wide, map_ref[...], preferred_element_type=jnp.float32)
            result = part if result is None else result + part
        return result.astype(jnp.bfloat16)

    queries = product(query_pair, query_refs)
    values = product(value_pair, value_refs)
    query_width = queries.shape[1]
    per_message = message_refs[0].shape[0]
    for number, ref in enumerate(message_refs):
        span = slice(number * per_message, (number + 1) * per_message)
        ref[:, :query_width] = queries[span]
        ref[:, query_width:] = values[span]


def attend_kernel(before, steps, rows, cache, groups, lanes, subs, last, *refs):
    places_ref, length_ref, cos_ref, sin_ref, key_ref, value_ref = refs[:6]
    qkv_refs, refs = refs[6:9], refs[9:]
    delta_refs, refs = refs[:lanes], refs[lanes:]
    if before:
        earlier_ref, refs = refs[0], refs[1:]
    if not last:
        fresh_ref, refs = refs[0], refs[1:]
    message_refs = refs[:lanes]
    delta_ref, context_ref, bias_ref = refs[lanes:]
    per_message = delta_refs[0].shape[0]
    spots = per_message // steps
    query_width = PER_GROUP * HEAD_WIDTH
    known = before + steps

    def qkv_tile(span, group, head):
        part, begin = divmod((group * (PER_GROUP + 2) + head) * HEAD_WIDTH, qkv_refs[0].shape[1])
        return qkv_refs[part][span, begin : begin + HEAD_WIDTH]

    wide = groups * HEAD_WIDTH

    column = as_column(places_ref[0:1, :])
    column = jnp.concatenate([column] * steps, axis=0)
    shape = (steps * rows, lanes * per_message)
    out_row = iota(shape, 1)
    wanted = out_row // per_message * spots + out_row % spots
    pick = (wanted == column) & (out_row % per_message // spots == iota(shape, 0) // rows)
    pick = pick.astype(jnp.float32).astype(jnp.bfloat16)
    delta_ref[...] = jnp.dot(
        pick,
        jnp.concatenate([ref[...] for ref in delta_refs], axis=0),
        preferred_element_type=jnp.float32,
    )

    shape = (rows, BATCH * cache)
    lengths = as_column(length_ref[...])
    slot_column = iota(shape, 1)
    allowed = (slot_column // cache == iota(shape, 0) % BATCH) & (slot_column % cache < lengths)
    bias_ref[...] = jnp.where(allowed, 0.0, -1e30)
    shape = (steps, BATCH, known * BATCH)
    fresh_column = iota(shape, 2)
    allowed = (fresh_column % BATCH == iota(shape, 1)) & (
        fresh_column // BATCH <= iota(shape, 0) + before
    )
    fresh_bias = jnp.where(allowed, 0.0, -1e30)
    scale = HEAD_WIDTH ** (-0.5)
    transposed = (((1,), (1,)), ((), ()))

    def scored(first, group):
        spans = [pl.ds(pl.multiple_of(step * rows + first, BATCH), BATCH) for step in range(known)]
        query_tiles, key_tiles, value_tiles = [], [], []
        lane_span = slice(group * HEAD_WIDTH, (group + 1) * HEAD_WIDTH)
        value_span = slice(wide + group * HEAD_WIDTH, wide + (group + 1) * HEAD_WIDTH)
        for span in spans[:before]:
            key_tiles.append(earlier_ref[span, lane_span])
            value_tiles.append(earlier_ref[span, value_span])
        for span in spans[:steps]:
            cosine, sine_part = cos_ref[span, :], sin_ref[span, :]

            def rotated(values):
                return values * cosine + pltpu.roll(values, HEAD_WIDTH // 2, 1) * sine_part

            for head in range(PER_GROUP):
                begin = group * query_width + head * HEAD_WIDTH
                change = delta_ref[span, begin : begin + HEAD_WIDTH]
                query_tiles.append(rotated(qkv_tile(span, group, head) + change))
            key = rotated(qkv_tile(span, group, PER_GROUP))
            begin = groups * query_width + group * HEAD_WIDTH
            change = delta_ref[span, begin : begin + HEAD_WIDTH]
            value = qkv_tile(span, group, PER_GROUP + 1) + change
            if not last:
                fresh_ref[span, lane_span] = key
                fresh_ref[span, value_span] = value
            key_tiles.append(key)
            value_tiles.append(value)
        queries = jnp.concatenate(query_tiles, axis=0).astype(jnp.bfloat16)
        new_keys = jnp.concatenate(key_tiles, axis=0).astype(jnp.bfloat16)
        new_values = jnp.concatenate(value_tiles, axis=0).astype(jnp.bfloat16)
        old_keys = key_ref[pl.ds(first, BATCH), :, lane_span].reshape(BATCH * cache, HEAD_WIDTH)
        old_scores = lax.dot_general(
            queries, old_keys, transposed, preferred_element_type=jnp.float32
        )
        new_scores = lax.dot_general(
            queries, new_keys, transposed, preferred_element_type=jnp.float32
        )
        return old_scores, new_scores, new_values

    def weighed(first, old_scores, new_scores):
        heads = steps * PER_GROUP
        old_scores = (old_scores * scale).reshape(heads, BATCH, BATCH * cache)
        old_scores = old_scores + bias_ref[pl.ds(first, BATCH), :][None]
        new_scores = (new_scores * scale).reshape(steps, PER_GROUP, BATCH, known * BATCH)
        new_scores = (new_scores + fresh_bias[:, None]).reshape(heads, BATCH, known * BATCH)
        peak = jnp.maximum(
            jnp.max(old_scores, axis=-1, keepdims=True),
            jnp.max(new_scores, axis=-1, keepdims=True),
        )
        old_scores = jnp.exp(old_scores - peak)
        new_scores = jnp.exp(new_scores - peak)
        share = 1.0 / (
            jnp.sum(old_scores, axis=-1, keepdims=True)
            + jnp.sum(new_scores, axis=-1, keepdims=True)
        )
        old_weights = (old_scores * share).reshape(heads * BATCH, BATCH * cache)
        new_weights = (new_scores * share).reshape(heads * BATCH, known * BATCH)
        return old_weights.astype(jnp.bfloat16), new_weights.astype(jnp.bfloat16)

    def batch(index, carry):
        chains = []
        for number in range(TOGETHER):
            first = pl.multiple_of((index * TOGETHER + number) * BATCH, BATCH)
            chains += [(first, group) for group in range(groups)]
        scores = [scored(*chain) for chain in chains]
        weights = [weighed(chain[0], *score[:2]) for chain, score in zip(chains, scores)]
        for (first, group), (old_weights, new_weights), score in zip(chains, weights, scores):
            lane_span = slice(group * HEAD_WIDTH, (group + 1) * HEAD_WIDTH)
            old_values = value_ref[pl.ds(first, BATCH), :, lane_span]
            old_values = old_values.reshape(BATCH * cache, HEAD_WIDTH)
            context = jnp.dot(
                old_weights, old_values, preferred_element_type=jnp.float32
            ) + jnp.dot(new_weights, score[2], preferred_element_type=jnp.float32)
            for step in range(steps):
                span = pl.ds(pl.multiple_of(step * rows + first, BATCH), BATCH)
                for head in range(PER_GROUP):
                    row = (step * PER_GROUP + head) * BATCH
                    begin = group * query_width + head * HEAD_WIDTH
                    context_ref[span, begin : begin + HEAD_WIDTH] = context[row : row + BATCH]
        return carry

    lax.fori_loop(0, rows // (BATCH * TOGETHER), batch, 0)

    flow_places = jnp.concatenate([places_ref[1:2, :]] * steps, axis=1)
    context = context_ref[...].astype(jnp.bfloat16)
    count = message_refs[0].shape[0]
    shape = (count, steps * rows)
    out_row = iota(shape, 0)
    same_step = out_row % steps == iota(shape, 1) // rows
    for number, message_ref in enumerate(message_refs):
        wanted = number * (count // steps) + out_row // steps
        pick = ((flow_places == wanted) & same_step).astype(jnp.float32).astype(jnp.bfloat16)
        message_ref[...] = jnp.dot(
            pick, context, preferred_element_type=jnp.float32
        ).astype(jnp.bfloat16)


def place_kernel(found, lanes, subs, most, *refs):
    chunks = len(found)
    out_ref = refs[-1]
    steps = out_ref.shape[1]
    chunk_steps = steps // chunks
    block = most * chunk_steps
    here = lax.axis_index("streams")
    core = lax.axis_index("sub")
    shape = (chunks * block, chunks * block)
    out_row, in_row = iota(shape, 0), iota(shape, 1)
    step = out_row % steps
    wanted = step // chunk_steps * block + out_row // steps * chunk_steps + step % chunk_steps
    pick = (wanted == in_row).astype(jnp.float32).astype(jnp.bfloat16)
    for number in range(lanes):
        for other in range(subs):
            pieces = []
            for chunk in range(chunks):
                array, begin = found[chunk][number][other]
                pieces.append(refs[array][...][begin : begin + block])
            rows = jnp.dot(
                pick, jnp.concatenate(pieces, axis=0), preferred_element_type=jnp.float32
            )
            source = (here ^ number) * subs + (core ^ other)
            out_ref[pl.ds(source * most, most)] = rows.reshape(
                most, steps, rows.shape[1]
            ).astype(jnp.bfloat16)


def traded(blocks, axes):
    landed = list(blocks)
    count = len(blocks)
    order = sorted(range(1, count), key=lambda shift: -(shift ^ (shift >> 1)))
    for shift in order:
        pairs = [(place, place ^ shift) for place in range(count)]
        landed[shift] = lax.ppermute(blocks[shift], axes, pairs)
    return landed


def from_others(block, axis):
    count = lax.axis_size(axis)
    landed = [block]
    for shift in range(1, count):
        pairs = [(place, place ^ shift) for place in range(count)]
        landed.append(lax.ppermute(block, axis, pairs))
    return landed


def held(value, others):
    return lax.optimization_barrier((value, others))[0]


SMALL = pl.CostEstimate(flops=1, bytes_accessed=1, transcendentals=0)


def on_device(
    inputs,
    input_norm_gain,
    projection_weight,
    projection_bias,
    speaker,
    speaker_adapter_slot,
    cache_fill_length,
    rotated_key_cache,
    value_cache_rows,
    adapter_down_maps,
    adapter_query_up,
    adapter_value_up,
    flow_decoder_owner,
):
    steps, rows, width = inputs.shape
    lanes = lax.axis_size("streams")
    subs = lax.axis_size("sub")
    heads = lax.axis_size("heads")
    flow_lanes = lanes * subs
    local_slots, sliced, _ = adapter_down_maps.shape
    query_columns = adapter_query_up.shape[2]
    value_columns = adapter_value_up.shape[2]
    groups = value_columns // HEAD_WIDTH
    cache = rotated_key_cache.shape[1]
    spots = subs * local_slots * MOST
    chunks = 2
    chunk_steps = steps // chunks
    chunk_rows = chunk_steps * rows
    per_message = chunk_steps * spots
    chip_slots = subs * local_slots
    flow_most = max(2, (2 * rows + flow_lanes - 1) // flow_lanes)
    bf16, f32 = jnp.bfloat16, jnp.float32

    def whole(shape):
        return pl.BlockSpec(shape, lambda i: (0,) * len(shape))

    in_hbm = pl.BlockSpec(memory_space=pltpu.HBM)

    down_maps = from_others(adapter_down_maps, "sub")
    query_maps = from_others(
        adapter_query_up.reshape(local_slots * ADAPTER_RANK, query_columns), "sub"
    )
    value_maps = from_others(
        adapter_value_up.reshape(local_slots * ADAPTER_RANK, value_columns), "sub"
    )

    pieces = 4
    flat = inputs.reshape(steps * rows, width)
    gain = input_norm_gain.reshape(width // 128, 128)
    message = jax.ShapeDtypeStruct((per_message, sliced), bf16)
    places_shape = jax.ShapeDtypeStruct((8, rows), jnp.int32)
    tables = [
        speaker.reshape(1, rows),
        speaker_adapter_slot.reshape(1, -1),
        flow_decoder_owner.reshape(1, rows),
    ]

    def row_buffers(count):
        return (
            [pltpu.VMEM((count, width), bf16), pltpu.VMEM(gain.shape, f32)]
            + [pltpu.VMEM(table.shape, jnp.int32) for table in tables]
            + [pltpu.SemaphoreType.DMA((pieces + 4,))]
        )

    messages = pl.pallas_call(
        functools.partial(norm_pack_kernel, chunk_steps, rows, flow_most, lanes, pieces),
        in_specs=[in_hbm] * 5,
        out_specs=[VMEM] * lanes,
        out_shape=[message] * lanes,
        scratch_shapes=row_buffers(chunk_rows) + [pltpu.VMEM((chunk_rows, width), bf16)],
        compiler_params=pltpu.CompilerParams(vmem_limit_bytes=PACK_LIMIT * MIB),
        cost_estimate=SMALL,
        name="norm_and_pack",
    )(*tables, gain, flat)
    arrived = [traded(messages, "streams")]

    adapters = down_maps[1:], query_maps[1:], value_maps[1:]
    normed, places, *messages = pl.pallas_call(
        functools.partial(
            norm_all_pack_kernel, chunk_steps, rows, flow_most, lanes, 2 * pieces, 1
        ),
        in_specs=[in_hbm] * 5,
        out_specs=[VMEM] * (2 + lanes),
        out_shape=[jax.ShapeDtypeStruct((steps * rows, width), bf16), places_shape]
        + [message] * lanes,
        scratch_shapes=row_buffers(steps * rows)[:-1]
        + [pltpu.SemaphoreType.DMA((2 * pieces + 4,))],
        compiler_params=pltpu.CompilerParams(vmem_limit_bytes=PROJECT_LIMIT * MIB),
        cost_estimate=SMALL,
        name="norm_and_pack_next",
    )(*tables, held(gain, (adapters, messages)), flat)
    arrived.append(traded(messages, "streams"))

    bias = projection_bias.reshape(-1, 128)
    columns = projection_weight.shape[1]
    block_columns = 256 if columns % 256 == 0 else 384
    third = columns // block_columns // 3
    qkv = []

    def project(after):
        begin = len(qkv) * third
        qkv.append(
            pl.pallas_call(
                functools.partial(project_kernel, begin),
                in_specs=[VMEM, VMEM, in_hbm],
                out_specs=VMEM,
                out_shape=jax.ShapeDtypeStruct((steps * rows, third * block_columns), f32),
                scratch_shapes=[
                    pltpu.VMEM((third, width, block_columns), bf16),
                    pltpu.SemaphoreType.DMA((third,)),
                ],
                compiler_params=pltpu.CompilerParams(vmem_limit_bytes=PROJECT_LIMIT * MIB),
                cost_estimate=SMALL,
                name="project",
            )(normed, held(bias, after), projection_weight)
        )

    def down(chunk, after):
        partial_latent = pl.pallas_call(
            functools.partial(down_kernel, lanes, spots),
            in_specs=[VMEM] * (lanes + subs),
            out_specs=VMEM,
            out_shape=jax.ShapeDtypeStruct((lanes * per_message, 2 * ADAPTER_RANK), f32),
            compiler_params=pltpu.CompilerParams(vmem_limit_bytes=16 * MIB),
            cost_estimate=SMALL,
            name="down",
        )(*arrived[chunk][:0:-1], held(arrived[chunk][0], after), *down_maps)
        return from_others(partial_latent, "heads")

    def up(partials, after):
        message = jax.ShapeDtypeStruct((per_message, query_columns + value_columns), bf16)
        messages = pl.pallas_call(
            functools.partial(up_kernel, heads, subs, spots),
            in_specs=[VMEM] * (heads + 2 * subs),
            out_specs=[VMEM] * lanes,
            out_shape=[message] * lanes,
            compiler_params=pltpu.CompilerParams(vmem_limit_bytes=24 * MIB),
            cost_estimate=SMALL,
            name="up",
        )(held(partials[0], after), *partials[1:], *query_maps, *value_maps)
        return messages

    half_width = HEAD_WIDTH // 2
    position = jnp.concatenate([cache_fill_length + step for step in range(steps)]).astype(f32)
    freq = jnp.exp(jnp.arange(half_width, dtype=f32) * (-math.log(1000000.0) / half_width))
    freq = jnp.concatenate([freq, freq])
    angle = position[:, None] * freq
    sign = jnp.where(jnp.arange(HEAD_WIDTH) < half_width, -1.0, 1.0).astype(f32)
    cosine = jnp.cos(angle)
    sine_part = jnp.sin(angle) * sign

    returned = []
    project(messages)
    after = qkv
    for chunk in range(chunks):
        partials = down(chunk, after)
        project(partials[0])
        after = up(partials, qkv)
        messages = list(after)
        if chunk:
            for lane in range(1, lanes):
                messages[lane] = held(messages[lane], returned[-1][lane])
        returned.append(traded(messages, "streams"))

    length_row = cache_fill_length.reshape(1, rows)
    block = flow_most * chunk_steps
    earlier, along, alongs = [], [], []
    for chunk in range(chunks):
        last = chunk == chunks - 1
        message = jax.ShapeDtypeStruct((subs * block, query_columns), bf16)
        fresh = jax.ShapeDtypeStruct((chunk_rows, 2 * value_columns), f32)
        rows_of = lambda shape: pl.BlockSpec(shape, lambda i, chunk=chunk: (chunk, 0))
        results = pl.pallas_call(
            functools.partial(
                attend_kernel,
                chunk * chunk_steps,
                chunk_steps,
                rows,
                cache,
                groups,
                lanes,
                subs,
                last,
            ),
            grid=(1,),
            in_specs=[whole(places.shape), whole(length_row.shape)]
            + [rows_of((chunk_rows, HEAD_WIDTH))] * 2
            + [whole(rotated_key_cache.shape)] * 2
            + [rows_of((chunk_rows, part.shape[1])) for part in qkv]
            + [whole((per_message, query_columns + value_columns))] * lanes
            + [whole(block_rows.shape) for block_rows in earlier],
            out_specs=[whole(fresh.shape)] * (not last) + [whole(message.shape)] * lanes,
            out_shape=[fresh] * (not last) + [message] * lanes,
            scratch_shapes=[
                pltpu.VMEM((chunk_rows, query_columns + value_columns), f32),
                pltpu.VMEM((chunk_rows, query_columns), f32),
                pltpu.VMEM((rows, BATCH * cache), f32),
            ],
            compiler_params=pltpu.CompilerParams(vmem_limit_bytes=32 * MIB),
            cost_estimate=SMALL,
            name="attend",
        )(
            places if chunk else held(places, after),
            length_row,
            cosine,
            sine_part,
            rotated_key_cache,
            value_cache_rows,
            *qkv,
            *returned[chunk],
            *earlier,
        )
        if not last:
            earlier, results = [results[0]], results[1:]
        results = list(results)
        ahead = along or returned[-1]
        for lane in range(1, lanes):
            results[lane] = held(results[lane], ahead[1:])
        along = traded(results, "streams")
        alongs.append(along)

    landed, found = [], []
    for chunk, along in enumerate(alongs):
        base = len(landed)
        landed += along
        where = [[(base + lane, 0)] for lane in range(lanes)]
        for shift in range(1, subs):
            pairs = [(core, core ^ shift) for core in range(subs)]
            span = slice(shift * block, (shift + 1) * block)
            if chunk < chunks - 1:
                joined = jnp.concatenate([block_rows[span] for block_rows in along])
                for lane in range(lanes):
                    where[lane].append((len(landed), lane * block))
                landed.append(lax.ppermute(joined, "sub", pairs))
            else:
                for lane, block_rows in enumerate(along):
                    where[lane].append((len(landed), shift * block))
                    landed.append(lax.ppermute(block_rows, "sub", pairs))
        found.append(where)

    flow = pl.pallas_call(
        functools.partial(place_kernel, found, lanes, subs, flow_most),
        in_specs=[VMEM] * len(landed),
        out_specs=VMEM,
        out_shape=jax.ShapeDtypeStruct((flow_lanes * flow_most, steps, query_columns), bf16),
        compiler_params=pltpu.CompilerParams(vmem_limit_bytes=24 * MIB),
        cost_estimate=SMALL,
        name="place",
    )(*landed)
    return flow[None]


def solution(mesh):
    placed = (
        P(None, ("groups", "streams", "sub"), None),
        P(),
        P(None, "heads"),
        P("heads"),
        P(("groups", "streams", "sub"), None),
        P("groups"),
        P(("groups", "streams", "sub")),
        P(("groups", "streams", "sub"), None, "heads"),
        P(("groups", "streams", "sub"), None, "heads"),
        P(("groups", "streams", "sub"), "heads", None),
        P(("groups", "streams", "sub"), None, "heads"),
        P(("groups", "streams", "sub"), None, "heads"),
        P(("groups", "streams", "sub"), None),
    )
    return jax.shard_map(
        on_device,
        mesh=mesh,
        in_specs=placed,
        out_specs=P(("groups", "streams", "sub"), None, None, "heads"),
        check_vma=False,
    )
```

```python
import functools
import math

import jax
import jax.numpy as jnp
from jax import lax
from jax.experimental import pallas as pl
from jax.experimental.pallas import tpu as pltpu
from jax.sharding import PartitionSpec as P

QUERY_HEADS = 28
KEY_VALUE_HEADS = 4
HEAD_WIDTH = 128
ADAPTER_RANK = 64
MOST = 2
PER_GROUP = QUERY_HEADS // KEY_VALUE_HEADS
LANE_AXES = ("streams", "sub")
BATCH = 8
TOGETHER = 2
PIECE = 32
VMEM = pl.BlockSpec(memory_space=pltpu.VMEM)
MIB = 1 << 20
PACK_LIMIT = 56
PROJECT_LIMIT = 49


def iota(shape, dim):
    return lax.broadcasted_iota(jnp.int32, shape, dim)


def as_column(row):
    count = row.shape[1]
    square = (count, count)
    same = iota(square, 0) == iota(square, 1)
    return jnp.sum(jnp.where(same, jnp.broadcast_to(row, square), 0), axis=1, keepdims=True)


def ranked(labels, most):
    count = labels.shape[1]
    square = (count, count)
    earlier = (as_column(labels) == labels) & (iota(square, 0) < iota(square, 1))
    return labels * most + jnp.sum(earlier.astype(jnp.int32), axis=0, keepdims=True)


def slot_places(speaker, table, lane_base):
    speakers_all = table.shape[1]
    rows = speaker.shape[1]
    match = iota((speakers_all, rows), 0) == speaker
    slots = jnp.sum(jnp.where(match, as_column(table), 0), axis=0, keepdims=True)
    return ranked(slots ^ lane_base, MOST)


def norm_in_pieces(
    pieces, begin, x_hbm, gain_hbm, x_buf, gain_buf, semaphores, normed_ref, started=None
):
    count, width = x_buf.shape
    size = count // pieces
    gain_copy = pltpu.make_async_copy(gain_hbm, gain_buf, semaphores.at[pieces])
    copies = []
    for piece in range(pieces):
        copies.append(
            pltpu.make_async_copy(
                x_hbm.at[pl.ds(begin + piece * size, size)],
                x_buf.at[pl.ds(piece * size, size)],
                semaphores.at[piece],
            )
        )
        copies[-1].start()
        if piece == 0:
            gain_copy.start()
    if started is not None:
        started()
    gain_copy.wait()
    gain = jnp.concatenate([gain_buf[i : i + 1, :] for i in range(gain_buf.shape[0])], axis=1)
    for piece in range(pieces):
        copies[piece].wait()

        def one(index, carry):
            span = pl.ds(pl.multiple_of(piece * size + index * 16, 16), 16)
            values = x_buf[span, :].astype(jnp.float32)
            mean_sq = jnp.sum(values * values, axis=1, keepdims=True) * (1.0 / width)
            normed = values * lax.rsqrt(mean_sq + 1e-06) * gain
            normed_ref[span, :] = normed.astype(jnp.bfloat16)
            return carry

        lax.fori_loop(0, size // 16, one, 0)


def pack_messages(steps, rows, places, normed_ref, message_refs):
    per_message, sliced = message_refs[0].shape
    spots = per_message // steps
    shape = (len(message_refs) * per_message, steps * rows)
    out_row = iota(shape, 0)
    wanted = out_row // per_message * spots + out_row % spots
    out_step = out_row % per_message // spots
    places = jnp.concatenate([places] * steps, axis=1)
    pick = (wanted == places) & (out_step == iota(shape, 1) // rows)
    pick = pick.astype(jnp.float32).astype(jnp.bfloat16)
    begin = pl.multiple_of(lax.axis_index("heads") * sliced, 128)
    own = normed_ref[:, pl.ds(begin, sliced)]
    packed = jnp.dot(pick, own, preferred_element_type=jnp.float32).astype(jnp.bfloat16)
    for number, message_ref in enumerate(message_refs):
        message_ref[...] = packed[number * per_message : (number + 1) * per_message]


def table_copies(table_hbms, table_bufs, semaphores, first):
    copies = [
        pltpu.make_async_copy(source, target, semaphores.at[first + number])
        for number, (source, target) in enumerate(zip(table_hbms, table_bufs))
    ]
    for copy in copies:
        copy.start()
    return copies


def places_from(table_bufs, spots, flow_most):
    speaker, table, owner = [buffer[...] for buffer in table_bufs]
    here, core, subs = lax.axis_index("streams"), lax.axis_index("sub"), lax.axis_size("sub")
    places = slot_places(speaker, table, here * (spots // MOST))
    return places, ranked(owner ^ (here * subs + core), flow_most)


def norm_pack_kernel(steps, rows, flow_most, lanes, pieces, *refs):
    table_hbms, gain_hbm, x_hbm, message_refs = refs[:3], refs[3], refs[4], refs[5 : 5 + lanes]
    x_buf, gain_buf, *table_bufs, semaphores, normed_ref = refs[5 + lanes :]
    copies = table_copies(table_hbms, table_bufs, semaphores, pieces + 1)
    norm_in_pieces(pieces, 0, x_hbm, gain_hbm, x_buf, gain_buf, semaphores, normed_ref)
    for copy in copies:
        copy.wait()
    spots = message_refs[0].shape[0] // steps
    places, _ = places_from(table_bufs, spots, flow_most)
    pack_messages(steps, rows, places, normed_ref, message_refs)


def weight_copies(begin, weight_hbm, weight_buf, semaphores):
    columns = weight_buf.shape[2]
    return [
        pltpu.make_async_copy(
            weight_hbm.at[:, pl.ds((begin + block) * columns, columns)],
            weight_buf.at[block],
            semaphores.at[block],
        )
        for block in range(weight_buf.shape[0])
    ]


def project_blocks(begin, copies, rows_ref, weight_buf, bias_ref, out_ref):
    columns = weight_buf.shape[2]
    tiles = columns // 128
    for block, copy in enumerate(copies):
        first = (begin + block) * tiles
        bias = [bias_ref[tile : tile + 1, :] for tile in range(first, first + tiles)]
        copy.wait()
        product = jnp.dot(rows_ref[...], weight_buf[block], preferred_element_type=jnp.float32)
        out_ref[:, block * columns : (block + 1) * columns] = product + jnp.concatenate(
            bias, axis=1
        )


def norm_pack_project_kernel(steps, rows, flow_most, lanes, pieces, begin, *refs):
    table_hbms, bias_ref, gain_hbm, x_hbm, weight_hbm = refs[:3], *refs[3:7]
    normed_ref, out_ref, places_ref, message_refs = *refs[7:10], refs[10 : 10 + lanes]
    x_buf, gain_buf, *table_bufs, semaphores, weight_buf, weight_semaphores = refs[10 + lanes :]
    copies = weight_copies(0, weight_hbm, weight_buf, weight_semaphores)
    tables = table_copies(table_hbms, table_bufs, semaphores, pieces + 1)

    def start_weights():
        for copy in copies:
            copy.start()

    norm_in_pieces(
        pieces, 0, x_hbm, gain_hbm, x_buf, gain_buf, semaphores, normed_ref, start_weights
    )
    for copy in tables:
        copy.wait()
    spots = message_refs[0].shape[0] // steps
    places, flow_places = places_from(table_bufs, spots, flow_most)
    places_ref[0:1, :] = places
    places_ref[1:2, :] = flow_places
    own_ref = normed_ref.at[pl.ds(begin, steps * rows)]
    pack_messages(steps, rows, places, own_ref, message_refs)
    project_blocks(0, copies, normed_ref, weight_buf, bias_ref, out_ref)


def project_kernel(begin, rows_ref, bias_ref, weight_hbm, out_ref, weight_buf, semaphores):
    copies = weight_copies(begin, weight_hbm, weight_buf, semaphores)
    for copy in copies:
        copy.start()
    project_blocks(begin, copies, rows_ref, weight_buf, bias_ref, out_ref)


def row_slots(shape, spots):
    return iota(shape, 0) % spots // MOST


def down_kernel(lanes, spots, *refs):
    message_refs, map_refs, partial_ref = refs[:lanes][::-1], refs[lanes:-1], refs[-1]
    local_slots = map_refs[0].shape[0]
    rows = jnp.concatenate([ref[...] for ref in message_refs], axis=0)
    own_slot = row_slots(partial_ref.shape, spots)
    total = jnp.zeros(partial_ref.shape, jnp.float32)
    for number, map_ref in enumerate(map_refs):
        shift = (lax.axis_index("sub") ^ number) * local_slots
        for slot in range(local_slots):
            part = jnp.dot(rows, map_ref[slot], preferred_element_type=jnp.float32)
            total = jnp.where(own_slot == shift + slot, part, total)
    partial_ref[...] = total


def up_kernel(heads, subs, spots, *refs):
    partial_refs, refs = refs[:heads], refs[heads:]
    query_refs, value_refs, message_refs = refs[:subs], refs[subs : 2 * subs], refs[2 * subs :]
    total = partial_refs[0][...]
    for ref in partial_refs[1:]:
        total = total + ref[...]
    latent = total.astype(jnp.bfloat16).astype(jnp.float32)
    own_slot = row_slots(latent.shape, spots)
    column = iota(latent.shape, 1) // ADAPTER_RANK
    turned = pltpu.roll(latent, ADAPTER_RANK, 1)
    low = iota(latent.shape, 1) < ADAPTER_RANK
    query_pair = jnp.where(low, latent, turned)
    value_pair = jnp.where(low, turned, latent)

    def product(pair, map_refs):
        result = None
        for number, map_ref in enumerate(map_refs):
            local_slots = map_ref.shape[0] // ADAPTER_RANK
            shift = (lax.axis_index("sub") ^ number) * local_slots
            pieces = []
            for slot in range(0, local_slots, 2):
                kept = jnp.where(own_slot == shift + slot + column, pair, 0.0)
                pieces.append(kept.astype(jnp.bfloat16))
            wide = jnp.concatenate(pieces, axis=1)
            part = jnp.dot(wide, map_ref[...], preferred_element_type=jnp.float32)
            result = part if result is None else result + part
        return result.astype(jnp.bfloat16)

    queries = product(query_pair, query_refs)
    values = product(value_pair, value_refs)
    query_width = queries.shape[1]
    per_message = message_refs[0].shape[0]
    for number, ref in enumerate(message_refs):
        span = slice(number * per_message, (number + 1) * per_message)
        ref[:, :query_width] = queries[span]
        ref[:, query_width:] = values[span]


def attend_kernel(before, steps, rows, cache, groups, lanes, subs, last, *refs):
    places_ref, length_ref, cos_ref, sin_ref, key_ref, value_ref = refs[:6]
    qkv_refs, refs = refs[6:9], refs[9:]
    delta_refs, refs = refs[:lanes], refs[lanes:]
    if before:
        earlier_ref, refs = refs[0], refs[1:]
    if not last:
        fresh_ref, refs = refs[0], refs[1:]
    message_refs = refs[:lanes]
    delta_ref, context_ref, bias_ref = refs[lanes:]
    per_message = delta_refs[0].shape[0]
    spots = per_message // steps
    query_width = PER_GROUP * HEAD_WIDTH
    known = before + steps

    def qkv_tile(span, group, head):
        part, begin = divmod((group * (PER_GROUP + 2) + head) * HEAD_WIDTH, qkv_refs[0].shape[1])
        return qkv_refs[part][span, begin : begin + HEAD_WIDTH]

    wide = groups * HEAD_WIDTH
    column = as_column(places_ref[0:1, :])
    column = jnp.concatenate([column] * steps, axis=0)
    shape = (steps * rows, lanes * per_message)
    out_row = iota(shape, 1)
    wanted = out_row // per_message * spots + out_row % spots
    pick = (wanted == column) & (out_row % per_message // spots == iota(shape, 0) // rows)
    pick = pick.astype(jnp.float32).astype(jnp.bfloat16)
    delta_ref[...] = jnp.dot(
        pick,
        jnp.concatenate([ref[...] for ref in delta_refs], axis=0),
        preferred_element_type=jnp.float32,
    )

    shape = (rows, BATCH * cache)
    lengths = as_column(length_ref[...])
    slot_column = iota(shape, 1)
    allowed = (slot_column // cache == iota(shape, 0) % BATCH) & (slot_column % cache < lengths)
    bias_ref[...] = jnp.where(allowed, 0.0, -1e30)
    shape = (steps, BATCH, known * BATCH)
    fresh_column = iota(shape, 2)
    allowed = (fresh_column % BATCH == iota(shape, 1)) & (
        fresh_column // BATCH <= iota(shape, 0) + before
    )
    fresh_bias = jnp.where(allowed, 0.0, -1e30)
    scale = HEAD_WIDTH ** (-0.5)
    transposed = (((1,), (1,)), ((), ()))

    def scored(first, group):
        spans = [pl.ds(pl.multiple_of(step * rows + first, BATCH), BATCH) for step in range(known)]
        query_tiles, key_tiles, value_tiles = [], [], []
        lane_span = slice(group * HEAD_WIDTH, (group + 1) * HEAD_WIDTH)
        value_span = slice(wide + group * HEAD_WIDTH, wide + (group + 1) * HEAD_WIDTH)
        for span in spans[:before]:
            key_tiles.append(earlier_ref[span, lane_span])
            value_tiles.append(earlier_ref[span, value_span])
        for span in spans[:steps]:
            cosine, sine_part = cos_ref[span, :], sin_ref[span, :]

            def rotated(values):
                return values * cosine + pltpu.roll(values, HEAD_WIDTH // 2, 1) * sine_part

            for head in range(PER_GROUP):
                begin = group * query_width + head * HEAD_WIDTH
                change = delta_ref[span, begin : begin + HEAD_WIDTH]
                query_tiles.append(rotated(qkv_tile(span, group, head) + change))
            key = rotated(qkv_tile(span, group, PER_GROUP))
            begin = groups * query_width + group * HEAD_WIDTH
            change = delta_ref[span, begin : begin + HEAD_WIDTH]
            value = qkv_tile(span, group, PER_GROUP + 1) + change
            if not last:
                fresh_ref[span, lane_span] = key
                fresh_ref[span, value_span] = value
            key_tiles.append(key)
            value_tiles.append(value)
        queries = jnp.concatenate(query_tiles, axis=0).astype(jnp.bfloat16)
        new_keys = jnp.concatenate(key_tiles, axis=0).astype(jnp.bfloat16)
        new_values = jnp.concatenate(value_tiles, axis=0).astype(jnp.bfloat16)
        old_keys = key_ref[pl.ds(first, BATCH), :, lane_span].reshape(BATCH * cache, HEAD_WIDTH)
        old_scores = lax.dot_general(
            queries, old_keys, transposed, preferred_element_type=jnp.float32
        )
        new_scores = lax.dot_general(
            queries, new_keys, transposed, preferred_element_type=jnp.float32
        )
        return old_scores, new_scores, new_values

    def weighed(first, old_scores, new_scores):
        heads = steps * PER_GROUP
        old_scores = (old_scores * scale).reshape(heads, BATCH, BATCH * cache)
        old_scores = old_scores + bias_ref[pl.ds(first, BATCH), :][None]
        new_scores = (new_scores * scale).reshape(steps, PER_GROUP, BATCH, known * BATCH)
        new_scores = (new_scores + fresh_bias[:, None]).reshape(heads, BATCH, known * BATCH)
        peak = jnp.maximum(
            jnp.max(old_scores, axis=-1, keepdims=True),
            jnp.max(new_scores, axis=-1, keepdims=True),
        )
        old_scores = jnp.exp(old_scores - peak)
        new_scores = jnp.exp(new_scores - peak)
        share = 1.0 / (
            jnp.sum(old_scores, axis=-1, keepdims=True)
            + jnp.sum(new_scores, axis=-1, keepdims=True)
        )
        old_weights = (old_scores * share).reshape(heads * BATCH, BATCH * cache)
        new_weights = (new_scores * share).reshape(heads * BATCH, known * BATCH)
        return old_weights.astype(jnp.bfloat16), new_weights.astype(jnp.bfloat16)

    def batch(index, carry):
        chains = []
        for number in range(TOGETHER):
            first = pl.multiple_of((index * TOGETHER + number) * BATCH, BATCH)
            chains += [(first, group) for group in range(groups)]
        scores = [scored(*chain) for chain in chains]
        weights = [weighed(chain[0], *score[:2]) for chain, score in zip(chains, scores)]
        for (first, group), (old_weights, new_weights), score in zip(chains, weights, scores):
            lane_span = slice(group * HEAD_WIDTH, (group + 1) * HEAD_WIDTH)
            old_values = value_ref[pl.ds(first, BATCH), :, lane_span]
            old_values = old_values.reshape(BATCH * cache, HEAD_WIDTH)
            context = jnp.dot(
                old_weights, old_values, preferred_element_type=jnp.float32
            ) + jnp.dot(new_weights, score[2], preferred_element_type=jnp.float32)
            for step in range(steps):
                span = pl.ds(pl.multiple_of(step * rows + first, BATCH), BATCH)
                for head in range(PER_GROUP):
                    row = (step * PER_GROUP + head) * BATCH
                    begin = group * query_width + head * HEAD_WIDTH
                    context_ref[span, begin : begin + HEAD_WIDTH] = context[row : row + BATCH]
        return carry

    lax.fori_loop(0, rows // (BATCH * TOGETHER), batch, 0)

    flow_places = jnp.concatenate([places_ref[1:2, :]] * steps, axis=1)
    context = context_ref[...].astype(jnp.bfloat16)
    count = message_refs[0].shape[0]
    shape = (count, steps * rows)
    out_row = iota(shape, 0)
    same_step = out_row % steps == iota(shape, 1) // rows
    for number, message_ref in enumerate(message_refs):
        wanted = number * (count // steps) + out_row // steps
        pick = ((flow_places == wanted) & same_step).astype(jnp.float32).astype(jnp.bfloat16)
        message_ref[...] = jnp.dot(
            pick, context, preferred_element_type=jnp.float32
        ).astype(jnp.bfloat16)


def place_kernel(parts, found, lanes, subs, most, *refs):
    out_ref = refs[-1]
    steps = out_ref.shape[1]
    here = lax.axis_index("streams")
    core = lax.axis_index("sub")
    shape = (most * steps, most * steps)
    out_row, in_row = iota(shape, 0), iota(shape, 1)
    step, rank = out_row % steps, out_row // steps
    pick = jnp.zeros(shape, jnp.float32)
    begin = 0
    for part in parts:
        here_step = (step >= begin) & (step < begin + part)
        wanted = most * begin + rank * part + step - begin
        pick = jnp.where(here_step & (wanted == in_row), 1.0, pick)
        begin += part
    pick = pick.astype(jnp.bfloat16)
    for number in range(lanes):
        for other in range(subs):
            pieces = []
            for part, where in zip(parts, found):
                array, begin = where[number][other]
                pieces.append(refs[array][...][begin : begin + most * part])
            rows = jnp.dot(
                pick, jnp.concatenate(pieces, axis=0), preferred_element_type=jnp.float32
            )
            source = (here ^ number) * subs + (core ^ other)
            out_ref[pl.ds(source * most, most)] = rows.reshape(
                most, steps, rows.shape[1]
            ).astype(jnp.bfloat16)


def traded(blocks, axes):
    landed = list(blocks)
    count = len(blocks)
    order = sorted(range(1, count), key=lambda shift: -(shift ^ (shift >> 1)))
    for shift in order:
        pairs = [(place, place ^ shift) for place in range(count)]
        landed[shift] = lax.ppermute(blocks[shift], axes, pairs)
    return landed


def from_others(block, axis):
    count = lax.axis_size(axis)
    landed = [block]
    for shift in range(1, count):
        pairs = [(place, place ^ shift) for place in range(count)]
        landed.append(lax.ppermute(block, axis, pairs))
    return landed


def held(value, others):
    return lax.optimization_barrier((value, others))[0]


SMALL = pl.CostEstimate(flops=1, bytes_accessed=1, transcendentals=0)


def on_device(
    inputs,
    input_norm_gain,
    projection_weight,
    projection_bias,
    speaker,
    speaker_adapter_slot,
    cache_fill_length,
    rotated_key_cache,
    value_cache_rows,
    adapter_down_maps,
    adapter_query_up,
    adapter_value_up,
    flow_decoder_owner,
):
    steps, rows, width = inputs.shape
    lanes = lax.axis_size("streams")
    subs = lax.axis_size("sub")
    heads = lax.axis_size("heads")
    flow_lanes = lanes * subs
    local_slots, sliced, _ = adapter_down_maps.shape
    query_columns = adapter_query_up.shape[2]
    value_columns = adapter_value_up.shape[2]
    groups = value_columns // HEAD_WIDTH
    cache = rotated_key_cache.shape[1]
    spots = subs * local_slots * MOST
    parts = [steps - 1, 1]
    chunks = len(parts)
    chip_slots = subs * local_slots
    flow_most = max(2, (2 * rows + flow_lanes - 1) // flow_lanes)
    bf16, f32 = jnp.bfloat16, jnp.float32

    def whole(shape):
        return pl.BlockSpec(shape, lambda i: (0,) * len(shape))

    in_hbm = pl.BlockSpec(memory_space=pltpu.HBM)

    down_maps = from_others(adapter_down_maps, "sub")
    query_maps = from_others(
        adapter_query_up.reshape(local_slots * ADAPTER_RANK, query_columns), "sub"
    )
    value_maps = from_others(
        adapter_value_up.reshape(local_slots * ADAPTER_RANK, value_columns), "sub"
    )

    flat = inputs.reshape(steps * rows, width)
    gain = input_norm_gain.reshape(width // 128, 128)
    messages_shape = [
        [jax.ShapeDtypeStruct((part * spots, sliced), bf16)] * lanes for part in parts
    ]
    places_shape = jax.ShapeDtypeStruct((8, rows), jnp.int32)
    tables = [
        speaker.reshape(1, rows),
        speaker_adapter_slot.reshape(1, -1),
        flow_decoder_owner.reshape(1, rows),
    ]

    def row_buffers(count, pieces):
        return (
            [pltpu.VMEM((count, width), bf16), pltpu.VMEM(gain.shape, f32)]
            + [pltpu.VMEM(table.shape, jnp.int32) for table in tables]
            + [pltpu.SemaphoreType.DMA((pieces + 4,))]
        )

    first_rows = parts[0] * rows
    pieces = first_rows // PIECE

    messages = pl.pallas_call(
        functools.partial(norm_pack_kernel, parts[0], rows, flow_most, lanes, pieces),
        in_specs=[in_hbm] * 5,
        out_specs=[VMEM] * lanes,
        out_shape=messages_shape[0],
        scratch_shapes=row_buffers(first_rows, pieces)
        + [pltpu.VMEM((first_rows, width), bf16)],
        compiler_params=pltpu.CompilerParams(vmem_limit_bytes=PACK_LIMIT * MIB),
        cost_estimate=SMALL,
        name="norm_and_pack",
    )(*tables, gain, flat)
    arrived = [traded(messages, "streams")]

    bias = projection_bias.reshape(-1, 128)
    columns = projection_weight.shape[1]
    block_columns = 256 if columns % 256 == 0 else 384
    blocks = columns // block_columns
    cut = blocks // 3

    def weight_buffers(count):
        return [
            pltpu.VMEM((count, width, block_columns), bf16),
            pltpu.SemaphoreType.DMA((count,)),
        ]

    def projected(count):
        return jax.ShapeDtypeStruct((steps * rows, count * block_columns), f32)

    adapters = down_maps[1:], query_maps[1:], value_maps[1:]
    weight_buf, weight_semaphores = weight_buffers(cut)
    pieces = steps * rows // PIECE
    normed, first_qkv, places, *messages = pl.pallas_call(
        functools.partial(
            norm_pack_project_kernel, parts[1], rows, flow_most, lanes, pieces, first_rows
        ),
        in_specs=[in_hbm] * 3 + [VMEM] + [in_hbm] * 3,
        out_specs=[VMEM] * (3 + lanes),
        out_shape=[jax.ShapeDtypeStruct((steps * rows, width), bf16), projected(cut)]
        + [places_shape]
        + messages_shape[1],
        scratch_shapes=row_buffers(steps * rows, pieces) + [weight_buf, weight_semaphores],
        compiler_params=pltpu.CompilerParams(vmem_limit_bytes=PROJECT_LIMIT * MIB),
        cost_estimate=SMALL,
        name="norm_pack_project",
    )(*tables, held(bias, (adapters, messages)), gain, flat, projection_weight)
    arrived.append(traded(messages, "streams"))
    qkv = [first_qkv]

    def project(after):
        return pl.pallas_call(
            functools.partial(project_kernel, cut * len(qkv)),
            in_specs=[VMEM, VMEM, in_hbm],
            out_specs=VMEM,
            out_shape=projected(cut),
            scratch_shapes=weight_buffers(cut),
            compiler_params=pltpu.CompilerParams(vmem_limit_bytes=PROJECT_LIMIT * MIB),
            cost_estimate=SMALL,
            name="project",
        )(normed, held(bias, after), projection_weight)

    def down(chunk, after):
        partial_latent = pl.pallas_call(
            functools.partial(down_kernel, lanes, spots),
            in_specs=[VMEM] * (lanes + subs),
            out_specs=VMEM,
            out_shape=jax.ShapeDtypeStruct(
                (lanes * parts[chunk] * spots, 2 * ADAPTER_RANK), f32
            ),
            compiler_params=pltpu.CompilerParams(vmem_limit_bytes=16 * MIB),
            cost_estimate=SMALL,
            name="down",
        )(*arrived[chunk][:0:-1], held(arrived[chunk][0], after), *down_maps)
        return from_others(partial_latent, "heads")

    def up(chunk, partials, after):
        message = jax.ShapeDtypeStruct(
            (parts[chunk] * spots, query_columns + value_columns), bf16
        )
        messages = pl.pallas_call(
            functools.partial(up_kernel, heads, subs, spots),
            in_specs=[VMEM] * (heads + 2 * subs),
            out_specs=[VMEM] * lanes,
            out_shape=[message] * lanes,
            compiler_params=pltpu.CompilerParams(vmem_limit_bytes=24 * MIB),
            cost_estimate=SMALL,
            name="up",
        )(held(partials[0], after), *partials[1:], *query_maps, *value_maps)
        return messages

    half_width = HEAD_WIDTH // 2
    position = jnp.concatenate([cache_fill_length + step for step in range(steps)]).astype(f32)
    freq = jnp.exp(jnp.arange(half_width, dtype=f32) * (-math.log(1000000.0) / half_width))
    freq = jnp.concatenate([freq, freq])
    angle = position[:, None] * freq
    sign = jnp.where(jnp.arange(HEAD_WIDTH) < half_width, -1.0, 1.0).astype(f32)
    cosine = jnp.cos(angle)
    sine_part = jnp.sin(angle) * sign

    returned = []
    after = qkv
    for chunk in range(chunks):
        partials = down(chunk, after)
        qkv.append(project(partials[0]))
        after = up(chunk, partials, qkv)
        messages = list(after)
        ahead = returned[-1] if chunk else arrived[-1]
        for lane in range(1, lanes):
            messages[lane] = held(messages[lane], ahead[lane:])
        returned.append(traded(messages, "streams"))

    length_row = cache_fill_length.reshape(1, rows)
    earlier, along, alongs = [], [], []
    for chunk in range(chunks):
        last = chunk == chunks - 1
        begin, part = sum(parts[:chunk]), parts[chunk]
        chunk_rows = part * rows
        message = jax.ShapeDtypeStruct((subs * flow_most * part, query_columns), bf16)
        fresh = jax.ShapeDtypeStruct((chunk_rows, 2 * value_columns), f32)
        rows_of = lambda shape: pl.BlockSpec(shape, lambda i, place=begin // part: (place, 0))
        results = pl.pallas_call(
            functools.partial(
                attend_kernel,
                begin,
                part,
                rows,
                cache,
                groups,
                lanes,
                subs,
                last,
            ),
            grid=(1,),
            in_specs=[whole(places.shape), whole(length_row.shape)]
            + [rows_of((chunk_rows, HEAD_WIDTH))] * 2
            + [whole(rotated_key_cache.shape)] * 2
            + [rows_of((chunk_rows, part.shape[1])) for part in qkv]
            + [whole((part * spots, query_columns + value_columns))] * lanes
            + [whole(block_rows.shape) for block_rows in earlier],
            out_specs=[whole(fresh.shape)] * (not last) + [whole(message.shape)] * lanes,
            out_shape=[fresh] * (not last) + [message] * lanes,
            scratch_shapes=[
                pltpu.VMEM((chunk_rows, query_columns + value_columns), f32),
                pltpu.VMEM((chunk_rows, query_columns), f32),
                pltpu.VMEM((rows, BATCH * cache), f32),
            ],
            compiler_params=pltpu.CompilerParams(vmem_limit_bytes=32 * MIB),
            cost_estimate=SMALL,
            name="attend",
        )(
            places if chunk else held(places, after),
            length_row,
            cosine,
            sine_part,
            rotated_key_cache,
            value_cache_rows,
            *qkv,
            *returned[chunk],
            *earlier,
        )
        if not last:
            earlier, results = [results[0]], results[1:]
        results = list(results)
        ahead = along or returned[-1]
        for lane in range(1, lanes):
            results[lane] = held(results[lane], ahead[1:])
        along = traded(results, "streams")
        alongs.append(along)

    landed, found = [], []
    for chunk, along in enumerate(alongs):
        base = len(landed)
        block = flow_most * parts[chunk]
        landed += along
        where = [[(base + lane, 0)] for lane in range(lanes)]
        for shift in range(1, subs):
            pairs = [(core, core ^ shift) for core in range(subs)]
            span = slice(shift * block, (shift + 1) * block)
            if chunk < chunks - 1:
                along = held(along[::-1], results)[::-1]
                joined = jnp.concatenate([block_rows[span] for block_rows in along])
                for lane in range(lanes):
                    where[lane].append((len(landed), lane * block))
                landed.append(lax.ppermute(joined, "sub", pairs))
            else:
                for lane, block_rows in enumerate(along):
                    where[lane].append((len(landed), shift * block))
                    landed.append(lax.ppermute(block_rows, "sub", pairs))
        found.append(where)

    flow = pl.pallas_call(
        functools.partial(place_kernel, parts, found, lanes, subs, flow_most),
        in_specs=[VMEM] * len(landed),
        out_specs=VMEM,
        out_shape=jax.ShapeDtypeStruct((flow_lanes * flow_most, steps, query_columns), bf16),
        compiler_params=pltpu.CompilerParams(vmem_limit_bytes=24 * MIB),
        cost_estimate=SMALL,
        name="place",
    )(*landed)
    return flow[None]


def solution(mesh):
    placed = (
        P(None, ("groups", "streams", "sub"), None),
        P(),
        P(None, "heads"),
        P("heads"),
        P(("groups", "streams", "sub"), None),
        P("groups"),
        P(("groups", "streams", "sub")),
        P(("groups", "streams", "sub"), None, "heads"),
        P(("groups", "streams", "sub"), None, "heads"),
        P(("groups", "streams", "sub"), "heads", None),
        P(("groups", "streams", "sub"), None, "heads"),
        P(("groups", "streams", "sub"), None, "heads"),
        P(("groups", "streams", "sub"), None),
    )
    return jax.shard_map(
        on_device,
        mesh=mesh,
        in_specs=placed,
        out_specs=P(("groups", "streams", "sub"), None, None, "heads"),
        check_vma=False,
    )
```

```python
import functools
import math

import jax
import jax.numpy as jnp
from jax import lax
from jax.experimental import pallas as pl
from jax.experimental.pallas import tpu as pltpu
from jax.sharding import PartitionSpec as P

QUERY_HEADS = 28
KEY_VALUE_HEADS = 4
HEAD_WIDTH = 128
ADAPTER_RANK = 64
MOST = 2
PER_GROUP = QUERY_HEADS // KEY_VALUE_HEADS
LANE_AXES = ("streams", "sub")
BATCH = 8
TOGETHER = 2
VMEM = pl.BlockSpec(memory_space=pltpu.VMEM)
MIB = 1 << 20
PACK_LIMIT = 56
PROJECT_LIMIT = 49


def iota(shape, dim):
    return lax.broadcasted_iota(jnp.int32, shape, dim)


def as_column(row):
    count = row.shape[1]
    square = (count, count)
    same = iota(square, 0) == iota(square, 1)
    return jnp.sum(jnp.where(same, jnp.broadcast_to(row, square), 0), axis=1, keepdims=True)


def ranked(labels, most):
    count = labels.shape[1]
    square = (count, count)
    earlier = (as_column(labels) == labels) & (iota(square, 0) < iota(square, 1))
    return labels * most + jnp.sum(earlier.astype(jnp.int32), axis=0, keepdims=True)


def slot_places(speaker, table, lane_base):
    speakers_all = table.shape[1]
    rows = speaker.shape[1]
    match = iota((speakers_all, rows), 0) == speaker
    slots = jnp.sum(jnp.where(match, as_column(table), 0), axis=0, keepdims=True)
    return ranked(slots ^ lane_base, MOST)


def norm_in_pieces(
    pieces, begin, x_hbm, gain_hbm, x_buf, gain_buf, semaphores, normed_ref, started=None
):
    count, width = x_buf.shape
    size = count // pieces
    gain_copy = pltpu.make_async_copy(gain_hbm, gain_buf, semaphores.at[pieces])
    copies = []
    for piece in range(pieces):
        copies.append(
            pltpu.make_async_copy(
                x_hbm.at[pl.ds(begin + piece * size, size)],
                x_buf.at[pl.ds(piece * size, size)],
                semaphores.at[piece],
            )
        )
        copies[-1].start()
        if piece == 0:
            gain_copy.start()
    if started is not None:
        started()
    gain_copy.wait()
    gain = jnp.concatenate([gain_buf[i : i + 1, :] for i in range(gain_buf.shape[0])], axis=1)
    for piece in range(pieces):
        copies[piece].wait()

        def one(index, carry):
            span = pl.ds(pl.multiple_of(piece * size + index * 16, 16), 16)
            values = x_buf[span, :].astype(jnp.float32)
            mean_sq = jnp.sum(values * values, axis=1, keepdims=True) * (1.0 / width)
            normed = values * lax.rsqrt(mean_sq + 1e-06) * gain
            normed_ref[span, :] = normed.astype(jnp.bfloat16)
            return carry

        lax.fori_loop(0, size // 16, one, 0)


def pack_messages(steps, rows, places, normed_ref, message_refs):
    per_message, sliced = message_refs[0].shape
    spots = per_message // steps
    shape = (len(message_refs) * per_message, steps * rows)
    out_row = iota(shape, 0)
    wanted = out_row // per_message * spots + out_row % spots
    out_step = out_row % per_message // spots
    places = jnp.concatenate([places] * steps, axis=1)
    pick = (wanted == places) & (out_step == iota(shape, 1) // rows)
    pick = pick.astype(jnp.float32).astype(jnp.bfloat16)
    begin = pl.multiple_of(lax.axis_index("heads") * sliced, 128)
    own = normed_ref[:, pl.ds(begin, sliced)]
    packed = jnp.dot(pick, own, preferred_element_type=jnp.float32).astype(jnp.bfloat16)
    for number, message_ref in enumerate(message_refs):
        message_ref[...] = packed[number * per_message : (number + 1) * per_message]


def table_copies(table_hbms, table_bufs, semaphores, first):
    copies = [
        pltpu.make_async_copy(source, target, semaphores.at[first + number])
        for number, (source, target) in enumerate(zip(table_hbms, table_bufs))
    ]
    for copy in copies:
        copy.start()
    return copies


def places_from(table_bufs, spots, flow_most):
    speaker, table, owner = [buffer[...] for buffer in table_bufs]
    here, core, subs = lax.axis_index("streams"), lax.axis_index("sub"), lax.axis_size("sub")
    places = slot_places(speaker, table, here * (spots // MOST))
    return places, ranked(owner ^ (here * subs + core), flow_most)


def norm_pack_kernel(steps, rows, flow_most, lanes, pieces, *refs):
    table_hbms, gain_hbm, x_hbm, message_refs = refs[:3], refs[3], refs[4], refs[5 : 5 + lanes]
    x_buf, gain_buf, *table_bufs, semaphores, normed_ref = refs[5 + lanes :]
    copies = table_copies(table_hbms, table_bufs, semaphores, pieces + 1)
    norm_in_pieces(pieces, 0, x_hbm, gain_hbm, x_buf, gain_buf, semaphores, normed_ref)
    for copy in copies:
        copy.wait()
    spots = message_refs[0].shape[0] // steps
    places, _ = places_from(table_bufs, spots, flow_most)
    pack_messages(steps, rows, places, normed_ref, message_refs)


def weight_copies(begin, weight_hbm, weight_buf, semaphores):
    columns = weight_buf.shape[2]
    return [
        pltpu.make_async_copy(
            weight_hbm.at[:, pl.ds((begin + block) * columns, columns)],
            weight_buf.at[block],
            semaphores.at[block],
        )
        for block in range(weight_buf.shape[0])
    ]


def project_blocks(begin, copies, rows_ref, weight_buf, bias_ref, out_ref):
    columns = weight_buf.shape[2]
    tiles = columns // 128
    for block, copy in enumerate(copies):
        first = (begin + block) * tiles
        bias = [bias_ref[tile : tile + 1, :] for tile in range(first, first + tiles)]
        copy.wait()
        product = jnp.dot(rows_ref[...], weight_buf[block], preferred_element_type=jnp.float32)
        out_ref[:, block * columns : (block + 1) * columns] = product + jnp.concatenate(
            bias, axis=1
        )


def norm_pack_project_kernel(steps, rows, flow_most, lanes, pieces, chunk, *refs):
    table_hbms, bias_ref, gain_hbm, x_hbm, weight_hbm = refs[:3], *refs[3:7]
    normed_ref, out_ref, places_ref, message_refs = *refs[7:10], refs[10 : 10 + lanes]
    x_buf, gain_buf, *table_bufs, semaphores, weight_buf, weight_semaphores = refs[10 + lanes :]
    copies = weight_copies(0, weight_hbm, weight_buf, weight_semaphores)
    tables = table_copies(table_hbms, table_bufs, semaphores, pieces + 1)

    def start_weights():
        for copy in copies:
            copy.start()

    norm_in_pieces(
        pieces, 0, x_hbm, gain_hbm, x_buf, gain_buf, semaphores, normed_ref, start_weights
    )
    for copy in tables:
        copy.wait()
    spots = message_refs[0].shape[0] // steps
    places, flow_places = places_from(table_bufs, spots, flow_most)
    places_ref[0:1, :] = places
    places_ref[1:2, :] = flow_places
    count = steps * rows
    own_ref = normed_ref.at[pl.ds(chunk * count, count)]
    pack_messages(steps, rows, places, own_ref, message_refs)
    project_blocks(0, copies, normed_ref, weight_buf, bias_ref, out_ref)


def project_kernel(begin, rows_ref, bias_ref, weight_hbm, out_ref, weight_buf, semaphores):
    copies = weight_copies(begin, weight_hbm, weight_buf, semaphores)
    for copy in copies:
        copy.start()
    project_blocks(begin, copies, rows_ref, weight_buf, bias_ref, out_ref)


def row_slots(shape, spots):
    return iota(shape, 0) % spots // MOST


def down_kernel(lanes, spots, *refs):
    message_refs, map_refs, partial_ref = refs[:lanes][::-1], refs[lanes:-1], refs[-1]
    local_slots = map_refs[0].shape[0]
    rows = jnp.concatenate([ref[...] for ref in message_refs], axis=0)
    own_slot = row_slots(partial_ref.shape, spots)
    total = jnp.zeros(partial_ref.shape, jnp.float32)
    for number, map_ref in enumerate(map_refs):
        shift = (lax.axis_index("sub") ^ number) * local_slots
        for slot in range(local_slots):
            part = jnp.dot(rows, map_ref[slot], preferred_element_type=jnp.float32)
            total = jnp.where(own_slot == shift + slot, part, total)
    partial_ref[...] = total


def up_kernel(heads, subs, spots, *refs):
    partial_refs, refs = refs[:heads], refs[heads:]
    query_refs, value_refs, message_refs = refs[:subs], refs[subs : 2 * subs], refs[2 * subs :]
    total = partial_refs[0][...]
    for ref in partial_refs[1:]:
        total = total + ref[...]
    latent = total.astype(jnp.bfloat16).astype(jnp.float32)
    own_slot = row_slots(latent.shape, spots)
    column = iota(latent.shape, 1) // ADAPTER_RANK
    turned = pltpu.roll(latent, ADAPTER_RANK, 1)
    low = iota(latent.shape, 1) < ADAPTER_RANK
    query_pair = jnp.where(low, latent, turned)
    value_pair = jnp.where(low, turned, latent)

    def product(pair, map_refs):
        result = None
        for number, map_ref in enumerate(map_refs):
            local_slots = map_ref.shape[0] // ADAPTER_RANK
            shift = (lax.axis_index("sub") ^ number) * local_slots
            pieces = []
            for slot in range(0, local_slots, 2):
                kept = jnp.where(own_slot == shift + slot + column, pair, 0.0)
                pieces.append(kept.astype(jnp.bfloat16))
            wide = jnp.concatenate(pieces, axis=1)
            part = jnp.dot(wide, map_ref[...], preferred_element_type=jnp.float32)
            result = part if result is None else result + part
        return result.astype(jnp.bfloat16)

    queries = product(query_pair, query_refs)
    values = product(value_pair, value_refs)
    query_width = queries.shape[1]
    per_message = message_refs[0].shape[0]
    for number, ref in enumerate(message_refs):
        span = slice(number * per_message, (number + 1) * per_message)
        ref[:, :query_width] = queries[span]
        ref[:, query_width:] = values[span]


def attend_kernel(before, steps, rows, cache, groups, lanes, subs, last, *refs):
    places_ref, length_ref, cos_ref, sin_ref, key_ref, value_ref = refs[:6]
    qkv_refs, refs = refs[6:8], refs[8:]
    delta_refs, refs = refs[:lanes][::-1], refs[lanes:]
    if before:
        earlier_ref, refs = refs[0], refs[1:]
    if not last:
        fresh_ref, refs = refs[0], refs[1:]
    message_refs = refs[:lanes]
    delta_ref, context_ref, bias_ref = refs[lanes:]
    per_message = delta_refs[0].shape[0]
    spots = per_message // steps
    query_width = PER_GROUP * HEAD_WIDTH
    known = before + steps

    def qkv_tile(span, group, head):
        begin = (group * (PER_GROUP + 2) + head) * HEAD_WIDTH
        edge = qkv_refs[0].shape[1]
        if begin < edge:
            return qkv_refs[0][span, begin : begin + HEAD_WIDTH]
        return qkv_refs[1][span, begin - edge : begin - edge + HEAD_WIDTH]

    wide = groups * HEAD_WIDTH

    column = as_column(places_ref[0:1, :])
    column = jnp.concatenate([column] * steps, axis=0)
    shape = (steps * rows, lanes * per_message)
    out_row = iota(shape, 1)
    wanted = out_row // per_message * spots + out_row % spots
    pick = (wanted == column) & (out_row % per_message // spots == iota(shape, 0) // rows)
    pick = pick.astype(jnp.float32).astype(jnp.bfloat16)
    delta_ref[...] = jnp.dot(
        pick,
        jnp.concatenate([ref[...] for ref in delta_refs], axis=0),
        preferred_element_type=jnp.float32,
    )

    shape = (rows, BATCH * cache)
    lengths = as_column(length_ref[...])
    slot_column = iota(shape, 1)
    allowed = (slot_column // cache == iota(shape, 0) % BATCH) & (slot_column % cache < lengths)
    bias_ref[...] = jnp.where(allowed, 0.0, -1e30)
    shape = (steps, BATCH, known * BATCH)
    fresh_column = iota(shape, 2)
    allowed = (fresh_column % BATCH == iota(shape, 1)) & (
        fresh_column // BATCH <= iota(shape, 0) + before
    )
    fresh_bias = jnp.where(allowed, 0.0, -1e30)
    scale = HEAD_WIDTH ** (-0.5)
    transposed = (((1,), (1,)), ((), ()))

    def scored(first, group):
        spans = [pl.ds(pl.multiple_of(step * rows + first, BATCH), BATCH) for step in range(known)]
        query_tiles, key_tiles, value_tiles = [], [], []
        lane_span = slice(group * HEAD_WIDTH, (group + 1) * HEAD_WIDTH)
        value_span = slice(wide + group * HEAD_WIDTH, wide + (group + 1) * HEAD_WIDTH)
        for span in spans[:before]:
            key_tiles.append(earlier_ref[span, lane_span])
            value_tiles.append(earlier_ref[span, value_span])
        for span in spans[:steps]:
            cosine, sine_part = cos_ref[span, :], sin_ref[span, :]

            def rotated(values):
                return values * cosine + pltpu.roll(values, HEAD_WIDTH // 2, 1) * sine_part

            for head in range(PER_GROUP):
                begin = group * query_width + head * HEAD_WIDTH
                change = delta_ref[span, begin : begin + HEAD_WIDTH]
                query_tiles.append(rotated(qkv_tile(span, group, head) + change))
            key = rotated(qkv_tile(span, group, PER_GROUP))
            begin = groups * query_width + group * HEAD_WIDTH
            change = delta_ref[span, begin : begin + HEAD_WIDTH]
            value = qkv_tile(span, group, PER_GROUP + 1) + change
            if not last:
                fresh_ref[span, lane_span] = key
                fresh_ref[span, value_span] = value
            key_tiles.append(key)
            value_tiles.append(value)
        queries = jnp.concatenate(query_tiles, axis=0).astype(jnp.bfloat16)
        new_keys = jnp.concatenate(key_tiles, axis=0).astype(jnp.bfloat16)
        new_values = jnp.concatenate(value_tiles, axis=0).astype(jnp.bfloat16)
        old_keys = key_ref[pl.ds(first, BATCH), :, lane_span].reshape(BATCH * cache, HEAD_WIDTH)
        old_scores = lax.dot_general(
            queries, old_keys, transposed, preferred_element_type=jnp.float32
        )
        new_scores = lax.dot_general(
            queries, new_keys, transposed, preferred_element_type=jnp.float32
        )
        return old_scores, new_scores, new_values

    def weighed(first, old_scores, new_scores):
        heads = steps * PER_GROUP
        old_scores = (old_scores * scale).reshape(heads, BATCH, BATCH * cache)
        old_scores = old_scores + bias_ref[pl.ds(first, BATCH), :][None]
        new_scores = (new_scores * scale).reshape(steps, PER_GROUP, BATCH, known * BATCH)
        new_scores = (new_scores + fresh_bias[:, None]).reshape(heads, BATCH, known * BATCH)
        peak = jnp.maximum(
            jnp.max(old_scores, axis=-1, keepdims=True),
            jnp.max(new_scores, axis=-1, keepdims=True),
        )
        old_scores = jnp.exp(old_scores - peak)
        new_scores = jnp.exp(new_scores - peak)
        share = 1.0 / (
            jnp.sum(old_scores, axis=-1, keepdims=True)
            + jnp.sum(new_scores, axis=-1, keepdims=True)
        )
        old_weights = (old_scores * share).reshape(heads * BATCH, BATCH * cache)
        new_weights = (new_scores * share).reshape(heads * BATCH, known * BATCH)
        return old_weights.astype(jnp.bfloat16), new_weights.astype(jnp.bfloat16)

    def batch(index, carry):
        chains = []
        for number in range(TOGETHER):
            first = pl.multiple_of((index * TOGETHER + number) * BATCH, BATCH)
            chains += [(first, group) for group in range(groups)]
        scores = [scored(*chain) for chain in chains]
        weights = [weighed(chain[0], *score[:2]) for chain, score in zip(chains, scores)]
        for (first, group), (old_weights, new_weights), score in zip(chains, weights, scores):
            lane_span = slice(group * HEAD_WIDTH, (group + 1) * HEAD_WIDTH)
            old_values = value_ref[pl.ds(first, BATCH), :, lane_span]
            old_values = old_values.reshape(BATCH * cache, HEAD_WIDTH)
            context = jnp.dot(
                old_weights, old_values, preferred_element_type=jnp.float32
            ) + jnp.dot(new_weights, score[2], preferred_element_type=jnp.float32)
            for step in range(steps):
                span = pl.ds(pl.multiple_of(step * rows + first, BATCH), BATCH)
                for head in range(PER_GROUP):
                    row = (step * PER_GROUP + head) * BATCH
                    begin = group * query_width + head * HEAD_WIDTH
                    context_ref[span, begin : begin + HEAD_WIDTH] = context[row : row + BATCH]
        return carry

    lax.fori_loop(0, rows // (BATCH * TOGETHER), batch, 0)

    flow_places = jnp.concatenate([places_ref[1:2, :]] * steps, axis=1)
    context = context_ref[...].astype(jnp.bfloat16)
    count = message_refs[0].shape[0]
    shape = (count, steps * rows)
    out_row = iota(shape, 0)
    same_step = out_row % steps == iota(shape, 1) // rows
    for number, message_ref in enumerate(message_refs):
        wanted = number * (count // steps) + out_row // steps
        pick = ((flow_places == wanted) & same_step).astype(jnp.float32).astype(jnp.bfloat16)
        message_ref[...] = jnp.dot(
            pick, context, preferred_element_type=jnp.float32
        ).astype(jnp.bfloat16)


def place_kernel(found, lanes, subs, most, *refs):
    chunks = len(found)
    *refs, out_ref = refs
    refs = refs[::-1]
    steps = out_ref.shape[1]
    chunk_steps = steps // chunks
    block = most * chunk_steps
    here = lax.axis_index("streams")
    core = lax.axis_index("sub")
    shape = (chunks * block, chunks * block)
    out_row, in_row = iota(shape, 0), iota(shape, 1)
    step = out_row % steps
    wanted = step // chunk_steps * block + out_row // steps * chunk_steps + step % chunk_steps
    pick = (wanted == in_row).astype(jnp.float32).astype(jnp.bfloat16)
    for number in range(lanes):
        for other in range(subs):
            pieces = []
            for chunk in range(chunks):
                array, begin = found[chunk][number][other]
                pieces.append(refs[array][...][begin : begin + block])
            rows = jnp.dot(
                pick, jnp.concatenate(pieces, axis=0), preferred_element_type=jnp.float32
            )
            source = (here ^ number) * subs + (core ^ other)
            out_ref[pl.ds(source * most, most)] = rows.reshape(
                most, steps, rows.shape[1]
            ).astype(jnp.bfloat16)


def traded(blocks, axes):
    landed = list(blocks)
    count = len(blocks)
    order = sorted(range(1, count), key=lambda shift: -(shift ^ (shift >> 1)))
    for shift in order:
        pairs = [(place, place ^ shift) for place in range(count)]
        landed[shift] = lax.ppermute(blocks[shift], axes, pairs)
    return landed


def from_others(block, axis):
    count = lax.axis_size(axis)
    landed = [block]
    for shift in range(1, count):
        pairs = [(place, place ^ shift) for place in range(count)]
        landed.append(lax.ppermute(block, axis, pairs))
    return landed


def held(value, others):
    return lax.optimization_barrier((value, others))[0]


SMALL = pl.CostEstimate(flops=1, bytes_accessed=1, transcendentals=0)


def on_device(
    inputs,
    input_norm_gain,
    projection_weight,
    projection_bias,
    speaker,
    speaker_adapter_slot,
    cache_fill_length,
    rotated_key_cache,
    value_cache_rows,
    adapter_down_maps,
    adapter_query_up,
    adapter_value_up,
    flow_decoder_owner,
):
    steps, rows, width = inputs.shape
    lanes = lax.axis_size("streams")
    subs = lax.axis_size("sub")
    heads = lax.axis_size("heads")
    flow_lanes = lanes * subs
    local_slots, sliced, _ = adapter_down_maps.shape
    query_columns = adapter_query_up.shape[2]
    value_columns = adapter_value_up.shape[2]
    groups = value_columns // HEAD_WIDTH
    cache = rotated_key_cache.shape[1]
    spots = subs * local_slots * MOST
    chunks = 2
    chunk_steps = steps // chunks
    chunk_rows = chunk_steps * rows
    per_message = chunk_steps * spots
    chip_slots = subs * local_slots
    flow_most = max(2, (2 * rows + flow_lanes - 1) // flow_lanes)
    bf16, f32 = jnp.bfloat16, jnp.float32

    def whole(shape):
        return pl.BlockSpec(shape, lambda i: (0,) * len(shape))

    in_hbm = pl.BlockSpec(memory_space=pltpu.HBM)

    down_maps = from_others(adapter_down_maps, "sub")
    query_maps = from_others(
        adapter_query_up.reshape(local_slots * ADAPTER_RANK, query_columns), "sub"
    )
    value_maps = from_others(
        adapter_value_up.reshape(local_slots * ADAPTER_RANK, value_columns), "sub"
    )

    pieces = 4
    flat = inputs.reshape(steps * rows, width)
    gain = input_norm_gain.reshape(width // 128, 128)
    message = jax.ShapeDtypeStruct((per_message, sliced), bf16)
    places_shape = jax.ShapeDtypeStruct((8, rows), jnp.int32)
    tables = [
        speaker.reshape(1, rows),
        speaker_adapter_slot.reshape(1, -1),
        flow_decoder_owner.reshape(1, rows),
    ]

    def row_buffers(count):
        return (
            [pltpu.VMEM((count, width), bf16), pltpu.VMEM(gain.shape, f32)]
            + [pltpu.VMEM(table.shape, jnp.int32) for table in tables]
            + [pltpu.SemaphoreType.DMA((pieces + 4,))]
        )

    messages = pl.pallas_call(
        functools.partial(norm_pack_kernel, chunk_steps, rows, flow_most, lanes, pieces),
        in_specs=[in_hbm] * 5,
        out_specs=[VMEM] * lanes,
        out_shape=[message] * lanes,
        scratch_shapes=row_buffers(chunk_rows) + [pltpu.VMEM((chunk_rows, width), bf16)],
        compiler_params=pltpu.CompilerParams(vmem_limit_bytes=PACK_LIMIT * MIB),
        cost_estimate=SMALL,
        name="norm_and_pack",
    )(*tables, gain, flat)
    arrived = [traded(messages, "streams")]

    bias = projection_bias.reshape(-1, 128)
    columns = projection_weight.shape[1]
    block_columns = 256 if columns % 256 == 0 else 384
    blocks = columns // block_columns
    cut = blocks // 2

    def weight_buffers(count):
        return [
            pltpu.VMEM((count, width, block_columns), bf16),
            pltpu.SemaphoreType.DMA((count,)),
        ]

    def projected(count):
        return jax.ShapeDtypeStruct((steps * rows, count * block_columns), f32)

    adapters = down_maps[1:], query_maps[1:], value_maps[1:]
    weight_buf, weight_semaphores = weight_buffers(cut)
    normed, first_qkv, places, *messages = pl.pallas_call(
        functools.partial(
            norm_pack_project_kernel, chunk_steps, rows, flow_most, lanes, 2 * pieces, 1
        ),
        in_specs=[in_hbm] * 3 + [VMEM] + [in_hbm] * 3,
        out_specs=[VMEM] * (3 + lanes),
        out_shape=[jax.ShapeDtypeStruct((steps * rows, width), bf16), projected(cut)]
        + [places_shape]
        + [message] * lanes,
        scratch_shapes=row_buffers(steps * rows)[:-1]
        + [pltpu.SemaphoreType.DMA((2 * pieces + 4,))]
        + [weight_buf, weight_semaphores],
        compiler_params=pltpu.CompilerParams(vmem_limit_bytes=PROJECT_LIMIT * MIB),
        cost_estimate=SMALL,
        name="norm_pack_project",
    )(*tables, held(bias, (adapters, messages)), gain, flat, projection_weight)
    arrived.append(traded(messages, "streams"))
    qkv = [first_qkv]

    def project(after):
        return pl.pallas_call(
            functools.partial(project_kernel, cut),
            in_specs=[VMEM, VMEM, in_hbm],
            out_specs=VMEM,
            out_shape=projected(blocks - cut),
            scratch_shapes=weight_buffers(blocks - cut),
            compiler_params=pltpu.CompilerParams(vmem_limit_bytes=PROJECT_LIMIT * MIB),
            cost_estimate=SMALL,
            name="project",
        )(normed, held(bias, after), projection_weight)

    def down(chunk, after):
        partial_latent = pl.pallas_call(
            functools.partial(down_kernel, lanes, spots),
            in_specs=[VMEM] * (lanes + subs),
            out_specs=VMEM,
            out_shape=jax.ShapeDtypeStruct((lanes * per_message, 2 * ADAPTER_RANK), f32),
            compiler_params=pltpu.CompilerParams(vmem_limit_bytes=16 * MIB),
            cost_estimate=SMALL,
            name="down",
        )(*arrived[chunk][:0:-1], held(arrived[chunk][0], after), *down_maps)
        return from_others(partial_latent, "heads")

    def up(partials, after):
        message = jax.ShapeDtypeStruct((per_message, query_columns + value_columns), bf16)
        messages = pl.pallas_call(
            functools.partial(up_kernel, heads, subs, spots),
            in_specs=[VMEM] * (heads + 2 * subs),
            out_specs=[VMEM] * lanes,
            out_shape=[message] * lanes,
            compiler_params=pltpu.CompilerParams(vmem_limit_bytes=24 * MIB),
            cost_estimate=SMALL,
            name="up",
        )(held(partials[0], after), *partials[1:], *query_maps, *value_maps)
        return messages

    half_width = HEAD_WIDTH // 2
    position = jnp.concatenate([cache_fill_length + step for step in range(steps)]).astype(f32)
    freq = jnp.exp(jnp.arange(half_width, dtype=f32) * (-math.log(1000000.0) / half_width))
    freq = jnp.concatenate([freq, freq])
    angle = position[:, None] * freq
    sign = jnp.where(jnp.arange(HEAD_WIDTH) < half_width, -1.0, 1.0).astype(f32)
    cosine = jnp.cos(angle)
    sine_part = jnp.sin(angle) * sign

    returned = []
    after = qkv
    for chunk in range(chunks):
        if chunk:
            qkv.append(project(after))
        partials = down(chunk, qkv)
        after = up(partials, qkv)
        messages = list(after)
        if chunk:
            for lane in range(1, lanes):
                messages[lane] = held(messages[lane], returned[-1][lane])
        returned.append(traded(messages, "streams"))

    length_row = cache_fill_length.reshape(1, rows)
    block = flow_most * chunk_steps
    earlier, along, alongs = [], [], []
    for chunk in range(chunks):
        last = chunk == chunks - 1
        message = jax.ShapeDtypeStruct((subs * block, query_columns), bf16)
        fresh = jax.ShapeDtypeStruct((chunk_rows, 2 * value_columns), f32)
        rows_of = lambda shape: pl.BlockSpec(shape, lambda i, chunk=chunk: (chunk, 0))
        results = pl.pallas_call(
            functools.partial(
                attend_kernel,
                chunk * chunk_steps,
                chunk_steps,
                rows,
                cache,
                groups,
                lanes,
                subs,
                last,
            ),
            grid=(1,),
            in_specs=[whole(places.shape), whole(length_row.shape)]
            + [rows_of((chunk_rows, HEAD_WIDTH))] * 2
            + [whole(rotated_key_cache.shape)] * 2
            + [rows_of((chunk_rows, part.shape[1])) for part in qkv]
            + [whole((per_message, query_columns + value_columns))] * lanes
            + [whole(block_rows.shape) for block_rows in earlier],
            out_specs=[whole(fresh.shape)] * (not last) + [whole(message.shape)] * lanes,
            out_shape=[fresh] * (not last) + [message] * lanes,
            scratch_shapes=[
                pltpu.VMEM((chunk_rows, query_columns + value_columns), f32),
                pltpu.VMEM((chunk_rows, query_columns), f32),
                pltpu.VMEM((rows, BATCH * cache), f32),
            ],
            compiler_params=pltpu.CompilerParams(vmem_limit_bytes=32 * MIB),
            cost_estimate=SMALL,
            name="attend",
        )(
            places if chunk else held(places, after),
            length_row,
            cosine,
            sine_part,
            rotated_key_cache,
            value_cache_rows,
            *qkv,
            *returned[chunk][::-1],
            *earlier,
        )
        if not last:
            earlier, results = [results[0]], results[1:]
        results = list(results)
        for lane in range(1, lanes):
            if not alongs:
                results[lane] = held(results[lane], returned[-1][1:])
        along = traded(results, "streams")
        alongs.append(along)

    landed, found = [], []
    for chunk, along in enumerate(alongs):
        base = len(landed)
        landed += along
        where = [[(base + lane, 0)] for lane in range(lanes)]
        for shift in range(1, subs):
            pairs = [(core, core ^ shift) for core in range(subs)]
            span = slice(shift * block, (shift + 1) * block)
            if chunk < chunks - 1:
                joined = jnp.concatenate([block_rows[span] for block_rows in along[::-1]])
                for lane in range(lanes):
                    where[lane].append((len(landed), (lanes - 1 - lane) * block))
                landed.append(lax.ppermute(joined, "sub", pairs))
            else:
                for lane, block_rows in enumerate(along):
                    where[lane].append((len(landed), shift * block))
                    landed.append(lax.ppermute(block_rows, "sub", pairs))
        found.append(where)

    flow = pl.pallas_call(
        functools.partial(place_kernel, found, lanes, subs, flow_most),
        in_specs=[VMEM] * len(landed),
        out_specs=VMEM,
        out_shape=jax.ShapeDtypeStruct((flow_lanes * flow_most, steps, query_columns), bf16),
        compiler_params=pltpu.CompilerParams(vmem_limit_bytes=24 * MIB),
        cost_estimate=SMALL,
        name="place",
    )(*landed[::-1])
    return flow[None]


def solution(mesh):
    placed = (
        P(None, ("groups", "streams", "sub"), None),
        P(),
        P(None, "heads"),
        P("heads"),
        P(("groups", "streams", "sub"), None),
        P("groups"),
        P(("groups", "streams", "sub")),
        P(("groups", "streams", "sub"), None, "heads"),
        P(("groups", "streams", "sub"), None, "heads"),
        P(("groups", "streams", "sub"), "heads", None),
        P(("groups", "streams", "sub"), None, "heads"),
        P(("groups", "streams", "sub"), None, "heads"),
        P(("groups", "streams", "sub"), None),
    )
    return jax.shard_map(
        on_device,
        mesh=mesh,
        in_specs=placed,
        out_specs=P(("groups", "streams", "sub"), None, None, "heads"),
        check_vma=False,
    )
```

```python
import functools
import math

import jax
import jax.numpy as jnp
from jax import lax
from jax.experimental import pallas as pl
from jax.experimental.pallas import tpu as pltpu
from jax.sharding import PartitionSpec as P

QUERY_HEADS = 28
KEY_VALUE_HEADS = 4
HEAD_WIDTH = 128
ADAPTER_RANK = 64
MOST = 2
PER_GROUP = QUERY_HEADS // KEY_VALUE_HEADS
LANE_AXES = ("streams", "sub")
BATCH = 8
TOGETHER = 2
VMEM = pl.BlockSpec(memory_space=pltpu.VMEM)
MIB = 1 << 20
PACK_LIMIT = 56
PROJECT_LIMIT = 49


def iota(shape, dim):
    return lax.broadcasted_iota(jnp.int32, shape, dim)


def as_column(row):
    count = row.shape[1]
    square = (count, count)
    same = iota(square, 0) == iota(square, 1)
    return jnp.sum(jnp.where(same, jnp.broadcast_to(row, square), 0), axis=1, keepdims=True)


def ranked(labels, most):
    count = labels.shape[1]
    square = (count, count)
    earlier = (as_column(labels) == labels) & (iota(square, 0) < iota(square, 1))
    return labels * most + jnp.sum(earlier.astype(jnp.int32), axis=0, keepdims=True)


def slot_places(speaker, table, lane_base):
    speakers_all = table.shape[1]
    rows = speaker.shape[1]
    match = iota((speakers_all, rows), 0) == speaker
    slots = jnp.sum(jnp.where(match, as_column(table), 0), axis=0, keepdims=True)
    return ranked(slots ^ lane_base, MOST)


def norm_in_pieces(
    pieces, begin, x_hbm, gain_hbm, x_buf, gain_buf, semaphores, normed_ref, started=None
):
    count, width = x_buf.shape
    size = count // pieces
    gain_copy = pltpu.make_async_copy(gain_hbm, gain_buf, semaphores.at[pieces])
    copies = []
    for piece in range(pieces):
        copies.append(
            pltpu.make_async_copy(
                x_hbm.at[pl.ds(begin + piece * size, size)],
                x_buf.at[pl.ds(piece * size, size)],
                semaphores.at[piece],
            )
        )
        copies[-1].start()
        if piece == 0:
            gain_copy.start()
    if started is not None:
        started()
    gain_copy.wait()
    gain = jnp.concatenate([gain_buf[i : i + 1, :] for i in range(gain_buf.shape[0])], axis=1)
    for piece in range(pieces):
        copies[piece].wait()

        def one(index, carry):
            span = pl.ds(pl.multiple_of(piece * size + index * 16, 16), 16)
            values = x_buf[span, :].astype(jnp.float32)
            mean_sq = jnp.sum(values * values, axis=1, keepdims=True) * (1.0 / width)
            normed = values * lax.rsqrt(mean_sq + 1e-06) * gain
            normed_ref[span, :] = normed.astype(jnp.bfloat16)
            return carry

        lax.fori_loop(0, size // 16, one, 0)


def pack_messages(steps, rows, places, normed_ref, message_refs):
    per_message, sliced = message_refs[0].shape
    spots = per_message // steps
    shape = (len(message_refs) * per_message, steps * rows)
    out_row = iota(shape, 0)
    wanted = out_row // per_message * spots + out_row % spots
    out_step = out_row % per_message // spots
    places = jnp.concatenate([places] * steps, axis=1)
    pick = (wanted == places) & (out_step == iota(shape, 1) // rows)
    pick = pick.astype(jnp.float32).astype(jnp.bfloat16)
    begin = pl.multiple_of(lax.axis_index("heads") * sliced, 128)
    own = normed_ref[:, pl.ds(begin, sliced)]
    packed = jnp.dot(pick, own, preferred_element_type=jnp.float32).astype(jnp.bfloat16)
    for number, message_ref in enumerate(message_refs):
        message_ref[...] = packed[number * per_message : (number + 1) * per_message]


def table_copies(table_hbms, table_bufs, semaphores, first):
    copies = [
        pltpu.make_async_copy(source, target, semaphores.at[first + number])
        for number, (source, target) in enumerate(zip(table_hbms, table_bufs))
    ]
    for copy in copies:
        copy.start()
    return copies


def places_from(table_bufs, spots, flow_most):
    speaker, table, owner = [buffer[...] for buffer in table_bufs]
    here, core, subs = lax.axis_index("streams"), lax.axis_index("sub"), lax.axis_size("sub")
    places = slot_places(speaker, table, here * (spots // MOST))
    return places, ranked(owner ^ (here * subs + core), flow_most)


def norm_pack_kernel(steps, rows, flow_most, lanes, pieces, *refs):
    table_hbms, gain_hbm, x_hbm, message_refs = refs[:3], refs[3], refs[4], refs[5 : 5 + lanes]
    x_buf, gain_buf, *table_bufs, semaphores, normed_ref = refs[5 + lanes :]
    copies = table_copies(table_hbms, table_bufs, semaphores, pieces + 1)
    norm_in_pieces(pieces, 0, x_hbm, gain_hbm, x_buf, gain_buf, semaphores, normed_ref)
    for copy in copies:
        copy.wait()
    spots = message_refs[0].shape[0] // steps
    places, _ = places_from(table_bufs, spots, flow_most)
    pack_messages(steps, rows, places, normed_ref, message_refs)


def weight_copies(begin, weight_hbm, weight_buf, semaphores):
    columns = weight_buf.shape[2]
    return [
        pltpu.make_async_copy(
            weight_hbm.at[:, pl.ds((begin + block) * columns, columns)],
            weight_buf.at[block],
            semaphores.at[block],
        )
        for block in range(weight_buf.shape[0])
    ]


def project_blocks(begin, copies, rows_ref, weight_buf, bias_ref, out_ref):
    columns = weight_buf.shape[2]
    tiles = columns // 128
    for block, copy in enumerate(copies):
        first = (begin + block) * tiles
        bias = [bias_ref[tile : tile + 1, :] for tile in range(first, first + tiles)]
        copy.wait()
        product = jnp.dot(rows_ref[...], weight_buf[block], preferred_element_type=jnp.float32)
        out_ref[:, block * columns : (block + 1) * columns] = product + jnp.concatenate(
            bias, axis=1
        )


def norm_pack_project_kernel(steps, rows, flow_most, lanes, pieces, chunk, *refs):
    table_hbms, bias_ref, gain_hbm, x_hbm, weight_hbm = refs[:3], *refs[3:7]
    normed_ref, out_ref, places_ref, message_refs = *refs[7:10], refs[10 : 10 + lanes]
    x_buf, gain_buf, *table_bufs, semaphores, weight_buf, weight_semaphores = refs[10 + lanes :]
    copies = weight_copies(0, weight_hbm, weight_buf, weight_semaphores)
    tables = table_copies(table_hbms, table_bufs, semaphores, pieces + 1)

    def start_weights():
        for copy in copies:
            copy.start()

    norm_in_pieces(
        pieces, 0, x_hbm, gain_hbm, x_buf, gain_buf, semaphores, normed_ref, start_weights
    )
    for copy in tables:
        copy.wait()
    spots = message_refs[0].shape[0] // steps
    places, flow_places = places_from(table_bufs, spots, flow_most)
    places_ref[0:1, :] = places
    places_ref[1:2, :] = flow_places
    count = steps * rows
    own_ref = normed_ref.at[pl.ds(chunk * count, count)]
    pack_messages(steps, rows, places, own_ref, message_refs)
    project_blocks(0, copies, normed_ref, weight_buf, bias_ref, out_ref)


def project_kernel(begin, rows_ref, bias_ref, weight_hbm, out_ref, weight_buf, semaphores):
    copies = weight_copies(begin, weight_hbm, weight_buf, semaphores)
    for copy in copies:
        copy.start()
    project_blocks(begin, copies, rows_ref, weight_buf, bias_ref, out_ref)


def row_slots(shape, spots):
    return iota(shape, 0) % spots // MOST


def down_kernel(lanes, spots, *refs):
    message_refs, map_refs, partial_ref = refs[:lanes][::-1], refs[lanes:-1], refs[-1]
    local_slots = map_refs[0].shape[0]
    rows = jnp.concatenate([ref[...] for ref in message_refs], axis=0)
    own_slot = row_slots(partial_ref.shape, spots)
    total = jnp.zeros(partial_ref.shape, jnp.float32)
    for number, map_ref in enumerate(map_refs):
        shift = (lax.axis_index("sub") ^ number) * local_slots
        for slot in range(local_slots):
            part = jnp.dot(rows, map_ref[slot], preferred_element_type=jnp.float32)
            total = jnp.where(own_slot == shift + slot, part, total)
    partial_ref[...] = total


def up_kernel(heads, subs, spots, *refs):
    partial_refs, refs = refs[:heads], refs[heads:]
    query_refs, value_refs, message_refs = refs[:subs], refs[subs : 2 * subs], refs[2 * subs :]
    total = partial_refs[0][...]
    for ref in partial_refs[1:]:
        total = total + ref[...]
    latent = total.astype(jnp.bfloat16).astype(jnp.float32)
    own_slot = row_slots(latent.shape, spots)
    column = iota(latent.shape, 1) // ADAPTER_RANK
    turned = pltpu.roll(latent, ADAPTER_RANK, 1)
    low = iota(latent.shape, 1) < ADAPTER_RANK
    query_pair = jnp.where(low, latent, turned)
    value_pair = jnp.where(low, turned, latent)

    def product(pair, map_refs):
        result = None
        for number, map_ref in enumerate(map_refs):
            local_slots = map_ref.shape[0] // ADAPTER_RANK
            shift = (lax.axis_index("sub") ^ number) * local_slots
            pieces = []
            for slot in range(0, local_slots, 2):
                kept = jnp.where(own_slot == shift + slot + column, pair, 0.0)
                pieces.append(kept.astype(jnp.bfloat16))
            wide = jnp.concatenate(pieces, axis=1)
            part = jnp.dot(wide, map_ref[...], preferred_element_type=jnp.float32)
            result = part if result is None else result + part
        return result.astype(jnp.bfloat16)

    queries = product(query_pair, query_refs)
    values = product(value_pair, value_refs)
    query_width = queries.shape[1]
    per_message = message_refs[0].shape[0]
    for number, ref in enumerate(message_refs):
        span = slice(number * per_message, (number + 1) * per_message)
        ref[:, :query_width] = queries[span]
        ref[:, query_width:] = values[span]


def attend_kernel(before, steps, rows, cache, groups, lanes, subs, last, *refs):
    places_ref, length_ref, cos_ref, sin_ref, key_ref, value_ref = refs[:6]
    qkv_refs, refs = refs[6:8], refs[8:]
    delta_refs, refs = refs[:lanes][::-1], refs[lanes:]
    if before:
        earlier_ref, refs = refs[0], refs[1:]
    if not last:
        fresh_ref, refs = refs[0], refs[1:]
    message_refs = refs[:lanes]
    delta_ref, context_ref, bias_ref = refs[lanes:]
    per_message = delta_refs[0].shape[0]
    spots = per_message // steps
    query_width = PER_GROUP * HEAD_WIDTH
    known = before + steps

    def qkv_tile(span, group, head):
        begin = (group * (PER_GROUP + 2) + head) * HEAD_WIDTH
        edge = qkv_refs[0].shape[1]
        if begin < edge:
            return qkv_refs[0][span, begin : begin + HEAD_WIDTH]
        return qkv_refs[1][span, begin - edge : begin - edge + HEAD_WIDTH]

    wide = groups * HEAD_WIDTH

    column = as_column(places_ref[0:1, :])
    column = jnp.concatenate([column] * steps, axis=0)
    shape = (steps * rows, lanes * per_message)
    out_row = iota(shape, 1)
    wanted = out_row // per_message * spots + out_row % spots
    pick = (wanted == column) & (out_row % per_message // spots == iota(shape, 0) // rows)
    pick = pick.astype(jnp.float32).astype(jnp.bfloat16)
    delta_ref[...] = jnp.dot(
        pick,
        jnp.concatenate([ref[...] for ref in delta_refs], axis=0),
        preferred_element_type=jnp.float32,
    )

    shape = (rows, BATCH * cache)
    lengths = as_column(length_ref[...])
    slot_column = iota(shape, 1)
    allowed = (slot_column // cache == iota(shape, 0) % BATCH) & (slot_column % cache < lengths)
    bias_ref[...] = jnp.where(allowed, 0.0, -1e30)
    shape = (steps, BATCH, known * BATCH)
    fresh_column = iota(shape, 2)
    allowed = (fresh_column % BATCH == iota(shape, 1)) & (
        fresh_column // BATCH <= iota(shape, 0) + before
    )
    fresh_bias = jnp.where(allowed, 0.0, -1e30)
    scale = HEAD_WIDTH ** (-0.5)
    transposed = (((1,), (1,)), ((), ()))

    def scored(first, group):
        spans = [pl.ds(pl.multiple_of(step * rows + first, BATCH), BATCH) for step in range(known)]
        query_tiles, key_tiles, value_tiles = [], [], []
        lane_span = slice(group * HEAD_WIDTH, (group + 1) * HEAD_WIDTH)
        value_span = slice(wide + group * HEAD_WIDTH, wide + (group + 1) * HEAD_WIDTH)
        for span in spans[:before]:
            key_tiles.append(earlier_ref[span, lane_span])
            value_tiles.append(earlier_ref[span, value_span])
        for span in spans[:steps]:
            cosine, sine_part = cos_ref[span, :], sin_ref[span, :]

            def rotated(values):
                return values * cosine + pltpu.roll(values, HEAD_WIDTH // 2, 1) * sine_part

            for head in range(PER_GROUP):
                begin = group * query_width + head * HEAD_WIDTH
                change = delta_ref[span, begin : begin + HEAD_WIDTH]
                query_tiles.append(rotated(qkv_tile(span, group, head) + change))
            key = rotated(qkv_tile(span, group, PER_GROUP))
            begin = groups * query_width + group * HEAD_WIDTH
            change = delta_ref[span, begin : begin + HEAD_WIDTH]
            value = qkv_tile(span, group, PER_GROUP + 1) + change
            if not last:
                fresh_ref[span, lane_span] = key
                fresh_ref[span, value_span] = value
            key_tiles.append(key)
            value_tiles.append(value)
        queries = jnp.concatenate(query_tiles, axis=0).astype(jnp.bfloat16)
        new_keys = jnp.concatenate(key_tiles, axis=0).astype(jnp.bfloat16)
        new_values = jnp.concatenate(value_tiles, axis=0).astype(jnp.bfloat16)
        old_keys = key_ref[pl.ds(first, BATCH), :, lane_span].reshape(BATCH * cache, HEAD_WIDTH)
        old_scores = lax.dot_general(
            queries, old_keys, transposed, preferred_element_type=jnp.float32
        )
        new_scores = lax.dot_general(
            queries, new_keys, transposed, preferred_element_type=jnp.float32
        )
        return old_scores, new_scores, new_values

    def weighed(first, old_scores, new_scores):
        heads = steps * PER_GROUP
        old_scores = (old_scores * scale).reshape(heads, BATCH, BATCH * cache)
        old_scores = old_scores + bias_ref[pl.ds(first, BATCH), :][None]
        new_scores = (new_scores * scale).reshape(steps, PER_GROUP, BATCH, known * BATCH)
        new_scores = (new_scores + fresh_bias[:, None]).reshape(heads, BATCH, known * BATCH)
        peak = jnp.maximum(
            jnp.max(old_scores, axis=-1, keepdims=True),
            jnp.max(new_scores, axis=-1, keepdims=True),
        )
        old_scores = jnp.exp(old_scores - peak)
        new_scores = jnp.exp(new_scores - peak)
        share = 1.0 / (
            jnp.sum(old_scores, axis=-1, keepdims=True)
            + jnp.sum(new_scores, axis=-1, keepdims=True)
        )
        old_weights = (old_scores * share).reshape(heads * BATCH, BATCH * cache)
        new_weights = (new_scores * share).reshape(heads * BATCH, known * BATCH)
        return old_weights.astype(jnp.bfloat16), new_weights.astype(jnp.bfloat16)

    def batch(index, carry):
        chains = []
        for number in range(TOGETHER):
            first = pl.multiple_of((index * TOGETHER + number) * BATCH, BATCH)
            chains += [(first, group) for group in range(groups)]
        scores = [scored(*chain) for chain in chains]
        weights = [weighed(chain[0], *score[:2]) for chain, score in zip(chains, scores)]
        for (first, group), (old_weights, new_weights), score in zip(chains, weights, scores):
            lane_span = slice(group * HEAD_WIDTH, (group + 1) * HEAD_WIDTH)
            old_values = value_ref[pl.ds(first, BATCH), :, lane_span]
            old_values = old_values.reshape(BATCH * cache, HEAD_WIDTH)
            context = jnp.dot(
                old_weights, old_values, preferred_element_type=jnp.float32
            ) + jnp.dot(new_weights, score[2], preferred_element_type=jnp.float32)
            for step in range(steps):
                span = pl.ds(pl.multiple_of(step * rows + first, BATCH), BATCH)
                for head in range(PER_GROUP):
                    row = (step * PER_GROUP + head) * BATCH
                    begin = group * query_width + head * HEAD_WIDTH
                    context_ref[span, begin : begin + HEAD_WIDTH] = context[row : row + BATCH]
        return carry

    lax.fori_loop(0, rows // (BATCH * TOGETHER), batch, 0)

    flow_places = jnp.concatenate([places_ref[1:2, :]] * steps, axis=1)
    context = context_ref[...].astype(jnp.bfloat16)
    count = message_refs[0].shape[0]
    shape = (count, steps * rows)
    out_row = iota(shape, 0)
    same_step = out_row % steps == iota(shape, 1) // rows
    for number, message_ref in enumerate(message_refs):
        wanted = number * (count // steps) + out_row // steps
        pick = ((flow_places == wanted) & same_step).astype(jnp.float32).astype(jnp.bfloat16)
        message_ref[...] = jnp.dot(
            pick, context, preferred_element_type=jnp.float32
        ).astype(jnp.bfloat16)


def place_kernel(found, lanes, subs, most, *refs):
    chunks = len(found)
    *refs, out_ref = refs
    refs = refs[::-1]
    steps = out_ref.shape[1]
    chunk_steps = steps // chunks
    block = most * chunk_steps
    here = lax.axis_index("streams")
    core = lax.axis_index("sub")
    shape = (chunks * block, chunks * block)
    out_row, in_row = iota(shape, 0), iota(shape, 1)
    step = out_row % steps
    wanted = step // chunk_steps * block + out_row // steps * chunk_steps + step % chunk_steps
    pick = (wanted == in_row).astype(jnp.float32).astype(jnp.bfloat16)
    for number in range(lanes):
        for other in range(subs):
            pieces = []
            for chunk in range(chunks):
                array, begin = found[chunk][number][other]
                pieces.append(refs[array][...][begin : begin + block])
            rows = jnp.dot(
                pick, jnp.concatenate(pieces, axis=0), preferred_element_type=jnp.float32
            )
            source = (here ^ number) * subs + (core ^ other)
            out_ref[pl.ds(source * most, most)] = rows.reshape(
                most, steps, rows.shape[1]
            ).astype(jnp.bfloat16)


def traded(blocks, axes):
    landed = list(blocks)
    count = len(blocks)
    order = sorted(range(1, count), key=lambda shift: -(shift ^ (shift >> 1)))
    for shift in order:
        pairs = [(place, place ^ shift) for place in range(count)]
        landed[shift] = lax.ppermute(blocks[shift], axes, pairs)
    return landed


def from_others(block, axis):
    count = lax.axis_size(axis)
    landed = [block]
    for shift in range(1, count):
        pairs = [(place, place ^ shift) for place in range(count)]
        landed.append(lax.ppermute(block, axis, pairs))
    return landed


def held(value, others):
    return lax.optimization_barrier((value, others))[0]


SMALL = pl.CostEstimate(flops=1, bytes_accessed=1, transcendentals=0)


def on_device(
    inputs,
    input_norm_gain,
    projection_weight,
    projection_bias,
    speaker,
    speaker_adapter_slot,
    cache_fill_length,
    rotated_key_cache,
    value_cache_rows,
    adapter_down_maps,
    adapter_query_up,
    adapter_value_up,
    flow_decoder_owner,
):
    steps, rows, width = inputs.shape
    lanes = lax.axis_size("streams")
    subs = lax.axis_size("sub")
    heads = lax.axis_size("heads")
    flow_lanes = lanes * subs
    local_slots, sliced, _ = adapter_down_maps.shape
    query_columns = adapter_query_up.shape[2]
    value_columns = adapter_value_up.shape[2]
    groups = value_columns // HEAD_WIDTH
    cache = rotated_key_cache.shape[1]
    spots = subs * local_slots * MOST
    chunks = 2
    chunk_steps = steps // chunks
    chunk_rows = chunk_steps * rows
    per_message = chunk_steps * spots
    chip_slots = subs * local_slots
    flow_most = max(2, (2 * rows + flow_lanes - 1) // flow_lanes)
    bf16, f32 = jnp.bfloat16, jnp.float32

    def whole(shape):
        return pl.BlockSpec(shape, lambda i: (0,) * len(shape))

    in_hbm = pl.BlockSpec(memory_space=pltpu.HBM)

    down_maps = from_others(adapter_down_maps, "sub")
    query_maps = from_others(
        adapter_query_up.reshape(local_slots * ADAPTER_RANK, query_columns), "sub"
    )
    value_maps = from_others(
        adapter_value_up.reshape(local_slots * ADAPTER_RANK, value_columns), "sub"
    )

    pieces = 4
    flat = inputs.reshape(steps * rows, width)
    gain = input_norm_gain.reshape(width // 128, 128)
    message = jax.ShapeDtypeStruct((per_message, sliced), bf16)
    places_shape = jax.ShapeDtypeStruct((8, rows), jnp.int32)
    tables = [
        speaker.reshape(1, rows),
        speaker_adapter_slot.reshape(1, -1),
        flow_decoder_owner.reshape(1, rows),
    ]

    def row_buffers(count):
        return (
            [pltpu.VMEM((count, width), bf16), pltpu.VMEM(gain.shape, f32)]
            + [pltpu.VMEM(table.shape, jnp.int32) for table in tables]
            + [pltpu.SemaphoreType.DMA((pieces + 4,))]
        )

    messages = pl.pallas_call(
        functools.partial(norm_pack_kernel, chunk_steps, rows, flow_most, lanes, pieces),
        in_specs=[in_hbm] * 5,
        out_specs=[VMEM] * lanes,
        out_shape=[message] * lanes,
        scratch_shapes=row_buffers(chunk_rows) + [pltpu.VMEM((chunk_rows, width), bf16)],
        compiler_params=pltpu.CompilerParams(vmem_limit_bytes=PACK_LIMIT * MIB),
        cost_estimate=SMALL,
        name="norm_and_pack",
    )(*tables, gain, flat)
    arrived = [traded(messages, "streams")]

    bias = projection_bias.reshape(-1, 128)
    columns = projection_weight.shape[1]
    block_columns = 256 if columns % 256 == 0 else 384
    blocks = columns // block_columns
    cut = blocks // 2

    def weight_buffers(count):
        return [
            pltpu.VMEM((count, width, block_columns), bf16),
            pltpu.SemaphoreType.DMA((count,)),
        ]

    def projected(count):
        return jax.ShapeDtypeStruct((steps * rows, count * block_columns), f32)

    adapters = down_maps[1:], query_maps[1:], value_maps[1:]
    weight_buf, weight_semaphores = weight_buffers(cut)
    normed, first_qkv, places, *messages = pl.pallas_call(
        functools.partial(
            norm_pack_project_kernel, chunk_steps, rows, flow_most, lanes, 2 * pieces, 1
        ),
        in_specs=[in_hbm] * 3 + [VMEM] + [in_hbm] * 3,
        out_specs=[VMEM] * (3 + lanes),
        out_shape=[jax.ShapeDtypeStruct((steps * rows, width), bf16), projected(cut)]
        + [places_shape]
        + [message] * lanes,
        scratch_shapes=row_buffers(steps * rows)[:-1]
        + [pltpu.SemaphoreType.DMA((2 * pieces + 4,))]
        + [weight_buf, weight_semaphores],
        compiler_params=pltpu.CompilerParams(vmem_limit_bytes=PROJECT_LIMIT * MIB),
        cost_estimate=SMALL,
        name="norm_pack_project",
    )(*tables, held(bias, (adapters, messages)), gain, flat, projection_weight)
    arrived.append(traded(messages, "streams"))
    qkv = [first_qkv]

    def project(after):
        return pl.pallas_call(
            functools.partial(project_kernel, cut),
            in_specs=[VMEM, VMEM, in_hbm],
            out_specs=VMEM,
            out_shape=projected(blocks - cut),
            scratch_shapes=weight_buffers(blocks - cut),
            compiler_params=pltpu.CompilerParams(vmem_limit_bytes=PROJECT_LIMIT * MIB),
            cost_estimate=SMALL,
            name="project",
        )(normed, held(bias, after), projection_weight)

    def down(chunk, after):
        partial_latent = pl.pallas_call(
            functools.partial(down_kernel, lanes, spots),
            in_specs=[VMEM] * (lanes + subs),
            out_specs=VMEM,
            out_shape=jax.ShapeDtypeStruct((lanes * per_message, 2 * ADAPTER_RANK), f32),
            compiler_params=pltpu.CompilerParams(vmem_limit_bytes=16 * MIB),
            cost_estimate=SMALL,
            name="down",
        )(*arrived[chunk][:0:-1], held(arrived[chunk][0], after), *down_maps)
        return from_others(partial_latent, "heads")

    def up(partials, after):
        message = jax.ShapeDtypeStruct((per_message, query_columns + value_columns), bf16)
        messages = pl.pallas_call(
            functools.partial(up_kernel, heads, subs, spots),
            in_specs=[VMEM] * (heads + 2 * subs),
            out_specs=[VMEM] * lanes,
            out_shape=[message] * lanes,
            compiler_params=pltpu.CompilerParams(vmem_limit_bytes=24 * MIB),
            cost_estimate=SMALL,
            name="up",
        )(held(partials[0], after), *partials[1:], *query_maps, *value_maps)
        return messages

    half_width = HEAD_WIDTH // 2
    position = jnp.concatenate([cache_fill_length + step for step in range(steps)]).astype(f32)
    freq = jnp.exp(jnp.arange(half_width, dtype=f32) * (-math.log(1000000.0) / half_width))
    freq = jnp.concatenate([freq, freq])
    angle = position[:, None] * freq
    sign = jnp.where(jnp.arange(HEAD_WIDTH) < half_width, -1.0, 1.0).astype(f32)
    cosine = jnp.cos(angle)
    sine_part = jnp.sin(angle) * sign

    returned = []
    after = qkv
    for chunk in range(chunks):
        partials = down(chunk, after)
        after = up(partials, qkv)
        messages = list(after)
        if chunk:
            for lane in range(1, lanes):
                messages[lane] = held(messages[lane], returned[-1][lane])
        returned.append(traded(messages, "streams"))

    qkv.append(project(after))
    length_row = cache_fill_length.reshape(1, rows)
    block = flow_most * chunk_steps
    earlier, along, alongs = [], [], []
    for chunk in range(chunks):
        last = chunk == chunks - 1
        message = jax.ShapeDtypeStruct((subs * block, query_columns), bf16)
        fresh = jax.ShapeDtypeStruct((chunk_rows, 2 * value_columns), f32)
        rows_of = lambda shape: pl.BlockSpec(shape, lambda i, chunk=chunk: (chunk, 0))
        results = pl.pallas_call(
            functools.partial(
                attend_kernel,
                chunk * chunk_steps,
                chunk_steps,
                rows,
                cache,
                groups,
                lanes,
                subs,
                last,
            ),
            grid=(1,),
            in_specs=[whole(places.shape), whole(length_row.shape)]
            + [rows_of((chunk_rows, HEAD_WIDTH))] * 2
            + [whole(rotated_key_cache.shape)] * 2
            + [rows_of((chunk_rows, part.shape[1])) for part in qkv]
            + [whole((per_message, query_columns + value_columns))] * lanes
            + [whole(block_rows.shape) for block_rows in earlier],
            out_specs=[whole(fresh.shape)] * (not last) + [whole(message.shape)] * lanes,
            out_shape=[fresh] * (not last) + [message] * lanes,
            scratch_shapes=[
                pltpu.VMEM((chunk_rows, query_columns + value_columns), f32),
                pltpu.VMEM((chunk_rows, query_columns), f32),
                pltpu.VMEM((rows, BATCH * cache), f32),
            ],
            compiler_params=pltpu.CompilerParams(vmem_limit_bytes=32 * MIB),
            cost_estimate=SMALL,
            name="attend",
        )(
            places if chunk else held(places, after),
            length_row,
            cosine,
            sine_part,
            rotated_key_cache,
            value_cache_rows,
            *qkv,
            *returned[chunk][::-1],
            *earlier,
        )
        if not last:
            earlier, results = [results[0]], results[1:]
        results = list(results)
        for lane in range(1, lanes):
            if not alongs:
                results[lane] = held(results[lane], returned[-1][1:])
        along = traded(results, "streams")
        alongs.append(along)

    landed, found = [], []
    for chunk, along in enumerate(alongs):
        base = len(landed)
        landed += along
        where = [[(base + lane, 0)] for lane in range(lanes)]
        for shift in range(1, subs):
            pairs = [(core, core ^ shift) for core in range(subs)]
            span = slice(shift * block, (shift + 1) * block)
            if chunk < chunks - 1:
                joined = jnp.concatenate([block_rows[span] for block_rows in along[::-1]])
                for lane in range(lanes):
                    where[lane].append((len(landed), (lanes - 1 - lane) * block))
                landed.append(lax.ppermute(joined, "sub", pairs))
            else:
                for lane, block_rows in enumerate(along):
                    where[lane].append((len(landed), shift * block))
                    landed.append(lax.ppermute(block_rows, "sub", pairs))
        found.append(where)

    flow = pl.pallas_call(
        functools.partial(place_kernel, found, lanes, subs, flow_most),
        in_specs=[VMEM] * len(landed),
        out_specs=VMEM,
        out_shape=jax.ShapeDtypeStruct((flow_lanes * flow_most, steps, query_columns), bf16),
        compiler_params=pltpu.CompilerParams(vmem_limit_bytes=24 * MIB),
        cost_estimate=SMALL,
        name="place",
    )(*landed[::-1])
    return flow[None]


def solution(mesh):
    placed = (
        P(None, ("groups", "streams", "sub"), None),
        P(),
        P(None, "heads"),
        P("heads"),
        P(("groups", "streams", "sub"), None),
        P("groups"),
        P(("groups", "streams", "sub")),
        P(("groups", "streams", "sub"), None, "heads"),
        P(("groups", "streams", "sub"), None, "heads"),
        P(("groups", "streams", "sub"), "heads", None),
        P(("groups", "streams", "sub"), None, "heads"),
        P(("groups", "streams", "sub"), None, "heads"),
        P(("groups", "streams", "sub"), None),
    )
    return jax.shard_map(
        on_device,
        mesh=mesh,
        in_specs=placed,
        out_specs=P(("groups", "streams", "sub"), None, None, "heads"),
        check_vma=False,
    )
```

```python
import functools
import math

import jax
import jax.numpy as jnp
from jax import lax
from jax.experimental import pallas as pl
from jax.experimental.pallas import tpu as pltpu
from jax.sharding import PartitionSpec as P

QUERY_HEADS = 28
KEY_VALUE_HEADS = 4
HEAD_WIDTH = 128
ADAPTER_RANK = 64
MOST = 2
PER_GROUP = QUERY_HEADS // KEY_VALUE_HEADS
LANE_AXES = ("streams", "sub")
BATCH = 8
TOGETHER = 2
VMEM = pl.BlockSpec(memory_space=pltpu.VMEM)
MIB = 1 << 20
PACK_LIMIT = 56
PROJECT_LIMIT = 49


def iota(shape, dim):
    return lax.broadcasted_iota(jnp.int32, shape, dim)


def as_column(row):
    count = row.shape[1]
    square = (count, count)
    same = iota(square, 0) == iota(square, 1)
    return jnp.sum(jnp.where(same, jnp.broadcast_to(row, square), 0), axis=1, keepdims=True)


def ranked(labels, most):
    count = labels.shape[1]
    square = (count, count)
    earlier = (as_column(labels) == labels) & (iota(square, 0) < iota(square, 1))
    return labels * most + jnp.sum(earlier.astype(jnp.int32), axis=0, keepdims=True)


def slot_places(speaker, table, lane_base):
    speakers_all = table.shape[1]
    rows = speaker.shape[1]
    match = iota((speakers_all, rows), 0) == speaker
    slots = jnp.sum(jnp.where(match, as_column(table), 0), axis=0, keepdims=True)
    return ranked(slots ^ lane_base, MOST)


def norm_in_pieces(
    pieces, begin, x_hbm, gain_hbm, x_buf, gain_buf, semaphores, normed_ref, started=None
):
    count, width = x_buf.shape
    size = count // pieces
    gain_copy = pltpu.make_async_copy(gain_hbm, gain_buf, semaphores.at[pieces])
    copies = []
    for piece in range(pieces):
        copies.append(
            pltpu.make_async_copy(
                x_hbm.at[pl.ds(begin + piece * size, size)],
                x_buf.at[pl.ds(piece * size, size)],
                semaphores.at[piece],
            )
        )
        copies[-1].start()
        if piece == 0:
            gain_copy.start()
    if started is not None:
        started()
    gain_copy.wait()
    gain = jnp.concatenate([gain_buf[i : i + 1, :] for i in range(gain_buf.shape[0])], axis=1)
    for piece in range(pieces):
        copies[piece].wait()

        def one(index, carry):
            span = pl.ds(pl.multiple_of(piece * size + index * 16, 16), 16)
            values = x_buf[span, :].astype(jnp.float32)
            mean_sq = jnp.sum(values * values, axis=1, keepdims=True) * (1.0 / width)
            normed = values * lax.rsqrt(mean_sq + 1e-06) * gain
            normed_ref[span, :] = normed.astype(jnp.bfloat16)
            return carry

        lax.fori_loop(0, size // 16, one, 0)


def pack_messages(steps, rows, places, normed_ref, message_refs):
    per_message, sliced = message_refs[0].shape
    spots = per_message // steps
    shape = (len(message_refs) * per_message, steps * rows)
    out_row = iota(shape, 0)
    wanted = out_row // per_message * spots + out_row % spots
    out_step = out_row % per_message // spots
    places = jnp.concatenate([places] * steps, axis=1)
    pick = (wanted == places) & (out_step == iota(shape, 1) // rows)
    pick = pick.astype(jnp.float32).astype(jnp.bfloat16)
    begin = pl.multiple_of(lax.axis_index("heads") * sliced, 128)
    own = normed_ref[:, pl.ds(begin, sliced)]
    packed = jnp.dot(pick, own, preferred_element_type=jnp.float32).astype(jnp.bfloat16)
    for number, message_ref in enumerate(message_refs):
        message_ref[...] = packed[number * per_message : (number + 1) * per_message]


def table_copies(table_hbms, table_bufs, semaphores, first):
    copies = [
        pltpu.make_async_copy(source, target, semaphores.at[first + number])
        for number, (source, target) in enumerate(zip(table_hbms, table_bufs))
    ]
    for copy in copies:
        copy.start()
    return copies


def places_from(table_bufs, spots, flow_most):
    speaker, table, owner = [buffer[...] for buffer in table_bufs]
    here, core, subs = lax.axis_index("streams"), lax.axis_index("sub"), lax.axis_size("sub")
    places = slot_places(speaker, table, here * (spots // MOST))
    return places, ranked(owner ^ (here * subs + core), flow_most)


def norm_pack_kernel(steps, rows, flow_most, lanes, pieces, *refs):
    table_hbms, gain_hbm, x_hbm, message_refs = refs[:3], refs[3], refs[4], refs[5 : 5 + lanes]
    x_buf, gain_buf, *table_bufs, semaphores, normed_ref = refs[5 + lanes :]
    copies = table_copies(table_hbms, table_bufs, semaphores, pieces + 1)
    norm_in_pieces(pieces, 0, x_hbm, gain_hbm, x_buf, gain_buf, semaphores, normed_ref)
    for copy in copies:
        copy.wait()
    spots = message_refs[0].shape[0] // steps
    places, _ = places_from(table_bufs, spots, flow_most)
    pack_messages(steps, rows, places, normed_ref, message_refs)


def weight_copies(begin, weight_hbm, weight_buf, semaphores):
    columns = weight_buf.shape[2]
    return [
        pltpu.make_async_copy(
            weight_hbm.at[:, pl.ds((begin + block) * columns, columns)],
            weight_buf.at[block],
            semaphores.at[block],
        )
        for block in range(weight_buf.shape[0])
    ]


def project_blocks(begin, copies, rows_ref, weight_buf, bias_ref, out_ref):
    columns = weight_buf.shape[2]
    tiles = columns // 128
    for block, copy in enumerate(copies):
        first = (begin + block) * tiles
        bias = [bias_ref[tile : tile + 1, :] for tile in range(first, first + tiles)]
        copy.wait()
        product = jnp.dot(rows_ref[...], weight_buf[block], preferred_element_type=jnp.float32)
        out_ref[:, block * columns : (block + 1) * columns] = product + jnp.concatenate(
            bias, axis=1
        )


def norm_pack_project_kernel(steps, rows, flow_most, lanes, pieces, chunk, *refs):
    table_hbms, bias_ref, gain_hbm, x_hbm, weight_hbm = refs[:3], *refs[3:7]
    normed_ref, out_ref, places_ref, message_refs = *refs[7:10], refs[10 : 10 + lanes]
    x_buf, gain_buf, *table_bufs, semaphores, weight_buf, weight_semaphores = refs[10 + lanes :]
    copies = weight_copies(0, weight_hbm, weight_buf, weight_semaphores)
    tables = table_copies(table_hbms, table_bufs, semaphores, pieces + 1)

    def start_weights():
        for copy in copies:
            copy.start()

    norm_in_pieces(
        pieces, 0, x_hbm, gain_hbm, x_buf, gain_buf, semaphores, normed_ref, start_weights
    )
    for copy in tables:
        copy.wait()
    spots = message_refs[0].shape[0] // steps
    places, flow_places = places_from(table_bufs, spots, flow_most)
    places_ref[0:1, :] = places
    places_ref[1:2, :] = flow_places
    count = steps * rows
    own_ref = normed_ref.at[pl.ds(chunk * count, count)]
    pack_messages(steps, rows, places, own_ref, message_refs)
    project_blocks(0, copies, normed_ref, weight_buf, bias_ref, out_ref)


def project_kernel(begin, rows_ref, bias_ref, weight_hbm, out_ref, weight_buf, semaphores):
    copies = weight_copies(begin, weight_hbm, weight_buf, semaphores)
    for copy in copies:
        copy.start()
    project_blocks(begin, copies, rows_ref, weight_buf, bias_ref, out_ref)


def row_slots(shape, spots):
    return iota(shape, 0) % spots // MOST


def down_kernel(lanes, spots, *refs):
    message_refs, map_refs, partial_ref = refs[:lanes][::-1], refs[lanes:-1], refs[-1]
    local_slots = map_refs[0].shape[0]
    rows = jnp.concatenate([ref[...] for ref in message_refs], axis=0)
    own_slot = row_slots(partial_ref.shape, spots)
    total = jnp.zeros(partial_ref.shape, jnp.float32)
    for number, map_ref in enumerate(map_refs):
        shift = (lax.axis_index("sub") ^ number) * local_slots
        for slot in range(local_slots):
            part = jnp.dot(rows, map_ref[slot], preferred_element_type=jnp.float32)
            total = jnp.where(own_slot == shift + slot, part, total)
    partial_ref[...] = total


def up_kernel(heads, subs, spots, *refs):
    partial_refs, refs = refs[:heads], refs[heads:]
    query_refs, value_refs, message_refs = refs[:subs], refs[subs : 2 * subs], refs[2 * subs :]
    total = partial_refs[0][...]
    for ref in partial_refs[1:]:
        total = total + ref[...]
    latent = total.astype(jnp.bfloat16).astype(jnp.float32)
    own_slot = row_slots(latent.shape, spots)
    column = iota(latent.shape, 1) // ADAPTER_RANK
    turned = pltpu.roll(latent, ADAPTER_RANK, 1)
    low = iota(latent.shape, 1) < ADAPTER_RANK
    query_pair = jnp.where(low, latent, turned)
    value_pair = jnp.where(low, turned, latent)

    def product(pair, map_refs):
        result = None
        for number, map_ref in enumerate(map_refs):
            local_slots = map_ref.shape[0] // ADAPTER_RANK
            shift = (lax.axis_index("sub") ^ number) * local_slots
            pieces = []
            for slot in range(0, local_slots, 2):
                kept = jnp.where(own_slot == shift + slot + column, pair, 0.0)
                pieces.append(kept.astype(jnp.bfloat16))
            wide = jnp.concatenate(pieces, axis=1)
            part = jnp.dot(wide, map_ref[...], preferred_element_type=jnp.float32)
            result = part if result is None else result + part
        return result.astype(jnp.bfloat16)

    queries = product(query_pair, query_refs)
    values = product(value_pair, value_refs)
    query_width = queries.shape[1]
    per_message = message_refs[0].shape[0]
    for number, ref in enumerate(message_refs):
        span = slice(number * per_message, (number + 1) * per_message)
        ref[:, :query_width] = queries[span]
        ref[:, query_width:] = values[span]


def attend_kernel(before, steps, rows, cache, groups, lanes, subs, last, *refs):
    places_ref, length_ref, cos_ref, sin_ref, key_ref, value_ref = refs[:6]
    qkv_refs, refs = refs[6:9], refs[9:]
    delta_refs, refs = refs[:lanes][::-1], refs[lanes:]
    if before:
        earlier_ref, refs = refs[0], refs[1:]
    if not last:
        fresh_ref, refs = refs[0], refs[1:]
    message_refs = refs[:lanes]
    delta_ref, context_ref, bias_ref = refs[lanes:]
    per_message = delta_refs[0].shape[0]
    spots = per_message // steps
    query_width = PER_GROUP * HEAD_WIDTH
    known = before + steps

    def qkv_tile(span, group, head):
        begin = (group * (PER_GROUP + 2) + head) * HEAD_WIDTH
        for ref in qkv_refs:
            if begin < ref.shape[1]:
                return ref[span, begin : begin + HEAD_WIDTH]
            begin -= ref.shape[1]

    wide = groups * HEAD_WIDTH
    column = as_column(places_ref[0:1, :])
    column = jnp.concatenate([column] * steps, axis=0)
    shape = (steps * rows, lanes * per_message)
    out_row = iota(shape, 1)
    wanted = out_row // per_message * spots + out_row % spots
    pick = (wanted == column) & (out_row % per_message // spots == iota(shape, 0) // rows)
    pick = pick.astype(jnp.float32).astype(jnp.bfloat16)
    delta_ref[...] = jnp.dot(
        pick,
        jnp.concatenate([ref[...] for ref in delta_refs], axis=0),
        preferred_element_type=jnp.float32,
    )

    shape = (rows, BATCH * cache)
    lengths = as_column(length_ref[...])
    slot_column = iota(shape, 1)
    allowed = (slot_column // cache == iota(shape, 0) % BATCH) & (slot_column % cache < lengths)
    bias_ref[...] = jnp.where(allowed, 0.0, -1e30)
    shape = (steps, BATCH, known * BATCH)
    fresh_column = iota(shape, 2)
    allowed = (fresh_column % BATCH == iota(shape, 1)) & (
        fresh_column // BATCH <= iota(shape, 0) + before
    )
    fresh_bias = jnp.where(allowed, 0.0, -1e30)
    scale = HEAD_WIDTH ** (-0.5)
    transposed = (((1,), (1,)), ((), ()))

    def scored(first, group):
        spans = [pl.ds(pl.multiple_of(step * rows + first, BATCH), BATCH) for step in range(known)]
        query_tiles, key_tiles, value_tiles = [], [], []
        lane_span = slice(group * HEAD_WIDTH, (group + 1) * HEAD_WIDTH)
        value_span = slice(wide + group * HEAD_WIDTH, wide + (group + 1) * HEAD_WIDTH)
        for span in spans[:before]:
            key_tiles.append(earlier_ref[span, lane_span])
            value_tiles.append(earlier_ref[span, value_span])
        for span in spans[:steps]:
            cosine, sine_part = cos_ref[span, :], sin_ref[span, :]

            def rotated(values):
                return values * cosine + pltpu.roll(values, HEAD_WIDTH // 2, 1) * sine_part

            for head in range(PER_GROUP):
                begin = group * query_width + head * HEAD_WIDTH
                change = delta_ref[span, begin : begin + HEAD_WIDTH]
                query_tiles.append(rotated(qkv_tile(span, group, head) + change))
            key = rotated(qkv_tile(span, group, PER_GROUP))
            begin = groups * query_width + group * HEAD_WIDTH
            change = delta_ref[span, begin : begin + HEAD_WIDTH]
            value = qkv_tile(span, group, PER_GROUP + 1) + change
            if not last:
                fresh_ref[span, lane_span] = key
                fresh_ref[span, value_span] = value
            key_tiles.append(key)
            value_tiles.append(value)
        queries = jnp.concatenate(query_tiles, axis=0).astype(jnp.bfloat16)
        new_keys = jnp.concatenate(key_tiles, axis=0).astype(jnp.bfloat16)
        new_values = jnp.concatenate(value_tiles, axis=0).astype(jnp.bfloat16)
        old_keys = key_ref[pl.ds(first, BATCH), :, lane_span].reshape(BATCH * cache, HEAD_WIDTH)
        old_scores = lax.dot_general(
            queries, old_keys, transposed, preferred_element_type=jnp.float32
        )
        new_scores = lax.dot_general(
            queries, new_keys, transposed, preferred_element_type=jnp.float32
        )
        return old_scores, new_scores, new_values

    def weighed(first, old_scores, new_scores):
        heads = steps * PER_GROUP
        old_scores = (old_scores * scale).reshape(heads, BATCH, BATCH * cache)
        old_scores = old_scores + bias_ref[pl.ds(first, BATCH), :][None]
        new_scores = (new_scores * scale).reshape(steps, PER_GROUP, BATCH, known * BATCH)
        new_scores = (new_scores + fresh_bias[:, None]).reshape(heads, BATCH, known * BATCH)
        peak = jnp.maximum(
            jnp.max(old_scores, axis=-1, keepdims=True),
            jnp.max(new_scores, axis=-1, keepdims=True),
        )
        old_scores = jnp.exp(old_scores - peak)
        new_scores = jnp.exp(new_scores - peak)
        share = 1.0 / (
            jnp.sum(old_scores, axis=-1, keepdims=True)
            + jnp.sum(new_scores, axis=-1, keepdims=True)
        )
        old_weights = (old_scores * share).reshape(heads * BATCH, BATCH * cache)
        new_weights = (new_scores * share).reshape(heads * BATCH, known * BATCH)
        return old_weights.astype(jnp.bfloat16), new_weights.astype(jnp.bfloat16)

    def batch(index, carry):
        chains = []
        for number in range(TOGETHER):
            first = pl.multiple_of((index * TOGETHER + number) * BATCH, BATCH)
            chains += [(first, group) for group in range(groups)]
        scores = [scored(*chain) for chain in chains]
        weights = [weighed(chain[0], *score[:2]) for chain, score in zip(chains, scores)]
        for (first, group), (old_weights, new_weights), score in zip(chains, weights, scores):
            lane_span = slice(group * HEAD_WIDTH, (group + 1) * HEAD_WIDTH)
            old_values = value_ref[pl.ds(first, BATCH), :, lane_span]
            old_values = old_values.reshape(BATCH * cache, HEAD_WIDTH)
            context = jnp.dot(
                old_weights, old_values, preferred_element_type=jnp.float32
            ) + jnp.dot(new_weights, score[2], preferred_element_type=jnp.float32)
            for step in range(steps):
                span = pl.ds(pl.multiple_of(step * rows + first, BATCH), BATCH)
                for head in range(PER_GROUP):
                    row = (step * PER_GROUP + head) * BATCH
                    begin = group * query_width + head * HEAD_WIDTH
                    context_ref[span, begin : begin + HEAD_WIDTH] = context[row : row + BATCH]
        return carry

    lax.fori_loop(0, rows // (BATCH * TOGETHER), batch, 0)

    flow_places = jnp.concatenate([places_ref[1:2, :]] * steps, axis=1)
    context = context_ref[...].astype(jnp.bfloat16)
    count = message_refs[0].shape[0]
    shape = (count, steps * rows)
    out_row = iota(shape, 0)
    same_step = out_row % steps == iota(shape, 1) // rows
    for number, message_ref in enumerate(message_refs):
        wanted = number * (count // steps) + out_row // steps
        pick = ((flow_places == wanted) & same_step).astype(jnp.float32).astype(jnp.bfloat16)
        message_ref[...] = jnp.dot(
            pick, context, preferred_element_type=jnp.float32
        ).astype(jnp.bfloat16)


def place_kernel(found, lanes, subs, most, *refs):
    chunks = len(found)
    out_ref = refs[-1]
    steps = out_ref.shape[1]
    chunk_steps = steps // chunks
    block = most * chunk_steps
    here = lax.axis_index("streams")
    core = lax.axis_index("sub")
    shape = (chunks * block, chunks * block)
    out_row, in_row = iota(shape, 0), iota(shape, 1)
    step = out_row % steps
    wanted = step // chunk_steps * block + out_row // steps * chunk_steps + step % chunk_steps
    pick = (wanted == in_row).astype(jnp.float32).astype(jnp.bfloat16)
    for number in range(lanes):
        for other in range(subs):
            pieces = []
            for chunk in range(chunks):
                array, begin = found[chunk][number][other]
                pieces.append(refs[array][...][begin : begin + block])
            rows = jnp.dot(
                pick, jnp.concatenate(pieces, axis=0), preferred_element_type=jnp.float32
            )
            source = (here ^ number) * subs + (core ^ other)
            out_ref[pl.ds(source * most, most)] = rows.reshape(
                most, steps, rows.shape[1]
            ).astype(jnp.bfloat16)


def traded(blocks, axes):
    landed = list(blocks)
    count = len(blocks)
    order = sorted(range(1, count), key=lambda shift: -(shift ^ (shift >> 1)))
    for shift in order:
        pairs = [(place, place ^ shift) for place in range(count)]
        landed[shift] = lax.ppermute(blocks[shift], axes, pairs)
    return landed


def from_others(block, axis):
    count = lax.axis_size(axis)
    landed = [block]
    for shift in range(1, count):
        pairs = [(place, place ^ shift) for place in range(count)]
        landed.append(lax.ppermute(block, axis, pairs))
    return landed


def held(value, others):
    return lax.optimization_barrier((value, others))[0]


SMALL = pl.CostEstimate(flops=1, bytes_accessed=1, transcendentals=0)


def on_device(
    inputs,
    input_norm_gain,
    projection_weight,
    projection_bias,
    speaker,
    speaker_adapter_slot,
    cache_fill_length,
    rotated_key_cache,
    value_cache_rows,
    adapter_down_maps,
    adapter_query_up,
    adapter_value_up,
    flow_decoder_owner,
):
    steps, rows, width = inputs.shape
    lanes = lax.axis_size("streams")
    subs = lax.axis_size("sub")
    heads = lax.axis_size("heads")
    flow_lanes = lanes * subs
    local_slots, sliced, _ = adapter_down_maps.shape
    query_columns = adapter_query_up.shape[2]
    value_columns = adapter_value_up.shape[2]
    groups = value_columns // HEAD_WIDTH
    cache = rotated_key_cache.shape[1]
    spots = subs * local_slots * MOST
    chunks = 2
    chunk_steps = steps // chunks
    chunk_rows = chunk_steps * rows
    per_message = chunk_steps * spots
    chip_slots = subs * local_slots
    flow_most = max(2, (2 * rows + flow_lanes - 1) // flow_lanes)
    bf16, f32 = jnp.bfloat16, jnp.float32

    def whole(shape):
        return pl.BlockSpec(shape, lambda i: (0,) * len(shape))

    in_hbm = pl.BlockSpec(memory_space=pltpu.HBM)

    down_maps = from_others(adapter_down_maps, "sub")
    query_maps = from_others(
        adapter_query_up.reshape(local_slots * ADAPTER_RANK, query_columns), "sub"
    )
    value_maps = from_others(
        adapter_value_up.reshape(local_slots * ADAPTER_RANK, value_columns), "sub"
    )

    pieces = 4
    flat = inputs.reshape(steps * rows, width)
    gain = input_norm_gain.reshape(width // 128, 128)
    message = jax.ShapeDtypeStruct((per_message, sliced), bf16)
    places_shape = jax.ShapeDtypeStruct((8, rows), jnp.int32)
    tables = [
        speaker.reshape(1, rows),
        speaker_adapter_slot.reshape(1, -1),
        flow_decoder_owner.reshape(1, rows),
    ]

    def row_buffers(count):
        return (
            [pltpu.VMEM((count, width), bf16), pltpu.VMEM(gain.shape, f32)]
            + [pltpu.VMEM(table.shape, jnp.int32) for table in tables]
            + [pltpu.SemaphoreType.DMA((pieces + 4,))]
        )

    messages = pl.pallas_call(
        functools.partial(norm_pack_kernel, chunk_steps, rows, flow_most, lanes, pieces),
        in_specs=[in_hbm] * 5,
        out_specs=[VMEM] * lanes,
        out_shape=[message] * lanes,
        scratch_shapes=row_buffers(chunk_rows) + [pltpu.VMEM((chunk_rows, width), bf16)],
        compiler_params=pltpu.CompilerParams(vmem_limit_bytes=PACK_LIMIT * MIB),
        cost_estimate=SMALL,
        name="norm_and_pack",
    )(*tables, gain, flat)
    arrived = [traded(messages, "streams")]

    bias = projection_bias.reshape(-1, 128)
    columns = projection_weight.shape[1]
    block_columns = 256 if columns % 256 == 0 else 384
    blocks = columns // block_columns
    cuts = [4, 6, 9] if blocks == 9 else [blocks // 3, 2 * blocks // 3, blocks]
    cut = cuts[0]

    def weight_buffers(count):
        return [
            pltpu.VMEM((count, width, block_columns), bf16),
            pltpu.SemaphoreType.DMA((count,)),
        ]

    def projected(count):
        return jax.ShapeDtypeStruct((steps * rows, count * block_columns), f32)

    adapters = down_maps[1:], query_maps[1:], value_maps[1:]
    weight_buf, weight_semaphores = weight_buffers(cut)
    normed, first_qkv, places, *messages = pl.pallas_call(
        functools.partial(
            norm_pack_project_kernel, chunk_steps, rows, flow_most, lanes, 2 * pieces, 1
        ),
        in_specs=[in_hbm] * 3 + [VMEM] + [in_hbm] * 3,
        out_specs=[VMEM] * (3 + lanes),
        out_shape=[jax.ShapeDtypeStruct((steps * rows, width), bf16), projected(cut)]
        + [places_shape]
        + [message] * lanes,
        scratch_shapes=row_buffers(steps * rows)[:-1]
        + [pltpu.SemaphoreType.DMA((2 * pieces + 4,))]
        + [weight_buf, weight_semaphores],
        compiler_params=pltpu.CompilerParams(vmem_limit_bytes=PROJECT_LIMIT * MIB),
        cost_estimate=SMALL,
        name="norm_pack_project",
    )(*tables, held(bias, (adapters, messages)), gain, flat, projection_weight)
    arrived.append(traded(messages, "streams"))
    qkv = [first_qkv]

    def project(after):
        begin, end = cuts[len(qkv) - 1 : len(qkv) + 1]
        return pl.pallas_call(
            functools.partial(project_kernel, begin),
            in_specs=[VMEM, VMEM, in_hbm],
            out_specs=VMEM,
            out_shape=projected(end - begin),
            scratch_shapes=weight_buffers(end - begin),
            compiler_params=pltpu.CompilerParams(vmem_limit_bytes=PROJECT_LIMIT * MIB),
            cost_estimate=SMALL,
            name="project",
        )(normed, held(bias, after), projection_weight)

    def down(chunk, after):
        partial_latent = pl.pallas_call(
            functools.partial(down_kernel, lanes, spots),
            in_specs=[VMEM] * (lanes + subs),
            out_specs=VMEM,
            out_shape=jax.ShapeDtypeStruct((lanes * per_message, 2 * ADAPTER_RANK), f32),
            compiler_params=pltpu.CompilerParams(vmem_limit_bytes=16 * MIB),
            cost_estimate=SMALL,
            name="down",
        )(*arrived[chunk][:0:-1], held(arrived[chunk][0], after), *down_maps)
        return from_others(partial_latent, "heads")

    def up(partials, after):
        message = jax.ShapeDtypeStruct((per_message, query_columns + value_columns), bf16)
        messages = pl.pallas_call(
            functools.partial(up_kernel, heads, subs, spots),
            in_specs=[VMEM] * (heads + 2 * subs),
            out_specs=[VMEM] * lanes,
            out_shape=[message] * lanes,
            compiler_params=pltpu.CompilerParams(vmem_limit_bytes=24 * MIB),
            cost_estimate=SMALL,
            name="up",
        )(held(partials[0], after), *partials[1:], *query_maps, *value_maps)
        return messages

    half_width = HEAD_WIDTH // 2
    position = jnp.concatenate([cache_fill_length + step for step in range(steps)]).astype(f32)
    freq = jnp.exp(jnp.arange(half_width, dtype=f32) * (-math.log(1000000.0) / half_width))
    freq = jnp.concatenate([freq, freq])
    angle = position[:, None] * freq
    sign = jnp.where(jnp.arange(HEAD_WIDTH) < half_width, -1.0, 1.0).astype(f32)
    cosine = jnp.cos(angle)
    sine_part = jnp.sin(angle) * sign

    returned = []
    after = qkv
    for chunk in range(chunks):
        if chunk:
            qkv.append(project(after))
        partials = down(chunk, qkv)
        if chunk:
            qkv.append(project(partials[0]))
        after = up(partials, qkv)
        messages = list(after)
        if chunk:
            for lane in range(1, lanes):
                messages[lane] = held(messages[lane], returned[-1][lane])
        returned.append(traded(messages, "streams"))

    length_row = cache_fill_length.reshape(1, rows)
    block = flow_most * chunk_steps
    earlier, along, alongs = [], [], []
    for chunk in range(chunks):
        last = chunk == chunks - 1
        message = jax.ShapeDtypeStruct((subs * block, query_columns), bf16)
        fresh = jax.ShapeDtypeStruct((chunk_rows, 2 * value_columns), f32)
        rows_of = lambda shape: pl.BlockSpec(shape, lambda i, chunk=chunk: (chunk, 0))
        results = pl.pallas_call(
            functools.partial(
                attend_kernel,
                chunk * chunk_steps,
                chunk_steps,
                rows,
                cache,
                groups,
                lanes,
                subs,
                last,
            ),
            grid=(1,),
            in_specs=[whole(places.shape), whole(length_row.shape)]
            + [rows_of((chunk_rows, HEAD_WIDTH))] * 2
            + [whole(rotated_key_cache.shape)] * 2
            + [rows_of((chunk_rows, part.shape[1])) for part in qkv]
            + [whole((per_message, query_columns + value_columns))] * lanes
            + [whole(block_rows.shape) for block_rows in earlier],
            out_specs=[whole(fresh.shape)] * (not last) + [whole(message.shape)] * lanes,
            out_shape=[fresh] * (not last) + [message] * lanes,
            scratch_shapes=[
                pltpu.VMEM((chunk_rows, query_columns + value_columns), f32),
                pltpu.VMEM((chunk_rows, query_columns), f32),
                pltpu.VMEM((rows, BATCH * cache), f32),
            ],
            compiler_params=pltpu.CompilerParams(vmem_limit_bytes=32 * MIB),
            cost_estimate=SMALL,
            name="attend",
        )(
            places if chunk else held(places, after),
            length_row,
            cosine,
            sine_part,
            rotated_key_cache,
            value_cache_rows,
            *qkv,
            *returned[chunk][::-1],
            *earlier,
        )
        if not last:
            earlier, results = [results[0]], results[1:]
        results = list(results)
        for lane in range(1, lanes):
            if not alongs:
                results[lane] = held(results[lane], returned[-1][1:])
        along = traded(results, "streams")
        alongs.append(along)

    landed, found = [], []
    for chunk, along in enumerate(alongs):
        base = len(landed)
        landed += along
        where = [[(base + lane, 0)] for lane in range(lanes)]
        for shift in range(1, subs):
            pairs = [(core, core ^ shift) for core in range(subs)]
            span = slice(shift * block, (shift + 1) * block)
            if chunk < chunks - 1:
                joined = jnp.concatenate([block_rows[span] for block_rows in along])
                for lane in range(lanes):
                    where[lane].append((len(landed), lane * block))
                landed.append(lax.ppermute(joined, "sub", pairs))
            else:
                for lane, block_rows in enumerate(along):
                    where[lane].append((len(landed), shift * block))
                    landed.append(lax.ppermute(block_rows, "sub", pairs))
        found.append(where)

    flow = pl.pallas_call(
        functools.partial(place_kernel, found, lanes, subs, flow_most),
        in_specs=[VMEM] * len(landed),
        out_specs=VMEM,
        out_shape=jax.ShapeDtypeStruct((flow_lanes * flow_most, steps, query_columns), bf16),
        compiler_params=pltpu.CompilerParams(vmem_limit_bytes=24 * MIB),
        cost_estimate=SMALL,
        name="place",
    )(*landed)
    return flow[None]


def solution(mesh):
    placed = (
        P(None, ("groups", "streams", "sub"), None),
        P(),
        P(None, "heads"),
        P("heads"),
        P(("groups", "streams", "sub"), None),
        P("groups"),
        P(("groups", "streams", "sub")),
        P(("groups", "streams", "sub"), None, "heads"),
        P(("groups", "streams", "sub"), None, "heads"),
        P(("groups", "streams", "sub"), "heads", None),
        P(("groups", "streams", "sub"), None, "heads"),
        P(("groups", "streams", "sub"), None, "heads"),
        P(("groups", "streams", "sub"), None),
    )
    return jax.shard_map(
        on_device,
        mesh=mesh,
        in_specs=placed,
        out_specs=P(("groups", "streams", "sub"), None, None, "heads"),
        check_vma=False,
    )
```

```python
import functools
import math

import jax
import jax.numpy as jnp
from jax import lax
from jax.experimental import pallas as pl
from jax.experimental.pallas import tpu as pltpu
from jax.sharding import PartitionSpec as P

QUERY_HEADS = 28
KEY_VALUE_HEADS = 4
HEAD_WIDTH = 128
ADAPTER_RANK = 64
MOST = 2
PER_GROUP = QUERY_HEADS // KEY_VALUE_HEADS
LANE_AXES = ("streams", "sub")
BATCH = 8
TOGETHER = 2
VMEM = pl.BlockSpec(memory_space=pltpu.VMEM)
MIB = 1 << 20
PACK_LIMIT = 56
PROJECT_LIMIT = 49


def iota(shape, dim):
    return lax.broadcasted_iota(jnp.int32, shape, dim)


def as_column(row):
    count = row.shape[1]
    square = (count, count)
    same = iota(square, 0) == iota(square, 1)
    return jnp.sum(jnp.where(same, jnp.broadcast_to(row, square), 0), axis=1, keepdims=True)


def ranked(labels, most):
    count = labels.shape[1]
    square = (count, count)
    earlier = (as_column(labels) == labels) & (iota(square, 0) < iota(square, 1))
    return labels * most + jnp.sum(earlier.astype(jnp.int32), axis=0, keepdims=True)


def slot_places(speaker, table, lane_base):
    speakers_all = table.shape[1]
    rows = speaker.shape[1]
    match = iota((speakers_all, rows), 0) == speaker
    slots = jnp.sum(jnp.where(match, as_column(table), 0), axis=0, keepdims=True)
    return ranked(slots ^ lane_base, MOST)


def norm_in_pieces(
    pieces, begin, x_hbm, gain_hbm, x_buf, gain_buf, semaphores, normed_ref, started=None
):
    count, width = x_buf.shape
    size = count // pieces
    gain_copy = pltpu.make_async_copy(gain_hbm, gain_buf, semaphores.at[pieces])
    copies = []
    for piece in range(pieces):
        copies.append(
            pltpu.make_async_copy(
                x_hbm.at[pl.ds(begin + piece * size, size)],
                x_buf.at[pl.ds(piece * size, size)],
                semaphores.at[piece],
            )
        )
        copies[-1].start()
        if piece == 0:
            gain_copy.start()
    if started is not None:
        started()
    gain_copy.wait()
    gain = jnp.concatenate([gain_buf[i : i + 1, :] for i in range(gain_buf.shape[0])], axis=1)
    for piece in range(pieces):
        copies[piece].wait()

        def one(index, carry):
            span = pl.ds(pl.multiple_of(piece * size + index * 16, 16), 16)
            values = x_buf[span, :].astype(jnp.float32)
            mean_sq = jnp.sum(values * values, axis=1, keepdims=True) * (1.0 / width)
            normed = values * lax.rsqrt(mean_sq + 1e-06) * gain
            normed_ref[span, :] = normed.astype(jnp.bfloat16)
            return carry

        lax.fori_loop(0, size // 16, one, 0)


def pack_messages(steps, rows, places, normed_ref, message_refs):
    per_message, sliced = message_refs[0].shape
    spots = per_message // steps
    shape = (len(message_refs) * per_message, steps * rows)
    out_row = iota(shape, 0)
    wanted = out_row // per_message * spots + out_row % spots
    out_step = out_row % per_message // spots
    places = jnp.concatenate([places] * steps, axis=1)
    pick = (wanted == places) & (out_step == iota(shape, 1) // rows)
    pick = pick.astype(jnp.float32).astype(jnp.bfloat16)
    begin = pl.multiple_of(lax.axis_index("heads") * sliced, 128)
    own = normed_ref[:, pl.ds(begin, sliced)]
    packed = jnp.dot(pick, own, preferred_element_type=jnp.float32).astype(jnp.bfloat16)
    for number, message_ref in enumerate(message_refs):
        message_ref[...] = packed[number * per_message : (number + 1) * per_message]


def table_copies(table_hbms, table_bufs, semaphores, first):
    copies = [
        pltpu.make_async_copy(source, target, semaphores.at[first + number])
        for number, (source, target) in enumerate(zip(table_hbms, table_bufs))
    ]
    for copy in copies:
        copy.start()
    return copies


def places_from(table_bufs, spots, flow_most):
    speaker, table, owner = [buffer[...] for buffer in table_bufs]
    here, core, subs = lax.axis_index("streams"), lax.axis_index("sub"), lax.axis_size("sub")
    places = slot_places(speaker, table, here * (spots // MOST))
    return places, ranked(owner ^ (here * subs + core), flow_most)


def norm_pack_kernel(steps, rows, flow_most, lanes, pieces, *refs):
    table_hbms, gain_hbm, x_hbm, message_refs = refs[:3], refs[3], refs[4], refs[5 : 5 + lanes]
    x_buf, gain_buf, *table_bufs, semaphores, normed_ref = refs[5 + lanes :]
    copies = table_copies(table_hbms, table_bufs, semaphores, pieces + 1)
    norm_in_pieces(pieces, 0, x_hbm, gain_hbm, x_buf, gain_buf, semaphores, normed_ref)
    for copy in copies:
        copy.wait()
    spots = message_refs[0].shape[0] // steps
    places, _ = places_from(table_bufs, spots, flow_most)
    pack_messages(steps, rows, places, normed_ref, message_refs)


def weight_copies(begin, weight_hbm, weight_buf, semaphores):
    columns = weight_buf.shape[2]
    return [
        pltpu.make_async_copy(
            weight_hbm.at[:, pl.ds((begin + block) * columns, columns)],
            weight_buf.at[block],
            semaphores.at[block],
        )
        for block in range(weight_buf.shape[0])
    ]


def project_blocks(begin, copies, rows_ref, weight_buf, bias_ref, out_ref):
    columns = weight_buf.shape[2]
    tiles = columns // 128
    for block, copy in enumerate(copies):
        first = (begin + block) * tiles
        bias = [bias_ref[tile : tile + 1, :] for tile in range(first, first + tiles)]
        copy.wait()
        product = jnp.dot(rows_ref[...], weight_buf[block], preferred_element_type=jnp.float32)
        out_ref[:, block * columns : (block + 1) * columns] = product + jnp.concatenate(
            bias, axis=1
        )


def norm_pack_project_kernel(steps, rows, flow_most, lanes, pieces, chunk, *refs):
    table_hbms, bias_ref, gain_hbm, x_hbm, weight_hbm = refs[:3], *refs[3:7]
    normed_ref, out_ref, places_ref, message_refs = *refs[7:10], refs[10 : 10 + lanes]
    x_buf, gain_buf, *table_bufs, semaphores, weight_buf, weight_semaphores = refs[10 + lanes :]
    copies = weight_copies(0, weight_hbm, weight_buf, weight_semaphores)
    tables = table_copies(table_hbms, table_bufs, semaphores, pieces + 1)

    def start_weights():
        for copy in copies:
            copy.start()

    norm_in_pieces(
        pieces, 0, x_hbm, gain_hbm, x_buf, gain_buf, semaphores, normed_ref, start_weights
    )
    for copy in tables:
        copy.wait()
    spots = message_refs[0].shape[0] // steps
    places, flow_places = places_from(table_bufs, spots, flow_most)
    places_ref[0:1, :] = places
    places_ref[1:2, :] = flow_places
    count = steps * rows
    own_ref = normed_ref.at[pl.ds(chunk * count, count)]
    pack_messages(steps, rows, places, own_ref, message_refs)
    project_blocks(0, copies, normed_ref, weight_buf, bias_ref, out_ref)


def project_kernel(begin, rows_ref, bias_ref, weight_hbm, out_ref, weight_buf, semaphores):
    copies = weight_copies(begin, weight_hbm, weight_buf, semaphores)
    for copy in copies:
        copy.start()
    project_blocks(begin, copies, rows_ref, weight_buf, bias_ref, out_ref)


def row_slots(shape, spots):
    return iota(shape, 0) % spots // MOST


def down_kernel(lanes, spots, *refs):
    message_refs, map_refs, partial_ref = refs[:lanes][::-1], refs[lanes:-1], refs[-1]
    local_slots = map_refs[0].shape[0]
    rows = jnp.concatenate([ref[...] for ref in message_refs], axis=0)
    own_slot = row_slots(partial_ref.shape, spots)
    total = jnp.zeros(partial_ref.shape, jnp.float32)
    for number, map_ref in enumerate(map_refs):
        shift = (lax.axis_index("sub") ^ number) * local_slots
        for slot in range(local_slots):
            part = jnp.dot(rows, map_ref[slot], preferred_element_type=jnp.float32)
            total = jnp.where(own_slot == shift + slot, part, total)
    partial_ref[...] = total


def up_kernel(heads, subs, spots, *refs):
    partial_refs, refs = refs[:heads], refs[heads:]
    query_refs, value_refs, message_refs = refs[:subs], refs[subs : 2 * subs], refs[2 * subs :]
    total = partial_refs[0][...]
    for ref in partial_refs[1:]:
        total = total + ref[...]
    latent = total.astype(jnp.bfloat16).astype(jnp.float32)
    own_slot = row_slots(latent.shape, spots)
    column = iota(latent.shape, 1) // ADAPTER_RANK
    turned = pltpu.roll(latent, ADAPTER_RANK, 1)
    low = iota(latent.shape, 1) < ADAPTER_RANK
    query_pair = jnp.where(low, latent, turned)
    value_pair = jnp.where(low, turned, latent)

    def product(pair, map_refs):
        result = None
        for number, map_ref in enumerate(map_refs):
            local_slots = map_ref.shape[0] // ADAPTER_RANK
            shift = (lax.axis_index("sub") ^ number) * local_slots
            pieces = []
            for slot in range(0, local_slots, 2):
                kept = jnp.where(own_slot == shift + slot + column, pair, 0.0)
                pieces.append(kept.astype(jnp.bfloat16))
            wide = jnp.concatenate(pieces, axis=1)
            part = jnp.dot(wide, map_ref[...], preferred_element_type=jnp.float32)
            result = part if result is None else result + part
        return result.astype(jnp.bfloat16)

    queries = product(query_pair, query_refs)
    values = product(value_pair, value_refs)
    query_width = queries.shape[1]
    per_message = message_refs[0].shape[0]
    for number, ref in enumerate(message_refs):
        span = slice(number * per_message, (number + 1) * per_message)
        ref[:, :query_width] = queries[span]
        ref[:, query_width:] = values[span]


def attend_kernel(before, steps, rows, cache, groups, lanes, subs, last, *refs):
    places_ref, length_ref, cos_ref, sin_ref, key_ref, value_ref = refs[:6]
    qkv_refs, refs = refs[6:9], refs[9:]
    delta_refs, refs = refs[:lanes][::-1], refs[lanes:]
    if before:
        earlier_ref, refs = refs[0], refs[1:]
    if not last:
        fresh_ref, refs = refs[0], refs[1:]
    message_refs = refs[:lanes]
    delta_ref, context_ref, bias_ref = refs[lanes:]
    per_message = delta_refs[0].shape[0]
    spots = per_message // steps
    query_width = PER_GROUP * HEAD_WIDTH
    known = before + steps

    def qkv_tile(span, group, head):
        begin = (group * (PER_GROUP + 2) + head) * HEAD_WIDTH
        for ref in qkv_refs:
            if begin < ref.shape[1]:
                return ref[span, begin : begin + HEAD_WIDTH]
            begin -= ref.shape[1]

    wide = groups * HEAD_WIDTH
    column = as_column(places_ref[0:1, :])
    column = jnp.concatenate([column] * steps, axis=0)
    shape = (steps * rows, lanes * per_message)
    out_row = iota(shape, 1)
    wanted = out_row // per_message * spots + out_row % spots
    pick = (wanted == column) & (out_row % per_message // spots == iota(shape, 0) // rows)
    pick = pick.astype(jnp.float32).astype(jnp.bfloat16)
    delta_ref[...] = jnp.dot(
        pick,
        jnp.concatenate([ref[...] for ref in delta_refs], axis=0),
        preferred_element_type=jnp.float32,
    )

    shape = (rows, BATCH * cache)
    lengths = as_column(length_ref[...])
    slot_column = iota(shape, 1)
    allowed = (slot_column // cache == iota(shape, 0) % BATCH) & (slot_column % cache < lengths)
    bias_ref[...] = jnp.where(allowed, 0.0, -1e30)
    shape = (steps, BATCH, known * BATCH)
    fresh_column = iota(shape, 2)
    allowed = (fresh_column % BATCH == iota(shape, 1)) & (
        fresh_column // BATCH <= iota(shape, 0) + before
    )
    fresh_bias = jnp.where(allowed, 0.0, -1e30)
    scale = HEAD_WIDTH ** (-0.5)
    transposed = (((1,), (1,)), ((), ()))

    def scored(first, group):
        spans = [pl.ds(pl.multiple_of(step * rows + first, BATCH), BATCH) for step in range(known)]
        query_tiles, key_tiles, value_tiles = [], [], []
        lane_span = slice(group * HEAD_WIDTH, (group + 1) * HEAD_WIDTH)
        value_span = slice(wide + group * HEAD_WIDTH, wide + (group + 1) * HEAD_WIDTH)
        for span in spans[:before]:
            key_tiles.append(earlier_ref[span, lane_span])
            value_tiles.append(earlier_ref[span, value_span])
        for span in spans[:steps]:
            cosine, sine_part = cos_ref[span, :], sin_ref[span, :]

            def rotated(values):
                return values * cosine + pltpu.roll(values, HEAD_WIDTH // 2, 1) * sine_part

            for head in range(PER_GROUP):
                begin = group * query_width + head * HEAD_WIDTH
                change = delta_ref[span, begin : begin + HEAD_WIDTH]
                query_tiles.append(rotated(qkv_tile(span, group, head) + change))
            key = rotated(qkv_tile(span, group, PER_GROUP))
            begin = groups * query_width + group * HEAD_WIDTH
            change = delta_ref[span, begin : begin + HEAD_WIDTH]
            value = qkv_tile(span, group, PER_GROUP + 1) + change
            if not last:
                fresh_ref[span, lane_span] = key
                fresh_ref[span, value_span] = value
            key_tiles.append(key)
            value_tiles.append(value)
        queries = jnp.concatenate(query_tiles, axis=0).astype(jnp.bfloat16)
        new_keys = jnp.concatenate(key_tiles, axis=0).astype(jnp.bfloat16)
        new_values = jnp.concatenate(value_tiles, axis=0).astype(jnp.bfloat16)
        old_keys = key_ref[pl.ds(first, BATCH), :, lane_span].reshape(BATCH * cache, HEAD_WIDTH)
        old_scores = lax.dot_general(
            queries, old_keys, transposed, preferred_element_type=jnp.float32
        )
        new_scores = lax.dot_general(
            queries, new_keys, transposed, preferred_element_type=jnp.float32
        )
        return old_scores, new_scores, new_values

    def weighed(first, old_scores, new_scores):
        heads = steps * PER_GROUP
        old_scores = (old_scores * scale).reshape(heads, BATCH, BATCH * cache)
        old_scores = old_scores + bias_ref[pl.ds(first, BATCH), :][None]
        new_scores = (new_scores * scale).reshape(steps, PER_GROUP, BATCH, known * BATCH)
        new_scores = (new_scores + fresh_bias[:, None]).reshape(heads, BATCH, known * BATCH)
        peak = jnp.maximum(
            jnp.max(old_scores, axis=-1, keepdims=True),
            jnp.max(new_scores, axis=-1, keepdims=True),
        )
        old_scores = jnp.exp(old_scores - peak)
        new_scores = jnp.exp(new_scores - peak)
        share = 1.0 / (
            jnp.sum(old_scores, axis=-1, keepdims=True)
            + jnp.sum(new_scores, axis=-1, keepdims=True)
        )
        old_weights = (old_scores * share).reshape(heads * BATCH, BATCH * cache)
        new_weights = (new_scores * share).reshape(heads * BATCH, known * BATCH)
        return old_weights.astype(jnp.bfloat16), new_weights.astype(jnp.bfloat16)

    def batch(index, carry):
        chains = []
        for number in range(TOGETHER):
            first = pl.multiple_of((index * TOGETHER + number) * BATCH, BATCH)
            chains += [(first, group) for group in range(groups)]
        scores = [scored(*chain) for chain in chains]
        weights = [weighed(chain[0], *score[:2]) for chain, score in zip(chains, scores)]
        for (first, group), (old_weights, new_weights), score in zip(chains, weights, scores):
            lane_span = slice(group * HEAD_WIDTH, (group + 1) * HEAD_WIDTH)
            old_values = value_ref[pl.ds(first, BATCH), :, lane_span]
            old_values = old_values.reshape(BATCH * cache, HEAD_WIDTH)
            context = jnp.dot(
                old_weights, old_values, preferred_element_type=jnp.float32
            ) + jnp.dot(new_weights, score[2], preferred_element_type=jnp.float32)
            for step in range(steps):
                span = pl.ds(pl.multiple_of(step * rows + first, BATCH), BATCH)
                for head in range(PER_GROUP):
                    row = (step * PER_GROUP + head) * BATCH
                    begin = group * query_width + head * HEAD_WIDTH
                    context_ref[span, begin : begin + HEAD_WIDTH] = context[row : row + BATCH]
        return carry

    lax.fori_loop(0, rows // (BATCH * TOGETHER), batch, 0)

    flow_places = jnp.concatenate([places_ref[1:2, :]] * steps, axis=1)
    context = context_ref[...].astype(jnp.bfloat16)
    count = message_refs[0].shape[0]
    shape = (count, steps * rows)
    out_row = iota(shape, 0)
    same_step = out_row % steps == iota(shape, 1) // rows
    for number, message_ref in enumerate(message_refs):
        wanted = number * (count // steps) + out_row // steps
        pick = ((flow_places == wanted) & same_step).astype(jnp.float32).astype(jnp.bfloat16)
        message_ref[...] = jnp.dot(
            pick, context, preferred_element_type=jnp.float32
        ).astype(jnp.bfloat16)


def place_kernel(found, lanes, subs, most, *refs):
    chunks = len(found)
    out_ref = refs[-1]
    steps = out_ref.shape[1]
    chunk_steps = steps // chunks
    block = most * chunk_steps
    here = lax.axis_index("streams")
    core = lax.axis_index("sub")
    shape = (chunks * block, chunks * block)
    out_row, in_row = iota(shape, 0), iota(shape, 1)
    step = out_row % steps
    wanted = step // chunk_steps * block + out_row // steps * chunk_steps + step % chunk_steps
    pick = (wanted == in_row).astype(jnp.float32).astype(jnp.bfloat16)
    for number in range(lanes):
        for other in range(subs):
            pieces = []
            for chunk in range(chunks):
                array, begin = found[chunk][number][other]
                pieces.append(refs[array][...][begin : begin + block])
            rows = jnp.dot(
                pick, jnp.concatenate(pieces, axis=0), preferred_element_type=jnp.float32
            )
            source = (here ^ number) * subs + (core ^ other)
            out_ref[pl.ds(source * most, most)] = rows.reshape(
                most, steps, rows.shape[1]
            ).astype(jnp.bfloat16)


def traded(blocks, axes):
    landed = list(blocks)
    count = len(blocks)
    order = sorted(range(1, count), key=lambda shift: -(shift ^ (shift >> 1)))
    for shift in order:
        pairs = [(place, place ^ shift) for place in range(count)]
        landed[shift] = lax.ppermute(blocks[shift], axes, pairs)
    return landed


def from_others(block, axis):
    count = lax.axis_size(axis)
    landed = [block]
    for shift in range(1, count):
        pairs = [(place, place ^ shift) for place in range(count)]
        landed.append(lax.ppermute(block, axis, pairs))
    return landed


def held(value, others):
    return lax.optimization_barrier((value, others))[0]


SMALL = pl.CostEstimate(flops=1, bytes_accessed=1, transcendentals=0)


def on_device(
    inputs,
    input_norm_gain,
    projection_weight,
    projection_bias,
    speaker,
    speaker_adapter_slot,
    cache_fill_length,
    rotated_key_cache,
    value_cache_rows,
    adapter_down_maps,
    adapter_query_up,
    adapter_value_up,
    flow_decoder_owner,
):
    steps, rows, width = inputs.shape
    lanes = lax.axis_size("streams")
    subs = lax.axis_size("sub")
    heads = lax.axis_size("heads")
    flow_lanes = lanes * subs
    local_slots, sliced, _ = adapter_down_maps.shape
    query_columns = adapter_query_up.shape[2]
    value_columns = adapter_value_up.shape[2]
    groups = value_columns // HEAD_WIDTH
    cache = rotated_key_cache.shape[1]
    spots = subs * local_slots * MOST
    chunks = 2
    chunk_steps = steps // chunks
    chunk_rows = chunk_steps * rows
    per_message = chunk_steps * spots
    chip_slots = subs * local_slots
    flow_most = max(2, (2 * rows + flow_lanes - 1) // flow_lanes)
    bf16, f32 = jnp.bfloat16, jnp.float32

    def whole(shape):
        return pl.BlockSpec(shape, lambda i: (0,) * len(shape))

    in_hbm = pl.BlockSpec(memory_space=pltpu.HBM)

    down_maps = from_others(adapter_down_maps, "sub")
    query_maps = from_others(
        adapter_query_up.reshape(local_slots * ADAPTER_RANK, query_columns), "sub"
    )
    value_maps = from_others(
        adapter_value_up.reshape(local_slots * ADAPTER_RANK, value_columns), "sub"
    )

    pieces = 4
    flat = inputs.reshape(steps * rows, width)
    gain = input_norm_gain.reshape(width // 128, 128)
    message = jax.ShapeDtypeStruct((per_message, sliced), bf16)
    places_shape = jax.ShapeDtypeStruct((8, rows), jnp.int32)
    tables = [
        speaker.reshape(1, rows),
        speaker_adapter_slot.reshape(1, -1),
        flow_decoder_owner.reshape(1, rows),
    ]

    def row_buffers(count):
        return (
            [pltpu.VMEM((count, width), bf16), pltpu.VMEM(gain.shape, f32)]
            + [pltpu.VMEM(table.shape, jnp.int32) for table in tables]
            + [pltpu.SemaphoreType.DMA((pieces + 4,))]
        )

    messages = pl.pallas_call(
        functools.partial(norm_pack_kernel, chunk_steps, rows, flow_most, lanes, pieces),
        in_specs=[in_hbm] * 5,
        out_specs=[VMEM] * lanes,
        out_shape=[message] * lanes,
        scratch_shapes=row_buffers(chunk_rows) + [pltpu.VMEM((chunk_rows, width), bf16)],
        compiler_params=pltpu.CompilerParams(vmem_limit_bytes=PACK_LIMIT * MIB),
        cost_estimate=SMALL,
        name="norm_and_pack",
    )(*tables, gain, flat)
    arrived = [traded(messages, "streams")]

    bias = projection_bias.reshape(-1, 128)
    columns = projection_weight.shape[1]
    block_columns = 256 if columns % 256 == 0 else 384
    blocks = columns // block_columns
    cuts = [4, 6, 9] if blocks == 9 else [blocks // 3, 2 * blocks // 3, blocks]
    cut = cuts[0]

    def weight_buffers(count):
        return [
            pltpu.VMEM((count, width, block_columns), bf16),
            pltpu.SemaphoreType.DMA((count,)),
        ]

    def projected(count):
        return jax.ShapeDtypeStruct((steps * rows, count * block_columns), f32)

    adapters = down_maps[1:], query_maps[1:], value_maps[1:]
    weight_buf, weight_semaphores = weight_buffers(cut)
    normed, first_qkv, places, *messages = pl.pallas_call(
        functools.partial(
            norm_pack_project_kernel, chunk_steps, rows, flow_most, lanes, 2 * pieces, 1
        ),
        in_specs=[in_hbm] * 3 + [VMEM] + [in_hbm] * 3,
        out_specs=[VMEM] * (3 + lanes),
        out_shape=[jax.ShapeDtypeStruct((steps * rows, width), bf16), projected(cut)]
        + [places_shape]
        + [message] * lanes,
        scratch_shapes=row_buffers(steps * rows)[:-1]
        + [pltpu.SemaphoreType.DMA((2 * pieces + 4,))]
        + [weight_buf, weight_semaphores],
        compiler_params=pltpu.CompilerParams(vmem_limit_bytes=PROJECT_LIMIT * MIB),
        cost_estimate=SMALL,
        name="norm_pack_project",
    )(*tables, held(bias, (adapters, messages)), gain, flat, projection_weight)
    arrived.append(traded(messages, "streams"))
    qkv = [first_qkv]

    def project(after):
        begin, end = cuts[len(qkv) - 1 : len(qkv) + 1]
        return pl.pallas_call(
            functools.partial(project_kernel, begin),
            in_specs=[VMEM, VMEM, in_hbm],
            out_specs=VMEM,
            out_shape=projected(end - begin),
            scratch_shapes=weight_buffers(end - begin),
            compiler_params=pltpu.CompilerParams(vmem_limit_bytes=PROJECT_LIMIT * MIB),
            cost_estimate=SMALL,
            name="project",
        )(normed, held(bias, after), projection_weight)

    def down(chunk, after):
        partial_latent = pl.pallas_call(
            functools.partial(down_kernel, lanes, spots),
            in_specs=[VMEM] * (lanes + subs),
            out_specs=VMEM,
            out_shape=jax.ShapeDtypeStruct((lanes * per_message, 2 * ADAPTER_RANK), f32),
            compiler_params=pltpu.CompilerParams(vmem_limit_bytes=16 * MIB),
            cost_estimate=SMALL,
            name="down",
        )(*arrived[chunk][:0:-1], held(arrived[chunk][0], after), *down_maps)
        return from_others(partial_latent, "heads")

    def up(partials, after):
        message = jax.ShapeDtypeStruct((per_message, query_columns + value_columns), bf16)
        messages = pl.pallas_call(
            functools.partial(up_kernel, heads, subs, spots),
            in_specs=[VMEM] * (heads + 2 * subs),
            out_specs=[VMEM] * lanes,
            out_shape=[message] * lanes,
            compiler_params=pltpu.CompilerParams(vmem_limit_bytes=24 * MIB),
            cost_estimate=SMALL,
            name="up",
        )(held(partials[0], after), *partials[1:], *query_maps, *value_maps)
        return messages

    half_width = HEAD_WIDTH // 2
    position = jnp.concatenate([cache_fill_length + step for step in range(steps)]).astype(f32)
    freq = jnp.exp(jnp.arange(half_width, dtype=f32) * (-math.log(1000000.0) / half_width))
    freq = jnp.concatenate([freq, freq])
    angle = position[:, None] * freq
    sign = jnp.where(jnp.arange(HEAD_WIDTH) < half_width, -1.0, 1.0).astype(f32)
    cosine = jnp.cos(angle)
    sine_part = jnp.sin(angle) * sign

    returned = []
    after = qkv
    for chunk in range(chunks):
        partials = down(chunk, after)
        qkv.append(project(partials[0]))
        after = up(partials, qkv)
        messages = list(after)
        if chunk:
            for lane in range(1, lanes):
                messages[lane] = held(messages[lane], returned[-1][lane])
        returned.append(traded(messages, "streams"))

    length_row = cache_fill_length.reshape(1, rows)
    block = flow_most * chunk_steps
    earlier, along, alongs = [], [], []
    for chunk in range(chunks):
        last = chunk == chunks - 1
        message = jax.ShapeDtypeStruct((subs * block, query_columns), bf16)
        fresh = jax.ShapeDtypeStruct((chunk_rows, 2 * value_columns), f32)
        rows_of = lambda shape: pl.BlockSpec(shape, lambda i, chunk=chunk: (chunk, 0))
        results = pl.pallas_call(
            functools.partial(
                attend_kernel,
                chunk * chunk_steps,
                chunk_steps,
                rows,
                cache,
                groups,
                lanes,
                subs,
                last,
            ),
            grid=(1,),
            in_specs=[whole(places.shape), whole(length_row.shape)]
            + [rows_of((chunk_rows, HEAD_WIDTH))] * 2
            + [whole(rotated_key_cache.shape)] * 2
            + [rows_of((chunk_rows, part.shape[1])) for part in qkv]
            + [whole((per_message, query_columns + value_columns))] * lanes
            + [whole(block_rows.shape) for block_rows in earlier],
            out_specs=[whole(fresh.shape)] * (not last) + [whole(message.shape)] * lanes,
            out_shape=[fresh] * (not last) + [message] * lanes,
            scratch_shapes=[
                pltpu.VMEM((chunk_rows, query_columns + value_columns), f32),
                pltpu.VMEM((chunk_rows, query_columns), f32),
                pltpu.VMEM((rows, BATCH * cache), f32),
            ],
            compiler_params=pltpu.CompilerParams(vmem_limit_bytes=32 * MIB),
            cost_estimate=SMALL,
            name="attend",
        )(
            places if chunk else held(places, after),
            length_row,
            cosine,
            sine_part,
            rotated_key_cache,
            value_cache_rows,
            *qkv,
            *returned[chunk][::-1],
            *earlier,
        )
        if not last:
            earlier, results = [results[0]], results[1:]
        results = list(results)
        for lane in range(1, lanes):
            if not alongs:
                results[lane] = held(results[lane], returned[-1][1:])
        along = traded(results, "streams")
        alongs.append(along)

    landed, found = [], []
    for chunk, along in enumerate(alongs):
        base = len(landed)
        landed += along
        where = [[(base + lane, 0)] for lane in range(lanes)]
        for shift in range(1, subs):
            pairs = [(core, core ^ shift) for core in range(subs)]
            span = slice(shift * block, (shift + 1) * block)
            if chunk < chunks - 1:
                joined = jnp.concatenate([block_rows[span] for block_rows in along])
                for lane in range(lanes):
                    where[lane].append((len(landed), lane * block))
                landed.append(lax.ppermute(joined, "sub", pairs))
            else:
                for lane, block_rows in enumerate(along):
                    where[lane].append((len(landed), shift * block))
                    landed.append(lax.ppermute(block_rows, "sub", pairs))
        found.append(where)

    flow = pl.pallas_call(
        functools.partial(place_kernel, found, lanes, subs, flow_most),
        in_specs=[VMEM] * len(landed),
        out_specs=VMEM,
        out_shape=jax.ShapeDtypeStruct((flow_lanes * flow_most, steps, query_columns), bf16),
        compiler_params=pltpu.CompilerParams(vmem_limit_bytes=24 * MIB),
        cost_estimate=SMALL,
        name="place",
    )(*landed)
    return flow[None]


def solution(mesh):
    placed = (
        P(None, ("groups", "streams", "sub"), None),
        P(),
        P(None, "heads"),
        P("heads"),
        P(("groups", "streams", "sub"), None),
        P("groups"),
        P(("groups", "streams", "sub")),
        P(("groups", "streams", "sub"), None, "heads"),
        P(("groups", "streams", "sub"), None, "heads"),
        P(("groups", "streams", "sub"), "heads", None),
        P(("groups", "streams", "sub"), None, "heads"),
        P(("groups", "streams", "sub"), None, "heads"),
        P(("groups", "streams", "sub"), None),
    )
    return jax.shard_map(
        on_device,
        mesh=mesh,
        in_specs=placed,
        out_specs=P(("groups", "streams", "sub"), None, None, "heads"),
        check_vma=False,
    )
```

```python
import functools
import math

import jax
import jax.numpy as jnp
from jax import lax
from jax.experimental import pallas as pl
from jax.experimental.pallas import tpu as pltpu
from jax.sharding import PartitionSpec as P

QUERY_HEADS = 28
KEY_VALUE_HEADS = 4
HEAD_WIDTH = 128
ADAPTER_RANK = 64
MOST = 2
PER_GROUP = QUERY_HEADS // KEY_VALUE_HEADS
LANE_AXES = ("streams", "sub")
BATCH = 8
TOGETHER = 2
VMEM = pl.BlockSpec(memory_space=pltpu.VMEM)
MIB = 1 << 20
PACK_LIMIT = 56
PROJECT_LIMIT = 49


def iota(shape, dim):
    return lax.broadcasted_iota(jnp.int32, shape, dim)


def as_column(row):
    count = row.shape[1]
    square = (count, count)
    same = iota(square, 0) == iota(square, 1)
    return jnp.sum(jnp.where(same, jnp.broadcast_to(row, square), 0), axis=1, keepdims=True)


def ranked(labels, most):
    count = labels.shape[1]
    square = (count, count)
    earlier = (as_column(labels) == labels) & (iota(square, 0) < iota(square, 1))
    return labels * most + jnp.sum(earlier.astype(jnp.int32), axis=0, keepdims=True)


def slot_places(speaker, table, lane_base):
    speakers_all = table.shape[1]
    rows = speaker.shape[1]
    match = iota((speakers_all, rows), 0) == speaker
    slots = jnp.sum(jnp.where(match, as_column(table), 0), axis=0, keepdims=True)
    return ranked(slots ^ lane_base, MOST)


def norm_in_pieces(
    pieces, begin, x_hbm, gain_hbm, x_buf, gain_buf, semaphores, normed_ref, started=None
):
    count, width = x_buf.shape
    size = count // pieces
    gain_copy = pltpu.make_async_copy(gain_hbm, gain_buf, semaphores.at[pieces])
    copies = []
    for piece in range(pieces):
        copies.append(
            pltpu.make_async_copy(
                x_hbm.at[pl.ds(begin + piece * size, size)],
                x_buf.at[pl.ds(piece * size, size)],
                semaphores.at[piece],
            )
        )
        copies[-1].start()
        if piece == 0:
            gain_copy.start()
    if started is not None:
        started()
    gain_copy.wait()
    gain = jnp.concatenate([gain_buf[i : i + 1, :] for i in range(gain_buf.shape[0])], axis=1)
    for piece in range(pieces):
        copies[piece].wait()

        def one(index, carry):
            span = pl.ds(pl.multiple_of(piece * size + index * 16, 16), 16)
            values = x_buf[span, :].astype(jnp.float32)
            mean_sq = jnp.sum(values * values, axis=1, keepdims=True) * (1.0 / width)
            normed = values * lax.rsqrt(mean_sq + 1e-06) * gain
            normed_ref[span, :] = normed.astype(jnp.bfloat16)
            return carry

        lax.fori_loop(0, size // 16, one, 0)


def pack_messages(steps, rows, places, normed_ref, message_refs):
    per_message, sliced = message_refs[0].shape
    spots = per_message // steps
    shape = (len(message_refs) * per_message, steps * rows)
    out_row = iota(shape, 0)
    wanted = out_row // per_message * spots + out_row % spots
    out_step = out_row % per_message // spots
    places = jnp.concatenate([places] * steps, axis=1)
    pick = (wanted == places) & (out_step == iota(shape, 1) // rows)
    pick = pick.astype(jnp.float32).astype(jnp.bfloat16)
    begin = pl.multiple_of(lax.axis_index("heads") * sliced, 128)
    own = normed_ref[:, pl.ds(begin, sliced)]
    packed = jnp.dot(pick, own, preferred_element_type=jnp.float32).astype(jnp.bfloat16)
    for number, message_ref in enumerate(message_refs):
        message_ref[...] = packed[number * per_message : (number + 1) * per_message]


def table_copies(table_hbms, table_bufs, semaphores, first):
    copies = [
        pltpu.make_async_copy(source, target, semaphores.at[first + number])
        for number, (source, target) in enumerate(zip(table_hbms, table_bufs))
    ]
    for copy in copies:
        copy.start()
    return copies


def places_from(table_bufs, spots, flow_most):
    speaker, table, owner = [buffer[...] for buffer in table_bufs]
    here, core, subs = lax.axis_index("streams"), lax.axis_index("sub"), lax.axis_size("sub")
    places = slot_places(speaker, table, here * (spots // MOST))
    return places, ranked(owner ^ (here * subs + core), flow_most)


def norm_pack_kernel(steps, rows, flow_most, lanes, pieces, *refs):
    table_hbms, gain_hbm, x_hbm, message_refs = refs[:3], refs[3], refs[4], refs[5 : 5 + lanes]
    x_buf, gain_buf, *table_bufs, semaphores, normed_ref = refs[5 + lanes :]
    copies = table_copies(table_hbms, table_bufs, semaphores, pieces + 1)
    norm_in_pieces(pieces, 0, x_hbm, gain_hbm, x_buf, gain_buf, semaphores, normed_ref)
    for copy in copies:
        copy.wait()
    spots = message_refs[0].shape[0] // steps
    places, _ = places_from(table_bufs, spots, flow_most)
    pack_messages(steps, rows, places, normed_ref, message_refs)


def weight_copies(begin, weight_hbm, weight_buf, semaphores):
    columns = weight_buf.shape[2]
    return [
        pltpu.make_async_copy(
            weight_hbm.at[:, pl.ds((begin + block) * columns, columns)],
            weight_buf.at[block],
            semaphores.at[block],
        )
        for block in range(weight_buf.shape[0])
    ]


def project_blocks(begin, copies, rows_ref, weight_buf, bias_ref, out_ref):
    columns = weight_buf.shape[2]
    tiles = columns // 128
    for block, copy in enumerate(copies):
        first = (begin + block) * tiles
        bias = [bias_ref[tile : tile + 1, :] for tile in range(first, first + tiles)]
        copy.wait()
        product = jnp.dot(rows_ref[...], weight_buf[block], preferred_element_type=jnp.float32)
        out_ref[:, block * columns : (block + 1) * columns] = product + jnp.concatenate(
            bias, axis=1
        )


def norm_pack_project_kernel(steps, rows, flow_most, lanes, pieces, chunk, *refs):
    table_hbms, bias_ref, gain_hbm, x_hbm, weight_hbm = refs[:3], *refs[3:7]
    normed_ref, out_ref, places_ref, message_refs = *refs[7:10], refs[10 : 10 + lanes]
    x_buf, gain_buf, *table_bufs, semaphores, weight_buf, weight_semaphores = refs[10 + lanes :]
    copies = weight_copies(0, weight_hbm, weight_buf, weight_semaphores)
    tables = table_copies(table_hbms, table_bufs, semaphores, pieces + 1)

    def start_weights():
        for copy in copies:
            copy.start()

    norm_in_pieces(
        pieces, 0, x_hbm, gain_hbm, x_buf, gain_buf, semaphores, normed_ref, start_weights
    )
    for copy in tables:
        copy.wait()
    spots = message_refs[0].shape[0] // steps
    places, flow_places = places_from(table_bufs, spots, flow_most)
    places_ref[0:1, :] = places
    places_ref[1:2, :] = flow_places
    count = steps * rows
    own_ref = normed_ref.at[pl.ds(chunk * count, count)]
    pack_messages(steps, rows, places, own_ref, message_refs)
    project_blocks(0, copies, normed_ref, weight_buf, bias_ref, out_ref)


def project_kernel(begin, rows_ref, bias_ref, weight_hbm, out_ref, weight_buf, semaphores):
    copies = weight_copies(begin, weight_hbm, weight_buf, semaphores)
    for copy in copies:
        copy.start()
    project_blocks(begin, copies, rows_ref, weight_buf, bias_ref, out_ref)


def row_slots(shape, spots):
    return iota(shape, 0) % spots // MOST


def down_kernel(lanes, spots, *refs):
    message_refs, map_refs, partial_ref = refs[:lanes][::-1], refs[lanes:-1], refs[-1]
    local_slots = map_refs[0].shape[0]
    rows = jnp.concatenate([ref[...] for ref in message_refs], axis=0)
    own_slot = row_slots(partial_ref.shape, spots)
    total = jnp.zeros(partial_ref.shape, jnp.float32)
    for number, map_ref in enumerate(map_refs):
        shift = (lax.axis_index("sub") ^ number) * local_slots
        for slot in range(local_slots):
            part = jnp.dot(rows, map_ref[slot], preferred_element_type=jnp.float32)
            total = jnp.where(own_slot == shift + slot, part, total)
    partial_ref[...] = total


def up_kernel(heads, subs, spots, *refs):
    partial_refs, refs = refs[:heads], refs[heads:]
    query_refs, value_refs, message_refs = refs[:subs], refs[subs : 2 * subs], refs[2 * subs :]
    total = partial_refs[0][...]
    for ref in partial_refs[1:]:
        total = total + ref[...]
    latent = total.astype(jnp.bfloat16).astype(jnp.float32)
    own_slot = row_slots(latent.shape, spots)
    column = iota(latent.shape, 1) // ADAPTER_RANK
    turned = pltpu.roll(latent, ADAPTER_RANK, 1)
    low = iota(latent.shape, 1) < ADAPTER_RANK
    query_pair = jnp.where(low, latent, turned)
    value_pair = jnp.where(low, turned, latent)

    def product(pair, map_refs):
        result = None
        for number, map_ref in enumerate(map_refs):
            local_slots = map_ref.shape[0] // ADAPTER_RANK
            shift = (lax.axis_index("sub") ^ number) * local_slots
            pieces = []
            for slot in range(0, local_slots, 2):
                kept = jnp.where(own_slot == shift + slot + column, pair, 0.0)
                pieces.append(kept.astype(jnp.bfloat16))
            wide = jnp.concatenate(pieces, axis=1)
            part = jnp.dot(wide, map_ref[...], preferred_element_type=jnp.float32)
            result = part if result is None else result + part
        return result.astype(jnp.bfloat16)

    queries = product(query_pair, query_refs)
    values = product(value_pair, value_refs)
    query_width = queries.shape[1]
    per_message = message_refs[0].shape[0]
    for number, ref in enumerate(message_refs):
        span = slice(number * per_message, (number + 1) * per_message)
        ref[:, :query_width] = queries[span]
        ref[:, query_width:] = values[span]


def attend_kernel(before, steps, rows, cache, groups, lanes, subs, last, *refs):
    places_ref, length_ref, cos_ref, sin_ref, key_ref, value_ref = refs[:6]
    qkv_refs, refs = refs[6:9], refs[9:]
    delta_refs, refs = refs[:lanes][::-1], refs[lanes:]
    if before:
        earlier_ref, refs = refs[0], refs[1:]
    if not last:
        fresh_ref, refs = refs[0], refs[1:]
    message_refs = refs[:lanes]
    delta_ref, context_ref, bias_ref = refs[lanes:]
    per_message = delta_refs[0].shape[0]
    spots = per_message // steps
    query_width = PER_GROUP * HEAD_WIDTH
    known = before + steps

    def qkv_tile(span, group, head):
        begin = (group * (PER_GROUP + 2) + head) * HEAD_WIDTH
        for ref in qkv_refs:
            if begin < ref.shape[1]:
                return ref[span, begin : begin + HEAD_WIDTH]
            begin -= ref.shape[1]

    wide = groups * HEAD_WIDTH
    column = as_column(places_ref[0:1, :])
    column = jnp.concatenate([column] * steps, axis=0)
    shape = (steps * rows, lanes * per_message)
    out_row = iota(shape, 1)
    wanted = out_row // per_message * spots + out_row % spots
    pick = (wanted == column) & (out_row % per_message // spots == iota(shape, 0) // rows)
    pick = pick.astype(jnp.float32).astype(jnp.bfloat16)
    delta_ref[...] = jnp.dot(
        pick,
        jnp.concatenate([ref[...] for ref in delta_refs], axis=0),
        preferred_element_type=jnp.float32,
    )

    shape = (rows, BATCH * cache)
    lengths = as_column(length_ref[...])
    slot_column = iota(shape, 1)
    allowed = (slot_column // cache == iota(shape, 0) % BATCH) & (slot_column % cache < lengths)
    bias_ref[...] = jnp.where(allowed, 0.0, -1e30)
    shape = (steps, BATCH, known * BATCH)
    fresh_column = iota(shape, 2)
    allowed = (fresh_column % BATCH == iota(shape, 1)) & (
        fresh_column // BATCH <= iota(shape, 0) + before
    )
    fresh_bias = jnp.where(allowed, 0.0, -1e30)
    scale = HEAD_WIDTH ** (-0.5)
    transposed = (((1,), (1,)), ((), ()))

    def scored(first, group):
        spans = [pl.ds(pl.multiple_of(step * rows + first, BATCH), BATCH) for step in range(known)]
        query_tiles, key_tiles, value_tiles = [], [], []
        lane_span = slice(group * HEAD_WIDTH, (group + 1) * HEAD_WIDTH)
        value_span = slice(wide + group * HEAD_WIDTH, wide + (group + 1) * HEAD_WIDTH)
        for span in spans[:before]:
            key_tiles.append(earlier_ref[span, lane_span])
            value_tiles.append(earlier_ref[span, value_span])
        for span in spans[:steps]:
            cosine, sine_part = cos_ref[span, :], sin_ref[span, :]

            def rotated(values):
                return values * cosine + pltpu.roll(values, HEAD_WIDTH // 2, 1) * sine_part

            for head in range(PER_GROUP):
                begin = group * query_width + head * HEAD_WIDTH
                change = delta_ref[span, begin : begin + HEAD_WIDTH]
                query_tiles.append(rotated(qkv_tile(span, group, head) + change))
            key = rotated(qkv_tile(span, group, PER_GROUP))
            begin = groups * query_width + group * HEAD_WIDTH
            change = delta_ref[span, begin : begin + HEAD_WIDTH]
            value = qkv_tile(span, group, PER_GROUP + 1) + change
            if not last:
                fresh_ref[span, lane_span] = key
                fresh_ref[span, value_span] = value
            key_tiles.append(key)
            value_tiles.append(value)
        queries = jnp.concatenate(query_tiles, axis=0).astype(jnp.bfloat16)
        new_keys = jnp.concatenate(key_tiles, axis=0).astype(jnp.bfloat16)
        new_values = jnp.concatenate(value_tiles, axis=0).astype(jnp.bfloat16)
        old_keys = key_ref[pl.ds(first, BATCH), :, lane_span].reshape(BATCH * cache, HEAD_WIDTH)
        old_scores = lax.dot_general(
            queries, old_keys, transposed, preferred_element_type=jnp.float32
        )
        new_scores = lax.dot_general(
            queries, new_keys, transposed, preferred_element_type=jnp.float32
        )
        return old_scores, new_scores, new_values

    def weighed(first, old_scores, new_scores):
        heads = steps * PER_GROUP
        old_scores = (old_scores * scale).reshape(heads, BATCH, BATCH * cache)
        old_scores = old_scores + bias_ref[pl.ds(first, BATCH), :][None]
        new_scores = (new_scores * scale).reshape(steps, PER_GROUP, BATCH, known * BATCH)
        new_scores = (new_scores + fresh_bias[:, None]).reshape(heads, BATCH, known * BATCH)
        peak = jnp.maximum(
            jnp.max(old_scores, axis=-1, keepdims=True),
            jnp.max(new_scores, axis=-1, keepdims=True),
        )
        old_scores = jnp.exp(old_scores - peak)
        new_scores = jnp.exp(new_scores - peak)
        share = 1.0 / (
            jnp.sum(old_scores, axis=-1, keepdims=True)
            + jnp.sum(new_scores, axis=-1, keepdims=True)
        )
        old_weights = (old_scores * share).reshape(heads * BATCH, BATCH * cache)
        new_weights = (new_scores * share).reshape(heads * BATCH, known * BATCH)
        return old_weights.astype(jnp.bfloat16), new_weights.astype(jnp.bfloat16)

    def batch(index, carry):
        chains = []
        for number in range(TOGETHER):
            first = pl.multiple_of((index * TOGETHER + number) * BATCH, BATCH)
            chains += [(first, group) for group in range(groups)]
        scores = [scored(*chain) for chain in chains]
        weights = [weighed(chain[0], *score[:2]) for chain, score in zip(chains, scores)]
        for (first, group), (old_weights, new_weights), score in zip(chains, weights, scores):
            lane_span = slice(group * HEAD_WIDTH, (group + 1) * HEAD_WIDTH)
            old_values = value_ref[pl.ds(first, BATCH), :, lane_span]
            old_values = old_values.reshape(BATCH * cache, HEAD_WIDTH)
            context = jnp.dot(
                old_weights, old_values, preferred_element_type=jnp.float32
            ) + jnp.dot(new_weights, score[2], preferred_element_type=jnp.float32)
            for step in range(steps):
                span = pl.ds(pl.multiple_of(step * rows + first, BATCH), BATCH)
                for head in range(PER_GROUP):
                    row = (step * PER_GROUP + head) * BATCH
                    begin = group * query_width + head * HEAD_WIDTH
                    context_ref[span, begin : begin + HEAD_WIDTH] = context[row : row + BATCH]
        return carry

    lax.fori_loop(0, rows // (BATCH * TOGETHER), batch, 0)

    flow_places = jnp.concatenate([places_ref[1:2, :]] * steps, axis=1)
    context = context_ref[...].astype(jnp.bfloat16)
    count = message_refs[0].shape[0]
    shape = (count, steps * rows)
    out_row = iota(shape, 0)
    same_step = out_row % steps == iota(shape, 1) // rows
    for number, message_ref in enumerate(message_refs):
        wanted = number * (count // steps) + out_row // steps
        pick = ((flow_places == wanted) & same_step).astype(jnp.float32).astype(jnp.bfloat16)
        message_ref[...] = jnp.dot(
            pick, context, preferred_element_type=jnp.float32
        ).astype(jnp.bfloat16)


def place_kernel(found, lanes, subs, most, *refs):
    chunks = len(found)
    out_ref = refs[-1]
    steps = out_ref.shape[1]
    chunk_steps = steps // chunks
    block = most * chunk_steps
    here = lax.axis_index("streams")
    core = lax.axis_index("sub")
    shape = (chunks * block, chunks * block)
    out_row, in_row = iota(shape, 0), iota(shape, 1)
    step = out_row % steps
    wanted = step // chunk_steps * block + out_row // steps * chunk_steps + step % chunk_steps
    pick = (wanted == in_row).astype(jnp.float32).astype(jnp.bfloat16)
    for number in range(lanes):
        for other in range(subs):
            pieces = []
            for chunk in range(chunks):
                array, begin = found[chunk][number][other]
                pieces.append(refs[array][...][begin : begin + block])
            rows = jnp.dot(
                pick, jnp.concatenate(pieces, axis=0), preferred_element_type=jnp.float32
            )
            source = (here ^ number) * subs + (core ^ other)
            out_ref[pl.ds(source * most, most)] = rows.reshape(
                most, steps, rows.shape[1]
            ).astype(jnp.bfloat16)


def traded(blocks, axes):
    landed = list(blocks)
    count = len(blocks)
    order = sorted(range(1, count), key=lambda shift: -(shift ^ (shift >> 1)))
    for shift in order:
        pairs = [(place, place ^ shift) for place in range(count)]
        landed[shift] = lax.ppermute(blocks[shift], axes, pairs)
    return landed


def from_others(block, axis):
    count = lax.axis_size(axis)
    landed = [block]
    for shift in range(1, count):
        pairs = [(place, place ^ shift) for place in range(count)]
        landed.append(lax.ppermute(block, axis, pairs))
    return landed


def held(value, others):
    return lax.optimization_barrier((value, others))[0]


SMALL = pl.CostEstimate(flops=1, bytes_accessed=1, transcendentals=0)


def on_device(
    inputs,
    input_norm_gain,
    projection_weight,
    projection_bias,
    speaker,
    speaker_adapter_slot,
    cache_fill_length,
    rotated_key_cache,
    value_cache_rows,
    adapter_down_maps,
    adapter_query_up,
    adapter_value_up,
    flow_decoder_owner,
):
    steps, rows, width = inputs.shape
    lanes = lax.axis_size("streams")
    subs = lax.axis_size("sub")
    heads = lax.axis_size("heads")
    flow_lanes = lanes * subs
    local_slots, sliced, _ = adapter_down_maps.shape
    query_columns = adapter_query_up.shape[2]
    value_columns = adapter_value_up.shape[2]
    groups = value_columns // HEAD_WIDTH
    cache = rotated_key_cache.shape[1]
    spots = subs * local_slots * MOST
    chunks = 2
    chunk_steps = steps // chunks
    chunk_rows = chunk_steps * rows
    per_message = chunk_steps * spots
    chip_slots = subs * local_slots
    flow_most = max(2, (2 * rows + flow_lanes - 1) // flow_lanes)
    bf16, f32 = jnp.bfloat16, jnp.float32

    def whole(shape):
        return pl.BlockSpec(shape, lambda i: (0,) * len(shape))

    in_hbm = pl.BlockSpec(memory_space=pltpu.HBM)

    down_maps = from_others(adapter_down_maps, "sub")
    query_maps = from_others(
        adapter_query_up.reshape(local_slots * ADAPTER_RANK, query_columns), "sub"
    )
    value_maps = from_others(
        adapter_value_up.reshape(local_slots * ADAPTER_RANK, value_columns), "sub"
    )

    pieces = 4
    flat = inputs.reshape(steps * rows, width)
    gain = input_norm_gain.reshape(width // 128, 128)
    message = jax.ShapeDtypeStruct((per_message, sliced), bf16)
    places_shape = jax.ShapeDtypeStruct((8, rows), jnp.int32)
    tables = [
        speaker.reshape(1, rows),
        speaker_adapter_slot.reshape(1, -1),
        flow_decoder_owner.reshape(1, rows),
    ]

    def row_buffers(count):
        return (
            [pltpu.VMEM((count, width), bf16), pltpu.VMEM(gain.shape, f32)]
            + [pltpu.VMEM(table.shape, jnp.int32) for table in tables]
            + [pltpu.SemaphoreType.DMA((pieces + 4,))]
        )

    messages = pl.pallas_call(
        functools.partial(norm_pack_kernel, chunk_steps, rows, flow_most, lanes, pieces),
        in_specs=[in_hbm] * 5,
        out_specs=[VMEM] * lanes,
        out_shape=[message] * lanes,
        scratch_shapes=row_buffers(chunk_rows) + [pltpu.VMEM((chunk_rows, width), bf16)],
        compiler_params=pltpu.CompilerParams(vmem_limit_bytes=PACK_LIMIT * MIB),
        cost_estimate=SMALL,
        name="norm_and_pack",
    )(*tables, gain, flat)
    arrived = [traded(messages, "streams")]

    bias = projection_bias.reshape(-1, 128)
    columns = projection_weight.shape[1]
    block_columns = 256 if columns % 256 == 0 else 384
    blocks = columns // block_columns
    cuts = [4, 6, 9] if blocks == 9 else [blocks // 3, 2 * blocks // 3, blocks]
    cut = cuts[0]

    def weight_buffers(count):
        return [
            pltpu.VMEM((count, width, block_columns), bf16),
            pltpu.SemaphoreType.DMA((count,)),
        ]

    def projected(count):
        return jax.ShapeDtypeStruct((steps * rows, count * block_columns), f32)

    adapters = down_maps[1:], query_maps[1:], value_maps[1:]
    weight_buf, weight_semaphores = weight_buffers(cut)
    normed, first_qkv, places, *messages = pl.pallas_call(
        functools.partial(
            norm_pack_project_kernel, chunk_steps, rows, flow_most, lanes, 2 * pieces, 1
        ),
        in_specs=[in_hbm] * 3 + [VMEM] + [in_hbm] * 3,
        out_specs=[VMEM] * (3 + lanes),
        out_shape=[jax.ShapeDtypeStruct((steps * rows, width), bf16), projected(cut)]
        + [places_shape]
        + [message] * lanes,
        scratch_shapes=row_buffers(steps * rows)[:-1]
        + [pltpu.SemaphoreType.DMA((2 * pieces + 4,))]
        + [weight_buf, weight_semaphores],
        compiler_params=pltpu.CompilerParams(vmem_limit_bytes=PROJECT_LIMIT * MIB),
        cost_estimate=SMALL,
        name="norm_pack_project",
    )(*tables, held(bias, (adapters, messages)), gain, flat, projection_weight)
    arrived.append(traded(messages, "streams"))
    qkv = [first_qkv]

    def project(after):
        begin, end = cuts[len(qkv) - 1 : len(qkv) + 1]
        return pl.pallas_call(
            functools.partial(project_kernel, begin),
            in_specs=[VMEM, VMEM, in_hbm],
            out_specs=VMEM,
            out_shape=projected(end - begin),
            scratch_shapes=weight_buffers(end - begin),
            compiler_params=pltpu.CompilerParams(vmem_limit_bytes=PROJECT_LIMIT * MIB),
            cost_estimate=SMALL,
            name="project",
        )(normed, held(bias, after), projection_weight)

    def down(chunk, after):
        partial_latent = pl.pallas_call(
            functools.partial(down_kernel, lanes, spots),
            in_specs=[VMEM] * (lanes + subs),
            out_specs=VMEM,
            out_shape=jax.ShapeDtypeStruct((lanes * per_message, 2 * ADAPTER_RANK), f32),
            compiler_params=pltpu.CompilerParams(vmem_limit_bytes=16 * MIB),
            cost_estimate=SMALL,
            name="down",
        )(*arrived[chunk][:0:-1], held(arrived[chunk][0], after), *down_maps)
        return from_others(partial_latent, "heads")

    def up(partials, after):
        message = jax.ShapeDtypeStruct((per_message, query_columns + value_columns), bf16)
        messages = pl.pallas_call(
            functools.partial(up_kernel, heads, subs, spots),
            in_specs=[VMEM] * (heads + 2 * subs),
            out_specs=[VMEM] * lanes,
            out_shape=[message] * lanes,
            compiler_params=pltpu.CompilerParams(vmem_limit_bytes=24 * MIB),
            cost_estimate=SMALL,
            name="up",
        )(held(partials[0], after), *partials[1:], *query_maps, *value_maps)
        return messages

    half_width = HEAD_WIDTH // 2
    position = jnp.concatenate([cache_fill_length + step for step in range(steps)]).astype(f32)
    freq = jnp.exp(jnp.arange(half_width, dtype=f32) * (-math.log(1000000.0) / half_width))
    freq = jnp.concatenate([freq, freq])
    angle = position[:, None] * freq
    sign = jnp.where(jnp.arange(HEAD_WIDTH) < half_width, -1.0, 1.0).astype(f32)
    cosine = jnp.cos(angle)
    sine_part = jnp.sin(angle) * sign

    returned = []
    after = qkv
    for chunk in range(chunks):
        partials = down(chunk, after)
        qkv.append(project(partials[0]))
        after = up(partials, qkv)
        messages = list(after)
        if chunk:
            for lane in range(1, lanes):
                messages[lane] = held(messages[lane], returned[-1][lane])
        returned.append(traded(messages, "streams"))

    length_row = cache_fill_length.reshape(1, rows)
    block = flow_most * chunk_steps
    earlier, along, alongs = [], [], []
    for chunk in range(chunks):
        last = chunk == chunks - 1
        message = jax.ShapeDtypeStruct((subs * block, query_columns), bf16)
        fresh = jax.ShapeDtypeStruct((chunk_rows, 2 * value_columns), f32)
        rows_of = lambda shape: pl.BlockSpec(shape, lambda i, chunk=chunk: (chunk, 0))
        results = pl.pallas_call(
            functools.partial(
                attend_kernel,
                chunk * chunk_steps,
                chunk_steps,
                rows,
                cache,
                groups,
                lanes,
                subs,
                last,
            ),
            grid=(1,),
            in_specs=[whole(places.shape), whole(length_row.shape)]
            + [rows_of((chunk_rows, HEAD_WIDTH))] * 2
            + [whole(rotated_key_cache.shape)] * 2
            + [rows_of((chunk_rows, part.shape[1])) for part in qkv]
            + [whole((per_message, query_columns + value_columns))] * lanes
            + [whole(block_rows.shape) for block_rows in earlier],
            out_specs=[whole(fresh.shape)] * (not last) + [whole(message.shape)] * lanes,
            out_shape=[fresh] * (not last) + [message] * lanes,
            scratch_shapes=[
                pltpu.VMEM((chunk_rows, query_columns + value_columns), f32),
                pltpu.VMEM((chunk_rows, query_columns), f32),
                pltpu.VMEM((rows, BATCH * cache), f32),
            ],
            compiler_params=pltpu.CompilerParams(vmem_limit_bytes=32 * MIB),
            cost_estimate=SMALL,
            name="attend",
        )(
            places if chunk else held(places, after),
            length_row,
            cosine,
            sine_part,
            rotated_key_cache,
            value_cache_rows,
            *qkv,
            *returned[chunk][::-1],
            *earlier,
        )
        if not last:
            earlier, results = [results[0]], results[1:]
        results = list(results)
        for lane in range(1, lanes):
            if not alongs:
                results[lane] = held(results[lane], returned[-1][lanes - lane])
        along = traded(results, "streams")
        alongs.append(along)

    landed, found = [], []
    for chunk, along in enumerate(alongs):
        base = len(landed)
        landed += along
        where = [[(base + lane, 0)] for lane in range(lanes)]
        for shift in range(1, subs):
            pairs = [(core, core ^ shift) for core in range(subs)]
            span = slice(shift * block, (shift + 1) * block)
            if chunk < chunks - 1:
                joined = jnp.concatenate([block_rows[span] for block_rows in along])
                for lane in range(lanes):
                    where[lane].append((len(landed), lane * block))
                landed.append(lax.ppermute(joined, "sub", pairs))
            else:
                for lane, block_rows in enumerate(along):
                    where[lane].append((len(landed), shift * block))
                    landed.append(lax.ppermute(block_rows, "sub", pairs))
        found.append(where)

    flow = pl.pallas_call(
        functools.partial(place_kernel, found, lanes, subs, flow_most),
        in_specs=[VMEM] * len(landed),
        out_specs=VMEM,
        out_shape=jax.ShapeDtypeStruct((flow_lanes * flow_most, steps, query_columns), bf16),
        compiler_params=pltpu.CompilerParams(vmem_limit_bytes=24 * MIB),
        cost_estimate=SMALL,
        name="place",
    )(*landed)
    return flow[None]


def solution(mesh):
    placed = (
        P(None, ("groups", "streams", "sub"), None),
        P(),
        P(None, "heads"),
        P("heads"),
        P(("groups", "streams", "sub"), None),
        P("groups"),
        P(("groups", "streams", "sub")),
        P(("groups", "streams", "sub"), None, "heads"),
        P(("groups", "streams", "sub"), None, "heads"),
        P(("groups", "streams", "sub"), "heads", None),
        P(("groups", "streams", "sub"), None, "heads"),
        P(("groups", "streams", "sub"), None, "heads"),
        P(("groups", "streams", "sub"), None),
    )
    return jax.shard_map(
        on_device,
        mesh=mesh,
        in_specs=placed,
        out_specs=P(("groups", "streams", "sub"), None, None, "heads"),
        check_vma=False,
    )
```

```python
import functools
import math

import jax
import jax.numpy as jnp
from jax import lax
from jax.experimental import pallas as pl
from jax.experimental.pallas import tpu as pltpu
from jax.sharding import PartitionSpec as P

QUERY_HEADS = 28
KEY_VALUE_HEADS = 4
HEAD_WIDTH = 128
ADAPTER_RANK = 64
MOST = 2
PER_GROUP = QUERY_HEADS // KEY_VALUE_HEADS
LANE_AXES = ("streams", "sub")
BATCH = 8
TOGETHER = 2
VMEM = pl.BlockSpec(memory_space=pltpu.VMEM)
MIB = 1 << 20
PACK_LIMIT = 56
PROJECT_LIMIT = 49


def iota(shape, dim):
    return lax.broadcasted_iota(jnp.int32, shape, dim)


def as_column(row):
    count = row.shape[1]
    square = (count, count)
    same = iota(square, 0) == iota(square, 1)
    return jnp.sum(jnp.where(same, jnp.broadcast_to(row, square), 0), axis=1, keepdims=True)


def ranked(labels, most):
    count = labels.shape[1]
    square = (count, count)
    earlier = (as_column(labels) == labels) & (iota(square, 0) < iota(square, 1))
    return labels * most + jnp.sum(earlier.astype(jnp.int32), axis=0, keepdims=True)


def slot_places(speaker, table, lane_base):
    speakers_all = table.shape[1]
    rows = speaker.shape[1]
    match = iota((speakers_all, rows), 0) == speaker
    slots = jnp.sum(jnp.where(match, as_column(table), 0), axis=0, keepdims=True)
    return ranked(slots ^ lane_base, MOST)


def norm_in_pieces(
    pieces, begin, x_hbm, gain_hbm, x_buf, gain_buf, semaphores, normed_ref, started=None
):
    count, width = x_buf.shape
    size = count // pieces
    gain_copy = pltpu.make_async_copy(gain_hbm, gain_buf, semaphores.at[pieces])
    copies = []
    for piece in range(pieces):
        copies.append(
            pltpu.make_async_copy(
                x_hbm.at[pl.ds(begin + piece * size, size)],
                x_buf.at[pl.ds(piece * size, size)],
                semaphores.at[piece],
            )
        )
        copies[-1].start()
        if piece == 0:
            gain_copy.start()
    if started is not None:
        started()
    gain_copy.wait()
    gain = jnp.concatenate([gain_buf[i : i + 1, :] for i in range(gain_buf.shape[0])], axis=1)
    for piece in range(pieces):
        copies[piece].wait()

        def one(index, carry):
            span = pl.ds(pl.multiple_of(piece * size + index * 16, 16), 16)
            values = x_buf[span, :].astype(jnp.float32)
            mean_sq = jnp.sum(values * values, axis=1, keepdims=True) * (1.0 / width)
            normed = values * lax.rsqrt(mean_sq + 1e-06) * gain
            normed_ref[span, :] = normed.astype(jnp.bfloat16)
            return carry

        lax.fori_loop(0, size // 16, one, 0)


def pack_messages(steps, rows, places, normed_ref, message_refs):
    per_message, sliced = message_refs[0].shape
    spots = per_message // steps
    shape = (len(message_refs) * per_message, steps * rows)
    out_row = iota(shape, 0)
    wanted = out_row // per_message * spots + out_row % spots
    out_step = out_row % per_message // spots
    places = jnp.concatenate([places] * steps, axis=1)
    pick = (wanted == places) & (out_step == iota(shape, 1) // rows)
    pick = pick.astype(jnp.float32).astype(jnp.bfloat16)
    begin = pl.multiple_of(lax.axis_index("heads") * sliced, 128)
    own = normed_ref[:, pl.ds(begin, sliced)]
    packed = jnp.dot(pick, own, preferred_element_type=jnp.float32).astype(jnp.bfloat16)
    for number, message_ref in enumerate(message_refs):
        message_ref[...] = packed[number * per_message : (number + 1) * per_message]


def table_copies(table_hbms, table_bufs, semaphores, first):
    copies = [
        pltpu.make_async_copy(source, target, semaphores.at[first + number])
        for number, (source, target) in enumerate(zip(table_hbms, table_bufs))
    ]
    for copy in copies:
        copy.start()
    return copies


def places_from(table_bufs, spots, flow_most):
    speaker, table, owner = [buffer[...] for buffer in table_bufs]
    here, core, subs = lax.axis_index("streams"), lax.axis_index("sub"), lax.axis_size("sub")
    places = slot_places(speaker, table, here * (spots // MOST))
    return places, ranked(owner ^ (here * subs + core), flow_most)


def norm_pack_kernel(steps, rows, flow_most, lanes, pieces, *refs):
    table_hbms, gain_hbm, x_hbm, message_refs = refs[:3], refs[3], refs[4], refs[5 : 5 + lanes]
    x_buf, gain_buf, *table_bufs, semaphores, normed_ref = refs[5 + lanes :]
    copies = table_copies(table_hbms, table_bufs, semaphores, pieces + 1)
    norm_in_pieces(pieces, 0, x_hbm, gain_hbm, x_buf, gain_buf, semaphores, normed_ref)
    for copy in copies:
        copy.wait()
    spots = message_refs[0].shape[0] // steps
    places, _ = places_from(table_bufs, spots, flow_most)
    pack_messages(steps, rows, places, normed_ref, message_refs)


def weight_copies(begin, weight_hbm, weight_buf, semaphores):
    columns = weight_buf.shape[2]
    return [
        pltpu.make_async_copy(
            weight_hbm.at[:, pl.ds((begin + block) * columns, columns)],
            weight_buf.at[block],
            semaphores.at[block],
        )
        for block in range(weight_buf.shape[0])
    ]


def project_blocks(begin, copies, rows_ref, weight_buf, bias_ref, out_ref):
    columns = weight_buf.shape[2]
    tiles = columns // 128
    for block, copy in enumerate(copies):
        first = (begin + block) * tiles
        bias = [bias_ref[tile : tile + 1, :] for tile in range(first, first + tiles)]
        copy.wait()
        product = jnp.dot(rows_ref[...], weight_buf[block], preferred_element_type=jnp.float32)
        out_ref[:, block * columns : (block + 1) * columns] = product + jnp.concatenate(
            bias, axis=1
        )


def norm_pack_project_kernel(steps, rows, flow_most, lanes, pieces, chunk, *refs):
    table_hbms, bias_ref, gain_hbm, x_hbm, weight_hbm = refs[:3], *refs[3:7]
    normed_ref, out_ref, places_ref, message_refs = *refs[7:10], refs[10 : 10 + lanes]
    x_buf, gain_buf, *table_bufs, semaphores, weight_buf, weight_semaphores = refs[10 + lanes :]
    copies = weight_copies(0, weight_hbm, weight_buf, weight_semaphores)
    tables = table_copies(table_hbms, table_bufs, semaphores, pieces + 1)

    def start_weights():
        for copy in copies:
            copy.start()

    norm_in_pieces(
        pieces, 0, x_hbm, gain_hbm, x_buf, gain_buf, semaphores, normed_ref, start_weights
    )
    for copy in tables:
        copy.wait()
    spots = message_refs[0].shape[0] // steps
    places, flow_places = places_from(table_bufs, spots, flow_most)
    places_ref[0:1, :] = places
    places_ref[1:2, :] = flow_places
    count = steps * rows
    own_ref = normed_ref.at[pl.ds(chunk * count, count)]
    pack_messages(steps, rows, places, own_ref, message_refs)
    project_blocks(0, copies, normed_ref, weight_buf, bias_ref, out_ref)


def project_kernel(begin, rows_ref, bias_ref, weight_hbm, out_ref, weight_buf, semaphores):
    copies = weight_copies(begin, weight_hbm, weight_buf, semaphores)
    for copy in copies:
        copy.start()
    project_blocks(begin, copies, rows_ref, weight_buf, bias_ref, out_ref)


def row_slots(shape, spots):
    return iota(shape, 0) % spots // MOST


def down_kernel(lanes, spots, *refs):
    message_refs, map_refs, partial_ref = refs[:lanes][::-1], refs[lanes:-1], refs[-1]
    local_slots = map_refs[0].shape[0]
    rows = jnp.concatenate([ref[...] for ref in message_refs], axis=0)
    own_slot = row_slots(partial_ref.shape, spots)
    total = jnp.zeros(partial_ref.shape, jnp.float32)
    for number, map_ref in enumerate(map_refs):
        shift = (lax.axis_index("sub") ^ number) * local_slots
        for slot in range(local_slots):
            part = jnp.dot(rows, map_ref[slot], preferred_element_type=jnp.float32)
            total = jnp.where(own_slot == shift + slot, part, total)
    partial_ref[...] = total


def up_kernel(heads, subs, spots, *refs):
    partial_refs, refs = refs[:heads], refs[heads:]
    query_refs, value_refs, message_refs = refs[:subs], refs[subs : 2 * subs], refs[2 * subs :]
    total = partial_refs[0][...]
    for ref in partial_refs[1:]:
        total = total + ref[...]
    latent = total.astype(jnp.bfloat16).astype(jnp.float32)
    own_slot = row_slots(latent.shape, spots)
    column = iota(latent.shape, 1) // ADAPTER_RANK
    turned = pltpu.roll(latent, ADAPTER_RANK, 1)
    low = iota(latent.shape, 1) < ADAPTER_RANK
    query_pair = jnp.where(low, latent, turned)
    value_pair = jnp.where(low, turned, latent)

    def product(pair, map_refs):
        result = None
        for number, map_ref in enumerate(map_refs):
            local_slots = map_ref.shape[0] // ADAPTER_RANK
            shift = (lax.axis_index("sub") ^ number) * local_slots
            pieces = []
            for slot in range(0, local_slots, 2):
                kept = jnp.where(own_slot == shift + slot + column, pair, 0.0)
                pieces.append(kept.astype(jnp.bfloat16))
            wide = jnp.concatenate(pieces, axis=1)
            part = jnp.dot(wide, map_ref[...], preferred_element_type=jnp.float32)
            result = part if result is None else result + part
        return result.astype(jnp.bfloat16)

    queries = product(query_pair, query_refs)
    values = product(value_pair, value_refs)
    query_width = queries.shape[1]
    per_message = message_refs[0].shape[0]
    for number, ref in enumerate(message_refs):
        span = slice(number * per_message, (number + 1) * per_message)
        ref[:, :query_width] = queries[span]
        ref[:, query_width:] = values[span]


def attend_kernel(before, steps, rows, cache, groups, lanes, subs, last, *refs):
    places_ref, length_ref, cos_ref, sin_ref, key_ref, value_ref = refs[:6]
    qkv_refs, refs = refs[6:9], refs[9:]
    delta_refs, refs = refs[:lanes][::-1], refs[lanes:]
    if before:
        earlier_ref, refs = refs[0], refs[1:]
    if not last:
        fresh_ref, refs = refs[0], refs[1:]
    message_refs = refs[:lanes]
    delta_ref, context_ref, bias_ref = refs[lanes:]
    per_message = delta_refs[0].shape[0]
    spots = per_message // steps
    query_width = PER_GROUP * HEAD_WIDTH
    known = before + steps

    def qkv_tile(span, group, head):
        begin = (group * (PER_GROUP + 2) + head) * HEAD_WIDTH
        for ref in qkv_refs:
            if begin < ref.shape[1]:
                return ref[span, begin : begin + HEAD_WIDTH]
            begin -= ref.shape[1]

    wide = groups * HEAD_WIDTH
    column = as_column(places_ref[0:1, :])
    column = jnp.concatenate([column] * steps, axis=0)
    shape = (steps * rows, lanes * per_message)
    out_row = iota(shape, 1)
    wanted = out_row // per_message * spots + out_row % spots
    pick = (wanted == column) & (out_row % per_message // spots == iota(shape, 0) // rows)
    pick = pick.astype(jnp.float32).astype(jnp.bfloat16)
    delta_ref[...] = jnp.dot(
        pick,
        jnp.concatenate([ref[...] for ref in delta_refs], axis=0),
        preferred_element_type=jnp.float32,
    )

    shape = (rows, BATCH * cache)
    lengths = as_column(length_ref[...])
    slot_column = iota(shape, 1)
    allowed = (slot_column // cache == iota(shape, 0) % BATCH) & (slot_column % cache < lengths)
    bias_ref[...] = jnp.where(allowed, 0.0, -1e30)
    shape = (steps, BATCH, known * BATCH)
    fresh_column = iota(shape, 2)
    allowed = (fresh_column % BATCH == iota(shape, 1)) & (
        fresh_column // BATCH <= iota(shape, 0) + before
    )
    fresh_bias = jnp.where(allowed, 0.0, -1e30)
    scale = HEAD_WIDTH ** (-0.5)
    transposed = (((1,), (1,)), ((), ()))

    def scored(first, group):
        spans = [pl.ds(pl.multiple_of(step * rows + first, BATCH), BATCH) for step in range(known)]
        query_tiles, key_tiles, value_tiles = [], [], []
        lane_span = slice(group * HEAD_WIDTH, (group + 1) * HEAD_WIDTH)
        value_span = slice(wide + group * HEAD_WIDTH, wide + (group + 1) * HEAD_WIDTH)
        for span in spans[:before]:
            key_tiles.append(earlier_ref[span, lane_span])
            value_tiles.append(earlier_ref[span, value_span])
        for span in spans[:steps]:
            cosine, sine_part = cos_ref[span, :], sin_ref[span, :]

            def rotated(values):
                return values * cosine + pltpu.roll(values, HEAD_WIDTH // 2, 1) * sine_part

            for head in range(PER_GROUP):
                begin = group * query_width + head * HEAD_WIDTH
                change = delta_ref[span, begin : begin + HEAD_WIDTH]
                query_tiles.append(rotated(qkv_tile(span, group, head) + change))
            key = rotated(qkv_tile(span, group, PER_GROUP))
            begin = groups * query_width + group * HEAD_WIDTH
            change = delta_ref[span, begin : begin + HEAD_WIDTH]
            value = qkv_tile(span, group, PER_GROUP + 1) + change
            if not last:
                fresh_ref[span, lane_span] = key
                fresh_ref[span, value_span] = value
            key_tiles.append(key)
            value_tiles.append(value)
        queries = jnp.concatenate(query_tiles, axis=0).astype(jnp.bfloat16)
        new_keys = jnp.concatenate(key_tiles, axis=0).astype(jnp.bfloat16)
        new_values = jnp.concatenate(value_tiles, axis=0).astype(jnp.bfloat16)
        old_keys = key_ref[pl.ds(first, BATCH), :, lane_span].reshape(BATCH * cache, HEAD_WIDTH)
        old_scores = lax.dot_general(
            queries, old_keys, transposed, preferred_element_type=jnp.float32
        )
        new_scores = lax.dot_general(
            queries, new_keys, transposed, preferred_element_type=jnp.float32
        )
        return old_scores, new_scores, new_values

    def weighed(first, old_scores, new_scores):
        heads = steps * PER_GROUP
        old_scores = (old_scores * scale).reshape(heads, BATCH, BATCH * cache)
        old_scores = old_scores + bias_ref[pl.ds(first, BATCH), :][None]
        new_scores = (new_scores * scale).reshape(steps, PER_GROUP, BATCH, known * BATCH)
        new_scores = (new_scores + fresh_bias[:, None]).reshape(heads, BATCH, known * BATCH)
        peak = jnp.maximum(
            jnp.max(old_scores, axis=-1, keepdims=True),
            jnp.max(new_scores, axis=-1, keepdims=True),
        )
        old_scores = jnp.exp(old_scores - peak)
        new_scores = jnp.exp(new_scores - peak)
        share = 1.0 / (
            jnp.sum(old_scores, axis=-1, keepdims=True)
            + jnp.sum(new_scores, axis=-1, keepdims=True)
        )
        old_weights = (old_scores * share).reshape(heads * BATCH, BATCH * cache)
        new_weights = (new_scores * share).reshape(heads * BATCH, known * BATCH)
        return old_weights.astype(jnp.bfloat16), new_weights.astype(jnp.bfloat16)

    def batch(index, carry):
        chains = []
        for number in range(TOGETHER):
            first = pl.multiple_of((index * TOGETHER + number) * BATCH, BATCH)
            chains += [(first, group) for group in range(groups)]
        scores = [scored(*chain) for chain in chains]
        weights = [weighed(chain[0], *score[:2]) for chain, score in zip(chains, scores)]
        for (first, group), (old_weights, new_weights), score in zip(chains, weights, scores):
            lane_span = slice(group * HEAD_WIDTH, (group + 1) * HEAD_WIDTH)
            old_values = value_ref[pl.ds(first, BATCH), :, lane_span]
            old_values = old_values.reshape(BATCH * cache, HEAD_WIDTH)
            context = jnp.dot(
                old_weights, old_values, preferred_element_type=jnp.float32
            ) + jnp.dot(new_weights, score[2], preferred_element_type=jnp.float32)
            for step in range(steps):
                span = pl.ds(pl.multiple_of(step * rows + first, BATCH), BATCH)
                for head in range(PER_GROUP):
                    row = (step * PER_GROUP + head) * BATCH
                    begin = group * query_width + head * HEAD_WIDTH
                    context_ref[span, begin : begin + HEAD_WIDTH] = context[row : row + BATCH]
        return carry

    lax.fori_loop(0, rows // (BATCH * TOGETHER), batch, 0)

    flow_places = jnp.concatenate([places_ref[1:2, :]] * steps, axis=1)
    context = context_ref[...].astype(jnp.bfloat16)
    count = message_refs[0].shape[0]
    shape = (count, steps * rows)
    out_row = iota(shape, 0)
    same_step = out_row % steps == iota(shape, 1) // rows
    for number, message_ref in enumerate(message_refs):
        wanted = number * (count // steps) + out_row // steps
        pick = ((flow_places == wanted) & same_step).astype(jnp.float32).astype(jnp.bfloat16)
        message_ref[...] = jnp.dot(
            pick, context, preferred_element_type=jnp.float32
        ).astype(jnp.bfloat16)


def place_kernel(found, lanes, subs, most, *refs):
    chunks = len(found)
    out_ref = refs[-1]
    steps = out_ref.shape[1]
    chunk_steps = steps // chunks
    block = most * chunk_steps
    here = lax.axis_index("streams")
    core = lax.axis_index("sub")
    shape = (chunks * block, chunks * block)
    out_row, in_row = iota(shape, 0), iota(shape, 1)
    step = out_row % steps
    wanted = step // chunk_steps * block + out_row // steps * chunk_steps + step % chunk_steps
    pick = (wanted == in_row).astype(jnp.float32).astype(jnp.bfloat16)
    for number in range(lanes):
        for other in range(subs):
            pieces = []
            for chunk in range(chunks):
                array, begin = found[chunk][number][other]
                pieces.append(refs[array][...][begin : begin + block])
            rows = jnp.dot(
                pick, jnp.concatenate(pieces, axis=0), preferred_element_type=jnp.float32
            )
            source = (here ^ number) * subs + (core ^ other)
            out_ref[pl.ds(source * most, most)] = rows.reshape(
                most, steps, rows.shape[1]
            ).astype(jnp.bfloat16)


def traded(blocks, axes):
    landed = list(blocks)
    count = len(blocks)
    order = sorted(range(1, count), key=lambda shift: -(shift ^ (shift >> 1)))
    for shift in order:
        pairs = [(place, place ^ shift) for place in range(count)]
        landed[shift] = lax.ppermute(blocks[shift], axes, pairs)
    return landed


def from_others(block, axis):
    count = lax.axis_size(axis)
    landed = [block]
    for shift in range(1, count):
        pairs = [(place, place ^ shift) for place in range(count)]
        landed.append(lax.ppermute(block, axis, pairs))
    return landed


def held(value, others):
    return lax.optimization_barrier((value, others))[0]


SMALL = pl.CostEstimate(flops=1, bytes_accessed=1, transcendentals=0)


def on_device(
    inputs,
    input_norm_gain,
    projection_weight,
    projection_bias,
    speaker,
    speaker_adapter_slot,
    cache_fill_length,
    rotated_key_cache,
    value_cache_rows,
    adapter_down_maps,
    adapter_query_up,
    adapter_value_up,
    flow_decoder_owner,
):
    steps, rows, width = inputs.shape
    lanes = lax.axis_size("streams")
    subs = lax.axis_size("sub")
    heads = lax.axis_size("heads")
    flow_lanes = lanes * subs
    local_slots, sliced, _ = adapter_down_maps.shape
    query_columns = adapter_query_up.shape[2]
    value_columns = adapter_value_up.shape[2]
    groups = value_columns // HEAD_WIDTH
    cache = rotated_key_cache.shape[1]
    spots = subs * local_slots * MOST
    chunks = 2
    chunk_steps = steps // chunks
    chunk_rows = chunk_steps * rows
    per_message = chunk_steps * spots
    chip_slots = subs * local_slots
    flow_most = max(2, (2 * rows + flow_lanes - 1) // flow_lanes)
    bf16, f32 = jnp.bfloat16, jnp.float32

    def whole(shape):
        return pl.BlockSpec(shape, lambda i: (0,) * len(shape))

    in_hbm = pl.BlockSpec(memory_space=pltpu.HBM)

    down_maps = from_others(adapter_down_maps, "sub")
    query_maps = from_others(
        adapter_query_up.reshape(local_slots * ADAPTER_RANK, query_columns), "sub"
    )
    value_maps = from_others(
        adapter_value_up.reshape(local_slots * ADAPTER_RANK, value_columns), "sub"
    )

    pieces = 4
    flat = inputs.reshape(steps * rows, width)
    gain = input_norm_gain.reshape(width // 128, 128)
    message = jax.ShapeDtypeStruct((per_message, sliced), bf16)
    places_shape = jax.ShapeDtypeStruct((8, rows), jnp.int32)
    tables = [
        speaker.reshape(1, rows),
        speaker_adapter_slot.reshape(1, -1),
        flow_decoder_owner.reshape(1, rows),
    ]

    def row_buffers(count):
        return (
            [pltpu.VMEM((count, width), bf16), pltpu.VMEM(gain.shape, f32)]
            + [pltpu.VMEM(table.shape, jnp.int32) for table in tables]
            + [pltpu.SemaphoreType.DMA((pieces + 4,))]
        )

    messages = pl.pallas_call(
        functools.partial(norm_pack_kernel, chunk_steps, rows, flow_most, lanes, pieces),
        in_specs=[in_hbm] * 5,
        out_specs=[VMEM] * lanes,
        out_shape=[message] * lanes,
        scratch_shapes=row_buffers(chunk_rows) + [pltpu.VMEM((chunk_rows, width), bf16)],
        compiler_params=pltpu.CompilerParams(vmem_limit_bytes=PACK_LIMIT * MIB),
        cost_estimate=SMALL,
        name="norm_and_pack",
    )(*tables, gain, flat)
    arrived = [traded(messages, "streams")]

    bias = projection_bias.reshape(-1, 128)
    columns = projection_weight.shape[1]
    block_columns = 256 if columns % 256 == 0 else 384
    blocks = columns // block_columns
    cuts = [4, 6, 9] if blocks == 9 else [blocks // 3, 2 * blocks // 3, blocks]
    cut = cuts[0]

    def weight_buffers(count):
        return [
            pltpu.VMEM((count, width, block_columns), bf16),
            pltpu.SemaphoreType.DMA((count,)),
        ]

    def projected(count):
        return jax.ShapeDtypeStruct((steps * rows, count * block_columns), f32)

    adapters = down_maps[1:], query_maps[1:], value_maps[1:]
    weight_buf, weight_semaphores = weight_buffers(cut)
    normed, first_qkv, places, *messages = pl.pallas_call(
        functools.partial(
            norm_pack_project_kernel, chunk_steps, rows, flow_most, lanes, 2 * pieces, 1
        ),
        in_specs=[in_hbm] * 3 + [VMEM] + [in_hbm] * 3,
        out_specs=[VMEM] * (3 + lanes),
        out_shape=[jax.ShapeDtypeStruct((steps * rows, width), bf16), projected(cut)]
        + [places_shape]
        + [message] * lanes,
        scratch_shapes=row_buffers(steps * rows)[:-1]
        + [pltpu.SemaphoreType.DMA((2 * pieces + 4,))]
        + [weight_buf, weight_semaphores],
        compiler_params=pltpu.CompilerParams(vmem_limit_bytes=PROJECT_LIMIT * MIB),
        cost_estimate=SMALL,
        name="norm_pack_project",
    )(*tables, held(bias, (adapters, messages)), gain, flat, projection_weight)
    arrived.append(traded(messages, "streams"))
    qkv = [first_qkv]

    def project(after):
        begin, end = cuts[len(qkv) - 1 : len(qkv) + 1]
        return pl.pallas_call(
            functools.partial(project_kernel, begin),
            in_specs=[VMEM, VMEM, in_hbm],
            out_specs=VMEM,
            out_shape=projected(end - begin),
            scratch_shapes=weight_buffers(end - begin),
            compiler_params=pltpu.CompilerParams(vmem_limit_bytes=PROJECT_LIMIT * MIB),
            cost_estimate=SMALL,
            name="project",
        )(normed, held(bias, after), projection_weight)

    def down(chunk, after):
        partial_latent = pl.pallas_call(
            functools.partial(down_kernel, lanes, spots),
            in_specs=[VMEM] * (lanes + subs),
            out_specs=VMEM,
            out_shape=jax.ShapeDtypeStruct((lanes * per_message, 2 * ADAPTER_RANK), f32),
            compiler_params=pltpu.CompilerParams(vmem_limit_bytes=16 * MIB),
            cost_estimate=SMALL,
            name="down",
        )(*arrived[chunk][:0:-1], held(arrived[chunk][0], after), *down_maps)
        return from_others(partial_latent, "heads")

    def up(partials, after):
        message = jax.ShapeDtypeStruct((per_message, query_columns + value_columns), bf16)
        messages = pl.pallas_call(
            functools.partial(up_kernel, heads, subs, spots),
            in_specs=[VMEM] * (heads + 2 * subs),
            out_specs=[VMEM] * lanes,
            out_shape=[message] * lanes,
            compiler_params=pltpu.CompilerParams(vmem_limit_bytes=24 * MIB),
            cost_estimate=SMALL,
            name="up",
        )(held(partials[0], after), *partials[1:], *query_maps, *value_maps)
        return messages

    half_width = HEAD_WIDTH // 2
    position = jnp.concatenate([cache_fill_length + step for step in range(steps)]).astype(f32)
    freq = jnp.exp(jnp.arange(half_width, dtype=f32) * (-math.log(1000000.0) / half_width))
    freq = jnp.concatenate([freq, freq])
    angle = position[:, None] * freq
    sign = jnp.where(jnp.arange(HEAD_WIDTH) < half_width, -1.0, 1.0).astype(f32)
    cosine = jnp.cos(angle)
    sine_part = jnp.sin(angle) * sign

    returned = []
    after = qkv
    for chunk in range(chunks):
        partials = down(chunk, after)
        qkv.append(project(partials[0]))
        after = up(partials, qkv)
        messages = list(after)
        if chunk:
            for lane in range(1, lanes):
                messages[lane] = held(messages[lane], returned[-1][min(lane + 1, lanes - 1)])
        returned.append(traded(messages, "streams"))

    length_row = cache_fill_length.reshape(1, rows)
    block = flow_most * chunk_steps
    earlier, along, alongs = [], [], []
    for chunk in range(chunks):
        last = chunk == chunks - 1
        message = jax.ShapeDtypeStruct((subs * block, query_columns), bf16)
        fresh = jax.ShapeDtypeStruct((chunk_rows, 2 * value_columns), f32)
        rows_of = lambda shape: pl.BlockSpec(shape, lambda i, chunk=chunk: (chunk, 0))
        results = pl.pallas_call(
            functools.partial(
                attend_kernel,
                chunk * chunk_steps,
                chunk_steps,
                rows,
                cache,
                groups,
                lanes,
                subs,
                last,
            ),
            grid=(1,),
            in_specs=[whole(places.shape), whole(length_row.shape)]
            + [rows_of((chunk_rows, HEAD_WIDTH))] * 2
            + [whole(rotated_key_cache.shape)] * 2
            + [rows_of((chunk_rows, part.shape[1])) for part in qkv]
            + [whole((per_message, query_columns + value_columns))] * lanes
            + [whole(block_rows.shape) for block_rows in earlier],
            out_specs=[whole(fresh.shape)] * (not last) + [whole(message.shape)] * lanes,
            out_shape=[fresh] * (not last) + [message] * lanes,
            scratch_shapes=[
                pltpu.VMEM((chunk_rows, query_columns + value_columns), f32),
                pltpu.VMEM((chunk_rows, query_columns), f32),
                pltpu.VMEM((rows, BATCH * cache), f32),
            ],
            compiler_params=pltpu.CompilerParams(vmem_limit_bytes=32 * MIB),
            cost_estimate=SMALL,
            name="attend",
        )(
            places if chunk else held(places, after),
            length_row,
            cosine,
            sine_part,
            rotated_key_cache,
            value_cache_rows,
            *qkv,
            *returned[chunk][::-1],
            *earlier,
        )
        if not last:
            earlier, results = [results[0]], results[1:]
        results = list(results)
        for lane in range(1, lanes):
            if not alongs:
                results[lane] = held(results[lane], returned[-1][lanes - lane])
        along = traded(results, "streams")
        alongs.append(along)

    landed, found = [], []
    for chunk, along in enumerate(alongs):
        base = len(landed)
        landed += along
        where = [[(base + lane, 0)] for lane in range(lanes)]
        for shift in range(1, subs):
            pairs = [(core, core ^ shift) for core in range(subs)]
            span = slice(shift * block, (shift + 1) * block)
            if chunk < chunks - 1:
                joined = jnp.concatenate([block_rows[span] for block_rows in along])
                for lane in range(lanes):
                    where[lane].append((len(landed), lane * block))
                landed.append(lax.ppermute(joined, "sub", pairs))
            else:
                for lane, block_rows in enumerate(along):
                    where[lane].append((len(landed), shift * block))
                    landed.append(lax.ppermute(block_rows, "sub", pairs))
        found.append(where)

    flow = pl.pallas_call(
        functools.partial(place_kernel, found, lanes, subs, flow_most),
        in_specs=[VMEM] * len(landed),
        out_specs=VMEM,
        out_shape=jax.ShapeDtypeStruct((flow_lanes * flow_most, steps, query_columns), bf16),
        compiler_params=pltpu.CompilerParams(vmem_limit_bytes=24 * MIB),
        cost_estimate=SMALL,
        name="place",
    )(*landed)
    return flow[None]


def solution(mesh):
    placed = (
        P(None, ("groups", "streams", "sub"), None),
        P(),
        P(None, "heads"),
        P("heads"),
        P(("groups", "streams", "sub"), None),
        P("groups"),
        P(("groups", "streams", "sub")),
        P(("groups", "streams", "sub"), None, "heads"),
        P(("groups", "streams", "sub"), None, "heads"),
        P(("groups", "streams", "sub"), "heads", None),
        P(("groups", "streams", "sub"), None, "heads"),
        P(("groups", "streams", "sub"), None, "heads"),
        P(("groups", "streams", "sub"), None),
    )
    return jax.shard_map(
        on_device,
        mesh=mesh,
        in_specs=placed,
        out_specs=P(("groups", "streams", "sub"), None, None, "heads"),
        check_vma=False,
    )
```

```python
import functools
import math

import jax
import jax.numpy as jnp
from jax import lax
from jax.experimental import pallas as pl
from jax.experimental.pallas import tpu as pltpu
from jax.sharding import PartitionSpec as P

QUERY_HEADS = 28
KEY_VALUE_HEADS = 4
HEAD_WIDTH = 128
ADAPTER_RANK = 64
MOST = 2
PER_GROUP = QUERY_HEADS // KEY_VALUE_HEADS
LANE_AXES = ("streams", "sub")
BATCH = 8
TOGETHER = 2
VMEM = pl.BlockSpec(memory_space=pltpu.VMEM)
MIB = 1 << 20
PACK_LIMIT = 56
PROJECT_LIMIT = 49


def iota(shape, dim):
    return lax.broadcasted_iota(jnp.int32, shape, dim)


def as_column(row):
    count = row.shape[1]
    square = (count, count)
    same = iota(square, 0) == iota(square, 1)
    return jnp.sum(jnp.where(same, jnp.broadcast_to(row, square), 0), axis=1, keepdims=True)


def ranked(labels, most):
    count = labels.shape[1]
    square = (count, count)
    earlier = (as_column(labels) == labels) & (iota(square, 0) < iota(square, 1))
    return labels * most + jnp.sum(earlier.astype(jnp.int32), axis=0, keepdims=True)


def slot_places(speaker, table, lane_base):
    speakers_all = table.shape[1]
    rows = speaker.shape[1]
    match = iota((speakers_all, rows), 0) == speaker
    slots = jnp.sum(jnp.where(match, as_column(table), 0), axis=0, keepdims=True)
    return ranked(slots ^ lane_base, MOST)


def norm_in_pieces(
    pieces, begin, x_hbm, gain_hbm, x_buf, gain_buf, semaphores, normed_ref, started=None
):
    count, width = x_buf.shape
    size = count // pieces
    gain_copy = pltpu.make_async_copy(gain_hbm, gain_buf, semaphores.at[pieces])
    copies = []
    for piece in range(pieces):
        copies.append(
            pltpu.make_async_copy(
                x_hbm.at[pl.ds(begin + piece * size, size)],
                x_buf.at[pl.ds(piece * size, size)],
                semaphores.at[piece],
            )
        )
        copies[-1].start()
        if piece == 0:
            gain_copy.start()
    if started is not None:
        started()
    gain_copy.wait()
    gain = jnp.concatenate([gain_buf[i : i + 1, :] for i in range(gain_buf.shape[0])], axis=1)
    for piece in range(pieces):
        copies[piece].wait()

        def one(index, carry):
            span = pl.ds(pl.multiple_of(piece * size + index * 16, 16), 16)
            values = x_buf[span, :].astype(jnp.float32)
            mean_sq = jnp.sum(values * values, axis=1, keepdims=True) * (1.0 / width)
            normed = values * lax.rsqrt(mean_sq + 1e-06) * gain
            normed_ref[span, :] = normed.astype(jnp.bfloat16)
            return carry

        lax.fori_loop(0, size // 16, one, 0)


def pack_messages(steps, rows, places, normed_ref, message_refs):
    per_message, sliced = message_refs[0].shape
    spots = per_message // steps
    shape = (len(message_refs) * per_message, steps * rows)
    out_row = iota(shape, 0)
    wanted = out_row // per_message * spots + out_row % spots
    out_step = out_row % per_message // spots
    places = jnp.concatenate([places] * steps, axis=1)
    pick = (wanted == places) & (out_step == iota(shape, 1) // rows)
    pick = pick.astype(jnp.float32).astype(jnp.bfloat16)
    begin = pl.multiple_of(lax.axis_index("heads") * sliced, 128)
    own = normed_ref[:, pl.ds(begin, sliced)]
    packed = jnp.dot(pick, own, preferred_element_type=jnp.float32).astype(jnp.bfloat16)
    for number, message_ref in enumerate(message_refs):
        message_ref[...] = packed[number * per_message : (number + 1) * per_message]


def table_copies(table_hbms, table_bufs, semaphores, first):
    copies = [
        pltpu.make_async_copy(source, target, semaphores.at[first + number])
        for number, (source, target) in enumerate(zip(table_hbms, table_bufs))
    ]
    for copy in copies:
        copy.start()
    return copies


def places_from(table_bufs, spots, flow_most):
    speaker, table, owner = [buffer[...] for buffer in table_bufs]
    here, core, subs = lax.axis_index("streams"), lax.axis_index("sub"), lax.axis_size("sub")
    places = slot_places(speaker, table, here * (spots // MOST))
    return places, ranked(owner ^ (here * subs + core), flow_most)


def norm_pack_kernel(steps, rows, flow_most, lanes, pieces, *refs):
    table_hbms, gain_hbm, x_hbm, message_refs = refs[:3], refs[3], refs[4], refs[5 : 5 + lanes]
    x_buf, gain_buf, *table_bufs, semaphores, normed_ref = refs[5 + lanes :]
    copies = table_copies(table_hbms, table_bufs, semaphores, pieces + 1)
    norm_in_pieces(pieces, 0, x_hbm, gain_hbm, x_buf, gain_buf, semaphores, normed_ref)
    for copy in copies:
        copy.wait()
    spots = message_refs[0].shape[0] // steps
    places, _ = places_from(table_bufs, spots, flow_most)
    pack_messages(steps, rows, places, normed_ref, message_refs)


def weight_copies(begin, weight_hbm, weight_buf, semaphores):
    columns = weight_buf.shape[2]
    return [
        pltpu.make_async_copy(
            weight_hbm.at[:, pl.ds((begin + block) * columns, columns)],
            weight_buf.at[block],
            semaphores.at[block],
        )
        for block in range(weight_buf.shape[0])
    ]


def project_blocks(begin, copies, rows_ref, weight_buf, bias_ref, out_ref):
    columns = weight_buf.shape[2]
    tiles = columns // 128
    for block, copy in enumerate(copies):
        first = (begin + block) * tiles
        bias = [bias_ref[tile : tile + 1, :] for tile in range(first, first + tiles)]
        copy.wait()
        product = jnp.dot(rows_ref[...], weight_buf[block], preferred_element_type=jnp.float32)
        out_ref[:, block * columns : (block + 1) * columns] = product + jnp.concatenate(
            bias, axis=1
        )


def norm_pack_project_kernel(steps, rows, flow_most, lanes, pieces, chunk, *refs):
    table_hbms, bias_ref, gain_hbm, x_hbm, weight_hbm = refs[:3], *refs[3:7]
    normed_ref, out_ref, places_ref, message_refs = *refs[7:10], refs[10 : 10 + lanes]
    x_buf, gain_buf, *table_bufs, semaphores, weight_buf, weight_semaphores = refs[10 + lanes :]
    copies = weight_copies(0, weight_hbm, weight_buf, weight_semaphores)
    tables = table_copies(table_hbms, table_bufs, semaphores, pieces + 1)

    def start_weights():
        for copy in copies:
            copy.start()

    norm_in_pieces(
        pieces, 0, x_hbm, gain_hbm, x_buf, gain_buf, semaphores, normed_ref, start_weights
    )
    for copy in tables:
        copy.wait()
    spots = message_refs[0].shape[0] // steps
    places, flow_places = places_from(table_bufs, spots, flow_most)
    places_ref[0:1, :] = places
    places_ref[1:2, :] = flow_places
    count = steps * rows
    own_ref = normed_ref.at[pl.ds(chunk * count, count)]
    pack_messages(steps, rows, places, own_ref, message_refs)
    project_blocks(0, copies, normed_ref, weight_buf, bias_ref, out_ref)


def project_kernel(begin, rows_ref, bias_ref, weight_hbm, out_ref, weight_buf, semaphores):
    copies = weight_copies(begin, weight_hbm, weight_buf, semaphores)
    for copy in copies:
        copy.start()
    project_blocks(begin, copies, rows_ref, weight_buf, bias_ref, out_ref)


def row_slots(shape, spots):
    return iota(shape, 0) % spots // MOST


def down_kernel(lanes, spots, *refs):
    message_refs, map_refs, partial_ref = refs[:lanes][::-1], refs[lanes:-1], refs[-1]
    local_slots = map_refs[0].shape[0]
    rows = jnp.concatenate([ref[...] for ref in message_refs], axis=0)
    own_slot = row_slots(partial_ref.shape, spots)
    total = jnp.zeros(partial_ref.shape, jnp.float32)
    for number, map_ref in enumerate(map_refs):
        shift = (lax.axis_index("sub") ^ number) * local_slots
        for slot in range(local_slots):
            part = jnp.dot(rows, map_ref[slot], preferred_element_type=jnp.float32)
            total = jnp.where(own_slot == shift + slot, part, total)
    partial_ref[...] = total


def up_kernel(heads, subs, spots, *refs):
    partial_refs, refs = refs[:heads], refs[heads:]
    query_refs, value_refs, message_refs = refs[:subs], refs[subs : 2 * subs], refs[2 * subs :]
    total = partial_refs[0][...]
    for ref in partial_refs[1:]:
        total = total + ref[...]
    latent = total.astype(jnp.bfloat16).astype(jnp.float32)
    own_slot = row_slots(latent.shape, spots)
    column = iota(latent.shape, 1) // ADAPTER_RANK
    turned = pltpu.roll(latent, ADAPTER_RANK, 1)
    low = iota(latent.shape, 1) < ADAPTER_RANK
    query_pair = jnp.where(low, latent, turned)
    value_pair = jnp.where(low, turned, latent)

    def product(pair, map_refs):
        result = None
        for number, map_ref in enumerate(map_refs):
            local_slots = map_ref.shape[0] // ADAPTER_RANK
            shift = (lax.axis_index("sub") ^ number) * local_slots
            pieces = []
            for slot in range(0, local_slots, 2):
                kept = jnp.where(own_slot == shift + slot + column, pair, 0.0)
                pieces.append(kept.astype(jnp.bfloat16))
            wide = jnp.concatenate(pieces, axis=1)
            part = jnp.dot(wide, map_ref[...], preferred_element_type=jnp.float32)
            result = part if result is None else result + part
        return result.astype(jnp.bfloat16)

    queries = product(query_pair, query_refs)
    values = product(value_pair, value_refs)
    query_width = queries.shape[1]
    per_message = message_refs[0].shape[0]
    for number, ref in enumerate(message_refs):
        span = slice(number * per_message, (number + 1) * per_message)
        ref[:, :query_width] = queries[span]
        ref[:, query_width:] = values[span]


def attend_kernel(before, steps, rows, cache, groups, lanes, subs, last, *refs):
    places_ref, length_ref, cos_ref, sin_ref, key_ref, value_ref = refs[:6]
    qkv_refs, refs = refs[6:9], refs[9:]
    delta_refs, refs = refs[:lanes][::-1], refs[lanes:]
    if before:
        earlier_ref, refs = refs[0], refs[1:]
    if not last:
        fresh_ref, refs = refs[0], refs[1:]
    message_refs = refs[:lanes]
    delta_ref, context_ref, bias_ref = refs[lanes:]
    per_message = delta_refs[0].shape[0]
    spots = per_message // steps
    query_width = PER_GROUP * HEAD_WIDTH
    known = before + steps

    def qkv_tile(span, group, head):
        begin = (group * (PER_GROUP + 2) + head) * HEAD_WIDTH
        for ref in qkv_refs:
            if begin < ref.shape[1]:
                return ref[span, begin : begin + HEAD_WIDTH]
            begin -= ref.shape[1]

    wide = groups * HEAD_WIDTH
    column = as_column(places_ref[0:1, :])
    column = jnp.concatenate([column] * steps, axis=0)
    shape = (steps * rows, lanes * per_message)
    out_row = iota(shape, 1)
    wanted = out_row // per_message * spots + out_row % spots
    pick = (wanted == column) & (out_row % per_message // spots == iota(shape, 0) // rows)
    pick = pick.astype(jnp.float32).astype(jnp.bfloat16)
    delta_ref[...] = jnp.dot(
        pick,
        jnp.concatenate([ref[...] for ref in delta_refs], axis=0),
        preferred_element_type=jnp.float32,
    )

    shape = (rows, BATCH * cache)
    lengths = as_column(length_ref[...])
    slot_column = iota(shape, 1)
    allowed = (slot_column // cache == iota(shape, 0) % BATCH) & (slot_column % cache < lengths)
    bias_ref[...] = jnp.where(allowed, 0.0, -1e30)
    shape = (steps, BATCH, known * BATCH)
    fresh_column = iota(shape, 2)
    allowed = (fresh_column % BATCH == iota(shape, 1)) & (
        fresh_column // BATCH <= iota(shape, 0) + before
    )
    fresh_bias = jnp.where(allowed, 0.0, -1e30)
    scale = HEAD_WIDTH ** (-0.5)
    transposed = (((1,), (1,)), ((), ()))

    def scored(first, group):
        spans = [pl.ds(pl.multiple_of(step * rows + first, BATCH), BATCH) for step in range(known)]
        query_tiles, key_tiles, value_tiles = [], [], []
        lane_span = slice(group * HEAD_WIDTH, (group + 1) * HEAD_WIDTH)
        value_span = slice(wide + group * HEAD_WIDTH, wide + (group + 1) * HEAD_WIDTH)
        for span in spans[:before]:
            key_tiles.append(earlier_ref[span, lane_span])
            value_tiles.append(earlier_ref[span, value_span])
        for span in spans[:steps]:
            cosine, sine_part = cos_ref[span, :], sin_ref[span, :]

            def rotated(values):
                return values * cosine + pltpu.roll(values, HEAD_WIDTH // 2, 1) * sine_part

            for head in range(PER_GROUP):
                begin = group * query_width + head * HEAD_WIDTH
                change = delta_ref[span, begin : begin + HEAD_WIDTH]
                query_tiles.append(rotated(qkv_tile(span, group, head) + change))
            key = rotated(qkv_tile(span, group, PER_GROUP))
            begin = groups * query_width + group * HEAD_WIDTH
            change = delta_ref[span, begin : begin + HEAD_WIDTH]
            value = qkv_tile(span, group, PER_GROUP + 1) + change
            if not last:
                fresh_ref[span, lane_span] = key
                fresh_ref[span, value_span] = value
            key_tiles.append(key)
            value_tiles.append(value)
        queries = jnp.concatenate(query_tiles, axis=0).astype(jnp.bfloat16)
        new_keys = jnp.concatenate(key_tiles, axis=0).astype(jnp.bfloat16)
        new_values = jnp.concatenate(value_tiles, axis=0).astype(jnp.bfloat16)
        old_keys = key_ref[pl.ds(first, BATCH), :, lane_span].reshape(BATCH * cache, HEAD_WIDTH)
        old_scores = lax.dot_general(
            queries, old_keys, transposed, preferred_element_type=jnp.float32
        )
        new_scores = lax.dot_general(
            queries, new_keys, transposed, preferred_element_type=jnp.float32
        )
        return old_scores, new_scores, new_values

    def weighed(first, old_scores, new_scores):
        heads = steps * PER_GROUP
        old_scores = (old_scores * scale).reshape(heads, BATCH, BATCH * cache)
        old_scores = old_scores + bias_ref[pl.ds(first, BATCH), :][None]
        new_scores = (new_scores * scale).reshape(steps, PER_GROUP, BATCH, known * BATCH)
        new_scores = (new_scores + fresh_bias[:, None]).reshape(heads, BATCH, known * BATCH)
        peak = jnp.maximum(
            jnp.max(old_scores, axis=-1, keepdims=True),
            jnp.max(new_scores, axis=-1, keepdims=True),
        )
        old_scores = jnp.exp(old_scores - peak)
        new_scores = jnp.exp(new_scores - peak)
        share = 1.0 / (
            jnp.sum(old_scores, axis=-1, keepdims=True)
            + jnp.sum(new_scores, axis=-1, keepdims=True)
        )
        old_weights = (old_scores * share).reshape(heads * BATCH, BATCH * cache)
        new_weights = (new_scores * share).reshape(heads * BATCH, known * BATCH)
        return old_weights.astype(jnp.bfloat16), new_weights.astype(jnp.bfloat16)

    def batch(index, carry):
        chains = []
        for number in range(TOGETHER):
            first = pl.multiple_of((index * TOGETHER + number) * BATCH, BATCH)
            chains += [(first, group) for group in range(groups)]
        scores = [scored(*chain) for chain in chains]
        weights = [weighed(chain[0], *score[:2]) for chain, score in zip(chains, scores)]
        for (first, group), (old_weights, new_weights), score in zip(chains, weights, scores):
            lane_span = slice(group * HEAD_WIDTH, (group + 1) * HEAD_WIDTH)
            old_values = value_ref[pl.ds(first, BATCH), :, lane_span]
            old_values = old_values.reshape(BATCH * cache, HEAD_WIDTH)
            context = jnp.dot(
                old_weights, old_values, preferred_element_type=jnp.float32
            ) + jnp.dot(new_weights, score[2], preferred_element_type=jnp.float32)
            for step in range(steps):
                span = pl.ds(pl.multiple_of(step * rows + first, BATCH), BATCH)
                for head in range(PER_GROUP):
                    row = (step * PER_GROUP + head) * BATCH
                    begin = group * query_width + head * HEAD_WIDTH
                    context_ref[span, begin : begin + HEAD_WIDTH] = context[row : row + BATCH]
        return carry

    lax.fori_loop(0, rows // (BATCH * TOGETHER), batch, 0)

    flow_places = jnp.concatenate([places_ref[1:2, :]] * steps, axis=1)
    context = context_ref[...].astype(jnp.bfloat16)
    count = message_refs[0].shape[0]
    shape = (count, steps * rows)
    out_row = iota(shape, 0)
    same_step = out_row % steps == iota(shape, 1) // rows
    for number, message_ref in enumerate(message_refs):
        wanted = number * (count // steps) + out_row // steps
        pick = ((flow_places == wanted) & same_step).astype(jnp.float32).astype(jnp.bfloat16)
        message_ref[...] = jnp.dot(
            pick, context, preferred_element_type=jnp.float32
        ).astype(jnp.bfloat16)


def place_kernel(found, lanes, subs, most, *refs):
    chunks = len(found)
    out_ref = refs[-1]
    steps = out_ref.shape[1]
    chunk_steps = steps // chunks
    block = most * chunk_steps
    here = lax.axis_index("streams")
    core = lax.axis_index("sub")
    shape = (chunks * block, chunks * block)
    out_row, in_row = iota(shape, 0), iota(shape, 1)
    step = out_row % steps
    wanted = step // chunk_steps * block + out_row // steps * chunk_steps + step % chunk_steps
    pick = (wanted == in_row).astype(jnp.float32).astype(jnp.bfloat16)
    for number in range(lanes):
        for other in range(subs):
            pieces = []
            for chunk in range(chunks):
                array, begin = found[chunk][number][other]
                pieces.append(refs[array][...][begin : begin + block])
            rows = jnp.dot(
                pick, jnp.concatenate(pieces, axis=0), preferred_element_type=jnp.float32
            )
            source = (here ^ number) * subs + (core ^ other)
            rows = rows.astype(jnp.bfloat16)
            out_ref[pl.ds(source * most, most)] = rows.reshape(most, steps, rows.shape[1])


def traded(blocks, axes):
    landed = list(blocks)
    count = len(blocks)
    order = sorted(range(1, count), key=lambda shift: -(shift ^ (shift >> 1)))
    for shift in order:
        pairs = [(place, place ^ shift) for place in range(count)]
        landed[shift] = lax.ppermute(blocks[shift], axes, pairs)
    return landed


def from_others(block, axis):
    count = lax.axis_size(axis)
    landed = [block]
    for shift in range(1, count):
        pairs = [(place, place ^ shift) for place in range(count)]
        landed.append(lax.ppermute(block, axis, pairs))
    return landed


def held(value, others):
    return lax.optimization_barrier((value, others))[0]


SMALL = pl.CostEstimate(flops=1, bytes_accessed=1, transcendentals=0)


def on_device(
    inputs,
    input_norm_gain,
    projection_weight,
    projection_bias,
    speaker,
    speaker_adapter_slot,
    cache_fill_length,
    rotated_key_cache,
    value_cache_rows,
    adapter_down_maps,
    adapter_query_up,
    adapter_value_up,
    flow_decoder_owner,
):
    steps, rows, width = inputs.shape
    lanes = lax.axis_size("streams")
    subs = lax.axis_size("sub")
    heads = lax.axis_size("heads")
    flow_lanes = lanes * subs
    local_slots, sliced, _ = adapter_down_maps.shape
    query_columns = adapter_query_up.shape[2]
    value_columns = adapter_value_up.shape[2]
    groups = value_columns // HEAD_WIDTH
    cache = rotated_key_cache.shape[1]
    spots = subs * local_slots * MOST
    chunks = 2
    chunk_steps = steps // chunks
    chunk_rows = chunk_steps * rows
    per_message = chunk_steps * spots
    chip_slots = subs * local_slots
    flow_most = max(2, (2 * rows + flow_lanes - 1) // flow_lanes)
    bf16, f32 = jnp.bfloat16, jnp.float32

    def whole(shape):
        return pl.BlockSpec(shape, lambda i: (0,) * len(shape))

    in_hbm = pl.BlockSpec(memory_space=pltpu.HBM)

    down_maps = from_others(adapter_down_maps, "sub")
    query_maps = from_others(
        adapter_query_up.reshape(local_slots * ADAPTER_RANK, query_columns), "sub"
    )
    value_maps = from_others(
        adapter_value_up.reshape(local_slots * ADAPTER_RANK, value_columns), "sub"
    )

    pieces = 4
    flat = inputs.reshape(steps * rows, width)
    gain = input_norm_gain.reshape(width // 128, 128)
    message = jax.ShapeDtypeStruct((per_message, sliced), bf16)
    places_shape = jax.ShapeDtypeStruct((8, rows), jnp.int32)
    tables = [
        speaker.reshape(1, rows),
        speaker_adapter_slot.reshape(1, -1),
        flow_decoder_owner.reshape(1, rows),
    ]

    def row_buffers(count):
        return (
            [pltpu.VMEM((count, width), bf16), pltpu.VMEM(gain.shape, f32)]
            + [pltpu.VMEM(table.shape, jnp.int32) for table in tables]
            + [pltpu.SemaphoreType.DMA((pieces + 4,))]
        )

    messages = pl.pallas_call(
        functools.partial(norm_pack_kernel, chunk_steps, rows, flow_most, lanes, pieces),
        in_specs=[in_hbm] * 5,
        out_specs=[VMEM] * lanes,
        out_shape=[message] * lanes,
        scratch_shapes=row_buffers(chunk_rows) + [pltpu.VMEM((chunk_rows, width), bf16)],
        compiler_params=pltpu.CompilerParams(vmem_limit_bytes=PACK_LIMIT * MIB),
        cost_estimate=SMALL,
        name="norm_and_pack",
    )(*tables, gain, flat)
    arrived = [traded(messages, "streams")]

    bias = projection_bias.reshape(-1, 128)
    columns = projection_weight.shape[1]
    block_columns = 256 if columns % 256 == 0 else 384
    blocks = columns // block_columns
    cuts = [4, 6, 9] if blocks == 9 else [blocks // 3, 2 * blocks // 3, blocks]
    cut = cuts[0]

    def weight_buffers(count):
        return [
            pltpu.VMEM((count, width, block_columns), bf16),
            pltpu.SemaphoreType.DMA((count,)),
        ]

    def projected(count):
        return jax.ShapeDtypeStruct((steps * rows, count * block_columns), f32)

    adapters = down_maps[1:], query_maps[1:], value_maps[1:]
    weight_buf, weight_semaphores = weight_buffers(cut)
    normed, first_qkv, places, *messages = pl.pallas_call(
        functools.partial(
            norm_pack_project_kernel, chunk_steps, rows, flow_most, lanes, 2 * pieces, 1
        ),
        in_specs=[in_hbm] * 3 + [VMEM] + [in_hbm] * 3,
        out_specs=[VMEM] * (3 + lanes),
        out_shape=[jax.ShapeDtypeStruct((steps * rows, width), bf16), projected(cut)]
        + [places_shape]
        + [message] * lanes,
        scratch_shapes=row_buffers(steps * rows)[:-1]
        + [pltpu.SemaphoreType.DMA((2 * pieces + 4,))]
        + [weight_buf, weight_semaphores],
        compiler_params=pltpu.CompilerParams(vmem_limit_bytes=PROJECT_LIMIT * MIB),
        cost_estimate=SMALL,
        name="norm_pack_project",
    )(*tables, held(bias, (adapters, messages)), gain, flat, projection_weight)
    arrived.append(traded(messages, "streams"))
    qkv = [first_qkv]

    def project(after):
        begin, end = cuts[len(qkv) - 1 : len(qkv) + 1]
        return pl.pallas_call(
            functools.partial(project_kernel, begin),
            in_specs=[VMEM, VMEM, in_hbm],
            out_specs=VMEM,
            out_shape=projected(end - begin),
            scratch_shapes=weight_buffers(end - begin),
            compiler_params=pltpu.CompilerParams(vmem_limit_bytes=PROJECT_LIMIT * MIB),
            cost_estimate=SMALL,
            name="project",
        )(normed, held(bias, after), projection_weight)

    def down(chunk, after):
        partial_latent = pl.pallas_call(
            functools.partial(down_kernel, lanes, spots),
            in_specs=[VMEM] * (lanes + subs),
            out_specs=VMEM,
            out_shape=jax.ShapeDtypeStruct((lanes * per_message, 2 * ADAPTER_RANK), f32),
            compiler_params=pltpu.CompilerParams(vmem_limit_bytes=16 * MIB),
            cost_estimate=SMALL,
            name="down",
        )(*arrived[chunk][:0:-1], held(arrived[chunk][0], after), *down_maps)
        return from_others(partial_latent, "heads")

    def up(partials, after):
        message = jax.ShapeDtypeStruct((per_message, query_columns + value_columns), bf16)
        messages = pl.pallas_call(
            functools.partial(up_kernel, heads, subs, spots),
            in_specs=[VMEM] * (heads + 2 * subs),
            out_specs=[VMEM] * lanes,
            out_shape=[message] * lanes,
            compiler_params=pltpu.CompilerParams(vmem_limit_bytes=24 * MIB),
            cost_estimate=SMALL,
            name="up",
        )(held(partials[0], after), *partials[1:], *query_maps, *value_maps)
        return messages

    half_width = HEAD_WIDTH // 2
    position = jnp.concatenate([cache_fill_length + step for step in range(steps)]).astype(f32)
    freq = jnp.exp(jnp.arange(half_width, dtype=f32) * (-math.log(1000000.0) / half_width))
    freq = jnp.concatenate([freq, freq])
    angle = position[:, None] * freq
    sign = jnp.where(jnp.arange(HEAD_WIDTH) < half_width, -1.0, 1.0).astype(f32)
    cosine = jnp.cos(angle)
    sine_part = jnp.sin(angle) * sign

    returned = []
    after = qkv
    for chunk in range(chunks):
        partials = down(chunk, after)
        qkv.append(project(partials[0]))
        after = up(partials, qkv)
        messages = list(after)
        if chunk:
            for lane in range(1, lanes):
                messages[lane] = held(messages[lane], returned[-1][lane])
        returned.append(traded(messages, "streams"))

    length_row = cache_fill_length.reshape(1, rows)
    block = flow_most * chunk_steps
    earlier, along, alongs = [], [], []
    for chunk in range(chunks):
        last = chunk == chunks - 1
        message = jax.ShapeDtypeStruct((subs * block, query_columns), bf16)
        fresh = jax.ShapeDtypeStruct((chunk_rows, 2 * value_columns), f32)
        rows_of = lambda shape: pl.BlockSpec(shape, lambda i, chunk=chunk: (chunk, 0))
        results = pl.pallas_call(
            functools.partial(
                attend_kernel,
                chunk * chunk_steps,
                chunk_steps,
                rows,
                cache,
                groups,
                lanes,
                subs,
                last,
            ),
            grid=(1,),
            in_specs=[whole(places.shape), whole(length_row.shape)]
            + [rows_of((chunk_rows, HEAD_WIDTH))] * 2
            + [whole(rotated_key_cache.shape)] * 2
            + [rows_of((chunk_rows, part.shape[1])) for part in qkv]
            + [whole((per_message, query_columns + value_columns))] * lanes
            + [whole(block_rows.shape) for block_rows in earlier],
            out_specs=[whole(fresh.shape)] * (not last) + [whole(message.shape)] * lanes,
            out_shape=[fresh] * (not last) + [message] * lanes,
            scratch_shapes=[
                pltpu.VMEM((chunk_rows, query_columns + value_columns), f32),
                pltpu.VMEM((chunk_rows, query_columns), f32),
                pltpu.VMEM((rows, BATCH * cache), f32),
            ],
            compiler_params=pltpu.CompilerParams(vmem_limit_bytes=32 * MIB),
            cost_estimate=SMALL,
            name="attend",
        )(
            places if chunk else held(places, after),
            length_row,
            cosine,
            sine_part,
            rotated_key_cache,
            value_cache_rows,
            *qkv,
            *returned[chunk][::-1],
            *earlier,
        )
        if not last:
            earlier, results = [results[0]], results[1:]
        results = list(results)
        for lane in range(1, lanes):
            if not alongs:
                results[lane] = held(results[lane], returned[-1][lanes - lane])
        along = traded(results, "streams")
        alongs.append(along)

    landed, found = [], []
    for chunk, along in enumerate(alongs):
        base = len(landed)
        landed += along
        where = [[(base + lane, 0)] for lane in range(lanes)]
        for shift in range(1, subs):
            pairs = [(core, core ^ shift) for core in range(subs)]
            span = slice(shift * block, (shift + 1) * block)
            if chunk < chunks - 1:
                joined = jnp.concatenate([block_rows[span] for block_rows in along])
                for lane in range(lanes):
                    where[lane].append((len(landed), lane * block))
                landed.append(lax.ppermute(joined, "sub", pairs))
            else:
                for lane, block_rows in enumerate(along):
                    where[lane].append((len(landed), shift * block))
                    landed.append(lax.ppermute(block_rows, "sub", pairs))
        found.append(where)

    flow = pl.pallas_call(
        functools.partial(place_kernel, found, lanes, subs, flow_most),
        in_specs=[VMEM] * len(landed),
        out_specs=VMEM,
        out_shape=jax.ShapeDtypeStruct((flow_lanes * flow_most, steps, query_columns), bf16),
        compiler_params=pltpu.CompilerParams(vmem_limit_bytes=24 * MIB),
        cost_estimate=SMALL,
        name="place",
    )(*landed)
    return flow[None]


def solution(mesh):
    placed = (
        P(None, ("groups", "streams", "sub"), None),
        P(),
        P(None, "heads"),
        P("heads"),
        P(("groups", "streams", "sub"), None),
        P("groups"),
        P(("groups", "streams", "sub")),
        P(("groups", "streams", "sub"), None, "heads"),
        P(("groups", "streams", "sub"), None, "heads"),
        P(("groups", "streams", "sub"), "heads", None),
        P(("groups", "streams", "sub"), None, "heads"),
        P(("groups", "streams", "sub"), None, "heads"),
        P(("groups", "streams", "sub"), None),
    )
    return jax.shard_map(
        on_device,
        mesh=mesh,
        in_specs=placed,
        out_specs=P(("groups", "streams", "sub"), None, None, "heads"),
        check_vma=False,
    )
```
